32 devices in a mesh: rows: 4 (over y, x), seq: 8 (over z, core).
Axes of the slice: x: 2, y: 2, z: 4, core: 2. Of those that a mesh axis runs over, the one named last changes fastest.
Arguments:
- tokens: bfloat16 [16, 1024, 768], P('rows', 'seq'), may hold values from -6 to 6
- cotangent: bfloat16 [16, 1024, 768], P('rows', 'seq'), may hold values from -6 to 6
- qkv_weight: float32 [768, 2304], P(('rows', 'seq')), may hold values from -0.21875 to 0.21875
- out_weight: float32 [768, 768], P(('rows', 'seq')), may hold values from -0.875 to 0.875
- up_weight: float32 [768, 3072], P(('rows', 'seq')), may hold values from -0.21875 to 0.21875
- down_weight: float32 [3072, 768], P(('rows', 'seq')), may hold values from -0.109375 to 0.109375
- vectors: float32 [12, 768], P(None, ('rows', 'seq')), may hold values from -1.2 to 1.6
- taps: float32 [12, 33], replicated, may hold values from -0.3 to 0.3
- qkv_first: float32 [768, 2304], P(('rows', 'seq')), may hold values from -80 to 80
- qkv_second: float32 [768, 2304], P(('rows', 'seq')), may hold values from 13.1072 to 52.4288
- out_first: float32 [768, 768], P(('rows', 'seq')), may hold values from -24 to 24
- out_second: float32 [768, 768], P(('rows', 'seq')), may hold values from 1.47456 to 5.89824
- up_first: float32 [768, 3072], P(('rows', 'seq')), may hold values from -24 to 24
- up_second: float32 [768, 3072], P(('rows', 'seq')), may hold values from 1.47456 to 5.89824
- down_first: float32 [3072, 768], P(('rows', 'seq')), may hold values from -48 to 48
- down_second: float32 [3072, 768], P(('rows', 'seq')), may hold values from 5.89824 to 23.59296
- vec_first: float32 [12, 768], P(None, ('rows', 'seq')), may hold values from -80 to 80
- vec_second: float32 [12, 768], P(None, ('rows', 'seq')), may hold values from 16.384 to 65.536
- tap_first: float32 [12, 33], replicated, may hold values from -1280 to 1280
- tap_second: float32 [12, 33], replicated, may hold values from 3276.8 to 13107.2
Outputs:
- layer_out: bfloat16 [16, 1024, 768], P('rows', 'seq')
- input_grad: bfloat16 [16, 1024, 768], P('rows', 'seq')
- new_qkv_first: float32 [768, 2304], P(('rows', 'seq'))
- new_qkv_second: float32 [768, 2304], P(('rows', 'seq'))
- new_qkv_weight: float32 [768, 2304], P(('rows', 'seq'))
- new_out_first: float32 [768, 768], P(('rows', 'seq'))
- new_out_second: float32 [768, 768], P(('rows', 'seq'))
- new_out_weight: float32 [768, 768], P(('rows', 'seq'))
- new_up_first: float32 [768, 3072], P(('rows', 'seq'))
- new_up_second: float32 [768, 3072], P(('rows', 'seq'))
- new_up_weight: float32 [768, 3072], P(('rows', 'seq'))
- new_down_first: float32 [3072, 768], P(('rows', 'seq'))
- new_down_second: float32 [3072, 768], P(('rows', 'seq'))
- new_down_weight: float32 [3072, 768], P(('rows', 'seq'))
- new_vec_first: float32 [12, 768], P(None, ('rows', 'seq'))
- new_vec_second: float32 [12, 768], P(None, ('rows', 'seq'))
- new_vectors: float32 [12, 768], P(None, ('rows', 'seq'))
- new_tap_first: float32 [12, 33], replicated
- new_tap_second: float32 [12, 33], replicated
- new_taps: float32 [12, 33], replicated
The draws below stay inside these ranges and needn't reach their ends.
All inputs are finite; a program needn't handle non-finite values.
Results may differ from the reference program's by a relative error of at most 0.033.
Values may be sent and summed in bfloat16 or wider, within the bound.
A program may use at most 256 MiB of HBM per device.

```python
import math
import jax
import jax.numpy as jnp
from jax import lax

D = 768
HEADS = 12
HEAD_DIM = 64
FF = 3072
LAND = 64
KSIZE = 33
PINV_ITERS = 6
SEQ_LEN = 1024
BATCH = 16
TOTAL_TOKENS = 16384
NVEC = 12


def draw_tokens(key, part):
    keys_all = jax.random.split(key, 4)
    rough = jax.random.truncated_normal(keys_all[0], -4.0, 4.0, (BATCH, SEQ_LEN, D), jnp.float32)
    amplitude = jax.random.uniform(keys_all[1], (BATCH, 1, D), jnp.float32, 0.8, 2.0)
    frequency = jax.random.randint(keys_all[2], (BATCH, 1, D), 1, 9).astype(jnp.float32)
    phase_shift = jax.random.uniform(keys_all[3], (BATCH, 1, D), jnp.float32, -math.pi, math.pi)
    position = jnp.arange(SEQ_LEN, dtype=jnp.float32)[None, :, None] / SEQ_LEN
    return (rough + amplitude * jnp.sin(2.0 * math.pi * frequency * position + phase_shift)).astype(jnp.bfloat16)


def draw_vectors(key, part):
    raw_rows = jax.random.truncated_normal(key, -4.0, 4.0, (NVEC, D), jnp.float32)
    row_index = jnp.arange(NVEC)
    gain_rows = (row_index == 6) | (row_index == 7)
    return jnp.where(gain_rows[:, None], 1.0 + 0.15 * raw_rows, 0.3 * raw_rows)


def block_levels(own_key, dims, cuts, smallest, high):
    factor_of = 1.0
    for dim, parts in cuts:
        draws = jax.random.uniform(jax.random.fold_in(jax.random.fold_in(own_key, 6), dim), (parts,), jnp.float32, smallest / len(cuts), high / len(cuts))
        factor_of = factor_of * jnp.repeat(jnp.exp(draws), dims[dim] // parts).reshape((-1,) + (1,) * (len(dims) - 1 - dim))
    return factor_of


def noise(own_key, shape, scale, limit, cuts=(), held_as=jnp.bfloat16):
    values = scale * jax.random.normal(own_key, shape, jnp.float32)
    if cuts:
        values = values * block_levels(own_key, shape, cuts, -0.22, 0.18)
    return jnp.clip(values, -limit, limit).astype(held_as)


def setup_inputs(seed: int = 0) -> dict:
    key_list = jax.random.split(jax.random.key(seed), 21)
    return {
        "tokens": draw_tokens(jax.random.fold_in(key_list[20], 71), 0),
        "cotangent": noise(key_list[1], (BATCH, SEQ_LEN, D), 1.0, 6.0, ((0, 4), (1, 8))),
        "qkv_weight": noise(key_list[2], (D, 3 * D), D ** -0.5, 0.21875, ((0, 32),), jnp.float32),
        "out_weight": noise(key_list[3], (D, D), (D // 16) ** -0.5, 0.875, ((0, 32),), jnp.float32),
        "up_weight": noise(key_list[4], (D, FF), D ** -0.5, 0.21875, ((0, 32),), jnp.float32),
        "down_weight": noise(key_list[5], (FF, D), FF ** -0.5, 0.109375, ((0, 32),), jnp.float32),
        "vectors": draw_vectors(jax.random.fold_in(key_list[20], 71), 0),
        "taps": noise(key_list[7], (HEADS, KSIZE), 0.06, 0.3, (), jnp.float32),
        "qkv_first": noise(key_list[8], (D, 3 * D), (0.1 * TOTAL_TOKENS ** 0.5), 80.0, ((0, 32),), jnp.float32),
        "qkv_second": jnp.clip(jnp.exp(math.log(52.4288) - 1.3862944 * jax.random.uniform(key_list[9], (D, 3 * D), jnp.float32) ** block_levels(key_list[9], (D, 3 * D), ((0, 32),), -0.2, 0.2)), 13.1072, 52.4288),
        "out_first": noise(key_list[10], (D, D), (0.033 * TOTAL_TOKENS ** 0.5), 24.0, ((0, 32),), jnp.float32),
        "out_second": jnp.clip(jnp.exp(math.log(5.89824) - 1.3862944 * jax.random.uniform(key_list[11], (D, D), jnp.float32) ** block_levels(key_list[11], (D, D), ((0, 32),), -0.2, 0.2)), 1.47456, 5.89824),
        "up_first": noise(key_list[12], (D, FF), (0.033 * TOTAL_TOKENS ** 0.5), 24.0, ((0, 32),), jnp.float32),
        "up_second": jnp.clip(jnp.exp(math.log(5.89824) - 1.3862944 * jax.random.uniform(key_list[13], (D, FF), jnp.float32) ** block_levels(key_list[13], (D, FF), ((0, 32),), -0.2, 0.2)), 1.47456, 5.89824),
        "down_first": noise(key_list[14], (FF, D), (0.066 * TOTAL_TOKENS ** 0.5), 48.0, ((0, 32),), jnp.float32),
        "down_second": jnp.clip(jnp.exp(math.log(23.59296) - 1.3862944 * jax.random.uniform(key_list[15], (FF, D), jnp.float32) ** block_levels(key_list[15], (FF, D), ((0, 32),), -0.2, 0.2)), 5.89824, 23.59296),
        "vec_first": noise(key_list[16], (NVEC, D), (0.11 * TOTAL_TOKENS ** 0.5), 80.0, ((1, 32),), jnp.float32),
        "vec_second": jnp.clip(jnp.exp(math.log(65.536) - 1.3862944 * jax.random.uniform(key_list[17], (NVEC, D), jnp.float32) ** block_levels(key_list[17], (NVEC, D), ((1, 32),), -0.2, 0.2)), 16.384, 65.536),
        "tap_first": noise(key_list[18], (HEADS, KSIZE), (1.6 * TOTAL_TOKENS ** 0.5), 1280.0, (), jnp.float32),
        "tap_second": jnp.clip(jnp.exp(jax.random.uniform(key_list[19], (HEADS, KSIZE), jnp.float32, math.log(3276.8), math.log(13107.2))), 3276.8, 13107.2),
    }


@jax.custom_vjp
def reduced_precision(v):
    return lax.optimization_barrier(v.astype(jnp.bfloat16)).astype(jnp.float32)

@jax.custom_vjp
def low_back(v):
    return v

def low_keep(v):
    return (reduced_precision(v), None)

def low_pass(kept, grad):
    return (grad,)

def back_keep(v):
    return (v, None)

def back_low(kept, grad):
    return (reduced_precision(grad),)
reduced_precision.defvjp(low_keep, low_pass)
low_back.defvjp(back_keep, back_low)
top_precision = lax.Precision.HIGHEST
norm_eps = 1e-05
beta_one = 0.9
beta_two = 0.999
corr_one = 1.0 - 0.9 ** 10
corr_two = 1.0 - 0.999 ** 10
adam_eps = 1e-08
decay_rate = 0.01
rate_matrix = 0.03
rate_output = 0.12
rate_vector = 0.3
rate_taps = 0.08

def layer_norm(residual, gain_row, shift_row):
    center = residual - lax.optimization_barrier(jnp.mean(residual, axis=-1, keepdims=True))
    spread = lax.optimization_barrier(jnp.mean(center * center, axis=-1, keepdims=True))
    return center * lax.rsqrt(spread + norm_eps) * gain_row + shift_row

def normalized_rows(scores):
    expo = jnp.exp(scores - lax.optimization_barrier(jnp.max(scores, axis=-1, keepdims=True)))
    return expo / lax.optimization_barrier(jnp.sum(expo, axis=-1, keepdims=True))

def gelu_exact(inputs):
    return jax.nn.gelu(inputs, approximate=False)

def pseudo_inverse(matrix):
    identity = jnp.eye(matrix.shape[-1], dtype=jnp.float32)
    approx = jnp.swapaxes(matrix, -1, -2) / lax.optimization_barrier(jnp.sum(matrix * matrix, axis=(-2, -1), keepdims=True))
    for sweep_index in range(PINV_ITERS):
        product = jnp.matmul(matrix, approx, precision=top_precision)
        inner_term = 7.0 * identity - product
        inner_term = 15.0 * identity - jnp.matmul(product, inner_term, precision=top_precision)
        inner_term = 13.0 * identity - jnp.matmul(product, inner_term, precision=top_precision)
        approx = 0.25 * jnp.matmul(approx, inner_term, precision=top_precision)
    return approx

def adam_step(weight, first_moment, second, gradient, step_rate, decay_coef):
    new_first = beta_one * first_moment + (1.0 - beta_one) * gradient
    new_second = beta_two * second + (1.0 - beta_two) * gradient * gradient
    update = new_first / corr_one / (jnp.sqrt(new_second / corr_two) + adam_eps)
    return (new_first, new_second, weight - step_rate * (update + decay_coef * weight))

def layer(tokens, qkv_weight, out_weight, up_weight, down_weight, vectors, taps):
    full_qkv = reduced_precision(qkv_weight)
    full_out = reduced_precision(out_weight)
    full_up = reduced_precision(up_weight)
    full_down = reduced_precision(down_weight)
    full_vec = reduced_precision(vectors)
    seq_len = tokens.shape[0]
    seg_len = seq_len // LAND
    logit_scale_factor = HEAD_DIM ** (-0.5)
    project = jnp.matmul(tokens, full_qkv, precision=top_precision)
    queries = reduced_precision(low_back(project[:, :D] + full_vec[0]))
    key_rows = reduced_precision(low_back(project[:, D:2 * D]))
    values = reduced_precision(low_back(project[:, 2 * D:] + full_vec[1]))
    land_q = reduced_precision(lax.optimization_barrier(jnp.mean(queries.reshape(LAND, seg_len, D), axis=1)))
    land_k = reduced_precision(lax.optimization_barrier(jnp.mean(key_rows.reshape(LAND, seg_len, D), axis=1)))
    query_heads = queries.reshape(seq_len, HEADS, HEAD_DIM)
    key_heads = key_rows.reshape(seq_len, HEADS, HEAD_DIM)
    value_heads = values.reshape(seq_len, HEADS, HEAD_DIM)
    landmark_query_heads = land_q.reshape(LAND, HEADS, HEAD_DIM)
    landmark_key_heads = land_k.reshape(LAND, HEADS, HEAD_DIM)
    score_one = low_back(jnp.einsum('thd,lhd->htl', query_heads, landmark_key_heads, precision=top_precision) * logit_scale_factor)
    prob_one = normalized_rows(score_one)
    second_probability = normalized_rows(jnp.einsum('zbs,ibs->bzi', landmark_query_heads, landmark_key_heads, precision=top_precision) * logit_scale_factor)
    inverse_matrix = pseudo_inverse(second_probability)
    score_three = low_back(jnp.einsum('lhd,thd->hlt', landmark_query_heads, key_heads, precision=top_precision) * logit_scale_factor)
    expo_three = jnp.exp(score_three - lax.optimization_barrier(jnp.max(score_three, axis=-1, keepdims=True)))
    numer = jnp.einsum('hlt,thd->lhd', reduced_precision(expo_three), value_heads, precision=top_precision)
    denom = jnp.swapaxes(lax.optimization_barrier(jnp.sum(expo_three, axis=-1)), 0, 1)[:, :, None]
    landmark_value_rows = low_back(numer / denom)
    mixing_kernel = reduced_precision(jnp.einsum('vwe,evb->wvb', inverse_matrix, landmark_value_rows, precision=top_precision))
    attend = jnp.einsum('htl,lhd->thd', reduced_precision(prob_one), mixing_kernel, precision=top_precision).reshape(seq_len, D)
    tap_chan = jnp.repeat(taps, HEAD_DIM, axis=0)
    reach_width = KSIZE // 2
    padded_values = jnp.pad(values, ((reach_width, reach_width), (0, 0)))
    conv_out = jnp.zeros((seq_len, D), jnp.float32)
    for offset in range(KSIZE):
        conv_out = conv_out + tap_chan[:, offset] * padded_values[offset:offset + seq_len]
    attn_low = reduced_precision(low_back(attend + conv_out))
    branch = low_back(jnp.matmul(attn_low, full_out, precision=top_precision) + full_vec[2])
    normed = layer_norm(tokens + branch, full_vec[6], full_vec[3])
    hidden_pre = low_back(jnp.matmul(reduced_precision(normed), full_up, precision=top_precision) + full_vec[8:].reshape(FF))
    active = reduced_precision(gelu_exact(hidden_pre))
    ff_out = low_back(jnp.matmul(active, full_down, precision=top_precision) + full_vec[4])
    return layer_norm(normed + ff_out, full_vec[7], full_vec[5])

def reference(tokens, cotangent, qkv_weight, out_weight, up_weight, down_weight, vectors, taps, qkv_first, qkv_second, out_first, out_second, up_first, up_second, down_first, down_second, vec_first, vec_second, tap_first, tap_second):
    params = (qkv_weight, out_weight, up_weight, down_weight, vectors, taps)

    def one_sequence(carry, pair):
        seq_in, seq_cot = pair
        result, pull = jax.vjp(layer, seq_in.astype(jnp.float32), *params)
        grads = pull(seq_cot.astype(jnp.float32))
        carry = tuple((total + grad_part for total, grad_part in zip(carry, grads[1:])))
        return (carry, (result.astype(jnp.bfloat16), grads[0].astype(jnp.bfloat16)))
    zero_grads = tuple((jnp.zeros_like(item) for item in params))
    totals, outputs = lax.scan(one_sequence, zero_grads, (tokens, cotangent))
    layer_out, input_grad = outputs
    new_qkv = adam_step(qkv_weight, qkv_first, qkv_second, totals[0], rate_matrix, decay_rate)
    new_out = adam_step(out_weight, out_first, out_second, totals[1], rate_output, decay_rate)
    new_up = adam_step(up_weight, up_first, up_second, totals[2], rate_matrix, decay_rate)
    new_down = adam_step(down_weight, down_first, down_second, totals[3], rate_matrix, decay_rate)
    new_vec = adam_step(vectors, vec_first, vec_second, totals[4], rate_vector, 0.0)
    new_taps = adam_step(taps, tap_first, tap_second, totals[5], rate_taps, 0.0)
    return (layer_out, input_grad, new_qkv[0], new_qkv[1], new_qkv[2], new_out[0], new_out[1], new_out[2], new_up[0], new_up[1], new_up[2], new_down[0], new_down[1], new_down[2], new_vec[0], new_vec[1], new_vec[2], new_taps[0], new_taps[1], new_taps[2])
```

```python
import functools

import jax
import jax.numpy as jnp
from jax import lax
from jax.experimental import pallas as pl
from jax.experimental.pallas import tpu as pltpu
from jax.sharding import PartitionSpec as P

BF = jnp.bfloat16
F32 = jnp.float32
MESH = pl.DeviceIdType.MESH


def remote(src, dst, send_sem, recv_sem, device):
    return pltpu.make_async_remote_copy(
        src_ref=src, dst_ref=dst, send_sem=send_sem, recv_sem=recv_sem,
        device_id=device, device_id_type=MESH,
    )


def place():
    row, spot = lax.axis_index("rows"), lax.axis_index("seq")
    line, core = spot // 2, spot % 2
    flip_one = row + 1 - 2 * (row % 2)
    flip_two = row + 2 - 4 * (row // 2)
    first = (1 - core) * flip_one + core * flip_two
    second = (1 - core) * flip_two + core * flip_one
    return row, line, core, first, second, 3 - row


def greet(devices):
    barrier = pltpu.get_barrier_semaphore()
    for device in devices:
        pl.semaphore_signal(barrier, inc=1, device_id=device, device_id_type=MESH)
    pl.semaphore_wait(barrier, len(devices))


def gather_kernel(line_size, n_w, *refs):
    ins, outs = refs[:n_w], refs[n_w : 2 * n_w]
    asm, stage = refs[2 * n_w : 3 * n_w], refs[3 * n_w : 4 * n_w]
    send, recv, local = refs[4 * n_w :]
    row, line, core, first, second, across = place()
    own_spot, sibling = 2 * line + core, (row, 2 * line + 1 - core)
    peers = [(row, 2 * ((line + k) % line_size) + core) for k in range(1, line_size)]
    to_first, to_second = (first, own_spot), (second, own_spot)
    greet(peers + [to_first, to_second, sibling])
    rows = [x.shape[0] for x in ins]
    half = [x.shape[1] // 2 for x in ins]
    started = []

    def go(w, k, src, dst, device):
        copy = remote(src, dst, send.at[w, k], recv.at[w, k], device)
        copy.start()
        started.append(copy)
        return copy

    def cols(w, which):
        return pl.ds(pl.multiple_of(which * half[w], 128), half[w])

    def slab(w, index):
        size = 2 * rows[w] * line_size
        return outs[w].at[pl.ds(pl.multiple_of(index * size, size), size), cols(w, core)]

    asm_copy, z_copy, own_copy, hop, sib = {}, {}, {}, {}, {}
    z0 = line_size
    for w in range(n_w):
        part = pl.ds(pl.multiple_of(core * rows[w], 8), rows[w])
        asm_copy[w] = go(w, 0, ins[w].at[:, cols(w, 1 - core)], asm[w].at[part, :], sibling)
        asm[w][part, :] = ins[w][:, cols(w, core)]

    def spread(w):
        asm_copy[w].wait_recv()
        stage[w][...] = asm[w][...].astype(BF)
        size = 2 * rows[w]
        at = pl.ds(pl.multiple_of((row * line_size + line) * size, size), size)
        block = outs[w].at[at, cols(w, core)]
        z_copy[w] = [go(w, 1 + k, stage[w], block, peers[k]) for k in range(line_size - 1)]
        own_copy[w] = pltpu.make_async_copy(stage[w], block, local.at[w])
        own_copy[w].start()

    def step_one(w):
        own_copy[w].wait()
        for copy in z_copy[w]:
            copy.wait_recv()
        mine = slab(w, row)
        hop[w] = [go(w, z0, mine, mine, to_first), go(w, z0 + 1, mine, mine, to_second)]
        sib[w] = [go(w, z0 + 3, mine, mine, sibling)]

    def step_two(w):
        hop[w][0].wait_recv()
        got = slab(w, first)
        hop[w].append(go(w, z0 + 2, got, got, to_second))
        sib[w].append(go(w, z0 + 4, got, got, sibling))

    def step_three(w):
        hop[w][1].wait_recv()
        got = slab(w, second)
        sib[w].append(go(w, z0 + 5, got, got, sibling))
        hop[w][2].wait_recv()
        got = slab(w, across)
        sib[w].append(go(w, z0 + 6, got, got, sibling))

    for w in range(n_w):
        spread(w)
    for t in range(n_w + 2):
        if t < n_w:
            step_one(t)
        if 0 <= t - 1 < n_w:
            step_two(t - 1)
        if 0 <= t - 2 < n_w:
            step_three(t - 2)
    for w in range(n_w):
        for copy in sib[w]:
            copy.wait_recv()
    for copy in started:
        copy.wait_send()


def gather_weights(shards, seq_size):
    line_size, n_w = seq_size // 2, len(shards)
    n_dev = 4 * seq_size
    n_sem = line_size + 7
    vmem = pl.BlockSpec(memory_space=pltpu.VMEM)
    return pl.pallas_call(
        functools.partial(gather_kernel, line_size, n_w),
        out_shape=[jax.ShapeDtypeStruct((n_dev * x.shape[0], x.shape[1]), BF) for x in shards],
        in_specs=[vmem] * n_w,
        out_specs=[pl.BlockSpec(memory_space=pltpu.HBM)] * n_w,
        scratch_shapes=[pltpu.VMEM((2 * x.shape[0], x.shape[1] // 2), F32) for x in shards]
        + [pltpu.VMEM((2 * x.shape[0], x.shape[1] // 2), BF) for x in shards]
        + [
            pltpu.SemaphoreType.DMA((n_w, n_sem)),
            pltpu.SemaphoreType.DMA((n_w, n_sem)),
            pltpu.SemaphoreType.DMA((n_w,)),
        ],
        compiler_params=pltpu.CompilerParams(
            collective_id=0, has_side_effects=True, vmem_limit_bytes=32 * 1024 * 1024
        ),
        name="gather_weights",
    )(*shards)


def scatter_kernel(line_size, n_w, *refs):
    ins, outs = refs[:n_w], refs[n_w : 2 * n_w]
    acc, buf0, buf1, buf2, buf3, fin = [refs[(2 + i) * n_w : (3 + i) * n_w] for i in range(6)]
    send, recv, local = refs[8 * n_w :]
    row, line, core, first, second, across = place()
    own_spot, sibling = 2 * line + core, (row, 2 * line + 1 - core)
    peers = [(row, 2 * ((line + k) % line_size) + core) for k in range(1, line_size)]
    to_first, to_second = (first, own_spot), (second, own_spot)
    greet(peers + [to_first, to_second, sibling])
    rows = [x.shape[0] for x in outs]
    half = [x.shape[1] // 2 for x in ins]
    started = []
    copies = {}

    def go(w, k, src, dst, device):
        copy = remote(src, dst, send.at[w, k], recv.at[w, k], device)
        copy.start()
        started.append(copy)
        return copy

    def cols(w, which):
        return pl.ds(pl.multiple_of(which * half[w], 128), half[w])

    def size(w):
        return 2 * rows[w] * line_size

    def slab(w, index):
        return pl.ds(pl.multiple_of(index * size(w), size(w)), size(w))

    def add(w, index, other, other_start):
        step = 48
        base = index * size(w)

        def one(i, carry):
            at = pl.ds(pl.multiple_of(base + i * step, 16), step)
            there = pl.ds(pl.multiple_of(other_start + i * step, 16), step)
            acc[w][at, :] = acc[w][at, :] + other[there, :]
            return carry

        lax.fori_loop(0, size(w) // step, one, 0)

    def open_up(w):
        copies[w, 0] = go(w, 0, ins[w].at[:, cols(w, 1 - core)], buf0[w], sibling)
        copies[w, "own"] = pltpu.make_async_copy(ins[w].at[:, cols(w, core)], acc[w], local.at[w])
        copies[w, "own"].start()

    def step_one(w):
        copies[w, "own"].wait()
        copies[w, 0].wait_recv()
        add(w, across, buf0[w], across * size(w))
        copies[w, 1] = go(w, 1, acc[w].at[slab(w, across), :], buf1[w].at[0], to_second)
        add(w, second, buf0[w], second * size(w))
        copies[w, 2] = go(w, 2, acc[w].at[slab(w, second), :], buf1[w].at[1], to_second)
        add(w, first, buf0[w], first * size(w))
        add(w, row, buf0[w], row * size(w))

    def step_two(w):
        copies[w, 1].wait_recv()
        add(w, first, buf1[w].at[0], 0)
        copies[w, 3] = go(w, 3, acc[w].at[slab(w, first), :], buf2[w], to_first)
        copies[w, 2].wait_recv()
        add(w, row, buf1[w].at[1], 0)

    def step_three(w):
        copies[w, 3].wait_recv()
        add(w, row, buf2[w], 0)
        block = 2 * rows[w]
        for k in range(1, line_size):
            there = (line + k) % line_size
            at = pl.ds(pl.multiple_of((row * line_size + there) * block, block), block)
            copies[w, 3 + k] = go(w, 3 + k, acc[w].at[at, :], buf3[w].at[line], peers[k - 1])
        at = pl.ds(pl.multiple_of((row * line_size + line) * block, block), block)
        buf3[w][line] = acc[w][at, :]

    def step_four(w):
        for k in range(1, line_size):
            copies[w, 3 + k].wait_recv()
        total = buf3[w][0].astype(F32)
        for k in range(1, line_size):
            total = total + buf3[w][k].astype(F32)
        fin[w][...] = total
        part = pl.ds(pl.multiple_of((1 - core) * rows[w], 8), rows[w])
        copies[w, 9] = go(w, 3 + line_size, fin[w].at[part, :], outs[w].at[:, cols(w, core)], sibling)
        part = pl.ds(pl.multiple_of(core * rows[w], 8), rows[w])
        outs[w][:, cols(w, core)] = fin[w][part, :]

    for w in range(n_w):
        open_up(w)
    for t in range(n_w + 3):
        if t < n_w:
            step_one(t)
        if 0 <= t - 1 < n_w:
            step_two(t - 1)
        if 0 <= t - 2 < n_w:
            step_three(t - 2)
        if 0 <= t - 3 < n_w:
            step_four(t - 3)
    for w in range(n_w):
        copies[w, 9].wait_recv()
    for copy in started:
        copy.wait_send()


def scatter_grads(grads, seq_size):
    line_size, n_w = seq_size // 2, len(grads)
    n_dev = 4 * seq_size
    n_sem = line_size + 4
    rows = [x.shape[0] // n_dev for x in grads]
    half = [x.shape[1] // 2 for x in grads]
    kinds = [x.dtype for x in grads]
    vmem = pl.BlockSpec(memory_space=pltpu.VMEM)
    every = range(n_w)
    quarter = [2 * rows[w] * line_size for w in every]
    return pl.pallas_call(
        functools.partial(scatter_kernel, line_size, n_w),
        out_shape=[jax.ShapeDtypeStruct((rows[w], 2 * half[w]), F32) for w in every],
        in_specs=[pl.BlockSpec(memory_space=pltpu.HBM)] * n_w,
        out_specs=[vmem] * n_w,
        scratch_shapes=[pltpu.VMEM((4 * quarter[w], half[w]), kinds[w]) for w in every]
        + [pltpu.VMEM((4 * quarter[w], half[w]), kinds[w]) for w in every]
        + [pltpu.VMEM((2, quarter[w], half[w]), kinds[w]) for w in every]
        + [pltpu.VMEM((quarter[w], half[w]), kinds[w]) for w in every]
        + [pltpu.VMEM((line_size, 2 * rows[w], half[w]), kinds[w]) for w in every]
        + [pltpu.VMEM((2 * rows[w], half[w]), F32) for w in every]
        + [
            pltpu.SemaphoreType.DMA((n_w, n_sem)),
            pltpu.SemaphoreType.DMA((n_w, n_sem)),
            pltpu.SemaphoreType.DMA((n_w,)),
        ],
        compiler_params=pltpu.CompilerParams(
            collective_id=1, has_side_effects=True, vmem_limit_bytes=48 * 1024 * 1024
        ),
        name="scatter_grads",
    )(*grads)

LAND = 64
PINV_ITERS = 6


top_precision = lax.Precision.HIGHEST
norm_eps = 1e-05
beta_one = 0.9
beta_two = 0.999
corr_one = 1.0 - 0.9**10
corr_two = 1.0 - 0.999**10
adam_eps = 1e-08
decay_rate = 0.01
rate_matrix = 0.03
rate_output = 0.12
rate_vector = 0.3
rate_taps = 0.08


def with_halo(x, sides, width):
    for axis, dim in sides:
        size, length = (lax.axis_size(axis), x.shape[dim])
        up = [(i, (i + 1) % size) for i in range(size - 1)]
        down = [(j, i) for i, j in up]
        last = lax.slice_in_dim(x, length - width, length, axis=dim)
        initial = lax.slice_in_dim(x, 0, width, axis=dim)
        before = lax.ppermute(last, axis, up)
        after = lax.ppermute(initial, axis, down)
        x = jnp.concatenate([before, x, after], axis=dim)
    return x


def layer_norm(residual, gain_row, shift_row):
    center = residual - jnp.mean(residual, axis=-1, keepdims=True)
    spread = jnp.mean(center * center, axis=-1, keepdims=True)
    return center * lax.rsqrt(spread + norm_eps) * gain_row + shift_row


def normalized_rows(scores):
    expo = jnp.exp(scores - jnp.max(scores, axis=-1, keepdims=True))
    return expo / jnp.sum(expo, axis=-1, keepdims=True)


def softmax_back(probability, grad_in):
    return probability * (grad_in - jnp.sum(probability * grad_in, axis=-1, keepdims=True))


def gelu_exact(inputs):
    return jax.nn.gelu(inputs, approximate=False)


def pseudo_inverse(matrix):
    identity = jnp.eye(matrix.shape[-1], dtype=jnp.float32)
    approx = jnp.swapaxes(matrix, -1, -2) / jnp.sum(matrix * matrix, axis=(-2, -1), keepdims=True)
    for sweep_index in range(PINV_ITERS):
        product = jnp.matmul(matrix, approx, precision=top_precision)
        inner_term = 7.0 * identity - product
        inner_term = 15.0 * identity - jnp.matmul(product, inner_term, precision=top_precision)
        inner_term = 13.0 * identity - jnp.matmul(product, inner_term, precision=top_precision)
        approx = 0.25 * jnp.matmul(approx, inner_term, precision=top_precision)
    return approx


def adam_step(weight, first_moment, second, gradient, step_rate, decay_coef):
    new_first = beta_one * first_moment + (1.0 - beta_one) * gradient
    new_second = beta_two * second + (1.0 - beta_two) * gradient * gradient
    update = new_first / corr_one / (jnp.sqrt(new_second / corr_two) + adam_eps)
    return (new_first, new_second, weight - step_rate * (update + decay_coef * weight))


def kernels_fit(rows_each):
    return (
        lax.axis_size("rows") == 4
        and lax.axis_size("seq") % 2 == 0
        and all(rows % 24 == 0 for rows in rows_each)
    )


def all_weights(qkv_weight, out_weight, up_weight, down_weight, vectors):
    axes = ("rows", "seq")
    matrices = (qkv_weight, out_weight, up_weight, down_weight)
    if kernels_fit([x.shape[0] for x in matrices]):
        count = vectors.shape[0]
        table = jnp.pad(vectors.T, ((0, 0), (0, 256 - count)))
        whole = gather_weights(matrices + (table,), lax.axis_size("seq"))
        return (*whole[:4], whole[4][:, :count].T)
    return tuple(
        lax.all_gather(x.astype(BF), axes, axis=0, tiled=True) for x in matrices
    ) + (lax.all_gather(vectors.astype(BF), axes, axis=1, tiled=True),)


def all_grads(grad_qkv, grad_out, grad_up, grad_down, grad_vec, grad_taps):
    axes = ("rows", "seq")
    matrices = (grad_qkv, grad_out, grad_up, grad_down)
    n_dev = lax.axis_size("rows") * lax.axis_size("seq")
    if kernels_fit([x.shape[0] // n_dev for x in matrices]):
        count, width = grad_vec.shape
        heads, taps = grad_taps.shape
        each = jnp.pad(grad_taps, ((0, width // n_dev - heads), (0, 0)))
        small = jnp.concatenate([grad_vec.T, jnp.tile(each, (n_dev, 1))], axis=1)
        small = jnp.pad(small, ((0, 0), (0, 256 - count - taps)))
        sums = scatter_grads([x.astype(BF) for x in matrices] + [small], lax.axis_size("seq"))
        return (*sums[:4], sums[4][:, :count].T, sums[4][:heads, count : count + taps])
    return tuple(
        lax.psum_scatter(x, axes, scatter_dimension=0, tiled=True) for x in matrices
    ) + (
        lax.psum_scatter(grad_vec, axes, scatter_dimension=1, tiled=True),
        lax.psum(grad_taps, axes),
    )


def on_device(
    tokens,
    cotangent,
    qkv_weight,
    out_weight,
    up_weight,
    down_weight,
    vectors,
    taps,
    qkv_first,
    qkv_second,
    out_first,
    out_second,
    up_first,
    up_second,
    down_first,
    down_second,
    vec_first,
    vec_second,
    tap_first,
    tap_second,
):
    seq_count, local_len, model_width = tokens.shape
    head_count, tap_count = taps.shape
    head_size = model_width // head_count
    hidden_width = up_weight.shape[1]
    land_local = LAND // lax.axis_size("seq")
    seg_len = local_len // land_local
    reach_width = tap_count // 2
    logit_scale_factor = head_size ** (-0.5)
    row_count = seq_count * local_len
    head_shape = (seq_count, local_len, head_count, head_size)
    land_shape = (seq_count, LAND, head_count, head_size)
    full_qkv, full_out, full_up, full_down, full_vec = all_weights(
        qkv_weight, out_weight, up_weight, down_weight, vectors
    )
    vec_float = full_vec.astype(jnp.float32)
    flat_in = tokens.reshape(row_count, model_width)
    project = jnp.dot(flat_in, full_qkv, preferred_element_type=jnp.float32)
    queries = (project[:, :model_width] + vec_float[0]).astype(jnp.bfloat16)
    key_rows = project[:, model_width : 2 * model_width].astype(jnp.bfloat16)
    values = (project[:, 2 * model_width :] + vec_float[1]).astype(jnp.bfloat16)
    seg_shape = (seq_count, land_local, seg_len, model_width)
    own_q = jnp.mean(queries.reshape(seg_shape), axis=2, dtype=jnp.float32).astype(jnp.bfloat16)
    own_k = jnp.mean(key_rows.reshape(seg_shape), axis=2, dtype=jnp.float32).astype(jnp.bfloat16)
    land_q, land_k = (
        lax.all_gather(own_q, "seq", axis=1, tiled=True),
        lax.all_gather(own_k, "seq", axis=1, tiled=True),
    )
    query_heads = queries.reshape(head_shape)
    key_heads = key_rows.reshape(head_shape)
    value_heads = values.reshape(head_shape)
    landmark_query_heads = land_q.reshape(land_shape)
    landmark_key_heads = land_k.reshape(land_shape)
    lq_float = landmark_query_heads.astype(jnp.float32)
    lk_float = landmark_key_heads.astype(jnp.float32)
    score_one = (
        jnp.einsum(
            "sthd,slhd->shtl", query_heads, landmark_key_heads, preferred_element_type=jnp.float32
        )
        * logit_scale_factor
    )
    prob_one = normalized_rows(score_one)
    second_probability = normalized_rows(
        jnp.einsum("slhd,smhd->shlm", lq_float, lk_float, precision=top_precision)
        * logit_scale_factor
    )
    inverse_matrix, inverse_pull = jax.vjp(pseudo_inverse, second_probability)
    score_three = (
        jnp.einsum(
            "slhd,sthd->shlt", landmark_query_heads, key_heads, preferred_element_type=jnp.float32
        )
        * logit_scale_factor
    )
    row_max = lax.pmax(jnp.max(score_three, axis=-1), "seq")
    expo_three = jnp.exp(score_three - row_max[..., None])
    numer_local = jnp.einsum(
        "shlt,sthd->slhd",
        expo_three.astype(jnp.bfloat16),
        value_heads,
        preferred_element_type=jnp.float32,
    )
    numer, denom = (
        lax.psum(numer_local.astype(jnp.bfloat16), "seq").astype(jnp.float32),
        lax.psum(jnp.sum(expo_three, axis=-1).astype(jnp.bfloat16), "seq").astype(jnp.float32),
    )
    denom_swap = jnp.swapaxes(denom, 1, 2)[..., None]
    landmark_value_rows = numer / denom_swap
    mixing_kernel = jnp.einsum(
        "shlm,smhd->slhd", inverse_matrix, landmark_value_rows, precision=top_precision
    )
    mix_low = mixing_kernel.astype(jnp.bfloat16)
    prob_low = prob_one.astype(jnp.bfloat16)
    attend = jnp.einsum("shtl,slhd->sthd", prob_low, mix_low, preferred_element_type=jnp.float32)
    attend = attend.reshape(seq_count, local_len, model_width)
    tap_chan = jnp.repeat(taps, head_size, axis=0)
    padded_values = with_halo(
        values.reshape(seq_count, local_len, model_width), (("seq", 1),), reach_width
    )
    conv_out = jnp.zeros((seq_count, local_len, model_width), jnp.float32)
    for offset in range(tap_count):
        conv_out = conv_out + tap_chan[:, offset] * padded_values[
            :, offset : offset + local_len
        ].astype(jnp.float32)
    attn_low = (attend + conv_out).reshape(row_count, model_width).astype(jnp.bfloat16)
    branch = jnp.dot(attn_low, full_out, preferred_element_type=jnp.float32) + vec_float[2]
    resid_one = flat_in.astype(jnp.float32) + branch
    normed, norm_pull_one = jax.vjp(layer_norm, resid_one, vec_float[6], vec_float[3])
    normed_low = normed.astype(jnp.bfloat16)
    hidden_pre = jnp.dot(normed_low, full_up, preferred_element_type=jnp.float32) + vec_float[
        8:
    ].reshape(hidden_width)
    active, gelu_pull = jax.vjp(gelu_exact, hidden_pre)
    active_low = active.astype(jnp.bfloat16)
    ff_out = jnp.dot(active_low, full_down, preferred_element_type=jnp.float32) + vec_float[4]
    layer_out, norm_pull_two = jax.vjp(layer_norm, normed + ff_out, vec_float[7], vec_float[5])
    grad_resid_two, grad_gain_two, grad_shift_two = norm_pull_two(
        cotangent.reshape(row_count, model_width).astype(jnp.float32)
    )
    grad_ff = grad_resid_two.astype(jnp.bfloat16)
    grad_down = jnp.einsum("nf,nd->fd", active_low, grad_ff, preferred_element_type=jnp.float32)
    grad_active = jnp.einsum("nd,fd->nf", grad_ff, full_down, preferred_element_type=jnp.float32)
    grad_hidden = gelu_pull(grad_active)[0].astype(jnp.bfloat16)
    grad_up = jnp.einsum("nd,nf->df", normed_low, grad_hidden, preferred_element_type=jnp.float32)
    grad_normed = (
        jnp.einsum("nf,df->nd", grad_hidden, full_up, preferred_element_type=jnp.float32)
        + grad_resid_two
    )
    grad_resid_one, grad_gain_one, grad_shift_one = norm_pull_one(grad_normed)
    grad_branch = grad_resid_one.astype(jnp.bfloat16)
    grad_out = jnp.einsum("nd,ne->de", attn_low, grad_branch, preferred_element_type=jnp.float32)
    grad_attn = jnp.einsum(
        "ne,de->nd", grad_branch, full_out, preferred_element_type=jnp.float32
    ).astype(jnp.bfloat16)
    grad_attn_heads = grad_attn.reshape(head_shape)
    grad_prob_one = jnp.einsum(
        "sthd,slhd->shtl", grad_attn_heads, mix_low, preferred_element_type=jnp.float32
    )
    mixing_part = jnp.einsum(
        "shtl,sthd->slhd", prob_low, grad_attn_heads, preferred_element_type=jnp.float32
    )
    grad_mixing = lax.psum(mixing_part.astype(jnp.bfloat16), "seq").astype(jnp.float32)
    grad_score_one = softmax_back(prob_one, grad_prob_one).astype(jnp.bfloat16)
    query_local = (
        jnp.einsum(
            "shtl,slhd->sthd",
            grad_score_one,
            landmark_key_heads,
            preferred_element_type=jnp.float32,
        )
        * logit_scale_factor
    )
    land_k_part = (
        jnp.einsum(
            "shtl,sthd->slhd", grad_score_one, query_heads, preferred_element_type=jnp.float32
        )
        * logit_scale_factor
    )
    grad_pad = with_halo(
        grad_attn.reshape(seq_count, local_len, model_width), (("seq", 1),), reach_width
    )
    attn_float = grad_attn.reshape(seq_count, local_len, model_width).astype(jnp.float32)
    conv_back = jnp.zeros((seq_count, local_len, model_width), jnp.float32)
    tap_terms = []
    for offset in range(tap_count):
        start_row = 2 * reach_width - offset
        conv_back = conv_back + tap_chan[:, offset] * grad_pad[
            :, start_row : start_row + local_len
        ].astype(jnp.float32)
        tap_terms.append(
            jnp.sum(
                attn_float * padded_values[:, offset : offset + local_len].astype(jnp.float32),
                axis=(0, 1),
            )
        )
    grad_taps = jnp.sum(
        jnp.stack(tap_terms, axis=1).reshape(head_count, head_size, tap_count), axis=1
    )
    grad_inverse = jnp.einsum(
        "slhd,smhd->shlm", grad_mixing, landmark_value_rows, precision=top_precision
    )
    grad_land_values = jnp.einsum(
        "shlm,slhd->smhd", inverse_matrix, grad_mixing, precision=top_precision
    )
    land_grad_low = grad_land_values.astype(jnp.bfloat16).astype(jnp.float32)
    grad_prob_two = inverse_pull(grad_inverse)[0]
    grad_score_two = softmax_back(second_probability, grad_prob_two)
    query_two = (
        jnp.einsum("shlm,smhd->slhd", grad_score_two, lk_float, precision=top_precision)
        * logit_scale_factor
    )
    key_two = (
        jnp.einsum("shlm,slhd->smhd", grad_score_two, lq_float, precision=top_precision)
        * logit_scale_factor
    )
    grad_numer = land_grad_low / denom_swap
    expo_low = expo_three.astype(jnp.bfloat16).astype(jnp.float32)
    value_three = jnp.einsum("shlt,slhd->sthd", expo_low, grad_numer, precision=top_precision)
    grad_expo = jnp.einsum(
        "slhd,sthd->shlt", grad_numer, value_heads.astype(jnp.float32), precision=top_precision
    )
    grad_denom = jnp.swapaxes(jnp.sum(land_grad_low * landmark_value_rows, axis=-1), 1, 2) / denom
    grad_score_three = (expo_three * (grad_expo - grad_denom[..., None])).astype(jnp.bfloat16)
    land_q_part = (
        jnp.einsum(
            "shlt,sthd->slhd", grad_score_three, key_heads, preferred_element_type=jnp.float32
        )
        * logit_scale_factor
    )
    key_local = (
        jnp.einsum(
            "shlt,slhd->sthd",
            grad_score_three,
            landmark_query_heads,
            preferred_element_type=jnp.float32,
        )
        * logit_scale_factor
    )
    land_q_own, land_k_own = (
        lax.psum_scatter(
            land_q_part.astype(jnp.bfloat16), "seq", scatter_dimension=1, tiled=True
        ).astype(jnp.float32),
        lax.psum_scatter(
            land_k_part.astype(jnp.bfloat16), "seq", scatter_dimension=1, tiled=True
        ).astype(jnp.float32),
    )
    first_land = lax.axis_index("seq") * land_local
    land_q_own = land_q_own + lax.dynamic_slice_in_dim(query_two, first_land, land_local, 1)
    land_k_own = land_k_own + lax.dynamic_slice_in_dim(key_two, first_land, land_local, 1)
    spread_shape = (seq_count, land_local, seg_len, head_count, head_size)
    spread_q = jnp.broadcast_to((land_q_own / seg_len)[:, :, None], spread_shape).reshape(
        head_shape
    )
    spread_k = jnp.broadcast_to((land_k_own / seg_len)[:, :, None], spread_shape).reshape(
        head_shape
    )
    grad_query = (query_local + spread_q).reshape(row_count, model_width)
    grad_key = (key_local + spread_k).reshape(row_count, model_width)
    grad_value = value_three.reshape(row_count, model_width) + conv_back.reshape(
        row_count, model_width
    )
    grad_proj = jnp.concatenate([grad_query, grad_key, grad_value], axis=1).astype(jnp.bfloat16)
    grad_qkv = jnp.einsum("nd,ne->de", flat_in, grad_proj, preferred_element_type=jnp.float32)
    input_grad = (
        jnp.einsum("ne,de->nd", grad_proj, full_qkv, preferred_element_type=jnp.float32)
        + grad_resid_one
    )
    input_grad = input_grad.astype(jnp.bfloat16).reshape(tokens.shape)
    bias_sums = jnp.sum(grad_proj.astype(jnp.float32), axis=0)
    grad_vec = jnp.concatenate(
        [
            bias_sums[None, :model_width],
            bias_sums[None, 2 * model_width :],
            jnp.sum(grad_branch.astype(jnp.float32), axis=0)[None],
            grad_shift_one[None],
            jnp.sum(grad_ff.astype(jnp.float32), axis=0)[None],
            grad_shift_two[None],
            grad_gain_one[None],
            grad_gain_two[None],
            jnp.sum(grad_hidden.astype(jnp.float32), axis=0).reshape(-1, model_width),
        ],
        axis=0,
    )
    summed_qkv, summed_out, summed_up, summed_down, summed_vec, summed_taps = all_grads(
        grad_qkv, grad_out, grad_up, grad_down, grad_vec, grad_taps
    )
    new_qkv = adam_step(qkv_weight, qkv_first, qkv_second, summed_qkv, rate_matrix, decay_rate)
    new_out = adam_step(out_weight, out_first, out_second, summed_out, rate_output, decay_rate)
    new_up = adam_step(up_weight, up_first, up_second, summed_up, rate_matrix, decay_rate)
    new_down = adam_step(down_weight, down_first, down_second, summed_down, rate_matrix, decay_rate)
    new_vec = adam_step(vectors, vec_first, vec_second, summed_vec, rate_vector, 0.0)
    new_taps = adam_step(taps, tap_first, tap_second, summed_taps, rate_taps, 0.0)
    out_tokens = layer_out.astype(jnp.bfloat16).reshape(tokens.shape)
    return (out_tokens, input_grad) + new_qkv + new_out + new_up + new_down + new_vec + new_taps


def solution(mesh):
    return jax.shard_map(
        on_device,
        mesh=mesh,
        in_specs=(
            P("rows", "seq", None),
            P("rows", "seq", None),
            P(("rows", "seq"), None),
            P(("rows", "seq"), None),
            P(("rows", "seq"), None),
            P(("rows", "seq"), None),
            P(None, ("rows", "seq")),
            P(),
            P(("rows", "seq"), None),
            P(("rows", "seq"), None),
            P(("rows", "seq"), None),
            P(("rows", "seq"), None),
            P(("rows", "seq"), None),
            P(("rows", "seq"), None),
            P(("rows", "seq"), None),
            P(("rows", "seq"), None),
            P(None, ("rows", "seq")),
            P(None, ("rows", "seq")),
            P(),
            P(),
        ),
        out_specs=(
            P("rows", "seq", None),
            P("rows", "seq", None),
            P(("rows", "seq"), None),
            P(("rows", "seq"), None),
            P(("rows", "seq"), None),
            P(("rows", "seq"), None),
            P(("rows", "seq"), None),
            P(("rows", "seq"), None),
            P(("rows", "seq"), None),
            P(("rows", "seq"), None),
            P(("rows", "seq"), None),
            P(("rows", "seq"), None),
            P(("rows", "seq"), None),
            P(("rows", "seq"), None),
            P(None, ("rows", "seq")),
            P(None, ("rows", "seq")),
            P(None, ("rows", "seq")),
            P(),
            P(),
            P(),
        ),
        check_vma=False,
    )
```

```python
import functools

import jax
import jax.numpy as jnp
from jax import lax
from jax.experimental import pallas as pl
from jax.experimental.pallas import tpu as pltpu
from jax.sharding import PartitionSpec as P

LAND = 64
PINV_ITERS = 6


top_precision = lax.Precision.HIGHEST
norm_eps = 1e-05
beta_one = 0.9
beta_two = 0.999
corr_one = 1.0 - 0.9**10
corr_two = 1.0 - 0.999**10
adam_eps = 1e-08
decay_rate = 0.01
rate_matrix = 0.03
rate_output = 0.12
rate_vector = 0.3
rate_taps = 0.08


def with_halo(x, sides, width):
    for axis, dim in sides:
        size, length = (lax.axis_size(axis), x.shape[dim])
        up = [(i, (i + 1) % size) for i in range(size - 1)]
        down = [(j, i) for i, j in up]
        last = lax.slice_in_dim(x, length - width, length, axis=dim)
        initial = lax.slice_in_dim(x, 0, width, axis=dim)
        before = lax.ppermute(last, axis, up)
        after = lax.ppermute(initial, axis, down)
        x = jnp.concatenate([before, x, after], axis=dim)
    return x


def layer_norm(residual, gain_row, shift_row):
    center = residual - jnp.mean(residual, axis=-1, keepdims=True)
    spread = jnp.mean(center * center, axis=-1, keepdims=True)
    return center * lax.rsqrt(spread + norm_eps) * gain_row + shift_row


def normalized_rows(scores):
    expo = jnp.exp(scores - jnp.max(scores, axis=-1, keepdims=True))
    return expo / jnp.sum(expo, axis=-1, keepdims=True)


def softmax_back(probability, grad_in):
    return probability * (grad_in - jnp.sum(probability * grad_in, axis=-1, keepdims=True))


def gelu_exact(inputs):
    return jax.nn.gelu(inputs, approximate=False)


def pseudo_inverse(matrix):
    identity = jnp.eye(matrix.shape[-1], dtype=jnp.float32)
    approx = jnp.swapaxes(matrix, -1, -2) / jnp.sum(matrix * matrix, axis=(-2, -1), keepdims=True)
    for sweep_index in range(PINV_ITERS):
        product = jnp.matmul(matrix, approx, precision=top_precision)
        inner_term = 7.0 * identity - product
        inner_term = 15.0 * identity - jnp.matmul(product, inner_term, precision=top_precision)
        inner_term = 13.0 * identity - jnp.matmul(product, inner_term, precision=top_precision)
        approx = 0.25 * jnp.matmul(approx, inner_term, precision=top_precision)
    return approx


def adam_step(weight, first_moment, second, gradient, step_rate, decay_coef):
    new_first = beta_one * first_moment + (1.0 - beta_one) * gradient
    new_second = beta_two * second + (1.0 - beta_two) * gradient * gradient
    update = new_first / corr_one / (jnp.sqrt(new_second / corr_two) + adam_eps)
    return (new_first, new_second, weight - step_rate * (update + decay_coef * weight))


def with_collectives(
    tokens,
    cotangent,
    qkv_weight,
    out_weight,
    up_weight,
    down_weight,
    vectors,
    taps,
    qkv_first,
    qkv_second,
    out_first,
    out_second,
    up_first,
    up_second,
    down_first,
    down_second,
    vec_first,
    vec_second,
    tap_first,
    tap_second,
):
    seq_count, local_len, model_width = tokens.shape
    head_count, tap_count = taps.shape
    head_size = model_width // head_count
    hidden_width = up_weight.shape[1]
    land_local = LAND // lax.axis_size("seq")
    seg_len = local_len // land_local
    reach_width = tap_count // 2
    logit_scale_factor = head_size ** (-0.5)
    row_count = seq_count * local_len
    head_shape = (seq_count, local_len, head_count, head_size)
    land_shape = (seq_count, LAND, head_count, head_size)
    full_qkv, full_out, full_up, full_down, full_vec = (
        lax.all_gather(qkv_weight.astype(jnp.bfloat16), ("rows", "seq"), axis=0, tiled=True),
        lax.all_gather(out_weight.astype(jnp.bfloat16), ("rows", "seq"), axis=0, tiled=True),
        lax.all_gather(up_weight.astype(jnp.bfloat16), ("rows", "seq"), axis=0, tiled=True),
        lax.all_gather(down_weight.astype(jnp.bfloat16), ("rows", "seq"), axis=0, tiled=True),
        lax.all_gather(vectors.astype(jnp.bfloat16), ("rows", "seq"), axis=1, tiled=True),
    )
    vec_float = full_vec.astype(jnp.float32)
    flat_in = tokens.reshape(row_count, model_width)
    project = jnp.dot(flat_in, full_qkv, preferred_element_type=jnp.float32)
    queries = (project[:, :model_width] + vec_float[0]).astype(jnp.bfloat16)
    key_rows = project[:, model_width : 2 * model_width].astype(jnp.bfloat16)
    values = (project[:, 2 * model_width :] + vec_float[1]).astype(jnp.bfloat16)
    seg_shape = (seq_count, land_local, seg_len, model_width)
    own_q = jnp.mean(queries.reshape(seg_shape), axis=2, dtype=jnp.float32).astype(jnp.bfloat16)
    own_k = jnp.mean(key_rows.reshape(seg_shape), axis=2, dtype=jnp.float32).astype(jnp.bfloat16)
    land_q, land_k = (
        lax.all_gather(own_q, "seq", axis=1, tiled=True),
        lax.all_gather(own_k, "seq", axis=1, tiled=True),
    )
    query_heads = queries.reshape(head_shape)
    key_heads = key_rows.reshape(head_shape)
    value_heads = values.reshape(head_shape)
    landmark_query_heads = land_q.reshape(land_shape)
    landmark_key_heads = land_k.reshape(land_shape)
    lq_float = landmark_query_heads.astype(jnp.float32)
    lk_float = landmark_key_heads.astype(jnp.float32)
    score_one = (
        jnp.einsum(
            "sthd,slhd->shtl", query_heads, landmark_key_heads, preferred_element_type=jnp.float32
        )
        * logit_scale_factor
    )
    prob_one = normalized_rows(score_one)
    second_probability = normalized_rows(
        jnp.einsum("slhd,smhd->shlm", lq_float, lk_float, precision=top_precision)
        * logit_scale_factor
    )
    inverse_matrix, inverse_pull = jax.vjp(pseudo_inverse, second_probability)
    score_three = (
        jnp.einsum(
            "slhd,sthd->shlt", landmark_query_heads, key_heads, preferred_element_type=jnp.float32
        )
        * logit_scale_factor
    )
    row_max = lax.pmax(jnp.max(score_three, axis=-1), "seq")
    expo_three = jnp.exp(score_three - row_max[..., None])
    numer_local = jnp.einsum(
        "shlt,sthd->slhd",
        expo_three.astype(jnp.bfloat16),
        value_heads,
        preferred_element_type=jnp.float32,
    )
    numer, denom = (
        lax.psum(numer_local.astype(jnp.bfloat16), "seq").astype(jnp.float32),
        lax.psum(jnp.sum(expo_three, axis=-1).astype(jnp.bfloat16), "seq").astype(jnp.float32),
    )
    denom_swap = jnp.swapaxes(denom, 1, 2)[..., None]
    landmark_value_rows = numer / denom_swap
    mixing_kernel = jnp.einsum(
        "shlm,smhd->slhd", inverse_matrix, landmark_value_rows, precision=top_precision
    )
    mix_low = mixing_kernel.astype(jnp.bfloat16)
    prob_low = prob_one.astype(jnp.bfloat16)
    attend = jnp.einsum("shtl,slhd->sthd", prob_low, mix_low, preferred_element_type=jnp.float32)
    attend = attend.reshape(seq_count, local_len, model_width)
    tap_chan = jnp.repeat(taps, head_size, axis=0)
    padded_values = with_halo(
        values.reshape(seq_count, local_len, model_width), (("seq", 1),), reach_width
    )
    conv_out = jnp.zeros((seq_count, local_len, model_width), jnp.float32)
    for offset in range(tap_count):
        conv_out = conv_out + tap_chan[:, offset] * padded_values[
            :, offset : offset + local_len
        ].astype(jnp.float32)
    attn_low = (attend + conv_out).reshape(row_count, model_width).astype(jnp.bfloat16)
    branch = jnp.dot(attn_low, full_out, preferred_element_type=jnp.float32) + vec_float[2]
    resid_one = flat_in.astype(jnp.float32) + branch
    normed, norm_pull_one = jax.vjp(layer_norm, resid_one, vec_float[6], vec_float[3])
    normed_low = normed.astype(jnp.bfloat16)
    hidden_pre = jnp.dot(normed_low, full_up, preferred_element_type=jnp.float32) + vec_float[
        8:
    ].reshape(hidden_width)
    active, gelu_pull = jax.vjp(gelu_exact, hidden_pre)
    active_low = active.astype(jnp.bfloat16)
    ff_out = jnp.dot(active_low, full_down, preferred_element_type=jnp.float32) + vec_float[4]
    layer_out, norm_pull_two = jax.vjp(layer_norm, normed + ff_out, vec_float[7], vec_float[5])
    grad_resid_two, grad_gain_two, grad_shift_two = norm_pull_two(
        cotangent.reshape(row_count, model_width).astype(jnp.float32)
    )
    grad_ff = grad_resid_two.astype(jnp.bfloat16)
    grad_down = jnp.einsum("nf,nd->fd", active_low, grad_ff, preferred_element_type=jnp.float32)
    grad_active = jnp.einsum("nd,fd->nf", grad_ff, full_down, preferred_element_type=jnp.float32)
    grad_hidden = gelu_pull(grad_active)[0].astype(jnp.bfloat16)
    grad_up = jnp.einsum("nd,nf->df", normed_low, grad_hidden, preferred_element_type=jnp.float32)
    grad_normed = (
        jnp.einsum("nf,df->nd", grad_hidden, full_up, preferred_element_type=jnp.float32)
        + grad_resid_two
    )
    grad_resid_one, grad_gain_one, grad_shift_one = norm_pull_one(grad_normed)
    grad_branch = grad_resid_one.astype(jnp.bfloat16)
    grad_out = jnp.einsum("nd,ne->de", attn_low, grad_branch, preferred_element_type=jnp.float32)
    grad_attn = jnp.einsum(
        "ne,de->nd", grad_branch, full_out, preferred_element_type=jnp.float32
    ).astype(jnp.bfloat16)
    grad_attn_heads = grad_attn.reshape(head_shape)
    grad_prob_one = jnp.einsum(
        "sthd,slhd->shtl", grad_attn_heads, mix_low, preferred_element_type=jnp.float32
    )
    mixing_part = jnp.einsum(
        "shtl,sthd->slhd", prob_low, grad_attn_heads, preferred_element_type=jnp.float32
    )
    grad_mixing = lax.psum(mixing_part.astype(jnp.bfloat16), "seq").astype(jnp.float32)
    grad_score_one = softmax_back(prob_one, grad_prob_one).astype(jnp.bfloat16)
    query_local = (
        jnp.einsum(
            "shtl,slhd->sthd",
            grad_score_one,
            landmark_key_heads,
            preferred_element_type=jnp.float32,
        )
        * logit_scale_factor
    )
    land_k_part = (
        jnp.einsum(
            "shtl,sthd->slhd", grad_score_one, query_heads, preferred_element_type=jnp.float32
        )
        * logit_scale_factor
    )
    grad_pad = with_halo(
        grad_attn.reshape(seq_count, local_len, model_width), (("seq", 1),), reach_width
    )
    attn_float = grad_attn.reshape(seq_count, local_len, model_width).astype(jnp.float32)
    conv_back = jnp.zeros((seq_count, local_len, model_width), jnp.float32)
    tap_terms = []
    for offset in range(tap_count):
        start_row = 2 * reach_width - offset
        conv_back = conv_back + tap_chan[:, offset] * grad_pad[
            :, start_row : start_row + local_len
        ].astype(jnp.float32)
        tap_terms.append(
            jnp.sum(
                attn_float * padded_values[:, offset : offset + local_len].astype(jnp.float32),
                axis=(0, 1),
            )
        )
    grad_taps = jnp.sum(
        jnp.stack(tap_terms, axis=1).reshape(head_count, head_size, tap_count), axis=1
    )
    grad_inverse = jnp.einsum(
        "slhd,smhd->shlm", grad_mixing, landmark_value_rows, precision=top_precision
    )
    grad_land_values = jnp.einsum(
        "shlm,slhd->smhd", inverse_matrix, grad_mixing, precision=top_precision
    )
    land_grad_low = grad_land_values.astype(jnp.bfloat16).astype(jnp.float32)
    grad_prob_two = inverse_pull(grad_inverse)[0]
    grad_score_two = softmax_back(second_probability, grad_prob_two)
    query_two = (
        jnp.einsum("shlm,smhd->slhd", grad_score_two, lk_float, precision=top_precision)
        * logit_scale_factor
    )
    key_two = (
        jnp.einsum("shlm,slhd->smhd", grad_score_two, lq_float, precision=top_precision)
        * logit_scale_factor
    )
    grad_numer = land_grad_low / denom_swap
    expo_low = expo_three.astype(jnp.bfloat16).astype(jnp.float32)
    value_three = jnp.einsum("shlt,slhd->sthd", expo_low, grad_numer, precision=top_precision)
    grad_expo = jnp.einsum(
        "slhd,sthd->shlt", grad_numer, value_heads.astype(jnp.float32), precision=top_precision
    )
    grad_denom = jnp.swapaxes(jnp.sum(land_grad_low * landmark_value_rows, axis=-1), 1, 2) / denom
    grad_score_three = (expo_three * (grad_expo - grad_denom[..., None])).astype(jnp.bfloat16)
    land_q_part = (
        jnp.einsum(
            "shlt,sthd->slhd", grad_score_three, key_heads, preferred_element_type=jnp.float32
        )
        * logit_scale_factor
    )
    key_local = (
        jnp.einsum(
            "shlt,slhd->sthd",
            grad_score_three,
            landmark_query_heads,
            preferred_element_type=jnp.float32,
        )
        * logit_scale_factor
    )
    land_q_own, land_k_own = (
        lax.psum_scatter(
            land_q_part.astype(jnp.bfloat16), "seq", scatter_dimension=1, tiled=True
        ).astype(jnp.float32),
        lax.psum_scatter(
            land_k_part.astype(jnp.bfloat16), "seq", scatter_dimension=1, tiled=True
        ).astype(jnp.float32),
    )
    first_land = lax.axis_index("seq") * land_local
    land_q_own = land_q_own + lax.dynamic_slice_in_dim(query_two, first_land, land_local, 1)
    land_k_own = land_k_own + lax.dynamic_slice_in_dim(key_two, first_land, land_local, 1)
    spread_shape = (seq_count, land_local, seg_len, head_count, head_size)
    spread_q = jnp.broadcast_to((land_q_own / seg_len)[:, :, None], spread_shape).reshape(
        head_shape
    )
    spread_k = jnp.broadcast_to((land_k_own / seg_len)[:, :, None], spread_shape).reshape(
        head_shape
    )
    grad_query = (query_local + spread_q).reshape(row_count, model_width)
    grad_key = (key_local + spread_k).reshape(row_count, model_width)
    grad_value = value_three.reshape(row_count, model_width) + conv_back.reshape(
        row_count, model_width
    )
    grad_proj = jnp.concatenate([grad_query, grad_key, grad_value], axis=1).astype(jnp.bfloat16)
    grad_qkv = jnp.einsum("nd,ne->de", flat_in, grad_proj, preferred_element_type=jnp.float32)
    input_grad = (
        jnp.einsum("ne,de->nd", grad_proj, full_qkv, preferred_element_type=jnp.float32)
        + grad_resid_one
    )
    input_grad = input_grad.astype(jnp.bfloat16).reshape(tokens.shape)
    bias_sums = jnp.sum(grad_proj.astype(jnp.float32), axis=0)
    grad_vec = jnp.concatenate(
        [
            bias_sums[None, :model_width],
            bias_sums[None, 2 * model_width :],
            jnp.sum(grad_branch.astype(jnp.float32), axis=0)[None],
            grad_shift_one[None],
            jnp.sum(grad_ff.astype(jnp.float32), axis=0)[None],
            grad_shift_two[None],
            grad_gain_one[None],
            grad_gain_two[None],
            jnp.sum(grad_hidden.astype(jnp.float32), axis=0).reshape(-1, model_width),
        ],
        axis=0,
    )
    summed_qkv, summed_out, summed_up, summed_down, summed_vec = (
        lax.psum_scatter(grad_qkv, ("rows", "seq"), scatter_dimension=0, tiled=True),
        lax.psum_scatter(grad_out, ("rows", "seq"), scatter_dimension=0, tiled=True),
        lax.psum_scatter(grad_up, ("rows", "seq"), scatter_dimension=0, tiled=True),
        lax.psum_scatter(grad_down, ("rows", "seq"), scatter_dimension=0, tiled=True),
        lax.psum_scatter(grad_vec, ("rows", "seq"), scatter_dimension=1, tiled=True),
    )
    summed_taps = lax.psum(grad_taps, ("rows", "seq"))
    new_qkv = adam_step(qkv_weight, qkv_first, qkv_second, summed_qkv, rate_matrix, decay_rate)
    new_out = adam_step(out_weight, out_first, out_second, summed_out, rate_output, decay_rate)
    new_up = adam_step(up_weight, up_first, up_second, summed_up, rate_matrix, decay_rate)
    new_down = adam_step(down_weight, down_first, down_second, summed_down, rate_matrix, decay_rate)
    new_vec = adam_step(vectors, vec_first, vec_second, summed_vec, rate_vector, 0.0)
    new_taps = adam_step(taps, tap_first, tap_second, summed_taps, rate_taps, 0.0)
    out_tokens = layer_out.astype(jnp.bfloat16).reshape(tokens.shape)
    return (out_tokens, input_grad) + new_qkv + new_out + new_up + new_down + new_vec + new_taps


BF = jnp.bfloat16
F32 = jnp.float32
MESH = pl.DeviceIdType.MESH


def remote(src, dst, send_sem, recv_sem, device):
    return pltpu.make_async_remote_copy(
        src_ref=src, dst_ref=dst, send_sem=send_sem, recv_sem=recv_sem,
        device_id=device, device_id_type=MESH,
    )


def place():
    row, spot = lax.axis_index("rows"), lax.axis_index("seq")
    line, core = spot // 2, spot % 2
    flip_one = row + 1 - 2 * (row % 2)
    flip_two = row + 2 - 4 * (row // 2)
    first = (1 - core) * flip_one + core * flip_two
    second = (1 - core) * flip_two + core * flip_one
    return row, line, core, first, second, 3 - row


def greet(devices):
    barrier = pltpu.get_barrier_semaphore()
    for device in devices:
        pl.semaphore_signal(barrier, inc=1, device_id=device, device_id_type=MESH)
    pl.semaphore_wait(barrier, len(devices))


def gather_kernel(line_size, n_w, *refs):
    ins, outs = refs[:n_w], refs[n_w : 2 * n_w]
    asm, stage = refs[2 * n_w : 3 * n_w], refs[3 * n_w : 4 * n_w]
    send, recv, local = refs[4 * n_w :]
    row, line, core, first, second, across = place()
    own_spot, sibling = 2 * line + core, (row, 2 * line + 1 - core)
    peers = [(row, 2 * ((line + k) % line_size) + core) for k in range(1, line_size)]
    to_first, to_second = (first, own_spot), (second, own_spot)
    greet(peers + [to_first, to_second, sibling])
    rows = [x.shape[0] for x in ins]
    half = [x.shape[1] // 2 for x in ins]
    started = []

    def go(w, k, src, dst, device):
        copy = remote(src, dst, send.at[w, k], recv.at[w, k], device)
        copy.start()
        started.append(copy)
        return copy

    def cols(w, which):
        return pl.ds(pl.multiple_of(which * half[w], 128), half[w])

    def slab(w, index):
        size = 2 * rows[w] * line_size
        return outs[w].at[pl.ds(pl.multiple_of(index * size, size), size), cols(w, core)]

    asm_copy, z_copy, own_copy, hop, sib = {}, {}, {}, {}, {}
    z0 = line_size
    for w in range(n_w):
        part = pl.ds(pl.multiple_of(core * rows[w], 8), rows[w])
        asm_copy[w] = go(w, 0, ins[w].at[:, cols(w, 1 - core)], asm[w].at[part, :], sibling)
        asm[w][part, :] = ins[w][:, cols(w, core)]

    def spread(w):
        asm_copy[w].wait_recv()
        stage[w][...] = asm[w][...].astype(BF)
        size = 2 * rows[w]
        at = pl.ds(pl.multiple_of((row * line_size + line) * size, size), size)
        block = outs[w].at[at, cols(w, core)]
        z_copy[w] = [go(w, 1 + k, stage[w], block, peers[k]) for k in range(line_size - 1)]
        own_copy[w] = pltpu.make_async_copy(stage[w], block, local.at[w])
        own_copy[w].start()

    def step_one(w):
        own_copy[w].wait()
        for copy in z_copy[w]:
            copy.wait_recv()
        mine = slab(w, row)
        hop[w] = [go(w, z0, mine, mine, to_first), go(w, z0 + 1, mine, mine, to_second)]
        sib[w] = [go(w, z0 + 3, mine, mine, sibling)]

    def step_two(w):
        hop[w][0].wait_recv()
        got = slab(w, first)
        hop[w].append(go(w, z0 + 2, got, got, to_second))
        sib[w].append(go(w, z0 + 4, got, got, sibling))

    def step_three(w):
        hop[w][1].wait_recv()
        got = slab(w, second)
        sib[w].append(go(w, z0 + 5, got, got, sibling))
        hop[w][2].wait_recv()
        got = slab(w, across)
        sib[w].append(go(w, z0 + 6, got, got, sibling))

    for w in range(n_w):
        spread(w)
    for t in range(n_w + 2):
        if t < n_w:
            step_one(t)
        if 0 <= t - 1 < n_w:
            step_two(t - 1)
        if 0 <= t - 2 < n_w:
            step_three(t - 2)
    for w in range(n_w):
        for copy in sib[w]:
            copy.wait_recv()
    for copy in started:
        copy.wait_send()


def gather_weights(shards, seq_size):
    line_size, n_w = seq_size // 2, len(shards)
    n_dev = 4 * seq_size
    n_sem = line_size + 7
    vmem = pl.BlockSpec(memory_space=pltpu.VMEM)
    return pl.pallas_call(
        functools.partial(gather_kernel, line_size, n_w),
        out_shape=[jax.ShapeDtypeStruct((n_dev * x.shape[0], x.shape[1]), BF) for x in shards],
        in_specs=[vmem] * n_w,
        out_specs=[pl.BlockSpec(memory_space=pltpu.HBM)] * n_w,
        scratch_shapes=[pltpu.VMEM((2 * x.shape[0], x.shape[1] // 2), F32) for x in shards]
        + [pltpu.VMEM((2 * x.shape[0], x.shape[1] // 2), BF) for x in shards]
        + [
            pltpu.SemaphoreType.DMA((n_w, n_sem)),
            pltpu.SemaphoreType.DMA((n_w, n_sem)),
            pltpu.SemaphoreType.DMA((n_w,)),
        ],
        compiler_params=pltpu.CompilerParams(
            collective_id=0, has_side_effects=True, vmem_limit_bytes=32 * 1024 * 1024
        ),
        name="gather_weights",
    )(*shards)


def scatter_kernel(line_size, n_w, *refs):
    ins, outs = refs[:n_w], refs[n_w : 2 * n_w]
    acc, buf0, buf1, buf2, buf3, fin = [refs[(2 + i) * n_w : (3 + i) * n_w] for i in range(6)]
    send, recv, local = refs[8 * n_w :]
    row, line, core, first, second, across = place()
    own_spot, sibling = 2 * line + core, (row, 2 * line + 1 - core)
    peers = [(row, 2 * ((line + k) % line_size) + core) for k in range(1, line_size)]
    to_first, to_second = (first, own_spot), (second, own_spot)
    greet(peers + [to_first, to_second, sibling])
    rows = [x.shape[0] for x in outs]
    half = [x.shape[1] // 2 for x in ins]
    started = []
    copies = {}

    def go(w, k, src, dst, device):
        copy = remote(src, dst, send.at[w, k], recv.at[w, k], device)
        copy.start()
        started.append(copy)
        return copy

    def cols(w, which):
        return pl.ds(pl.multiple_of(which * half[w], 128), half[w])

    def size(w):
        return 2 * rows[w] * line_size

    def slab(w, index):
        return pl.ds(pl.multiple_of(index * size(w), size(w)), size(w))

    def add(w, index, other, other_start):
        step = 48
        base = index * size(w)

        def one(i, carry):
            at = pl.ds(pl.multiple_of(base + i * step, 16), step)
            there = pl.ds(pl.multiple_of(other_start + i * step, 16), step)
            acc[w][at, :] = acc[w][at, :] + other[there, :]
            return carry

        lax.fori_loop(0, size(w) // step, one, 0)

    def open_up(w):
        copies[w, 0] = go(w, 0, ins[w].at[:, cols(w, 1 - core)], buf0[w], sibling)
        copies[w, "own"] = pltpu.make_async_copy(ins[w].at[:, cols(w, core)], acc[w], local.at[w])
        copies[w, "own"].start()

    def step_one(w):
        copies[w, "own"].wait()
        copies[w, 0].wait_recv()
        add(w, across, buf0[w], across * size(w))
        copies[w, 1] = go(w, 1, acc[w].at[slab(w, across), :], buf1[w].at[0], to_second)
        add(w, second, buf0[w], second * size(w))
        copies[w, 2] = go(w, 2, acc[w].at[slab(w, second), :], buf1[w].at[1], to_second)
        add(w, first, buf0[w], first * size(w))
        add(w, row, buf0[w], row * size(w))

    def step_two(w):
        copies[w, 1].wait_recv()
        add(w, first, buf1[w].at[0], 0)
        copies[w, 3] = go(w, 3, acc[w].at[slab(w, first), :], buf2[w], to_first)
        copies[w, 2].wait_recv()
        add(w, row, buf1[w].at[1], 0)

    def step_three(w):
        copies[w, 3].wait_recv()
        add(w, row, buf2[w], 0)
        block = 2 * rows[w]
        for k in range(1, line_size):
            there = (line + k) % line_size
            at = pl.ds(pl.multiple_of((row * line_size + there) * block, block), block)
            copies[w, 3 + k] = go(w, 3 + k, acc[w].at[at, :], buf3[w].at[line], peers[k - 1])
        at = pl.ds(pl.multiple_of((row * line_size + line) * block, block), block)
        buf3[w][line] = acc[w][at, :]

    def step_four(w):
        for k in range(1, line_size):
            copies[w, 3 + k].wait_recv()
        total = buf3[w][0].astype(F32)
        for k in range(1, line_size):
            total = total + buf3[w][k].astype(F32)
        fin[w][...] = total
        part = pl.ds(pl.multiple_of((1 - core) * rows[w], 8), rows[w])
        copies[w, 9] = go(w, 3 + line_size, fin[w].at[part, :], outs[w].at[:, cols(w, core)], sibling)
        part = pl.ds(pl.multiple_of(core * rows[w], 8), rows[w])
        outs[w][:, cols(w, core)] = fin[w][part, :]

    for w in range(n_w):
        open_up(w)
    for t in range(n_w + 3):
        if t < n_w:
            step_one(t)
        if 0 <= t - 1 < n_w:
            step_two(t - 1)
        if 0 <= t - 2 < n_w:
            step_three(t - 2)
        if 0 <= t - 3 < n_w:
            step_four(t - 3)
    for w in range(n_w):
        copies[w, 9].wait_recv()
    for copy in started:
        copy.wait_send()


def scatter_grads(grads, seq_size):
    line_size, n_w = seq_size // 2, len(grads)
    n_dev = 4 * seq_size
    n_sem = line_size + 4
    rows = [x.shape[0] // n_dev for x in grads]
    half = [x.shape[1] // 2 for x in grads]
    kinds = [x.dtype for x in grads]
    vmem = pl.BlockSpec(memory_space=pltpu.VMEM)
    every = range(n_w)
    quarter = [2 * rows[w] * line_size for w in every]
    return pl.pallas_call(
        functools.partial(scatter_kernel, line_size, n_w),
        out_shape=[jax.ShapeDtypeStruct((rows[w], 2 * half[w]), F32) for w in every],
        in_specs=[pl.BlockSpec(memory_space=pltpu.HBM)] * n_w,
        out_specs=[vmem] * n_w,
        scratch_shapes=[pltpu.VMEM((4 * quarter[w], half[w]), kinds[w]) for w in every]
        + [pltpu.VMEM((4 * quarter[w], half[w]), kinds[w]) for w in every]
        + [pltpu.VMEM((2, quarter[w], half[w]), kinds[w]) for w in every]
        + [pltpu.VMEM((quarter[w], half[w]), kinds[w]) for w in every]
        + [pltpu.VMEM((line_size, 2 * rows[w], half[w]), kinds[w]) for w in every]
        + [pltpu.VMEM((2 * rows[w], half[w]), F32) for w in every]
        + [
            pltpu.SemaphoreType.DMA((n_w, n_sem)),
            pltpu.SemaphoreType.DMA((n_w, n_sem)),
            pltpu.SemaphoreType.DMA((n_w,)),
        ],
        compiler_params=pltpu.CompilerParams(
            collective_id=1, has_side_effects=True, vmem_limit_bytes=48 * 1024 * 1024
        ),
        name="scatter_grads",
    )(*grads)


PAIR = 128


def nn(a, b):
    return jnp.dot(a, b, preferred_element_type=F32)


def nt(a, b):
    return lax.dot_general(a, b, (((1,), (1,)), ((), ())), preferred_element_type=F32)


def tn(a, b):
    return lax.dot_general(a, b, (((0,), (0,)), ((), ())), preferred_element_type=F32)


def split(x):
    high = x.astype(BF)
    return high, (x - high.astype(F32)).astype(BF)


def three(dot, a, b):
    return dot(a[0], b[0]) + (dot(a[0], b[1]) + dot(a[1], b[0]))


def lane_masks(dtype):
    lane = lax.broadcasted_iota(jnp.int32, (1, PAIR), 1)
    one = (lane < PAIR // 2).astype(F32)
    return one.astype(dtype), (1.0 - one).astype(dtype)


def apart(x):
    one, two = lane_masks(x.dtype)
    return jnp.concatenate([x * one, x * two], axis=0)


def together(x):
    half = PAIR // 2
    lane = lax.broadcasted_iota(jnp.int32, (half, PAIR), 1)
    return jnp.where(lane < half, x[:half], x[half:])


def same_head():
    half = PAIR // 2
    a = lax.broadcasted_iota(jnp.int32, (PAIR, PAIR), 0) // half
    b = lax.broadcasted_iota(jnp.int32, (PAIR, PAIR), 1) // half
    return a == b


def eye():
    a = lax.broadcasted_iota(jnp.int32, (PAIR, PAIR), 0)
    b = lax.broadcasted_iota(jnp.int32, (PAIR, PAIR), 1)
    return (a == b).astype(F32)


def by_head(x, reduce):
    half, width = PAIR // 2, x.shape[1]
    parts = [reduce(x[h * half : (h + 1) * half], axis=0, keepdims=True) for h in (0, 1)]
    return jnp.concatenate([jnp.broadcast_to(y, (half, width)) for y in parts], axis=0)


def lanes(p):
    if isinstance(p, int):
        return pl.ds(p * PAIR, PAIR)
    return pl.ds(pl.multiple_of(p * PAIR, PAIR), PAIR)


def conv_pair(table, padded):
    size = table.shape[0] // 4
    out = nn(table, padded)
    lane = lax.broadcasted_iota(jnp.int32, (size, PAIR), 1)
    return jnp.where(
        lane < PAIR // 2,
        out[:size] + out[2 * size : 3 * size],
        out[size : 2 * size] + out[3 * size :],
    )


class Group:
    def __init__(self, send, recv):
        self.row, self.me = lax.axis_index("rows"), lax.axis_index("seq")
        self.size = lax.axis_size("seq")
        self.send, self.recv, self.started = send, recv, []

    def peers(self):
        return [(self.row, (self.me + k) % self.size) for k in range(1, self.size)]

    def push(self, channel, pick_src, dst):
        copies = []
        for k, device in enumerate(self.peers()):
            copy = remote(
                pick_src(device[1]), dst, self.send.at[channel, k], self.recv.at[channel, k], device
            )
            copy.start()
            copies.append(copy)
        self.started += copies
        return copies

    def halo(self, channel, source, padded, reach):
        length = source.shape[1]
        copies = []
        for which, (src_at, dst_at, step) in enumerate(
            ((length - reach, 0, 1), (0, length + reach, -1))
        ):
            there = (self.me + step + self.size) % self.size
            copy = remote(
                source.at[:, pl.ds(src_at, reach), :],
                padded.at[:, pl.ds(dst_at, reach), :],
                self.send.at[channel, which],
                self.recv.at[channel, which],
                (self.row, there),
            )
            goes = self.me < self.size - 1 if step == 1 else self.me > 0
            comes = self.me > 0 if step == 1 else self.me < self.size - 1
            pl.when(goes)(copy.start)
            copies.append((copy, goes, comes, dst_at))

        def arrive():
            for copy, goes, comes, dst_at in copies:
                pl.when(comes)(copy.wait_recv)

                @pl.when(jnp.logical_not(comes))
                def _():
                    shape = (padded.shape[0], reach, padded.shape[2])
                    padded[:, pl.ds(dst_at, reach), :] = jnp.zeros(shape, padded.dtype)

        def sent():
            for copy, goes, _, _ in copies:
                pl.when(goes)(copy.wait_send)

        return arrive, sent

    def finish(self):
        for copy in self.started:
            copy.wait_send()


def pinv_start(prob):
    total = by_head(jnp.sum(prob * prob, axis=1, keepdims=True), jnp.sum)
    return prob.T / total


def pinv_terms(p, z, unit):
    product = three(nn, p, z)
    prod = split(product)
    term_one = 7.0 * unit - product
    term_two = 15.0 * unit - three(nn, prod, split(term_one))
    term_three = 13.0 * unit - three(nn, prod, split(term_two))
    return prod, term_one, term_two, term_three


def attend_kernel(
    reach, q, k, v, table,
    attn, vpad, landq, landk, mix, p1, e, wt, p2o, zo, lvo,
    lb, numer, nrecv, stat, srecv, mstat, conv, fcol, send, recv,
):
    group = Group(send, recv)
    me, size = group.me, group.size
    n_seq, length, width = q.shape
    pairs = width // PAIR
    own = n_seq * pairs // size
    each = width // (pairs // own)
    land_local = LAND // size
    seg = length // land_local
    scale = (PAIR // 2) ** -0.5
    greet(group.peers())

    def owner_seq(d):
        return d * own // pairs

    def owner_lanes(d):
        return pl.ds(pl.multiple_of((d * own % pairs) * PAIR, PAIR), each)

    halo_in, halo_sent = group.halo(0, v, vpad, reach)

    def own_landmarks(s, carry):
        both = [
            jnp.mean(x[s].astype(F32).reshape(land_local, seg, width), axis=1) for x in (q, k)
        ]
        lb[me, s] = jnp.concatenate(both, axis=0).astype(BF)
        vpad[s, pl.ds(reach, length), :] = v[s]
        return carry

    lax.fori_loop(0, n_seq, own_landmarks, 0)
    landed = group.push(1, lambda d: lb.at[me], lb.at[me])
    for copy in landed:
        copy.wait_recv()

    def whole_landmarks(s, carry):
        x = lb[:, s].astype(F32)
        landq[s] = x[:, :land_local].reshape(LAND, width).astype(BF)
        landk[s] = x[:, land_local:].reshape(LAND, width).astype(BF)
        return carry

    lax.fori_loop(0, n_seq, whole_landmarks, 0)
    lane_at = lax.broadcasted_iota(jnp.int32, (PAIR, PAIR), 1)

    def over_tokens(s, tile):
        for p in range(pairs):
            score = nt(apart(landq[s, :, lanes(p)]), k[s, :, lanes(p)]) * scale
            top = jnp.max(score, axis=1, keepdims=True)
            expo = jnp.exp(score - top)
            low = expo.astype(BF)
            e[s * pairs + p] = low
            numer[s, :, lanes(p)] = together(nn(low, v[s, :, lanes(p)])).astype(BF)
            unit = s * pairs + p
            at = (unit // own) * 8 + unit % own
            tile = jnp.where(lane_at == at, top, tile)
            tile = jnp.where(lane_at == at + own, jnp.sum(expo, axis=1, keepdims=True), tile)
        return tile

    tile = lax.fori_loop(0, n_seq, over_tokens, jnp.zeros((PAIR, PAIR), F32))
    stat[...] = tile.T[: 8 * size].reshape(size, 8, PAIR)
    sums_in = group.push(
        2, lambda d: numer.at[owner_seq(d), :, owner_lanes(d)], nrecv.at[me]
    )
    stats_in = group.push(3, lambda d: stat.at[d], srecv.at[me])
    nrecv[me] = numer[owner_seq(me), :, owner_lanes(me)]
    srecv[me] = stat[me]

    block, unit_matrix = same_head(), eye()
    my_seq, my_pair = owner_seq(me), (me * own) % pairs
    for i in range(own):
        at = lanes(my_pair + i)
        score = nt(apart(landq[my_seq, :, at]), apart(landk[my_seq, :, at])) * scale
        score = jnp.where(block, score, -1e30)
        expo = jnp.exp(score - jnp.max(score, axis=1, keepdims=True))
        prob = expo / jnp.sum(expo, axis=1, keepdims=True)
        p2o[i] = prob
        zo[0, i] = pinv_start(prob)

    halo_in()
    per_step = n_seq * pairs // PINV_ITERS

    def over_landmarks(unit):
        s, p = unit // pairs, unit % pairs
        score = nt(apart(landk[s, :, lanes(p)]), q[s, :, lanes(p)]) * scale
        expo = jnp.exp(score - by_head(score, jnp.max))
        p1[unit] = expo / by_head(expo, jnp.sum)
        conv[s, :, lanes(p)] = conv_pair(table[p], vpad[s, :, lanes(p)])

    def pinv_step(step, carry):
        for i in range(own):
            z = split(zo[step, i])
            _, _, _, inner = pinv_terms(split(p2o[i]), z, unit_matrix)
            zo[step + 1, i] = 0.25 * three(nn, z, split(inner))
        for j in range(per_step):
            over_landmarks(step * per_step + j)
        return carry

    lax.fori_loop(0, PINV_ITERS, pinv_step, 0)

    for copy in sums_in + stats_in:
        copy.wait_recv()
    got = srecv[...]
    tops = got[:, :own]
    top = jnp.max(tops, axis=0, keepdims=True)
    factor = jnp.exp(tops - top)
    total = jnp.sum(factor * got[:, own : 2 * own], axis=0, keepdims=True)
    factor = factor / total
    spare = jnp.zeros((1, 8 - 2 * own, PAIR), F32)
    mstat[me] = jnp.concatenate([top, total, spare], axis=1)[0]
    spread = jnp.concatenate([factor, jnp.zeros((size, 8 - own, PAIR), F32)], axis=1)
    spread = spread.reshape(8 * size, PAIR)
    fcol[...] = jnp.concatenate([spread, jnp.zeros((PAIR - 8 * size, PAIR), F32)], axis=0).T
    half = PAIR // 2
    narrow = lax.broadcasted_iota(jnp.int32, (half, PAIR), 1) < half
    for i in range(own):
        at = pl.ds(i * PAIR, PAIR)
        mean = jnp.zeros((half, PAIR), F32)
        for src in range(size):
            column = fcol[:, src * 8 + i : src * 8 + i + 1]
            weight = jnp.where(narrow, column[:half], column[half:])
            mean = mean + weight * nrecv[src, :, at].astype(F32)
        lvo[:, at] = mean
        mixed = together(three(nn, split(zo[PINV_ITERS, i]), split(apart(mean))))
        mix[my_seq, :, lanes(my_pair + i)] = mixed.astype(BF)
    mine = mix.at[my_seq, :, owner_lanes(me)]
    mix_in = group.push(4, lambda d: mine, mine)
    back_in = group.push(5, lambda d: mstat.at[me], mstat.at[me])
    for copy in mix_in + back_in:
        copy.wait_recv()

    rows = jnp.concatenate(
        [mstat[...].reshape(8 * size, PAIR), jnp.zeros((PAIR - 8 * size, PAIR), F32)], axis=0
    )
    rows = rows.T
    valid = (lane_at % 8 < own) & (lane_at < 8 * size)
    shift = jnp.where(valid, tile - rows, 0.0)
    den = jnp.where(valid, pltpu.roll(rows, PAIR - own, 1), 1.0)
    wt[...] = jnp.exp(shift) / den

    def result(s, carry):
        for p in range(pairs):
            low = p1[s * pairs + p].astype(BF)
            out = tn(low, apart(mix[s, :, lanes(p)])) + conv[s, :, lanes(p)]
            attn[s, :, lanes(p)] = out.astype(BF)
        return carry

    lax.fori_loop(0, n_seq, result, 0)
    halo_sent()
    group.finish()


def attend(q, k, v, table, seq_size, reach):
    n_seq, length, width = q.shape
    pairs = width // PAIR
    units = n_seq * pairs
    own = units // seq_size
    vmem = pl.BlockSpec(memory_space=pltpu.VMEM)
    shape = jax.ShapeDtypeStruct
    land = shape((n_seq, LAND, width), BF)
    return pl.pallas_call(
        functools.partial(attend_kernel, reach),
        out_shape=[
            shape(q.shape, BF), shape((n_seq, length + 2 * reach, width), BF), land, land, land,
            shape((units, PAIR, length), F32), shape((units, PAIR, length), BF),
            shape((PAIR, PAIR), F32), shape((own, PAIR, PAIR), F32),
            shape((PINV_ITERS + 1, own, PAIR, PAIR), F32), shape((LAND, own * PAIR), F32),
        ],
        in_specs=[vmem] * 4,
        out_specs=[vmem] * 11,
        scratch_shapes=[
            pltpu.VMEM((seq_size, n_seq, 2 * LAND // seq_size, width), BF),
            pltpu.VMEM((n_seq, LAND, width), BF),
            pltpu.VMEM((seq_size, LAND, own * PAIR), BF),
            pltpu.VMEM((seq_size, 8, PAIR), F32),
            pltpu.VMEM((seq_size, 8, PAIR), F32),
            pltpu.VMEM((seq_size, 8, PAIR), F32),
            pltpu.VMEM((n_seq, length, width), F32),
            pltpu.VMEM((PAIR, PAIR), F32),
            pltpu.SemaphoreType.DMA((6, seq_size)),
            pltpu.SemaphoreType.DMA((6, seq_size)),
        ],
        compiler_params=pltpu.CompilerParams(
            collective_id=2, has_side_effects=True, vmem_limit_bytes=48 * 1024 * 1024
        ),
        name="attend",
    )(q, k, v, table)


def bands(taps, length, reach, flip):
    heads, count = taps.shape
    width = length + 2 * reach
    line = taps[:, ::-1] if flip else taps
    line = jnp.pad(line, ((0, 0), (0, width + 1 - count)))
    rows = jnp.tile(line, (1, length))[:, : length * width].reshape(heads, length, width)
    high = rows.astype(BF)
    low = (rows - high.astype(F32)).astype(BF)
    both = jnp.stack([high, low], axis=1).reshape(heads // 2, 2, 2, length, width)
    return jnp.swapaxes(both, 1, 2).reshape(heads // 2, 4 * length, width)


def attend_back_kernel(
    reach, n_taps, ga, q, k, vpad, table, landq, landk, mix, p1, e, wt, p2o, zo, lvo,
    grad, tapg,
    gpad, gmix, gmr, low, gfull, stat, mstat, gcol, gq, gv, lkp, lpart, lpr, two, twr, dz, dp,
    skew, own_g, send, recv,
):
    group = Group(send, recv)
    me, size = group.me, group.size
    n_seq, length, width = q.shape
    pairs = width // PAIR
    own = n_seq * pairs // size
    each = own * PAIR
    land_local = LAND // size
    seg = length // land_local
    half = PAIR // 2
    scale = half**-0.5
    greet(group.peers())

    def owner_seq(d):
        return d * own // pairs

    def owner_lanes(d):
        return pl.ds(pl.multiple_of((d * own % pairs) * PAIR, PAIR), each)

    halo_in, halo_sent = group.halo(0, ga, gpad, reach)

    def first(s, carry):
        for p in range(pairs):
            unit, at = s * pairs + p, lanes(p)
            own_ga = ga[s, :, at]
            gpad[s, pl.ds(reach, length), at] = own_ga
            prob = p1[unit]
            gmix[s, :, at] = together(nn(prob.astype(BF), own_ga)).astype(BF)
            back = nt(apart(mix[s, :, at]), own_ga)
            low[unit] = (prob * (back - by_head(prob * back, jnp.sum))).astype(BF)
        return carry

    lax.fori_loop(0, n_seq, first, 0)
    gmix_in = group.push(1, lambda d: gmix.at[owner_seq(d), :, owner_lanes(d)], gmr.at[me])
    gmr[me] = gmix[owner_seq(me), :, owner_lanes(me)]
    halo_in()
    skew[...] = jnp.zeros(skew.shape, F32)

    def beside(s, carry):
        one, two_mask = lane_masks(BF)
        for p in range(pairs):
            unit, at = s * pairs + p, lanes(p)
            own_ga, padded = ga[s, :, at], vpad[s, :, at]
            gs = low[unit]
            gq[s, :, at] = tn(gs, apart(landk[s, :, at])) * scale
            lkp[s, :, at] = together(nn(gs, q[s, :, at])) * scale
            gv[s, :, at] = conv_pair(table[p], gpad[s, :, at])
            both = jnp.concatenate([own_ga * one, own_ga * two_mask], axis=0)
            skew[2 * p : 2 * p + 2, :, : length + 2 * reach] += nt(both, padded).reshape(
                2, length, length + 2 * reach
            )
        return carry

    lax.fori_loop(0, n_seq, beside, 0)
    lane_at = lax.broadcasted_iota(jnp.int32, (PAIR, PAIR), 1)
    wide = skew.shape[2]
    for h in range(2 * pairs):
        total = skew[h, :8, :]
        for row in range(8, length, 8):
            total = total + pltpu.roll(skew[h, row : row + 8, :], wide - row, 1)
        tapg[h] = total[:, :PAIR]

    for copy in gmix_in:
        copy.wait_recv()
    my_seq, my_pair = owner_seq(me), (me * own) % pairs
    tile = jnp.zeros((PAIR, PAIR), F32)
    for i in range(own):
        at = pl.ds(i * PAIR, PAIR)
        total = gmr[0, :, at].astype(F32)
        for src in range(1, size):
            total = total + gmr[src, :, at].astype(F32)
        total = split(apart(total))
        means = apart(lvo[:, at])
        back = together(three(tn, split(zo[PINV_ITERS, i]), total)).astype(BF)
        own_g[:, at] = back
        column = jnp.sum(apart(back.astype(F32)) * means, axis=1, keepdims=True)
        tile = jnp.where(lane_at == i, column, tile)
        dz[i] = three(nt, total, split(means))
        dp[i] = jnp.zeros((PAIR, PAIR), F32)
    stat[...] = tile.T[:8]
    mstat[me] = stat[...]
    gfull[my_seq, :, owner_lanes(me)] = own_g[...]
    g_in = group.push(2, lambda d: own_g, gfull.at[my_seq, :, owner_lanes(me)])
    back_in = group.push(3, lambda d: stat, mstat.at[me])
    for copy in g_in + back_in:
        copy.wait_recv()
    rows = jnp.concatenate(
        [mstat[...].reshape(8 * size, PAIR), jnp.zeros((PAIR - 8 * size, PAIR), F32)], axis=0
    )
    gcol[...] = rows.T
    unit_matrix = eye()

    def third(unit):
        s, p = unit // pairs, unit % pairs
        at = lanes(p)
        here = (unit // own) * 8 + unit % own
        picked = lane_at == here
        weight = jnp.sum(jnp.where(picked, wt[...], 0.0), axis=1, keepdims=True)
        offset = jnp.sum(jnp.where(picked, gcol[...], 0.0), axis=1, keepdims=True)
        g = apart(gfull[s, :, at])
        prob = e[unit].astype(F32) * weight
        back = nt(g, vpad[s, pl.ds(reach, length), at]) - offset
        gs = (prob * back).astype(BF)
        gv[s, :, at] += tn(prob.astype(BF), g)
        grad[s, :, pl.ds(pl.multiple_of(width + p * PAIR, PAIR), PAIR)] = (
            tn(gs, apart(landq[s, :, at])) * scale
        ).astype(BF)
        lq = (together(nn(gs, k[s, :, at])) * scale).reshape(size, land_local, PAIR)
        lk = lkp[s, :, at].reshape(size, land_local, PAIR)
        lpart[:, s, :, at] = jnp.concatenate([lq, lk], axis=1).astype(BF)

    per_step = n_seq * pairs // PINV_ITERS

    def pinv_back(step, carry):
        at_step = PINV_ITERS - 1 - step
        for i in range(own):
            p, z = split(p2o[i]), split(zo[at_step, i])
            prod, one, two_term, three_term = pinv_terms(p, z, unit_matrix)
            d_out = dz[i] * 0.25
            d_out_s = split(d_out)
            d_three = split(three(tn, z, d_out_s))
            d_two = split(-three(tn, prod, d_three))
            d_one = -three(tn, prod, d_two)
            d_prod = -three(nt, d_three, split(two_term)) - three(nt, d_two, split(one)) - d_one
            d_prod = split(d_prod)
            dp[i] += three(nt, d_prod, z)
            dz[i] = three(nt, d_out_s, split(three_term)) + three(tn, p, d_prod)
        for j in range(per_step):
            third(step * per_step + j)
        return carry

    lax.fori_loop(0, PINV_ITERS, pinv_back, 0)

    for i in range(own):
        at = pl.ds(i * PAIR, PAIR)
        prob = p2o[i]
        squares = by_head(jnp.sum(prob * prob, axis=1, keepdims=True), jnp.sum)
        d_start = dz[i].T
        inner = by_head(jnp.sum(d_start * prob, axis=1, keepdims=True), jnp.sum)
        d_prob = dp[i] + d_start / squares - 2.0 * prob * inner / (squares * squares)
        gs = prob * (d_prob - jnp.sum(prob * d_prob, axis=1, keepdims=True))
        gs = split(gs)
        here = lanes(my_pair + i)
        lq, lk = apart(landq[my_seq, :, here]), apart(landk[my_seq, :, here])
        query = together(nn(gs[0], lk) + nn(gs[1], lk)) * scale
        key = together(tn(gs[0], lq) + tn(gs[1], lq)) * scale
        both = [x.reshape(size, land_local, PAIR) for x in (query, key)]
        two[:, :, at] = jnp.concatenate(both, axis=1).astype(BF)
    lpr[me] = lpart[me]
    twr[me] = two[me]
    part_in = group.push(4, lambda d: lpart.at[d], lpr.at[me])
    two_in = group.push(5, lambda d: two.at[d], twr.at[me])
    for copy in part_in + two_in:
        copy.wait_recv()

    def close(s, carry):
        for p in range(pairs):
            at = lanes(p)
            total = lpr[0, s, :, at].astype(F32)
            for src in range(1, size):
                total = total + lpr[src, s, :, at].astype(F32)
            owner = s * pairs + p
            spot = pl.ds(pl.multiple_of((owner % own) * PAIR, PAIR), PAIR)
            total = (total + twr[owner // own, :, spot].astype(F32)) * (1.0 / seg)
            spread = [
                jnp.concatenate(
                    [jnp.broadcast_to(x[i : i + 1], (seg, PAIR)) for i in range(land_local)], axis=0
                )
                for x in (total[:land_local], total[land_local:])
            ]
            grad[s, :, at] = (gq[s, :, at] + spread[0]).astype(BF)
            key_at = pl.ds(width + p * PAIR, PAIR)
            grad[s, :, key_at] = (grad[s, :, key_at].astype(F32) + spread[1]).astype(BF)
            grad[s, :, pl.ds(2 * width + p * PAIR, PAIR)] = gv[s, :, at].astype(BF)
        return carry

    lax.fori_loop(0, n_seq, close, 0)
    halo_sent()
    group.finish()


def attend_back(ga, q, k, vpad, table, landq, landk, mix, p1, e, wt, p2o, zo, lvo, seq_size, reach):
    n_seq, length, width = q.shape
    pairs = width // PAIR
    units = n_seq * pairs
    own = units // seq_size
    vmem = pl.BlockSpec(memory_space=pltpu.VMEM)
    shape = jax.ShapeDtypeStruct
    part = 2 * LAND // seq_size
    return pl.pallas_call(
        functools.partial(attend_back_kernel, reach, 2 * reach + 1),
        out_shape=[shape((n_seq, length, 3 * width), BF), shape((2 * pairs, 8, PAIR), F32)],
        in_specs=[vmem] * 14,
        out_specs=[vmem] * 2,
        scratch_shapes=[
            pltpu.VMEM((n_seq, length + 2 * reach, width), BF),
            pltpu.VMEM((n_seq, LAND, width), BF),
            pltpu.VMEM((seq_size, LAND, own * PAIR), BF),
            pltpu.VMEM((units, PAIR, length), BF),
            pltpu.VMEM((n_seq, LAND, width), BF),
            pltpu.VMEM((8, PAIR), F32),
            pltpu.VMEM((seq_size, 8, PAIR), F32),
            pltpu.VMEM((PAIR, PAIR), F32),
            pltpu.VMEM((n_seq, length, width), F32),
            pltpu.VMEM((n_seq, length, width), F32),
            pltpu.VMEM((n_seq, LAND, width), F32),
            pltpu.VMEM((seq_size, n_seq, part, width), BF),
            pltpu.VMEM((seq_size, n_seq, part, width), BF),
            pltpu.VMEM((seq_size, part, own * PAIR), BF),
            pltpu.VMEM((seq_size, part, own * PAIR), BF),
            pltpu.VMEM((own, PAIR, PAIR), F32),
            pltpu.VMEM((own, PAIR, PAIR), F32),
            pltpu.VMEM((2 * pairs, length, 2 * PAIR), F32),
            pltpu.VMEM((LAND, own * PAIR), BF),
            pltpu.SemaphoreType.DMA((6, seq_size)),
            pltpu.SemaphoreType.DMA((6, seq_size)),
        ],
        compiler_params=pltpu.CompilerParams(
            collective_id=3, has_side_effects=True, vmem_limit_bytes=56 * 1024 * 1024
        ),
        name="attend_back",
    )(ga, q, k, vpad, table, landq, landk, mix, p1, e, wt, p2o, zo, lvo)


def tap_sums(parts, count):
    return sum(parts[:, b, b : b + count] for b in range(8))


def kernels_fit(args):
    tokens, _, *matrices = args[:6]
    taps = args[7]
    seq_size = lax.axis_size("seq")
    n_seq, length, width = tokens.shape
    units = n_seq * width // PAIR
    own = units // seq_size
    return (
        lax.axis_size("rows") == 4
        and seq_size == 8
        and all(x.shape[0] % 24 == 0 and x.shape[1] % 256 == 0 for x in matrices)
        and width // taps.shape[0] == PAIR // 2
        and length == PAIR
        and taps.shape[1] == 33
        and taps.shape[0] <= matrices[0].shape[0]
        and units == own * seq_size
        and 2 * own <= 8
        and (width // PAIR) % own == 0
        and units % PINV_ITERS == 0
        and LAND == 8 * seq_size
    )


def all_weights(matrices, vectors):
    count = vectors.shape[0]
    table = jnp.pad(vectors.T, ((0, 0), (0, 256 - count)))
    whole = gather_weights(matrices + (table,), lax.axis_size("seq"))
    return (*whole[:4], whole[4][:, :count].T)


def all_grads(matrices, grad_vec, grad_taps):
    n_dev = lax.axis_size("rows") * lax.axis_size("seq")
    count, width = grad_vec.shape
    heads, taps = grad_taps.shape
    each = jnp.pad(grad_taps, ((0, width // n_dev - heads), (0, 0)))
    small = jnp.concatenate([grad_vec.T, jnp.tile(each, (n_dev, 1))], axis=1)
    small = jnp.pad(small, ((0, 0), (0, 256 - count - taps)))
    sums = scatter_grads([*matrices, small], lax.axis_size("seq"))
    return (*sums[:4], sums[4][:, :count].T, sums[4][:heads, count : count + taps])


def with_kernels(
    tokens, cotangent, qkv_weight, out_weight, up_weight, down_weight, vectors, taps,
    qkv_first, qkv_second, out_first, out_second, up_first, up_second, down_first, down_second,
    vec_first, vec_second, tap_first, tap_second,
):
    seq_count, local_len, model_width = tokens.shape
    head_count, tap_count = taps.shape
    hidden_width = up_weight.shape[1]
    seq_size = lax.axis_size("seq")
    reach = tap_count // 2
    row_count = seq_count * local_len
    full_qkv, full_out, full_up, full_down, full_vec = all_weights(
        (qkv_weight, out_weight, up_weight, down_weight), vectors
    )
    vec_float = full_vec.astype(jnp.float32)
    flat_in = tokens.reshape(row_count, model_width)
    project = jnp.dot(flat_in, full_qkv, preferred_element_type=jnp.float32)
    queries = (project[:, :model_width] + vec_float[0]).astype(BF).reshape(tokens.shape)
    key_rows = project[:, model_width : 2 * model_width].astype(BF).reshape(tokens.shape)
    values = (project[:, 2 * model_width :] + vec_float[1]).astype(BF).reshape(tokens.shape)
    attn, *kept = attend(
        queries, key_rows, values, bands(taps, local_len, reach, False), seq_size, reach
    )
    padded, land_q, land_k, mix, *rest = kept
    attn_low = attn.reshape(row_count, model_width)
    branch = jnp.dot(attn_low, full_out, preferred_element_type=jnp.float32) + vec_float[2]
    resid_one = flat_in.astype(jnp.float32) + branch
    normed, norm_pull_one = jax.vjp(layer_norm, resid_one, vec_float[6], vec_float[3])
    normed_low = normed.astype(BF)
    hidden_pre = jnp.dot(normed_low, full_up, preferred_element_type=jnp.float32) + vec_float[
        8:
    ].reshape(hidden_width)
    active, gelu_pull = jax.vjp(gelu_exact, hidden_pre)
    active_low = active.astype(BF)
    ff_out = jnp.dot(active_low, full_down, preferred_element_type=jnp.float32) + vec_float[4]
    layer_out, norm_pull_two = jax.vjp(layer_norm, normed + ff_out, vec_float[7], vec_float[5])
    grad_resid_two, grad_gain_two, grad_shift_two = norm_pull_two(
        cotangent.reshape(row_count, model_width).astype(jnp.float32)
    )
    grad_ff = grad_resid_two.astype(BF)
    grad_down = jnp.einsum("nf,nd->fd", active_low, grad_ff, preferred_element_type=jnp.float32)
    grad_active = jnp.einsum("nd,fd->nf", grad_ff, full_down, preferred_element_type=jnp.float32)
    grad_hidden = gelu_pull(grad_active)[0].astype(BF)
    grad_up = jnp.einsum("nd,nf->df", normed_low, grad_hidden, preferred_element_type=jnp.float32)
    grad_normed = (
        jnp.einsum("nf,df->nd", grad_hidden, full_up, preferred_element_type=jnp.float32)
        + grad_resid_two
    )
    grad_resid_one, grad_gain_one, grad_shift_one = norm_pull_one(grad_normed)
    grad_branch = grad_resid_one.astype(BF)
    grad_out = jnp.einsum("nd,ne->de", attn_low, grad_branch, preferred_element_type=jnp.float32)
    grad_attn = jnp.einsum(
        "ne,de->nd", grad_branch, full_out, preferred_element_type=jnp.float32
    ).astype(BF)
    grad_proj, tap_parts = attend_back(
        grad_attn.reshape(tokens.shape), queries, key_rows, padded,
        bands(taps, local_len, reach, True), land_q, land_k, mix, *rest, seq_size, reach,
    )
    grad_proj = grad_proj.reshape(row_count, 3 * model_width)
    grad_qkv = jnp.einsum("nd,ne->de", flat_in, grad_proj, preferred_element_type=jnp.float32)
    input_grad = (
        jnp.einsum("ne,de->nd", grad_proj, full_qkv, preferred_element_type=jnp.float32)
        + grad_resid_one
    )
    input_grad = input_grad.astype(BF).reshape(tokens.shape)
    bias_sums = jnp.sum(grad_proj.astype(jnp.float32), axis=0)
    grad_vec = jnp.concatenate(
        [
            bias_sums[None, :model_width],
            bias_sums[None, 2 * model_width :],
            jnp.sum(grad_branch.astype(jnp.float32), axis=0)[None],
            grad_shift_one[None],
            jnp.sum(grad_ff.astype(jnp.float32), axis=0)[None],
            grad_shift_two[None],
            grad_gain_one[None],
            grad_gain_two[None],
            jnp.sum(grad_hidden.astype(jnp.float32), axis=0).reshape(-1, model_width),
        ],
        axis=0,
    )
    summed_qkv, summed_out, summed_up, summed_down, summed_vec, summed_taps = all_grads(
        [x.astype(BF) for x in (grad_qkv, grad_out, grad_up, grad_down)],
        grad_vec,
        tap_sums(tap_parts, tap_count),
    )
    new_qkv = adam_step(qkv_weight, qkv_first, qkv_second, summed_qkv, rate_matrix, decay_rate)
    new_out = adam_step(out_weight, out_first, out_second, summed_out, rate_output, decay_rate)
    new_up = adam_step(up_weight, up_first, up_second, summed_up, rate_matrix, decay_rate)
    new_down = adam_step(down_weight, down_first, down_second, summed_down, rate_matrix, decay_rate)
    new_vec = adam_step(vectors, vec_first, vec_second, summed_vec, rate_vector, 0.0)
    new_taps = adam_step(taps, tap_first, tap_second, summed_taps, rate_taps, 0.0)
    out_tokens = layer_out.astype(BF).reshape(tokens.shape)
    return (out_tokens, input_grad) + new_qkv + new_out + new_up + new_down + new_vec + new_taps


def on_device(*args):
    return with_kernels(*args) if kernels_fit(args) else with_collectives(*args)


def solution(mesh):
    return jax.shard_map(
        on_device,
        mesh=mesh,
        in_specs=(
            P("rows", "seq", None),
            P("rows", "seq", None),
            P(("rows", "seq"), None),
            P(("rows", "seq"), None),
            P(("rows", "seq"), None),
            P(("rows", "seq"), None),
            P(None, ("rows", "seq")),
            P(),
            P(("rows", "seq"), None),
            P(("rows", "seq"), None),
            P(("rows", "seq"), None),
            P(("rows", "seq"), None),
            P(("rows", "seq"), None),
            P(("rows", "seq"), None),
            P(("rows", "seq"), None),
            P(("rows", "seq"), None),
            P(None, ("rows", "seq")),
            P(None, ("rows", "seq")),
            P(),
            P(),
        ),
        out_specs=(
            P("rows", "seq", None),
            P("rows", "seq", None),
            P(("rows", "seq"), None),
            P(("rows", "seq"), None),
            P(("rows", "seq"), None),
            P(("rows", "seq"), None),
            P(("rows", "seq"), None),
            P(("rows", "seq"), None),
            P(("rows", "seq"), None),
            P(("rows", "seq"), None),
            P(("rows", "seq"), None),
            P(("rows", "seq"), None),
            P(("rows", "seq"), None),
            P(("rows", "seq"), None),
            P(None, ("rows", "seq")),
            P(None, ("rows", "seq")),
            P(None, ("rows", "seq")),
            P(),
            P(),
            P(),
        ),
        check_vma=False,
    )
```

```python
import functools

import jax
import jax.numpy as jnp
from jax import lax
from jax.experimental import pallas as pl
from jax.experimental.pallas import tpu as pltpu
from jax.sharding import PartitionSpec as P

LAND = 64
PINV_ITERS = 6


top_precision = lax.Precision.HIGHEST
norm_eps = 1e-05
beta_one = 0.9
beta_two = 0.999
corr_one = 1.0 - 0.9**10
corr_two = 1.0 - 0.999**10
adam_eps = 1e-08
decay_rate = 0.01
rate_matrix = 0.03
rate_output = 0.12
rate_vector = 0.3
rate_taps = 0.08


def with_halo(x, sides, width):
    for axis, dim in sides:
        size, length = (lax.axis_size(axis), x.shape[dim])
        up = [(i, (i + 1) % size) for i in range(size - 1)]
        down = [(j, i) for i, j in up]
        last = lax.slice_in_dim(x, length - width, length, axis=dim)
        initial = lax.slice_in_dim(x, 0, width, axis=dim)
        before = lax.ppermute(last, axis, up)
        after = lax.ppermute(initial, axis, down)
        x = jnp.concatenate([before, x, after], axis=dim)
    return x


def layer_norm(residual, gain_row, shift_row):
    center = residual - jnp.mean(residual, axis=-1, keepdims=True)
    spread = jnp.mean(center * center, axis=-1, keepdims=True)
    return center * lax.rsqrt(spread + norm_eps) * gain_row + shift_row


def normalized_rows(scores):
    expo = jnp.exp(scores - jnp.max(scores, axis=-1, keepdims=True))
    return expo / jnp.sum(expo, axis=-1, keepdims=True)


def softmax_back(probability, grad_in):
    return probability * (grad_in - jnp.sum(probability * grad_in, axis=-1, keepdims=True))


def gelu_exact(inputs):
    return jax.nn.gelu(inputs, approximate=False)


def pseudo_inverse(matrix):
    identity = jnp.eye(matrix.shape[-1], dtype=jnp.float32)
    approx = jnp.swapaxes(matrix, -1, -2) / jnp.sum(matrix * matrix, axis=(-2, -1), keepdims=True)
    for sweep_index in range(PINV_ITERS):
        product = jnp.matmul(matrix, approx, precision=top_precision)
        inner_term = 7.0 * identity - product
        inner_term = 15.0 * identity - jnp.matmul(product, inner_term, precision=top_precision)
        inner_term = 13.0 * identity - jnp.matmul(product, inner_term, precision=top_precision)
        approx = 0.25 * jnp.matmul(approx, inner_term, precision=top_precision)
    return approx


def adam_step(weight, first_moment, second, gradient, step_rate, decay_coef):
    new_first = beta_one * first_moment + (1.0 - beta_one) * gradient
    new_second = beta_two * second + (1.0 - beta_two) * gradient * gradient
    update = new_first / corr_one / (jnp.sqrt(new_second / corr_two) + adam_eps)
    return (new_first, new_second, weight - step_rate * (update + decay_coef * weight))


def with_collectives(
    tokens,
    cotangent,
    qkv_weight,
    out_weight,
    up_weight,
    down_weight,
    vectors,
    taps,
    qkv_first,
    qkv_second,
    out_first,
    out_second,
    up_first,
    up_second,
    down_first,
    down_second,
    vec_first,
    vec_second,
    tap_first,
    tap_second,
):
    seq_count, local_len, model_width = tokens.shape
    head_count, tap_count = taps.shape
    head_size = model_width // head_count
    hidden_width = up_weight.shape[1]
    land_local = LAND // lax.axis_size("seq")
    seg_len = local_len // land_local
    reach_width = tap_count // 2
    logit_scale_factor = head_size ** (-0.5)
    row_count = seq_count * local_len
    head_shape = (seq_count, local_len, head_count, head_size)
    land_shape = (seq_count, LAND, head_count, head_size)
    full_qkv, full_out, full_up, full_down, full_vec = (
        lax.all_gather(qkv_weight.astype(jnp.bfloat16), ("rows", "seq"), axis=0, tiled=True),
        lax.all_gather(out_weight.astype(jnp.bfloat16), ("rows", "seq"), axis=0, tiled=True),
        lax.all_gather(up_weight.astype(jnp.bfloat16), ("rows", "seq"), axis=0, tiled=True),
        lax.all_gather(down_weight.astype(jnp.bfloat16), ("rows", "seq"), axis=0, tiled=True),
        lax.all_gather(vectors.astype(jnp.bfloat16), ("rows", "seq"), axis=1, tiled=True),
    )
    vec_float = full_vec.astype(jnp.float32)
    flat_in = tokens.reshape(row_count, model_width)
    project = jnp.dot(flat_in, full_qkv, preferred_element_type=jnp.float32)
    queries = (project[:, :model_width] + vec_float[0]).astype(jnp.bfloat16)
    key_rows = project[:, model_width : 2 * model_width].astype(jnp.bfloat16)
    values = (project[:, 2 * model_width :] + vec_float[1]).astype(jnp.bfloat16)
    seg_shape = (seq_count, land_local, seg_len, model_width)
    own_q = jnp.mean(queries.reshape(seg_shape), axis=2, dtype=jnp.float32).astype(jnp.bfloat16)
    own_k = jnp.mean(key_rows.reshape(seg_shape), axis=2, dtype=jnp.float32).astype(jnp.bfloat16)
    land_q, land_k = (
        lax.all_gather(own_q, "seq", axis=1, tiled=True),
        lax.all_gather(own_k, "seq", axis=1, tiled=True),
    )
    query_heads = queries.reshape(head_shape)
    key_heads = key_rows.reshape(head_shape)
    value_heads = values.reshape(head_shape)
    landmark_query_heads = land_q.reshape(land_shape)
    landmark_key_heads = land_k.reshape(land_shape)
    lq_float = landmark_query_heads.astype(jnp.float32)
    lk_float = landmark_key_heads.astype(jnp.float32)
    score_one = (
        jnp.einsum(
            "sthd,slhd->shtl", query_heads, landmark_key_heads, preferred_element_type=jnp.float32
        )
        * logit_scale_factor
    )
    prob_one = normalized_rows(score_one)
    second_probability = normalized_rows(
        jnp.einsum("slhd,smhd->shlm", lq_float, lk_float, precision=top_precision)
        * logit_scale_factor
    )
    inverse_matrix, inverse_pull = jax.vjp(pseudo_inverse, second_probability)
    score_three = (
        jnp.einsum(
            "slhd,sthd->shlt", landmark_query_heads, key_heads, preferred_element_type=jnp.float32
        )
        * logit_scale_factor
    )
    row_max = lax.pmax(jnp.max(score_three, axis=-1), "seq")
    expo_three = jnp.exp(score_three - row_max[..., None])
    numer_local = jnp.einsum(
        "shlt,sthd->slhd",
        expo_three.astype(jnp.bfloat16),
        value_heads,
        preferred_element_type=jnp.float32,
    )
    numer, denom = (
        lax.psum(numer_local.astype(jnp.bfloat16), "seq").astype(jnp.float32),
        lax.psum(jnp.sum(expo_three, axis=-1).astype(jnp.bfloat16), "seq").astype(jnp.float32),
    )
    denom_swap = jnp.swapaxes(denom, 1, 2)[..., None]
    landmark_value_rows = numer / denom_swap
    mixing_kernel = jnp.einsum(
        "shlm,smhd->slhd", inverse_matrix, landmark_value_rows, precision=top_precision
    )
    mix_low = mixing_kernel.astype(jnp.bfloat16)
    prob_low = prob_one.astype(jnp.bfloat16)
    attend = jnp.einsum("shtl,slhd->sthd", prob_low, mix_low, preferred_element_type=jnp.float32)
    attend = attend.reshape(seq_count, local_len, model_width)
    tap_chan = jnp.repeat(taps, head_size, axis=0)
    padded_values = with_halo(
        values.reshape(seq_count, local_len, model_width), (("seq", 1),), reach_width
    )
    conv_out = jnp.zeros((seq_count, local_len, model_width), jnp.float32)
    for offset in range(tap_count):
        conv_out = conv_out + tap_chan[:, offset] * padded_values[
            :, offset : offset + local_len
        ].astype(jnp.float32)
    attn_low = (attend + conv_out).reshape(row_count, model_width).astype(jnp.bfloat16)
    branch = jnp.dot(attn_low, full_out, preferred_element_type=jnp.float32) + vec_float[2]
    resid_one = flat_in.astype(jnp.float32) + branch
    normed, norm_pull_one = jax.vjp(layer_norm, resid_one, vec_float[6], vec_float[3])
    normed_low = normed.astype(jnp.bfloat16)
    hidden_pre = jnp.dot(normed_low, full_up, preferred_element_type=jnp.float32) + vec_float[
        8:
    ].reshape(hidden_width)
    active, gelu_pull = jax.vjp(gelu_exact, hidden_pre)
    active_low = active.astype(jnp.bfloat16)
    ff_out = jnp.dot(active_low, full_down, preferred_element_type=jnp.float32) + vec_float[4]
    layer_out, norm_pull_two = jax.vjp(layer_norm, normed + ff_out, vec_float[7], vec_float[5])
    grad_resid_two, grad_gain_two, grad_shift_two = norm_pull_two(
        cotangent.reshape(row_count, model_width).astype(jnp.float32)
    )
    grad_ff = grad_resid_two.astype(jnp.bfloat16)
    grad_down = jnp.einsum("nf,nd->fd", active_low, grad_ff, preferred_element_type=jnp.float32)
    grad_active = jnp.einsum("nd,fd->nf", grad_ff, full_down, preferred_element_type=jnp.float32)
    grad_hidden = gelu_pull(grad_active)[0].astype(jnp.bfloat16)
    grad_up = jnp.einsum("nd,nf->df", normed_low, grad_hidden, preferred_element_type=jnp.float32)
    grad_normed = (
        jnp.einsum("nf,df->nd", grad_hidden, full_up, preferred_element_type=jnp.float32)
        + grad_resid_two
    )
    grad_resid_one, grad_gain_one, grad_shift_one = norm_pull_one(grad_normed)
    grad_branch = grad_resid_one.astype(jnp.bfloat16)
    grad_out = jnp.einsum("nd,ne->de", attn_low, grad_branch, preferred_element_type=jnp.float32)
    grad_attn = jnp.einsum(
        "ne,de->nd", grad_branch, full_out, preferred_element_type=jnp.float32
    ).astype(jnp.bfloat16)
    grad_attn_heads = grad_attn.reshape(head_shape)
    grad_prob_one = jnp.einsum(
        "sthd,slhd->shtl", grad_attn_heads, mix_low, preferred_element_type=jnp.float32
    )
    mixing_part = jnp.einsum(
        "shtl,sthd->slhd", prob_low, grad_attn_heads, preferred_element_type=jnp.float32
    )
    grad_mixing = lax.psum(mixing_part.astype(jnp.bfloat16), "seq").astype(jnp.float32)
    grad_score_one = softmax_back(prob_one, grad_prob_one).astype(jnp.bfloat16)
    query_local = (
        jnp.einsum(
            "shtl,slhd->sthd",
            grad_score_one,
            landmark_key_heads,
            preferred_element_type=jnp.float32,
        )
        * logit_scale_factor
    )
    land_k_part = (
        jnp.einsum(
            "shtl,sthd->slhd", grad_score_one, query_heads, preferred_element_type=jnp.float32
        )
        * logit_scale_factor
    )
    grad_pad = with_halo(
        grad_attn.reshape(seq_count, local_len, model_width), (("seq", 1),), reach_width
    )
    attn_float = grad_attn.reshape(seq_count, local_len, model_width).astype(jnp.float32)
    conv_back = jnp.zeros((seq_count, local_len, model_width), jnp.float32)
    tap_terms = []
    for offset in range(tap_count):
        start_row = 2 * reach_width - offset
        conv_back = conv_back + tap_chan[:, offset] * grad_pad[
            :, start_row : start_row + local_len
        ].astype(jnp.float32)
        tap_terms.append(
            jnp.sum(
                attn_float * padded_values[:, offset : offset + local_len].astype(jnp.float32),
                axis=(0, 1),
            )
        )
    grad_taps = jnp.sum(
        jnp.stack(tap_terms, axis=1).reshape(head_count, head_size, tap_count), axis=1
    )
    grad_inverse = jnp.einsum(
        "slhd,smhd->shlm", grad_mixing, landmark_value_rows, precision=top_precision
    )
    grad_land_values = jnp.einsum(
        "shlm,slhd->smhd", inverse_matrix, grad_mixing, precision=top_precision
    )
    land_grad_low = grad_land_values.astype(jnp.bfloat16).astype(jnp.float32)
    grad_prob_two = inverse_pull(grad_inverse)[0]
    grad_score_two = softmax_back(second_probability, grad_prob_two)
    query_two = (
        jnp.einsum("shlm,smhd->slhd", grad_score_two, lk_float, precision=top_precision)
        * logit_scale_factor
    )
    key_two = (
        jnp.einsum("shlm,slhd->smhd", grad_score_two, lq_float, precision=top_precision)
        * logit_scale_factor
    )
    grad_numer = land_grad_low / denom_swap
    expo_low = expo_three.astype(jnp.bfloat16).astype(jnp.float32)
    value_three = jnp.einsum("shlt,slhd->sthd", expo_low, grad_numer, precision=top_precision)
    grad_expo = jnp.einsum(
        "slhd,sthd->shlt", grad_numer, value_heads.astype(jnp.float32), precision=top_precision
    )
    grad_denom = jnp.swapaxes(jnp.sum(land_grad_low * landmark_value_rows, axis=-1), 1, 2) / denom
    grad_score_three = (expo_three * (grad_expo - grad_denom[..., None])).astype(jnp.bfloat16)
    land_q_part = (
        jnp.einsum(
            "shlt,sthd->slhd", grad_score_three, key_heads, preferred_element_type=jnp.float32
        )
        * logit_scale_factor
    )
    key_local = (
        jnp.einsum(
            "shlt,slhd->sthd",
            grad_score_three,
            landmark_query_heads,
            preferred_element_type=jnp.float32,
        )
        * logit_scale_factor
    )
    land_q_own, land_k_own = (
        lax.psum_scatter(
            land_q_part.astype(jnp.bfloat16), "seq", scatter_dimension=1, tiled=True
        ).astype(jnp.float32),
        lax.psum_scatter(
            land_k_part.astype(jnp.bfloat16), "seq", scatter_dimension=1, tiled=True
        ).astype(jnp.float32),
    )
    first_land = lax.axis_index("seq") * land_local
    land_q_own = land_q_own + lax.dynamic_slice_in_dim(query_two, first_land, land_local, 1)
    land_k_own = land_k_own + lax.dynamic_slice_in_dim(key_two, first_land, land_local, 1)
    spread_shape = (seq_count, land_local, seg_len, head_count, head_size)
    spread_q = jnp.broadcast_to((land_q_own / seg_len)[:, :, None], spread_shape).reshape(
        head_shape
    )
    spread_k = jnp.broadcast_to((land_k_own / seg_len)[:, :, None], spread_shape).reshape(
        head_shape
    )
    grad_query = (query_local + spread_q).reshape(row_count, model_width)
    grad_key = (key_local + spread_k).reshape(row_count, model_width)
    grad_value = value_three.reshape(row_count, model_width) + conv_back.reshape(
        row_count, model_width
    )
    grad_proj = jnp.concatenate([grad_query, grad_key, grad_value], axis=1).astype(jnp.bfloat16)
    grad_qkv = jnp.einsum("nd,ne->de", flat_in, grad_proj, preferred_element_type=jnp.float32)
    input_grad = (
        jnp.einsum("ne,de->nd", grad_proj, full_qkv, preferred_element_type=jnp.float32)
        + grad_resid_one
    )
    input_grad = input_grad.astype(jnp.bfloat16).reshape(tokens.shape)
    bias_sums = jnp.sum(grad_proj.astype(jnp.float32), axis=0)
    grad_vec = jnp.concatenate(
        [
            bias_sums[None, :model_width],
            bias_sums[None, 2 * model_width :],
            jnp.sum(grad_branch.astype(jnp.float32), axis=0)[None],
            grad_shift_one[None],
            jnp.sum(grad_ff.astype(jnp.float32), axis=0)[None],
            grad_shift_two[None],
            grad_gain_one[None],
            grad_gain_two[None],
            jnp.sum(grad_hidden.astype(jnp.float32), axis=0).reshape(-1, model_width),
        ],
        axis=0,
    )
    summed_qkv, summed_out, summed_up, summed_down, summed_vec = (
        lax.psum_scatter(grad_qkv, ("rows", "seq"), scatter_dimension=0, tiled=True),
        lax.psum_scatter(grad_out, ("rows", "seq"), scatter_dimension=0, tiled=True),
        lax.psum_scatter(grad_up, ("rows", "seq"), scatter_dimension=0, tiled=True),
        lax.psum_scatter(grad_down, ("rows", "seq"), scatter_dimension=0, tiled=True),
        lax.psum_scatter(grad_vec, ("rows", "seq"), scatter_dimension=1, tiled=True),
    )
    summed_taps = lax.psum(grad_taps, ("rows", "seq"))
    new_qkv = adam_step(qkv_weight, qkv_first, qkv_second, summed_qkv, rate_matrix, decay_rate)
    new_out = adam_step(out_weight, out_first, out_second, summed_out, rate_output, decay_rate)
    new_up = adam_step(up_weight, up_first, up_second, summed_up, rate_matrix, decay_rate)
    new_down = adam_step(down_weight, down_first, down_second, summed_down, rate_matrix, decay_rate)
    new_vec = adam_step(vectors, vec_first, vec_second, summed_vec, rate_vector, 0.0)
    new_taps = adam_step(taps, tap_first, tap_second, summed_taps, rate_taps, 0.0)
    out_tokens = layer_out.astype(jnp.bfloat16).reshape(tokens.shape)
    return (out_tokens, input_grad) + new_qkv + new_out + new_up + new_down + new_vec + new_taps


BF = jnp.bfloat16
F32 = jnp.float32
MESH = pl.DeviceIdType.MESH


def remote(src, dst, send_sem, recv_sem, device):
    return pltpu.make_async_remote_copy(
        src_ref=src, dst_ref=dst, send_sem=send_sem, recv_sem=recv_sem,
        device_id=device, device_id_type=MESH,
    )


def place():
    row, spot = lax.axis_index("rows"), lax.axis_index("seq")
    line, core = spot // 2, spot % 2
    flip_one = row + 1 - 2 * (row % 2)
    flip_two = row + 2 - 4 * (row // 2)
    first = (1 - core) * flip_one + core * flip_two
    second = (1 - core) * flip_two + core * flip_one
    return row, line, core, first, second, 3 - row


def greet(devices):
    barrier = pltpu.get_barrier_semaphore()
    for device in devices:
        pl.semaphore_signal(barrier, inc=1, device_id=device, device_id_type=MESH)
    pl.semaphore_wait(barrier, len(devices))


class Net:
    def __init__(self, send, recv):
        self.send, self.recv, self.started = send, recv, []
        self.row, self.line, self.core, self.first, self.second, self.across = place()
        self.line_size = lax.axis_size("seq") // 2
        own_spot = 2 * self.line + self.core
        self.sibling = (self.row, 2 * self.line + 1 - self.core)
        self.peers = [
            (self.row, 2 * ((self.line + k) % self.line_size) + self.core)
            for k in range(1, self.line_size)
        ]
        self.to_first, self.to_second = (self.first, own_spot), (self.second, own_spot)

    def go(self, w, k, src, dst, device):
        copy = remote(src, dst, self.send.at[w, k], self.recv.at[w, k], device)
        copy.start()
        self.started.append(copy)
        return copy

    def finish(self):
        for copy in self.started:
            copy.wait_send()


def columns(base, which, half):
    return pl.ds(pl.multiple_of(base + which * half, 128), half)


class Gather:
    def __init__(self, net, w, src, dst, base, half, asm, stage, local):
        self.net, self.w, self.dst, self.stage, self.asm = net, w, dst, stage, asm
        self.rows, self.base, self.half, self.local = src.shape[0], base, half, local
        part = pl.ds(pl.multiple_of(net.core * self.rows, 8), self.rows)
        there = columns(base, 1 - net.core, half)
        self.asm_copy = net.go(w, 0, src.at[:, there], asm.at[part, :], net.sibling)
        asm[part, :] = src[:, columns(base, net.core, half)]

    def block(self, start, size):
        at = pl.ds(pl.multiple_of(start, 16), size)
        return self.dst.at[at, columns(self.base, self.net.core, self.half)]

    def slab(self, index):
        size = 2 * self.rows * self.net.line_size
        return self.block(index * size, size)

    def spread(self):
        net = self.net
        self.asm_copy.wait_recv()
        self.stage[...] = self.asm[...].astype(BF)
        size = 2 * self.rows
        block = self.block((net.row * net.line_size + net.line) * size, size)
        self.z = [net.go(self.w, 1 + k, self.stage, block, d) for k, d in enumerate(net.peers)]
        self.own = pltpu.make_async_copy(self.stage, block, self.local)
        self.own.start()

    def step_one(self):
        net, w, z0 = self.net, self.w, self.net.line_size
        self.own.wait()
        for copy in self.z:
            copy.wait_recv()
        mine = self.slab(net.row)
        self.hop = [net.go(w, z0, mine, mine, net.to_first)]
        self.hop.append(net.go(w, z0 + 1, mine, mine, net.to_second))
        self.sib = [net.go(w, z0 + 3, mine, mine, net.sibling)]

    def step_two(self):
        net, w, z0 = self.net, self.w, self.net.line_size
        self.hop[0].wait_recv()
        got = self.slab(net.first)
        self.hop.append(net.go(w, z0 + 2, got, got, net.to_second))
        self.sib.append(net.go(w, z0 + 4, got, got, net.sibling))

    def step_three(self):
        net, w, z0 = self.net, self.w, self.net.line_size
        self.hop[1].wait_recv()
        got = self.slab(net.second)
        self.sib.append(net.go(w, z0 + 5, got, got, net.sibling))
        self.hop[2].wait_recv()
        got = self.slab(net.across)
        self.sib.append(net.go(w, z0 + 6, got, got, net.sibling))

    def close(self):
        for copy in self.sib:
            copy.wait_recv()


GATHER_SEMS = 7


class Scatter:
    def __init__(self, net, w, out, base, half, bufs):
        self.net, self.w, self.out, self.base, self.half = net, w, out, base, half
        self.acc, self.buf0, self.buf1, self.buf2, self.buf3, self.fin = bufs
        self.rows = out.shape[0]
        self.size = 2 * self.rows * net.line_size

    def open(self, outbox, own=None):
        self.sib = self.net.go(self.w, 0, outbox, self.buf0, self.net.sibling)
        self.own = own
        if own is not None:
            own.start()

    def slab(self, index):
        return pl.ds(pl.multiple_of(index * self.size, self.size), self.size)

    def add(self, index, other, start):
        step = 48
        acc = self.acc

        def one(i, carry):
            at = pl.ds(pl.multiple_of(index * self.size + i * step, 16), step)
            there = pl.ds(pl.multiple_of(start + i * step, 16), step)
            acc[at, :] = acc[at, :] + other[there, :]
            return carry

        lax.fori_loop(0, self.size // step, one, 0)

    def step_one(self):
        net, w = self.net, self.w
        if self.own is not None:
            self.own.wait()
        self.sib.wait_recv()
        self.add(net.across, self.buf0, net.across * self.size)
        acc = self.acc
        self.one = net.go(w, 1, acc.at[self.slab(net.across), :], self.buf1.at[0], net.to_second)
        self.add(net.second, self.buf0, net.second * self.size)
        self.two = net.go(w, 2, acc.at[self.slab(net.second), :], self.buf1.at[1], net.to_second)
        self.add(net.first, self.buf0, net.first * self.size)
        self.add(net.row, self.buf0, net.row * self.size)

    def step_two(self):
        net = self.net
        self.one.wait_recv()
        self.add(net.first, self.buf1.at[0], 0)
        src = self.acc.at[self.slab(net.first), :]
        self.three = net.go(self.w, 3, src, self.buf2, net.to_first)
        self.two.wait_recv()
        self.add(net.row, self.buf1.at[1], 0)

    def step_three(self):
        net = self.net
        self.three.wait_recv()
        self.add(net.row, self.buf2, 0)
        block, n = 2 * self.rows, net.line_size
        self.z = []

        def at(line):
            return pl.ds(pl.multiple_of((net.row * n + line) * block, block), block)

        for k, device in enumerate(net.peers):
            src = self.acc.at[at((net.line + 1 + k) % n), :]
            self.z.append(net.go(self.w, 4 + k, src, self.buf3.at[net.line], device))
        self.buf3[net.line] = self.acc[at(net.line), :]

    def step_four(self):
        net = self.net
        for copy in self.z:
            copy.wait_recv()
        total = self.buf3[0].astype(F32)
        for k in range(1, net.line_size):
            total = total + self.buf3[k].astype(F32)
        self.fin[...] = total
        part = pl.ds(pl.multiple_of((1 - net.core) * self.rows, 8), self.rows)
        here = columns(self.base, net.core, self.half)
        self.last = net.go(
            self.w, 3 + net.line_size, self.fin.at[part, :], self.out.at[:, here], net.sibling
        )
        part = pl.ds(pl.multiple_of(net.core * self.rows, 8), self.rows)
        self.out[:, here] = self.fin[part, :]

    def close(self):
        self.last.wait_recv()


SCATTER_SEMS = 4


def scatter_scratch(rows, half, dtype, line_size):
    quarter = 2 * rows * line_size
    return [
        pltpu.VMEM((4 * quarter, half), dtype),
        pltpu.VMEM((4 * quarter, half), dtype),
        pltpu.VMEM((2, quarter, half), dtype),
        pltpu.VMEM((quarter, half), dtype),
        pltpu.VMEM((line_size, 2 * rows, half), dtype),
        pltpu.VMEM((2 * rows, half), F32),
    ]


PAIR = 128


def nn(a, b):
    return jnp.dot(a, b, preferred_element_type=F32)


def nt(a, b):
    return lax.dot_general(a, b, (((1,), (1,)), ((), ())), preferred_element_type=F32)


def tn(a, b):
    return lax.dot_general(a, b, (((0,), (0,)), ((), ())), preferred_element_type=F32)


def split(x):
    high = x.astype(BF)
    return high, (x - high.astype(F32)).astype(BF)


def three(dot, a, b):
    return dot(a[0], b[0]) + (dot(a[0], b[1]) + dot(a[1], b[0]))


def lane_masks(dtype):
    lane = lax.broadcasted_iota(jnp.int32, (1, PAIR), 1)
    one = (lane < PAIR // 2).astype(F32)
    return one.astype(dtype), (1.0 - one).astype(dtype)


def apart(x):
    one, two = lane_masks(x.dtype)
    return jnp.concatenate([x * one, x * two], axis=0)


def together(x):
    half = PAIR // 2
    lane = lax.broadcasted_iota(jnp.int32, (half, PAIR), 1)
    return jnp.where(lane < half, x[:half], x[half:])


def same_head():
    half = PAIR // 2
    a = lax.broadcasted_iota(jnp.int32, (PAIR, PAIR), 0) // half
    b = lax.broadcasted_iota(jnp.int32, (PAIR, PAIR), 1) // half
    return a == b


def eye():
    a = lax.broadcasted_iota(jnp.int32, (PAIR, PAIR), 0)
    b = lax.broadcasted_iota(jnp.int32, (PAIR, PAIR), 1)
    return (a == b).astype(F32)


def by_head(x, reduce):
    half, width = PAIR // 2, x.shape[1]
    parts = [reduce(x[h * half : (h + 1) * half], axis=0, keepdims=True) for h in (0, 1)]
    return jnp.concatenate([jnp.broadcast_to(y, (half, width)) for y in parts], axis=0)


def lanes(p):
    if isinstance(p, int):
        return pl.ds(p * PAIR, PAIR)
    return pl.ds(pl.multiple_of(p * PAIR, PAIR), PAIR)


def conv_pair(table, padded):
    size = table.shape[0] // 4
    out = nn(table, padded)
    lane = lax.broadcasted_iota(jnp.int32, (size, PAIR), 1)
    return jnp.where(
        lane < PAIR // 2,
        out[:size] + out[2 * size : 3 * size],
        out[size : 2 * size] + out[3 * size :],
    )


class Group:
    def __init__(self, send, recv):
        self.row, self.me = lax.axis_index("rows"), lax.axis_index("seq")
        self.size = lax.axis_size("seq")
        self.send, self.recv, self.started = send, recv, []

    def peers(self):
        return [(self.row, (self.me + k) % self.size) for k in range(1, self.size)]

    def push(self, channel, pick_src, dst):
        copies = []
        for k, device in enumerate(self.peers()):
            copy = remote(
                pick_src(device[1]), dst, self.send.at[channel, k], self.recv.at[channel, k], device
            )
            copy.start()
            copies.append(copy)
        self.started += copies
        return copies

    def halo(self, channel, source, padded, reach):
        length = source.shape[1]
        copies = []
        for which, (src_at, dst_at, step) in enumerate(
            ((length - reach, 0, 1), (0, length + reach, -1))
        ):
            there = (self.me + step + self.size) % self.size
            copy = remote(
                source.at[:, pl.ds(src_at, reach), :],
                padded.at[:, pl.ds(dst_at, reach), :],
                self.send.at[channel, which],
                self.recv.at[channel, which],
                (self.row, there),
            )
            goes = self.me < self.size - 1 if step == 1 else self.me > 0
            comes = self.me > 0 if step == 1 else self.me < self.size - 1
            pl.when(goes)(copy.start)
            copies.append((copy, goes, comes, dst_at))

        def arrive():
            for copy, goes, comes, dst_at in copies:
                pl.when(comes)(copy.wait_recv)

                @pl.when(jnp.logical_not(comes))
                def _():
                    shape = (padded.shape[0], reach, padded.shape[2])
                    padded[:, pl.ds(dst_at, reach), :] = jnp.zeros(shape, padded.dtype)

        def sent():
            for copy, goes, _, _ in copies:
                pl.when(goes)(copy.wait_send)

        return arrive, sent

    def finish(self):
        for copy in self.started:
            copy.wait_send()


def pinv_start(prob):
    total = by_head(jnp.sum(prob * prob, axis=1, keepdims=True), jnp.sum)
    return prob.T / total


def pinv_terms(p, z, unit):
    product = three(nn, p, z)
    prod = split(product)
    term_one = 7.0 * unit - product
    term_two = 15.0 * unit - three(nn, prod, split(term_one))
    term_three = 13.0 * unit - three(nn, prod, split(term_two))
    return prod, term_one, term_two, term_three


def band(line, length, reach):
    wide = jnp.broadcast_to(line, (length, line.shape[1]))
    return pltpu.roll(wide, 0, 1, stride=1, stride_axis=0)[:, : length + 2 * reach]


def fill_bands(lines, table, reach):
    pairs, rows = table.shape[0], table.shape[1] // 4
    for p in range(pairs):
        for h in (0, 1):
            high, low = split(band(lines[2 * p + h : 2 * p + h + 1, :], rows, reach))
            table[p, h * rows : (h + 1) * rows, :] = high
            table[p, (2 + h) * rows : (3 + h) * rows, :] = low


def front_kernel(
    reach,
    tokens, qkv_w, out_w, up_w, down_w, vec_w, lines,
    f_qkv, f_out, f_up, f_down, f_rows,
    q, k, attn, vpad, landq, landk, mix, p1, e, wt, p2o, zo, lvo,
    v, table, f_vec, lb, numer, nrecv, stat, srecv, mstat, conv, fcol, *rest,
):
    asm, stage = rest[:7], rest[7:14]
    g_send, g_recv, g_local, send, recv = rest[14:]
    net, group = Net(g_send, g_recv), Group(send, recv)
    me, size = group.me, group.size
    n_seq, length, width = q.shape
    pairs = width // PAIR
    own = n_seq * pairs // size
    each = own * PAIR
    land_local = LAND // size
    seg = length // land_local
    scale = (PAIR // 2) ** -0.5
    greet(group.peers() + [net.to_first, net.to_second])

    def owner_seq(d):
        return d * own // pairs

    def owner_lanes(d):
        return pl.ds(pl.multiple_of((d * own % pairs) * PAIR, PAIR), each)

    plan = [(vec_w, f_vec, 0), (qkv_w, f_qkv, width), (qkv_w, f_qkv, 0), (qkv_w, f_qkv, 2 * width)]
    plan += [(out_w, f_out, 0), (up_w, f_up, 0), (down_w, f_down, 0)]
    pieces = []
    for w, (src, dst, base) in enumerate(plan):
        half = asm[w].shape[1]
        pieces.append(Gather(net, w, src, dst, base, half, asm[w], stage[w], g_local.at[w]))
    g_vec, g_k, g_q, g_v, g_out, g_up, g_down = pieces
    for piece in pieces[:4]:
        piece.spread()
    fill_bands(lines, table, reach)

    def project(dst, base, bias):
        step = 2 * PAIR
        for at in range(0, width, step):
            x = nn(tokens[...], f_qkv[:, base + at : base + at + step])
            if bias is not None:
                x = x + f_rows[bias : bias + 1, at : at + step]
            dst[:, :, at : at + step] = x.astype(BF).reshape(n_seq, length, step)

    g_vec.step_one()
    g_k.step_one()
    g_q.step_one()
    g_vec.step_two()
    g_k.step_two()
    g_v.step_one()
    g_out.spread()
    g_up.spread()
    g_vec.step_three()
    g_q.step_two()
    g_k.step_three()
    g_down.spread()
    g_vec.close()
    f_rows[...] = f_vec[:, :PAIR].astype(F32).T[: f_rows.shape[0]]
    g_v.step_two()
    g_k.close()
    project(k, width, None)
    g_q.step_three()
    g_q.close()
    project(q, 0, 0)
    g_v.step_three()
    g_out.step_one()
    g_up.step_one()
    g_v.close()
    project(v, 2 * width, 1)

    def own_landmarks(s, carry):
        both = [
            jnp.mean(x[s].astype(F32).reshape(land_local, seg, width), axis=1) for x in (q, k)
        ]
        lb[me, s] = jnp.concatenate(both, axis=0).astype(BF)
        vpad[s, pl.ds(reach, length), :] = v[s]
        return carry

    lax.fori_loop(0, n_seq, own_landmarks, 0)
    landed = group.push(1, lambda d: lb.at[me], lb.at[me])
    halo_in, halo_sent = group.halo(0, v, vpad, reach)
    g_out.step_two()
    g_down.step_one()
    for copy in landed:
        copy.wait_recv()

    def whole_landmarks(s, carry):
        x = lb[:, s].astype(F32)
        landq[s] = x[:, :land_local].reshape(LAND, width).astype(BF)
        landk[s] = x[:, land_local:].reshape(LAND, width).astype(BF)
        return carry

    lax.fori_loop(0, n_seq, whole_landmarks, 0)
    lane_at = lax.broadcasted_iota(jnp.int32, (PAIR, PAIR), 1)

    def over_tokens(s, tile):
        for p in range(pairs):
            score = nt(apart(landq[s, :, lanes(p)]), k[s, :, lanes(p)]) * scale
            top = jnp.max(score, axis=1, keepdims=True)
            expo = jnp.exp(score - top)
            low = expo.astype(BF)
            e[s * pairs + p] = low
            numer[s, :, lanes(p)] = together(nn(low, v[s, :, lanes(p)])).astype(BF)
            unit = s * pairs + p
            at = (unit // own) * 8 + unit % own
            tile = jnp.where(lane_at == at, top, tile)
            tile = jnp.where(lane_at == at + own, jnp.sum(expo, axis=1, keepdims=True), tile)
        return tile

    tile = lax.fori_loop(0, n_seq, over_tokens, jnp.zeros((PAIR, PAIR), F32))
    stat[...] = tile.T[: 8 * size].reshape(size, 8, PAIR)
    sums_in = group.push(
        2, lambda d: numer.at[owner_seq(d), :, owner_lanes(d)], nrecv.at[me]
    )
    stats_in = group.push(3, lambda d: stat.at[d], srecv.at[me])
    g_up.step_two()
    nrecv[me] = numer[owner_seq(me), :, owner_lanes(me)]
    srecv[me] = stat[me]

    block, unit_matrix = same_head(), eye()
    my_seq, my_pair = owner_seq(me), (me * own) % pairs
    for i in range(own):
        at = lanes(my_pair + i)
        score = nt(apart(landq[my_seq, :, at]), apart(landk[my_seq, :, at])) * scale
        score = jnp.where(block, score, -1e30)
        expo = jnp.exp(score - jnp.max(score, axis=1, keepdims=True))
        prob = expo / jnp.sum(expo, axis=1, keepdims=True)
        p2o[i] = prob
        zo[0, i] = pinv_start(prob)

    halo_in()
    per_step = n_seq * pairs // PINV_ITERS

    def over_landmarks(unit):
        s, p = unit // pairs, unit % pairs
        score = nt(apart(landk[s, :, lanes(p)]), q[s, :, lanes(p)]) * scale
        expo = jnp.exp(score - by_head(score, jnp.max))
        p1[unit] = expo / by_head(expo, jnp.sum)
        conv[s, :, lanes(p)] = conv_pair(table[p], vpad[s, :, lanes(p)])

    def pinv_step(step, carry):
        for i in range(own):
            z = split(zo[step, i])
            _, _, _, inner = pinv_terms(split(p2o[i]), z, unit_matrix)
            zo[step + 1, i] = 0.25 * three(nn, z, split(inner))
        for j in range(per_step):
            over_landmarks(step * per_step + j)
        return carry

    lax.fori_loop(0, PINV_ITERS // 2, pinv_step, 0)
    g_out.step_three()
    g_down.step_two()
    lax.fori_loop(PINV_ITERS // 2, PINV_ITERS, pinv_step, 0)

    for copy in sums_in + stats_in:
        copy.wait_recv()
    got = srecv[...]
    tops = got[:, :own]
    top = jnp.max(tops, axis=0, keepdims=True)
    factor = jnp.exp(tops - top)
    total = jnp.sum(factor * got[:, own : 2 * own], axis=0, keepdims=True)
    factor = factor / total
    spare = jnp.zeros((1, 8 - 2 * own, PAIR), F32)
    mstat[me] = jnp.concatenate([top, total, spare], axis=1)[0]
    spread = jnp.concatenate([factor, jnp.zeros((size, 8 - own, PAIR), F32)], axis=1)
    spread = spread.reshape(8 * size, PAIR)
    fcol[...] = jnp.concatenate([spread, jnp.zeros((PAIR - 8 * size, PAIR), F32)], axis=0).T
    half = PAIR // 2
    narrow = lax.broadcasted_iota(jnp.int32, (half, PAIR), 1) < half
    for i in range(own):
        at = pl.ds(i * PAIR, PAIR)
        mean = jnp.zeros((half, PAIR), F32)
        for src in range(size):
            column = fcol[:, src * 8 + i : src * 8 + i + 1]
            weight = jnp.where(narrow, column[:half], column[half:])
            mean = mean + weight * nrecv[src, :, at].astype(F32)
        lvo[:, at] = mean
        mixed = together(three(nn, split(zo[PINV_ITERS, i]), split(apart(mean))))
        mix[my_seq, :, lanes(my_pair + i)] = mixed.astype(BF)
    mine = mix.at[my_seq, :, owner_lanes(me)]
    mix_in = group.push(4, lambda d: mine, mine)
    back_in = group.push(5, lambda d: mstat.at[me], mstat.at[me])
    g_up.step_three()
    for copy in mix_in + back_in:
        copy.wait_recv()

    rows = jnp.concatenate(
        [mstat[...].reshape(8 * size, PAIR), jnp.zeros((PAIR - 8 * size, PAIR), F32)], axis=0
    )
    rows = rows.T
    valid = (lane_at % 8 < own) & (lane_at < 8 * size)
    shift = jnp.where(valid, tile - rows, 0.0)
    den = jnp.where(valid, pltpu.roll(rows, PAIR - own, 1), 1.0)
    wt[...] = jnp.exp(shift) / den

    def result(s, carry):
        for p in range(pairs):
            low = p1[s * pairs + p].astype(BF)
            out = tn(low, apart(mix[s, :, lanes(p)])) + conv[s, :, lanes(p)]
            attn[s, :, lanes(p)] = out.astype(BF)
        return carry

    lax.fori_loop(0, n_seq, result, 0)
    g_down.step_three()
    for piece in (g_out, g_up, g_down):
        piece.close()
    halo_sent()
    group.finish()
    net.finish()


def front(tokens, matrices, table, lines, seq_size, reach):
    n_seq, length, width = tokens.shape
    pairs = width // PAIR
    units = n_seq * pairs
    own = units // seq_size
    n_dev = 4 * seq_size
    line_size = seq_size // 2
    vmem, hbm = pl.BlockSpec(memory_space=pltpu.VMEM), pl.BlockSpec(memory_space=pltpu.HBM)
    shape = jax.ShapeDtypeStruct
    land = shape((n_seq, LAND, width), BF)
    qkv_w, out_w, up_w, down_w = matrices
    whole = [shape((n_dev * x.shape[0], x.shape[1]), BF) for x in matrices]
    asm = [(table.shape[0], table.shape[1] // 2)] + [(qkv_w.shape[0], width // 2)] * 3
    asm += [(x.shape[0], x.shape[1] // 2) for x in (out_w, up_w, down_w)]
    n_sem = line_size + GATHER_SEMS
    return pl.pallas_call(
        functools.partial(front_kernel, reach),
        out_shape=whole
        + [
            shape((16, width), F32),
            shape(tokens.shape, BF), shape(tokens.shape, BF), shape(tokens.shape, BF),
            shape((n_seq, length + 2 * reach, width), BF), land, land, land,
            shape((units, PAIR, length), F32), shape((units, PAIR, length), BF),
            shape((PAIR, PAIR), F32), shape((own, PAIR, PAIR), F32),
            shape((PINV_ITERS + 1, own, PAIR, PAIR), F32), shape((LAND, own * PAIR), F32),
        ],
        in_specs=[vmem] * 7,
        out_specs=[vmem, hbm, hbm, hbm] + [vmem] * 14,
        scratch_shapes=[
            pltpu.VMEM(tokens.shape, BF),
            pltpu.VMEM((pairs, 4 * length, length + 2 * reach), BF),
            pltpu.VMEM((n_dev * table.shape[0], table.shape[1]), BF),
            pltpu.VMEM((seq_size, n_seq, 2 * LAND // seq_size, width), BF),
            pltpu.VMEM((n_seq, LAND, width), BF),
            pltpu.VMEM((seq_size, LAND, own * PAIR), BF),
            pltpu.VMEM((seq_size, 8, PAIR), F32),
            pltpu.VMEM((seq_size, 8, PAIR), F32),
            pltpu.VMEM((seq_size, 8, PAIR), F32),
            pltpu.VMEM((n_seq, length, width), F32),
            pltpu.VMEM((PAIR, PAIR), F32),
        ]
        + [pltpu.VMEM((2 * r, h), F32) for r, h in asm]
        + [pltpu.VMEM((2 * r, h), BF) for r, h in asm]
        + [
            pltpu.SemaphoreType.DMA((7, n_sem)),
            pltpu.SemaphoreType.DMA((7, n_sem)),
            pltpu.SemaphoreType.DMA((7,)),
            pltpu.SemaphoreType.DMA((6, seq_size)),
            pltpu.SemaphoreType.DMA((6, seq_size)),
        ],
        compiler_params=pltpu.CompilerParams(
            collective_id=0, has_side_effects=True, vmem_limit_bytes=56 * 1024 * 1024
        ),
        name="front",
    )(tokens.reshape(n_seq * length, width), *matrices, table, lines)


def back_kernel(
    reach, n_taps,
    ga, tokens, resid, f_qkv, vec_rows, lines, d_down, d_up, d_out,
    q, k, vpad, landq, landk, mix, p1, e, wt, p2o, zo, lvo,
    input_grad, s_qkv, s_out, s_up, s_down, s_small,
    grad, tapg, table, tok_t, outbox, small_box,
    gpad, gmix, gmr, low, gfull, stat, mstat, gcol, gq, gv, lkp, lpart, lpr, two, twr, dz, dp,
    skew, own_g, *rest,
):
    bufs, (g_send, g_recv, g_local, send, recv) = rest[:-5], rest[-5:]
    net, group = Net(g_send, g_recv), Group(send, recv)
    me, size = group.me, group.size
    n_seq, length, width = q.shape
    pairs = width // PAIR
    own = n_seq * pairs // size
    each = own * PAIR
    land_local = LAND // size
    seg = length // land_local
    half = PAIR // 2
    scale = half**-0.5
    greet(group.peers() + [net.to_first, net.to_second])

    def owner_seq(d):
        return d * own // pairs

    def owner_lanes(d):
        return pl.ds(pl.multiple_of((d * own % pairs) * PAIR, PAIR), each)

    plan = [(s_down, 0), (s_up, 0), (s_out, 0)]
    plan += [(s_qkv, 2 * width), (s_qkv, 0), (s_qkv, width), (s_small, 0)]
    pieces = []
    for w, (out, base) in enumerate(plan):
        own_bufs = bufs[6 * w : 6 * w + 6]
        pieces.append(Scatter(net, w, out, base, own_bufs[0].shape[1], own_bufs))
    r_down, r_up, r_out, r_v, r_q, r_k, r_small = pieces

    def open_whole(w, src):
        piece = pieces[w]
        other, here = [columns(0, c, piece.half) for c in (1 - net.core, net.core)]
        own_part = pltpu.make_async_copy(src.at[:, here], piece.acc, g_local.at[w])
        piece.open(src.at[:, other], own_part)

    def open_weight(piece, box):
        step = 2 * PAIR
        rows = tok_t.shape[0]

        def one(i, carry):
            at = pl.ds(pl.multiple_of(i * step, step), step)
            x = tok_t[at, :]
            other, here = [columns(piece.base, c, piece.half) for c in (1 - net.core, net.core)]
            outbox[box, at, :] = nn(x, grad[:, other]).astype(BF)
            piece.acc[at, :] = nn(x, grad[:, here]).astype(BF)
            return carry

        lax.fori_loop(0, rows // step, one, 0)
        piece.open(outbox.at[box])

    open_whole(0, d_down)
    open_whole(1, d_up)
    open_whole(2, d_out)
    halo_in, halo_sent = group.halo(0, ga, gpad, reach)

    def first(s, carry):
        for p in range(pairs):
            unit, at = s * pairs + p, lanes(p)
            own_ga = ga[s, :, at]
            gpad[s, pl.ds(reach, length), at] = own_ga
            prob = p1[unit]
            gmix[s, :, at] = together(nn(prob.astype(BF), own_ga)).astype(BF)
            back = nt(apart(mix[s, :, at]), own_ga)
            low[unit] = (prob * (back - by_head(prob * back, jnp.sum))).astype(BF)
        return carry

    lax.fori_loop(0, n_seq, first, 0)
    gmix_in = group.push(1, lambda d: gmix.at[owner_seq(d), :, owner_lanes(d)], gmr.at[me])
    gmr[me] = gmix[owner_seq(me), :, owner_lanes(me)]
    r_down.step_one()
    r_up.step_one()
    fill_bands(lines, table, reach)
    halo_in()
    skew[...] = jnp.zeros(skew.shape, F32)

    def beside(s, carry):
        one, two_mask = lane_masks(BF)
        for p in range(pairs):
            unit, at = s * pairs + p, lanes(p)
            own_ga, padded = ga[s, :, at], vpad[s, :, at]
            gs = low[unit]
            gq[s, :, at] = tn(gs, apart(landk[s, :, at])) * scale
            lkp[s, :, at] = together(nn(gs, q[s, :, at])) * scale
            gv[s, :, at] = conv_pair(table[p], gpad[s, :, at])
            both = jnp.concatenate([own_ga * one, own_ga * two_mask], axis=0)
            skew[2 * p : 2 * p + 2, :, : length + 2 * reach] += nt(both, padded).reshape(
                2, length, length + 2 * reach
            )
        return carry

    lax.fori_loop(0, n_seq, beside, 0)
    lane_at = lax.broadcasted_iota(jnp.int32, (PAIR, PAIR), 1)
    wide = skew.shape[2]
    for h in range(2 * pairs):
        total = skew[h, :8, :]
        for row in range(8, length, 8):
            total = total + pltpu.roll(skew[h, row : row + 8, :], wide - row, 1)
        tapg[h] = total[:, :PAIR]
    r_down.step_two()
    r_out.step_one()
    tok_t[...] = tokens[...].T

    for copy in gmix_in:
        copy.wait_recv()
    my_seq, my_pair = owner_seq(me), (me * own) % pairs
    tile = jnp.zeros((PAIR, PAIR), F32)
    for i in range(own):
        at = pl.ds(i * PAIR, PAIR)
        total = gmr[0, :, at].astype(F32)
        for src in range(1, size):
            total = total + gmr[src, :, at].astype(F32)
        total = split(apart(total))
        means = apart(lvo[:, at])
        back = together(three(tn, split(zo[PINV_ITERS, i]), total)).astype(BF)
        own_g[:, at] = back
        column = jnp.sum(apart(back.astype(F32)) * means, axis=1, keepdims=True)
        tile = jnp.where(lane_at == i, column, tile)
        dz[i] = three(nt, total, split(means))
        dp[i] = jnp.zeros((PAIR, PAIR), F32)
    stat[...] = tile.T[:8]
    mstat[me] = stat[...]
    gfull[my_seq, :, owner_lanes(me)] = own_g[...]
    g_in = group.push(2, lambda d: own_g, gfull.at[my_seq, :, owner_lanes(me)])
    back_in = group.push(3, lambda d: stat, mstat.at[me])
    r_up.step_two()
    for copy in g_in + back_in:
        copy.wait_recv()
    rows = jnp.concatenate(
        [mstat[...].reshape(8 * size, PAIR), jnp.zeros((PAIR - 8 * size, PAIR), F32)], axis=0
    )
    gcol[...] = rows.T
    unit_matrix = eye()

    def third(unit):
        s, p = unit // pairs, unit % pairs
        at = lanes(p)
        here = (unit // own) * 8 + unit % own
        picked = lane_at == here
        weight = jnp.sum(jnp.where(picked, wt[...], 0.0), axis=1, keepdims=True)
        offset = jnp.sum(jnp.where(picked, gcol[...], 0.0), axis=1, keepdims=True)
        g = apart(gfull[s, :, at])
        prob = e[unit].astype(F32) * weight
        back = nt(g, vpad[s, pl.ds(reach, length), at]) - offset
        gs = (prob * back).astype(BF)
        values = gv[s, :, at] + tn(prob.astype(BF), g)
        v_at = pl.ds(pl.multiple_of(2 * width + p * PAIR, PAIR), PAIR)
        rows = pl.ds(pl.multiple_of(s * length, length), length)
        grad[rows, v_at] = values.astype(BF)
        rows = pl.ds(pl.multiple_of(s * length, length), length)
        grad[rows, pl.ds(pl.multiple_of(width + p * PAIR, PAIR), PAIR)] = (
            tn(gs, apart(landq[s, :, at])) * scale
        ).astype(BF)
        lq = (together(nn(gs, k[s, :, at])) * scale).reshape(size, land_local, PAIR)
        lk = lkp[s, :, at].reshape(size, land_local, PAIR)
        lpart[:, s, :, at] = jnp.concatenate([lq, lk], axis=1).astype(BF)

    per_step = n_seq * pairs // PINV_ITERS

    def pinv_back(step, carry):
        at_step = PINV_ITERS - 1 - step
        for i in range(own):
            p, z = split(p2o[i]), split(zo[at_step, i])
            prod, one, two_term, three_term = pinv_terms(p, z, unit_matrix)
            d_out = dz[i] * 0.25
            d_out_s = split(d_out)
            d_three = split(three(tn, z, d_out_s))
            d_two = split(-three(tn, prod, d_three))
            d_one = -three(tn, prod, d_two)
            d_prod = -three(nt, d_three, split(two_term)) - three(nt, d_two, split(one)) - d_one
            d_prod = split(d_prod)
            dp[i] += three(nt, d_prod, z)
            dz[i] = three(nt, d_out_s, split(three_term)) + three(tn, p, d_prod)
        for j in range(per_step):
            third(step * per_step + j)
        return carry

    lax.fori_loop(0, PINV_ITERS // 2, pinv_back, 0)
    r_down.step_three()
    r_out.step_two()
    lax.fori_loop(PINV_ITERS // 2, PINV_ITERS, pinv_back, 0)
    r_up.step_three()

    for i in range(own):
        at = pl.ds(i * PAIR, PAIR)
        prob = p2o[i]
        squares = by_head(jnp.sum(prob * prob, axis=1, keepdims=True), jnp.sum)
        d_start = dz[i].T
        inner = by_head(jnp.sum(d_start * prob, axis=1, keepdims=True), jnp.sum)
        d_prob = dp[i] + d_start / squares - 2.0 * prob * inner / (squares * squares)
        gs = prob * (d_prob - jnp.sum(prob * d_prob, axis=1, keepdims=True))
        gs = split(gs)
        here = lanes(my_pair + i)
        lq, lk = apart(landq[my_seq, :, here]), apart(landk[my_seq, :, here])
        query = together(nn(gs[0], lk) + nn(gs[1], lk)) * scale
        key = together(tn(gs[0], lq) + tn(gs[1], lq)) * scale
        both = [x.reshape(size, land_local, PAIR) for x in (query, key)]
        two[:, :, at] = jnp.concatenate(both, axis=1).astype(BF)
    lpr[me] = lpart[me]
    twr[me] = two[me]
    part_in = group.push(4, lambda d: lpart.at[d], lpr.at[me])
    two_in = group.push(5, lambda d: two.at[d], twr.at[me])
    open_weight(r_v, 0)
    r_down.step_four()
    for copy in part_in + two_in:
        copy.wait_recv()

    def close(s, carry):
        for p in range(pairs):
            at = lanes(p)
            total = lpr[0, s, :, at].astype(F32)
            for src in range(1, size):
                total = total + lpr[src, s, :, at].astype(F32)
            owner = s * pairs + p
            spot = pl.ds(pl.multiple_of((owner % own) * PAIR, PAIR), PAIR)
            total = (total + twr[owner // own, :, spot].astype(F32)) * (1.0 / seg)
            spread = [
                jnp.concatenate(
                    [jnp.broadcast_to(x[i : i + 1], (seg, PAIR)) for i in range(land_local)], axis=0
                )
                for x in (total[:land_local], total[land_local:])
            ]
            rows = pl.ds(pl.multiple_of(s * length, length), length)
            grad[rows, at] = (gq[s, :, at] + spread[0]).astype(BF)
            key_at = pl.ds(width + p * PAIR, PAIR)
            grad[rows, key_at] = (grad[rows, key_at].astype(F32) + spread[1]).astype(BF)
        return carry

    lax.fori_loop(0, n_seq, close, 0)
    open_weight(r_q, 1)
    r_v.step_one()
    open_weight(r_k, 2)
    r_q.step_one()
    r_out.step_three()

    def column_sums(base):
        total = jnp.zeros((1, width), F32)
        for s in range(n_seq):
            x = grad[s * length : (s + 1) * length, base : base + width].astype(F32)
            total = total + jnp.sum(x, axis=0, keepdims=True)
        return total

    count = vec_rows.shape[0]
    which = lax.broadcasted_iota(jnp.int32, (count, width), 0)
    table_rows = vec_rows[...]
    table_rows = jnp.where(which == 0, column_sums(0), table_rows)
    table_rows = jnp.where(which == 1, column_sums(2 * width), table_rows)
    table_rows = jnp.concatenate([table_rows, jnp.zeros((PAIR - count, width), F32)], axis=0)
    left = table_rows.T
    sums = tapg[:, 0, :]
    for b in range(1, 8):
        sums = sums + pltpu.roll(tapg[:, b, :], PAIR - b, 1)
    shard = r_small.rows
    sums = jnp.concatenate([sums, jnp.zeros((shard - sums.shape[0], PAIR), F32)], axis=0)
    right = jnp.broadcast_to(sums[None], (width // shard, shard, PAIR)).reshape(width, PAIR)
    zero = net.core == 0
    r_small.acc[...] = jnp.where(zero, left, right)
    small_box[...] = jnp.where(zero, right, left)
    r_small.open(small_box)
    r_v.step_two()
    r_k.step_one()

    def inputs(i, carry):
        step = 2 * PAIR
        rows = pl.ds(pl.multiple_of(i * step, step), step)
        for at in range(0, width, step):
            x = nt(grad[rows, :], f_qkv[at : at + step, :])
            out = x + resid[rows, at : at + step]
            input_grad[rows, at : at + step] = out.astype(BF)
        return carry

    lax.fori_loop(0, tokens.shape[0] // (2 * PAIR), inputs, 0)
    r_small.step_one()
    r_q.step_two()
    r_up.step_four()
    r_out.step_four()
    r_k.step_two()
    r_v.step_three()
    r_small.step_two()
    r_q.step_three()
    r_k.step_three()
    r_v.step_four()
    r_small.step_three()
    r_q.step_four()
    r_k.step_four()
    r_small.step_four()
    for piece in pieces:
        piece.close()
    halo_sent()
    group.finish()
    net.finish()


def back(
    ga, tokens, resid, f_qkv, vec_rows, lines, d_down, d_up, d_out, kept, shards, seq_size, reach
):
    q = kept[0]
    n_seq, length, width = q.shape
    pairs = width // PAIR
    units = n_seq * pairs
    own = units // seq_size
    line_size = seq_size // 2
    vmem, hbm = pl.BlockSpec(memory_space=pltpu.VMEM), pl.BlockSpec(memory_space=pltpu.HBM)
    shape = jax.ShapeDtypeStruct
    part = 2 * LAND // seq_size
    s_qkv, s_out, s_up, s_down = [shape(x.shape, F32) for x in shards]
    s_small = shape((s_qkv.shape[0], 2 * PAIR), F32)
    bufs = []
    for x in (s_down, s_up, s_out):
        bufs += scatter_scratch(x.shape[0], x.shape[1] // 2, BF, line_size)
    for _ in range(3):
        bufs += scatter_scratch(s_qkv.shape[0], width // 2, BF, line_size)
    bufs += scatter_scratch(s_qkv.shape[0], PAIR, F32, line_size)
    return pl.pallas_call(
        functools.partial(back_kernel, reach, 2 * reach + 1),
        out_shape=[shape(tokens.shape, BF), s_qkv, s_out, s_up, s_down, s_small],
        in_specs=[vmem] * 6 + [hbm] * 3 + [vmem] * 12,
        out_specs=[vmem] * 6,
        scratch_shapes=[
            pltpu.VMEM((n_seq * length, 3 * width), BF),
            pltpu.VMEM((2 * pairs, 8, PAIR), F32),
            pltpu.VMEM((pairs, 4 * length, length + 2 * reach), BF),
            pltpu.VMEM((width, n_seq * length), BF),
            pltpu.VMEM((3, width, width // 2), BF),
            pltpu.VMEM((width, PAIR), F32),
            pltpu.VMEM((n_seq, length + 2 * reach, width), BF),
            pltpu.VMEM((n_seq, LAND, width), BF),
            pltpu.VMEM((seq_size, LAND, own * PAIR), BF),
            pltpu.VMEM((units, PAIR, length), BF),
            pltpu.VMEM((n_seq, LAND, width), BF),
            pltpu.VMEM((8, PAIR), F32),
            pltpu.VMEM((seq_size, 8, PAIR), F32),
            pltpu.VMEM((PAIR, PAIR), F32),
            pltpu.VMEM((n_seq, length, width), F32),
            pltpu.VMEM((n_seq, length, width), F32),
            pltpu.VMEM((n_seq, LAND, width), F32),
            pltpu.VMEM((seq_size, n_seq, part, width), BF),
            pltpu.VMEM((seq_size, n_seq, part, width), BF),
            pltpu.VMEM((seq_size, part, own * PAIR), BF),
            pltpu.VMEM((seq_size, part, own * PAIR), BF),
            pltpu.VMEM((own, PAIR, PAIR), F32),
            pltpu.VMEM((own, PAIR, PAIR), F32),
            pltpu.VMEM((2 * pairs, length, 2 * PAIR), F32),
            pltpu.VMEM((LAND, own * PAIR), BF),
        ]
        + bufs
        + [
            pltpu.SemaphoreType.DMA((7, line_size + SCATTER_SEMS)),
            pltpu.SemaphoreType.DMA((7, line_size + SCATTER_SEMS)),
            pltpu.SemaphoreType.DMA((7,)),
            pltpu.SemaphoreType.DMA((6, seq_size)),
            pltpu.SemaphoreType.DMA((6, seq_size)),
        ],
        compiler_params=pltpu.CompilerParams(
            collective_id=1, has_side_effects=True, vmem_limit_bytes=60 * 1024 * 1024
        ),
        name="back",
    )(ga, tokens, resid, f_qkv, vec_rows, lines, d_down, d_up, d_out, *kept)


def kernels_fit(args):
    tokens, _, *matrices = args[:6]
    taps = args[7]
    seq_size = lax.axis_size("seq")
    n_seq, length, width = tokens.shape
    units = n_seq * width // PAIR
    own = units // seq_size
    return (
        lax.axis_size("rows") == 4
        and seq_size == 8
        and all(x.shape[0] % 24 == 0 and x.shape[1] % 256 == 0 for x in matrices)
        and width // taps.shape[0] == PAIR // 2
        and length == PAIR
        and taps.shape[1] == 33
        and taps.shape[0] <= matrices[0].shape[0]
        and units == own * seq_size
        and 2 * own <= 8
        and (width // PAIR) % own == 0
        and units % PINV_ITERS == 0
        and LAND == 8 * seq_size
    )


def with_kernels(
    tokens, cotangent, qkv_weight, out_weight, up_weight, down_weight, vectors, taps,
    qkv_first, qkv_second, out_first, out_second, up_first, up_second, down_first, down_second,
    vec_first, vec_second, tap_first, tap_second,
):
    seq_count, local_len, model_width = tokens.shape
    head_count, tap_count = taps.shape
    hidden_width = up_weight.shape[1]
    seq_size = lax.axis_size("seq")
    reach = tap_count // 2
    row_count = seq_count * local_len
    count = vectors.shape[0]
    matrices = (qkv_weight, out_weight, up_weight, down_weight)
    table = jnp.pad(vectors.T, ((0, 0), (0, 2 * PAIR - count)))
    lines = jnp.pad(taps, ((0, 0), (0, 2 * PAIR - tap_count)))
    flat_in = tokens.reshape(row_count, model_width)
    full_qkv, full_out, full_up, full_down, vec_float, *kept = front(
        tokens, matrices, table, lines, seq_size, reach
    )
    attn_low = kept.pop(2).reshape(row_count, model_width)
    queries, key_rows = kept[:2]
    branch = jnp.dot(attn_low, full_out, preferred_element_type=jnp.float32) + vec_float[2]
    resid_one = flat_in.astype(jnp.float32) + branch
    normed, norm_pull_one = jax.vjp(layer_norm, resid_one, vec_float[6], vec_float[3])
    normed_low = normed.astype(BF)
    hidden_pre = jnp.dot(normed_low, full_up, preferred_element_type=jnp.float32) + vec_float[
        8:count
    ].reshape(hidden_width)
    active, gelu_pull = jax.vjp(gelu_exact, hidden_pre)
    active_low = active.astype(BF)
    ff_out = jnp.dot(active_low, full_down, preferred_element_type=jnp.float32) + vec_float[4]
    layer_out, norm_pull_two = jax.vjp(layer_norm, normed + ff_out, vec_float[7], vec_float[5])
    grad_resid_two, grad_gain_two, grad_shift_two = norm_pull_two(
        cotangent.reshape(row_count, model_width).astype(jnp.float32)
    )
    grad_ff = grad_resid_two.astype(BF)
    grad_down = jnp.einsum("nf,nd->fd", active_low, grad_ff, preferred_element_type=jnp.float32)
    grad_active = jnp.einsum("nd,fd->nf", grad_ff, full_down, preferred_element_type=jnp.float32)
    grad_hidden = gelu_pull(grad_active)[0].astype(BF)
    grad_up = jnp.einsum("nd,nf->df", normed_low, grad_hidden, preferred_element_type=jnp.float32)
    grad_normed = (
        jnp.einsum("nf,df->nd", grad_hidden, full_up, preferred_element_type=jnp.float32)
        + grad_resid_two
    )
    grad_resid_one, grad_gain_one, grad_shift_one = norm_pull_one(grad_normed)
    grad_branch = grad_resid_one.astype(BF)
    grad_out = jnp.einsum("nd,ne->de", attn_low, grad_branch, preferred_element_type=jnp.float32)
    grad_attn = jnp.einsum(
        "ne,de->nd", grad_branch, full_out, preferred_element_type=jnp.float32
    ).astype(BF)
    nothing = jnp.zeros((1, model_width), F32)
    vec_rows = jnp.concatenate(
        [
            nothing,
            nothing,
            jnp.sum(grad_branch.astype(jnp.float32), axis=0)[None],
            grad_shift_one[None],
            jnp.sum(grad_ff.astype(jnp.float32), axis=0)[None],
            grad_shift_two[None],
            grad_gain_one[None],
            grad_gain_two[None],
            jnp.sum(grad_hidden.astype(jnp.float32), axis=0).reshape(-1, model_width),
            jnp.zeros((16 - count, model_width), F32),
        ],
        axis=0,
    )
    flipped = jnp.pad(taps[:, ::-1], ((0, 0), (0, 2 * PAIR - tap_count)))
    input_grad, summed_qkv, summed_out, summed_up, summed_down, small = back(
        grad_attn.reshape(tokens.shape), flat_in, grad_resid_one, full_qkv, vec_rows, flipped,
        *[x.astype(BF) for x in (grad_down, grad_up, grad_out)],
        kept, matrices, seq_size, reach,
    )
    input_grad = input_grad.reshape(tokens.shape)
    summed_vec = small[:, :count].T
    summed_taps = small[:head_count, PAIR : PAIR + tap_count]
    new_qkv = adam_step(qkv_weight, qkv_first, qkv_second, summed_qkv, rate_matrix, decay_rate)
    new_out = adam_step(out_weight, out_first, out_second, summed_out, rate_output, decay_rate)
    new_up = adam_step(up_weight, up_first, up_second, summed_up, rate_matrix, decay_rate)
    new_down = adam_step(down_weight, down_first, down_second, summed_down, rate_matrix, decay_rate)
    new_vec = adam_step(vectors, vec_first, vec_second, summed_vec, rate_vector, 0.0)
    new_taps = adam_step(taps, tap_first, tap_second, summed_taps, rate_taps, 0.0)
    out_tokens = layer_out.astype(BF).reshape(tokens.shape)
    return (out_tokens, input_grad) + new_qkv + new_out + new_up + new_down + new_vec + new_taps


def on_device(*args):
    return with_kernels(*args) if kernels_fit(args) else with_collectives(*args)


def solution(mesh):
    return jax.shard_map(
        on_device,
        mesh=mesh,
        in_specs=(
            P("rows", "seq", None),
            P("rows", "seq", None),
            P(("rows", "seq"), None),
            P(("rows", "seq"), None),
            P(("rows", "seq"), None),
            P(("rows", "seq"), None),
            P(None, ("rows", "seq")),
            P(),
            P(("rows", "seq"), None),
            P(("rows", "seq"), None),
            P(("rows", "seq"), None),
            P(("rows", "seq"), None),
            P(("rows", "seq"), None),
            P(("rows", "seq"), None),
            P(("rows", "seq"), None),
            P(("rows", "seq"), None),
            P(None, ("rows", "seq")),
            P(None, ("rows", "seq")),
            P(),
            P(),
        ),
        out_specs=(
            P("rows", "seq", None),
            P("rows", "seq", None),
            P(("rows", "seq"), None),
            P(("rows", "seq"), None),
            P(("rows", "seq"), None),
            P(("rows", "seq"), None),
            P(("rows", "seq"), None),
            P(("rows", "seq"), None),
            P(("rows", "seq"), None),
            P(("rows", "seq"), None),
            P(("rows", "seq"), None),
            P(("rows", "seq"), None),
            P(("rows", "seq"), None),
            P(("rows", "seq"), None),
            P(None, ("rows", "seq")),
            P(None, ("rows", "seq")),
            P(None, ("rows", "seq")),
            P(),
            P(),
            P(),
        ),
        check_vma=False,
    )
```

```python
import functools

import jax
import jax.numpy as jnp
from jax import lax
from jax.experimental import pallas as pl
from jax.experimental.pallas import tpu as pltpu
from jax.sharding import PartitionSpec as P

LAND = 64
PINV_ITERS = 6


top_precision = lax.Precision.HIGHEST
norm_eps = 1e-05
beta_one = 0.9
beta_two = 0.999
corr_one = 1.0 - 0.9**10
corr_two = 1.0 - 0.999**10
adam_eps = 1e-08
decay_rate = 0.01
rate_matrix = 0.03
rate_output = 0.12
rate_vector = 0.3
rate_taps = 0.08


def with_halo(x, sides, width):
    for axis, dim in sides:
        size, length = (lax.axis_size(axis), x.shape[dim])
        up = [(i, (i + 1) % size) for i in range(size - 1)]
        down = [(j, i) for i, j in up]
        last = lax.slice_in_dim(x, length - width, length, axis=dim)
        initial = lax.slice_in_dim(x, 0, width, axis=dim)
        before = lax.ppermute(last, axis, up)
        after = lax.ppermute(initial, axis, down)
        x = jnp.concatenate([before, x, after], axis=dim)
    return x


def layer_norm(residual, gain_row, shift_row):
    center = residual - jnp.mean(residual, axis=-1, keepdims=True)
    spread = jnp.mean(center * center, axis=-1, keepdims=True)
    return center * lax.rsqrt(spread + norm_eps) * gain_row + shift_row


def normalized_rows(scores):
    expo = jnp.exp(scores - jnp.max(scores, axis=-1, keepdims=True))
    return expo / jnp.sum(expo, axis=-1, keepdims=True)


def softmax_back(probability, grad_in):
    return probability * (grad_in - jnp.sum(probability * grad_in, axis=-1, keepdims=True))


def gelu_exact(inputs):
    return jax.nn.gelu(inputs, approximate=False)


def pseudo_inverse(matrix):
    identity = jnp.eye(matrix.shape[-1], dtype=jnp.float32)
    approx = jnp.swapaxes(matrix, -1, -2) / jnp.sum(matrix * matrix, axis=(-2, -1), keepdims=True)
    for sweep_index in range(PINV_ITERS):
        product = jnp.matmul(matrix, approx, precision=top_precision)
        inner_term = 7.0 * identity - product
        inner_term = 15.0 * identity - jnp.matmul(product, inner_term, precision=top_precision)
        inner_term = 13.0 * identity - jnp.matmul(product, inner_term, precision=top_precision)
        approx = 0.25 * jnp.matmul(approx, inner_term, precision=top_precision)
    return approx


def adam_step(weight, first_moment, second, gradient, step_rate, decay_coef):
    new_first = beta_one * first_moment + (1.0 - beta_one) * gradient
    new_second = beta_two * second + (1.0 - beta_two) * gradient * gradient
    update = new_first / corr_one / (jnp.sqrt(new_second / corr_two) + adam_eps)
    return (new_first, new_second, weight - step_rate * (update + decay_coef * weight))


def with_collectives(
    tokens,
    cotangent,
    qkv_weight,
    out_weight,
    up_weight,
    down_weight,
    vectors,
    taps,
    qkv_first,
    qkv_second,
    out_first,
    out_second,
    up_first,
    up_second,
    down_first,
    down_second,
    vec_first,
    vec_second,
    tap_first,
    tap_second,
):
    seq_count, local_len, model_width = tokens.shape
    head_count, tap_count = taps.shape
    head_size = model_width // head_count
    hidden_width = up_weight.shape[1]
    land_local = LAND // lax.axis_size("seq")
    seg_len = local_len // land_local
    reach_width = tap_count // 2
    logit_scale_factor = head_size ** (-0.5)
    row_count = seq_count * local_len
    head_shape = (seq_count, local_len, head_count, head_size)
    land_shape = (seq_count, LAND, head_count, head_size)
    full_qkv, full_out, full_up, full_down, full_vec = (
        lax.all_gather(qkv_weight.astype(jnp.bfloat16), ("rows", "seq"), axis=0, tiled=True),
        lax.all_gather(out_weight.astype(jnp.bfloat16), ("rows", "seq"), axis=0, tiled=True),
        lax.all_gather(up_weight.astype(jnp.bfloat16), ("rows", "seq"), axis=0, tiled=True),
        lax.all_gather(down_weight.astype(jnp.bfloat16), ("rows", "seq"), axis=0, tiled=True),
        lax.all_gather(vectors.astype(jnp.bfloat16), ("rows", "seq"), axis=1, tiled=True),
    )
    vec_float = full_vec.astype(jnp.float32)
    flat_in = tokens.reshape(row_count, model_width)
    project = jnp.dot(flat_in, full_qkv, preferred_element_type=jnp.float32)
    queries = (project[:, :model_width] + vec_float[0]).astype(jnp.bfloat16)
    key_rows = project[:, model_width : 2 * model_width].astype(jnp.bfloat16)
    values = (project[:, 2 * model_width :] + vec_float[1]).astype(jnp.bfloat16)
    seg_shape = (seq_count, land_local, seg_len, model_width)
    own_q = jnp.mean(queries.reshape(seg_shape), axis=2, dtype=jnp.float32).astype(jnp.bfloat16)
    own_k = jnp.mean(key_rows.reshape(seg_shape), axis=2, dtype=jnp.float32).astype(jnp.bfloat16)
    land_q, land_k = (
        lax.all_gather(own_q, "seq", axis=1, tiled=True),
        lax.all_gather(own_k, "seq", axis=1, tiled=True),
    )
    query_heads = queries.reshape(head_shape)
    key_heads = key_rows.reshape(head_shape)
    value_heads = values.reshape(head_shape)
    landmark_query_heads = land_q.reshape(land_shape)
    landmark_key_heads = land_k.reshape(land_shape)
    lq_float = landmark_query_heads.astype(jnp.float32)
    lk_float = landmark_key_heads.astype(jnp.float32)
    score_one = (
        jnp.einsum(
            "sthd,slhd->shtl", query_heads, landmark_key_heads, preferred_element_type=jnp.float32
        )
        * logit_scale_factor
    )
    prob_one = normalized_rows(score_one)
    second_probability = normalized_rows(
        jnp.einsum("slhd,smhd->shlm", lq_float, lk_float, precision=top_precision)
        * logit_scale_factor
    )
    inverse_matrix, inverse_pull = jax.vjp(pseudo_inverse, second_probability)
    score_three = (
        jnp.einsum(
            "slhd,sthd->shlt", landmark_query_heads, key_heads, preferred_element_type=jnp.float32
        )
        * logit_scale_factor
    )
    row_max = lax.pmax(jnp.max(score_three, axis=-1), "seq")
    expo_three = jnp.exp(score_three - row_max[..., None])
    numer_local = jnp.einsum(
        "shlt,sthd->slhd",
        expo_three.astype(jnp.bfloat16),
        value_heads,
        preferred_element_type=jnp.float32,
    )
    numer, denom = (
        lax.psum(numer_local.astype(jnp.bfloat16), "seq").astype(jnp.float32),
        lax.psum(jnp.sum(expo_three, axis=-1).astype(jnp.bfloat16), "seq").astype(jnp.float32),
    )
    denom_swap = jnp.swapaxes(denom, 1, 2)[..., None]
    landmark_value_rows = numer / denom_swap
    mixing_kernel = jnp.einsum(
        "shlm,smhd->slhd", inverse_matrix, landmark_value_rows, precision=top_precision
    )
    mix_low = mixing_kernel.astype(jnp.bfloat16)
    prob_low = prob_one.astype(jnp.bfloat16)
    attend = jnp.einsum("shtl,slhd->sthd", prob_low, mix_low, preferred_element_type=jnp.float32)
    attend = attend.reshape(seq_count, local_len, model_width)
    tap_chan = jnp.repeat(taps, head_size, axis=0)
    padded_values = with_halo(
        values.reshape(seq_count, local_len, model_width), (("seq", 1),), reach_width
    )
    conv_out = jnp.zeros((seq_count, local_len, model_width), jnp.float32)
    for offset in range(tap_count):
        conv_out = conv_out + tap_chan[:, offset] * padded_values[
            :, offset : offset + local_len
        ].astype(jnp.float32)
    attn_low = (attend + conv_out).reshape(row_count, model_width).astype(jnp.bfloat16)
    branch = jnp.dot(attn_low, full_out, preferred_element_type=jnp.float32) + vec_float[2]
    resid_one = flat_in.astype(jnp.float32) + branch
    normed, norm_pull_one = jax.vjp(layer_norm, resid_one, vec_float[6], vec_float[3])
    normed_low = normed.astype(jnp.bfloat16)
    hidden_pre = jnp.dot(normed_low, full_up, preferred_element_type=jnp.float32) + vec_float[
        8:
    ].reshape(hidden_width)
    active, gelu_pull = jax.vjp(gelu_exact, hidden_pre)
    active_low = active.astype(jnp.bfloat16)
    ff_out = jnp.dot(active_low, full_down, preferred_element_type=jnp.float32) + vec_float[4]
    layer_out, norm_pull_two = jax.vjp(layer_norm, normed + ff_out, vec_float[7], vec_float[5])
    grad_resid_two, grad_gain_two, grad_shift_two = norm_pull_two(
        cotangent.reshape(row_count, model_width).astype(jnp.float32)
    )
    grad_ff = grad_resid_two.astype(jnp.bfloat16)
    grad_down = jnp.einsum("nf,nd->fd", active_low, grad_ff, preferred_element_type=jnp.float32)
    grad_active = jnp.einsum("nd,fd->nf", grad_ff, full_down, preferred_element_type=jnp.float32)
    grad_hidden = gelu_pull(grad_active)[0].astype(jnp.bfloat16)
    grad_up = jnp.einsum("nd,nf->df", normed_low, grad_hidden, preferred_element_type=jnp.float32)
    grad_normed = (
        jnp.einsum("nf,df->nd", grad_hidden, full_up, preferred_element_type=jnp.float32)
        + grad_resid_two
    )
    grad_resid_one, grad_gain_one, grad_shift_one = norm_pull_one(grad_normed)
    grad_branch = grad_resid_one.astype(jnp.bfloat16)
    grad_out = jnp.einsum("nd,ne->de", attn_low, grad_branch, preferred_element_type=jnp.float32)
    grad_attn = jnp.einsum(
        "ne,de->nd", grad_branch, full_out, preferred_element_type=jnp.float32
    ).astype(jnp.bfloat16)
    grad_attn_heads = grad_attn.reshape(head_shape)
    grad_prob_one = jnp.einsum(
        "sthd,slhd->shtl", grad_attn_heads, mix_low, preferred_element_type=jnp.float32
    )
    mixing_part = jnp.einsum(
        "shtl,sthd->slhd", prob_low, grad_attn_heads, preferred_element_type=jnp.float32
    )
    grad_mixing = lax.psum(mixing_part.astype(jnp.bfloat16), "seq").astype(jnp.float32)
    grad_score_one = softmax_back(prob_one, grad_prob_one).astype(jnp.bfloat16)
    query_local = (
        jnp.einsum(
            "shtl,slhd->sthd",
            grad_score_one,
            landmark_key_heads,
            preferred_element_type=jnp.float32,
        )
        * logit_scale_factor
    )
    land_k_part = (
        jnp.einsum(
            "shtl,sthd->slhd", grad_score_one, query_heads, preferred_element_type=jnp.float32
        )
        * logit_scale_factor
    )
    grad_pad = with_halo(
        grad_attn.reshape(seq_count, local_len, model_width), (("seq", 1),), reach_width
    )
    attn_float = grad_attn.reshape(seq_count, local_len, model_width).astype(jnp.float32)
    conv_back = jnp.zeros((seq_count, local_len, model_width), jnp.float32)
    tap_terms = []
    for offset in range(tap_count):
        start_row = 2 * reach_width - offset
        conv_back = conv_back + tap_chan[:, offset] * grad_pad[
            :, start_row : start_row + local_len
        ].astype(jnp.float32)
        tap_terms.append(
            jnp.sum(
                attn_float * padded_values[:, offset : offset + local_len].astype(jnp.float32),
                axis=(0, 1),
            )
        )
    grad_taps = jnp.sum(
        jnp.stack(tap_terms, axis=1).reshape(head_count, head_size, tap_count), axis=1
    )
    grad_inverse = jnp.einsum(
        "slhd,smhd->shlm", grad_mixing, landmark_value_rows, precision=top_precision
    )
    grad_land_values = jnp.einsum(
        "shlm,slhd->smhd", inverse_matrix, grad_mixing, precision=top_precision
    )
    land_grad_low = grad_land_values.astype(jnp.bfloat16).astype(jnp.float32)
    grad_prob_two = inverse_pull(grad_inverse)[0]
    grad_score_two = softmax_back(second_probability, grad_prob_two)
    query_two = (
        jnp.einsum("shlm,smhd->slhd", grad_score_two, lk_float, precision=top_precision)
        * logit_scale_factor
    )
    key_two = (
        jnp.einsum("shlm,slhd->smhd", grad_score_two, lq_float, precision=top_precision)
        * logit_scale_factor
    )
    grad_numer = land_grad_low / denom_swap
    expo_low = expo_three.astype(jnp.bfloat16).astype(jnp.float32)
    value_three = jnp.einsum("shlt,slhd->sthd", expo_low, grad_numer, precision=top_precision)
    grad_expo = jnp.einsum(
        "slhd,sthd->shlt", grad_numer, value_heads.astype(jnp.float32), precision=top_precision
    )
    grad_denom = jnp.swapaxes(jnp.sum(land_grad_low * landmark_value_rows, axis=-1), 1, 2) / denom
    grad_score_three = (expo_three * (grad_expo - grad_denom[..., None])).astype(jnp.bfloat16)
    land_q_part = (
        jnp.einsum(
            "shlt,sthd->slhd", grad_score_three, key_heads, preferred_element_type=jnp.float32
        )
        * logit_scale_factor
    )
    key_local = (
        jnp.einsum(
            "shlt,slhd->sthd",
            grad_score_three,
            landmark_query_heads,
            preferred_element_type=jnp.float32,
        )
        * logit_scale_factor
    )
    land_q_own, land_k_own = (
        lax.psum_scatter(
            land_q_part.astype(jnp.bfloat16), "seq", scatter_dimension=1, tiled=True
        ).astype(jnp.float32),
        lax.psum_scatter(
            land_k_part.astype(jnp.bfloat16), "seq", scatter_dimension=1, tiled=True
        ).astype(jnp.float32),
    )
    first_land = lax.axis_index("seq") * land_local
    land_q_own = land_q_own + lax.dynamic_slice_in_dim(query_two, first_land, land_local, 1)
    land_k_own = land_k_own + lax.dynamic_slice_in_dim(key_two, first_land, land_local, 1)
    spread_shape = (seq_count, land_local, seg_len, head_count, head_size)
    spread_q = jnp.broadcast_to((land_q_own / seg_len)[:, :, None], spread_shape).reshape(
        head_shape
    )
    spread_k = jnp.broadcast_to((land_k_own / seg_len)[:, :, None], spread_shape).reshape(
        head_shape
    )
    grad_query = (query_local + spread_q).reshape(row_count, model_width)
    grad_key = (key_local + spread_k).reshape(row_count, model_width)
    grad_value = value_three.reshape(row_count, model_width) + conv_back.reshape(
        row_count, model_width
    )
    grad_proj = jnp.concatenate([grad_query, grad_key, grad_value], axis=1).astype(jnp.bfloat16)
    grad_qkv = jnp.einsum("nd,ne->de", flat_in, grad_proj, preferred_element_type=jnp.float32)
    input_grad = (
        jnp.einsum("ne,de->nd", grad_proj, full_qkv, preferred_element_type=jnp.float32)
        + grad_resid_one
    )
    input_grad = input_grad.astype(jnp.bfloat16).reshape(tokens.shape)
    bias_sums = jnp.sum(grad_proj.astype(jnp.float32), axis=0)
    grad_vec = jnp.concatenate(
        [
            bias_sums[None, :model_width],
            bias_sums[None, 2 * model_width :],
            jnp.sum(grad_branch.astype(jnp.float32), axis=0)[None],
            grad_shift_one[None],
            jnp.sum(grad_ff.astype(jnp.float32), axis=0)[None],
            grad_shift_two[None],
            grad_gain_one[None],
            grad_gain_two[None],
            jnp.sum(grad_hidden.astype(jnp.float32), axis=0).reshape(-1, model_width),
        ],
        axis=0,
    )
    summed_qkv, summed_out, summed_up, summed_down, summed_vec = (
        lax.psum_scatter(grad_qkv, ("rows", "seq"), scatter_dimension=0, tiled=True),
        lax.psum_scatter(grad_out, ("rows", "seq"), scatter_dimension=0, tiled=True),
        lax.psum_scatter(grad_up, ("rows", "seq"), scatter_dimension=0, tiled=True),
        lax.psum_scatter(grad_down, ("rows", "seq"), scatter_dimension=0, tiled=True),
        lax.psum_scatter(grad_vec, ("rows", "seq"), scatter_dimension=1, tiled=True),
    )
    summed_taps = lax.psum(grad_taps, ("rows", "seq"))
    new_qkv = adam_step(qkv_weight, qkv_first, qkv_second, summed_qkv, rate_matrix, decay_rate)
    new_out = adam_step(out_weight, out_first, out_second, summed_out, rate_output, decay_rate)
    new_up = adam_step(up_weight, up_first, up_second, summed_up, rate_matrix, decay_rate)
    new_down = adam_step(down_weight, down_first, down_second, summed_down, rate_matrix, decay_rate)
    new_vec = adam_step(vectors, vec_first, vec_second, summed_vec, rate_vector, 0.0)
    new_taps = adam_step(taps, tap_first, tap_second, summed_taps, rate_taps, 0.0)
    out_tokens = layer_out.astype(jnp.bfloat16).reshape(tokens.shape)
    return (out_tokens, input_grad) + new_qkv + new_out + new_up + new_down + new_vec + new_taps


BF = jnp.bfloat16
F32 = jnp.float32
MESH = pl.DeviceIdType.MESH


def remote(src, dst, send_sem, recv_sem, device):
    return pltpu.make_async_remote_copy(
        src_ref=src, dst_ref=dst, send_sem=send_sem, recv_sem=recv_sem,
        device_id=device, device_id_type=MESH,
    )


def place():
    row, spot = lax.axis_index("rows"), lax.axis_index("seq")
    line, core = spot // 2, spot % 2
    flip_one = row + 1 - 2 * (row % 2)
    flip_two = row + 2 - 4 * (row // 2)
    first = (1 - core) * flip_one + core * flip_two
    second = (1 - core) * flip_two + core * flip_one
    return row, line, core, first, second, 3 - row


def greet(devices):
    barrier = pltpu.get_barrier_semaphore()
    for device in devices:
        pl.semaphore_signal(barrier, inc=1, device_id=device, device_id_type=MESH)
    pl.semaphore_wait(barrier, len(devices))


class Net:
    def __init__(self, send, recv):
        self.send, self.recv, self.started = send, recv, []
        self.row, self.line, self.core, self.first, self.second, self.across = place()
        self.line_size = lax.axis_size("seq") // 2
        own_spot = 2 * self.line + self.core
        self.sibling = (self.row, 2 * self.line + 1 - self.core)
        self.peers = [
            (self.row, 2 * ((self.line + k) % self.line_size) + self.core)
            for k in range(1, self.line_size)
        ]
        self.to_first, self.to_second = (self.first, own_spot), (self.second, own_spot)

    def go(self, w, k, src, dst, device):
        copy = remote(src, dst, self.send.at[w, k], self.recv.at[w, k], device)
        copy.start()
        self.started.append(copy)
        return copy

    def finish(self):
        for copy in self.started:
            copy.wait_send()


def columns(base, which, half):
    return pl.ds(pl.multiple_of(base + which * half, 128), half)


class Gather:
    def __init__(self, net, w, src, dst, base, half, asm, stage, local):
        self.net, self.w, self.dst, self.stage, self.asm = net, w, dst, stage, asm
        self.rows, self.base, self.half, self.local = src.shape[0], base, half, local
        part = pl.ds(pl.multiple_of(net.core * self.rows, 8), self.rows)
        there = columns(base, 1 - net.core, half)
        self.asm_copy = net.go(w, 0, src.at[:, there], asm.at[part, :], net.sibling)
        asm[part, :] = src[:, columns(base, net.core, half)]

    def block(self, start, size):
        at = pl.ds(pl.multiple_of(start, 16), size)
        return self.dst.at[at, columns(self.base, self.net.core, self.half)]

    def slab(self, index):
        size = 2 * self.rows * self.net.line_size
        return self.block(index * size, size)

    def spread(self):
        net = self.net
        self.asm_copy.wait_recv()
        self.stage[...] = self.asm[...].astype(BF)
        size = 2 * self.rows
        block = self.block((net.row * net.line_size + net.line) * size, size)
        self.z = [net.go(self.w, 1 + k, self.stage, block, d) for k, d in enumerate(net.peers)]
        self.own = pltpu.make_async_copy(self.stage, block, self.local)
        self.own.start()

    def step_one(self):
        net, w, z0 = self.net, self.w, self.net.line_size
        self.own.wait()
        for copy in self.z:
            copy.wait_recv()
        mine = self.slab(net.row)
        self.hop = [net.go(w, z0, mine, mine, net.to_first)]
        self.hop.append(net.go(w, z0 + 1, mine, mine, net.to_second))
        self.sib = [net.go(w, z0 + 3, mine, mine, net.sibling)]

    def step_two(self):
        net, w, z0 = self.net, self.w, self.net.line_size
        self.hop[0].wait_recv()
        got = self.slab(net.first)
        self.hop.append(net.go(w, z0 + 2, got, got, net.to_second))
        self.sib.append(net.go(w, z0 + 4, got, got, net.sibling))

    def step_three(self):
        net, w, z0 = self.net, self.w, self.net.line_size
        self.hop[1].wait_recv()
        got = self.slab(net.second)
        self.sib.append(net.go(w, z0 + 5, got, got, net.sibling))
        self.hop[2].wait_recv()
        got = self.slab(net.across)
        self.sib.append(net.go(w, z0 + 6, got, got, net.sibling))

    def close(self):
        for copy in self.sib:
            copy.wait_recv()


GATHER_SEMS = 7


class Scatter:
    def __init__(self, net, w, out, base, half, bufs):
        self.net, self.w, self.out, self.base, self.half = net, w, out, base, half
        self.acc, self.buf0, self.buf1, self.buf2, self.buf3, self.fin = bufs
        self.rows = out.shape[0]
        self.size = 2 * self.rows * net.line_size

    def open(self, outbox, own=None):
        self.sib = self.net.go(self.w, 0, outbox, self.buf0, self.net.sibling)
        self.own = own
        if own is not None:
            own.start()

    def slab(self, index):
        return pl.ds(pl.multiple_of(index * self.size, self.size), self.size)

    def add(self, index, other, start):
        step = 48
        acc = self.acc

        def one(i, carry):
            at = pl.ds(pl.multiple_of(index * self.size + i * step, 16), step)
            there = pl.ds(pl.multiple_of(start + i * step, 16), step)
            acc[at, :] = acc[at, :] + other[there, :]
            return carry

        lax.fori_loop(0, self.size // step, one, 0)

    def step_one(self):
        net, w = self.net, self.w
        if self.own is not None:
            self.own.wait()
        self.sib.wait_recv()
        self.add(net.across, self.buf0, net.across * self.size)
        acc = self.acc
        self.one = net.go(w, 1, acc.at[self.slab(net.across), :], self.buf1.at[0], net.to_second)
        self.add(net.second, self.buf0, net.second * self.size)
        self.two = net.go(w, 2, acc.at[self.slab(net.second), :], self.buf1.at[1], net.to_second)
        self.add(net.first, self.buf0, net.first * self.size)
        self.add(net.row, self.buf0, net.row * self.size)

    def step_two(self):
        net = self.net
        self.one.wait_recv()
        self.add(net.first, self.buf1.at[0], 0)
        src = self.acc.at[self.slab(net.first), :]
        self.three = net.go(self.w, 3, src, self.buf2, net.to_first)
        self.two.wait_recv()
        self.add(net.row, self.buf1.at[1], 0)

    def step_three(self):
        net = self.net
        self.three.wait_recv()
        self.add(net.row, self.buf2, 0)
        block, n = 2 * self.rows, net.line_size
        self.z = []

        def at(line):
            return pl.ds(pl.multiple_of((net.row * n + line) * block, block), block)

        for k, device in enumerate(net.peers):
            src = self.acc.at[at((net.line + 1 + k) % n), :]
            self.z.append(net.go(self.w, 4 + k, src, self.buf3.at[net.line], device))
        self.buf3[net.line] = self.acc[at(net.line), :]

    def step_four(self):
        net = self.net
        for copy in self.z:
            copy.wait_recv()
        total = self.buf3[0].astype(F32)
        for k in range(1, net.line_size):
            total = total + self.buf3[k].astype(F32)
        self.fin[...] = total
        part = pl.ds(pl.multiple_of((1 - net.core) * self.rows, 8), self.rows)
        here = columns(self.base, net.core, self.half)
        self.last = net.go(
            self.w, 3 + net.line_size, self.fin.at[part, :], self.out.at[:, here], net.sibling
        )
        part = pl.ds(pl.multiple_of(net.core * self.rows, 8), self.rows)
        self.out[:, here] = self.fin[part, :]

    def close(self):
        self.last.wait_recv()


SCATTER_SEMS = 4


def scatter_scratch(rows, half, dtype, line_size):
    quarter = 2 * rows * line_size
    return [
        pltpu.VMEM((4 * quarter, half), dtype),
        pltpu.VMEM((4 * quarter, half), dtype),
        pltpu.VMEM((2, quarter, half), dtype),
        pltpu.VMEM((quarter, half), dtype),
        pltpu.VMEM((line_size, 2 * rows, half), dtype),
        pltpu.VMEM((2 * rows, half), F32),
    ]


PAIR = 128


def nn(a, b):
    return jnp.dot(a, b, preferred_element_type=F32)


def nt(a, b):
    return lax.dot_general(a, b, (((1,), (1,)), ((), ())), preferred_element_type=F32)


def tn(a, b):
    return lax.dot_general(a, b, (((0,), (0,)), ((), ())), preferred_element_type=F32)


def split(x):
    high = x.astype(BF)
    return high, (x - high.astype(F32)).astype(BF)


def three(dot, a, b):
    return dot(a[0], b[0]) + (dot(a[0], b[1]) + dot(a[1], b[0]))


def lane_masks(dtype):
    lane = lax.broadcasted_iota(jnp.int32, (1, PAIR), 1)
    one = (lane < PAIR // 2).astype(F32)
    return one.astype(dtype), (1.0 - one).astype(dtype)


def apart(x):
    one, two = lane_masks(x.dtype)
    return jnp.concatenate([x * one, x * two], axis=0)


def together(x):
    half = PAIR // 2
    lane = lax.broadcasted_iota(jnp.int32, (half, PAIR), 1)
    return jnp.where(lane < half, x[:half], x[half:])


def same_head():
    half = PAIR // 2
    a = lax.broadcasted_iota(jnp.int32, (PAIR, PAIR), 0) // half
    b = lax.broadcasted_iota(jnp.int32, (PAIR, PAIR), 1) // half
    return a == b


def eye():
    a = lax.broadcasted_iota(jnp.int32, (PAIR, PAIR), 0)
    b = lax.broadcasted_iota(jnp.int32, (PAIR, PAIR), 1)
    return (a == b).astype(F32)


def by_head(x, reduce):
    half, width = PAIR // 2, x.shape[1]
    parts = [reduce(x[h * half : (h + 1) * half], axis=0, keepdims=True) for h in (0, 1)]
    return jnp.concatenate([jnp.broadcast_to(y, (half, width)) for y in parts], axis=0)


def lanes(p):
    if isinstance(p, int):
        return pl.ds(p * PAIR, PAIR)
    return pl.ds(pl.multiple_of(p * PAIR, PAIR), PAIR)


def conv_pair(table, padded):
    size = table.shape[0] // 4
    out = nn(table, padded)
    lane = lax.broadcasted_iota(jnp.int32, (size, PAIR), 1)
    return jnp.where(
        lane < PAIR // 2,
        out[:size] + out[2 * size : 3 * size],
        out[size : 2 * size] + out[3 * size :],
    )


class Group:
    def __init__(self, send, recv):
        self.row, self.me = lax.axis_index("rows"), lax.axis_index("seq")
        self.size = lax.axis_size("seq")
        self.send, self.recv, self.started = send, recv, []

    def peers(self):
        return [(self.row, (self.me + k) % self.size) for k in range(1, self.size)]

    def push(self, channel, pick_src, dst):
        copies = []
        for k, device in enumerate(self.peers()):
            copy = remote(
                pick_src(device[1]), dst, self.send.at[channel, k], self.recv.at[channel, k], device
            )
            copy.start()
            copies.append(copy)
        self.started += copies
        return copies

    def line_peers(self):
        n, line, core = self.size // 2, self.me // 2, self.me % 2
        return [(self.row, 2 * ((line + k) % n) + core) for k in range(1, n)]

    def go(self, channel, k, src, dst, device):
        copy = remote(src, dst, self.send.at[channel, k], self.recv.at[channel, k], device)
        copy.start()
        self.started.append(copy)
        return copy

    def share(self, parts):
        n, line, core = self.size // 2, self.me // 2, self.me % 2
        sibling = (self.row, 2 * line + 1 - core)
        there, here = [], []
        for channel, block in parts:
            mine = block(self.me)
            there.append(
                [self.go(channel, k, mine, mine, d) for k, d in enumerate(self.line_peers())]
            )
        for channel, block in parts:
            here.append(self.go(channel, n - 1, block(self.me), block(self.me), sibling))

        def arrive():
            for k in range(1, n):
                source = 2 * ((line - k + n) % n) + core
                for (channel, block), copies in zip(parts, there):
                    copies[k - 1].wait_recv()
                    got = block(source)
                    here.append(self.go(channel, n - 1 + k, got, got, sibling))
            for copy in here:
                copy.wait_recv()

        return arrive

    def halo(self, channel, source, padded, reach):
        length = source.shape[1]
        copies = []
        for which, (src_at, dst_at, step) in enumerate(
            ((length - reach, 0, 1), (0, length + reach, -1))
        ):
            there = (self.me + step + self.size) % self.size
            copy = remote(
                source.at[:, pl.ds(src_at, reach), :],
                padded.at[:, pl.ds(dst_at, reach), :],
                self.send.at[channel, which],
                self.recv.at[channel, which],
                (self.row, there),
            )
            goes = self.me < self.size - 1 if step == 1 else self.me > 0
            comes = self.me > 0 if step == 1 else self.me < self.size - 1
            pl.when(goes)(copy.start)
            copies.append((copy, goes, comes, dst_at))

        def arrive():
            for copy, goes, comes, dst_at in copies:
                pl.when(comes)(copy.wait_recv)

                @pl.when(jnp.logical_not(comes))
                def _():
                    shape = (padded.shape[0], reach, padded.shape[2])
                    padded[:, pl.ds(dst_at, reach), :] = jnp.zeros(shape, padded.dtype)

        def sent():
            for copy, goes, _, _ in copies:
                pl.when(goes)(copy.wait_send)

        return arrive, sent

    def finish(self):
        for copy in self.started:
            copy.wait_send()


def pinv_start(prob):
    total = by_head(jnp.sum(prob * prob, axis=1, keepdims=True), jnp.sum)
    return prob.T / total


def pinv_terms(p, z, unit):
    product = three(nn, p, z)
    prod = split(product)
    term_one = 7.0 * unit - product
    term_two = 15.0 * unit - three(nn, prod, split(term_one))
    term_three = 13.0 * unit - three(nn, prod, split(term_two))
    return prod, term_one, term_two, term_three


def band(line, length, reach):
    wide = jnp.broadcast_to(line, (length, line.shape[1]))
    return pltpu.roll(wide, 0, 1, stride=1, stride_axis=0)[:, : length + 2 * reach]


def fill_bands(lines, table, reach):
    pairs, rows = table.shape[0], table.shape[1] // 4
    for p in range(pairs):
        for h in (0, 1):
            high, low = split(band(lines[2 * p + h : 2 * p + h + 1, :], rows, reach))
            table[p, h * rows : (h + 1) * rows, :] = high
            table[p, (2 + h) * rows : (3 + h) * rows, :] = low


def front_kernel(
    reach,
    tokens, qkv_w, out_w, up_w, down_w, vec_w, lines,
    f_qkv, f_out, f_up, f_down, f_rows,
    q, k, attn, vpad, landq, landk, mix, p1, e, wt, p2o, zo, lvo,
    v, table, f_vec, lb, numer, nrecv, stat, srecv, mstat, conv, fcol, *rest,
):
    asm, stage = rest[:7], rest[7:14]
    g_send, g_recv, g_local, send, recv = rest[14:]
    net, group = Net(g_send, g_recv), Group(send, recv)
    me, size = group.me, group.size
    n_seq, length, width = q.shape
    pairs = width // PAIR
    own = n_seq * pairs // size
    each = own * PAIR
    land_local = LAND // size
    seg = length // land_local
    scale = (PAIR // 2) ** -0.5
    greet(group.peers() + [net.to_first, net.to_second])

    def owner_seq(d):
        return d * own // pairs

    def owner_lanes(d):
        return pl.ds(pl.multiple_of((d * own % pairs) * PAIR, PAIR), each)

    plan = [(vec_w, f_vec, 0), (qkv_w, f_qkv, width), (qkv_w, f_qkv, 0), (qkv_w, f_qkv, 2 * width)]
    plan += [(out_w, f_out, 0), (up_w, f_up, 0), (down_w, f_down, 0)]
    pieces = []
    for w, (src, dst, base) in enumerate(plan):
        half = asm[w].shape[1]
        pieces.append(Gather(net, w, src, dst, base, half, asm[w], stage[w], g_local.at[w]))
    g_vec, g_k, g_q, g_v, g_out, g_up, g_down = pieces
    for piece in pieces[:4]:
        piece.spread()
    fill_bands(lines, table, reach)

    def project(dst, base, bias):
        step = 2 * PAIR
        for at in range(0, width, step):
            x = nn(tokens[...], f_qkv[:, base + at : base + at + step])
            if bias is not None:
                x = x + f_rows[bias : bias + 1, at : at + step]
            dst[:, :, at : at + step] = x.astype(BF).reshape(n_seq, length, step)

    g_vec.step_one()
    g_k.step_one()
    g_q.step_one()
    g_vec.step_two()
    g_k.step_two()
    g_v.step_one()
    g_out.spread()
    g_up.spread()
    g_vec.step_three()
    g_q.step_two()
    g_k.step_three()
    g_down.spread()
    g_vec.close()
    f_rows[...] = f_vec[:, :PAIR].astype(F32).T[: f_rows.shape[0]]
    g_v.step_two()
    g_k.close()
    project(k, width, None)
    g_q.step_three()
    g_q.close()
    project(q, 0, 0)
    g_v.step_three()
    g_out.step_one()
    g_up.step_one()
    g_v.close()
    project(v, 2 * width, 1)

    def own_landmarks(s, carry):
        both = [
            jnp.mean(x[s].astype(F32).reshape(land_local, seg, width), axis=1) for x in (q, k)
        ]
        lb[me, s] = jnp.concatenate(both, axis=0).astype(BF)
        vpad[s, pl.ds(reach, length), :] = v[s]
        return carry

    lax.fori_loop(0, n_seq, own_landmarks, 0)
    landed = group.share([(1, lambda d: lb.at[d])])
    halo_in, halo_sent = group.halo(0, v, vpad, reach)
    g_out.step_two()
    g_down.step_one()
    landed()

    def whole_landmarks(s, carry):
        x = lb[:, s].astype(F32)
        landq[s] = x[:, :land_local].reshape(LAND, width).astype(BF)
        landk[s] = x[:, land_local:].reshape(LAND, width).astype(BF)
        return carry

    lax.fori_loop(0, n_seq, whole_landmarks, 0)
    lane_at = lax.broadcasted_iota(jnp.int32, (PAIR, PAIR), 1)

    def over_tokens(s, tile):
        for p in range(pairs):
            score = nt(apart(landq[s, :, lanes(p)]), k[s, :, lanes(p)]) * scale
            top = jnp.max(score, axis=1, keepdims=True)
            expo = jnp.exp(score - top)
            low = expo.astype(BF)
            e[s * pairs + p] = low
            numer[s, :, lanes(p)] = together(nn(low, v[s, :, lanes(p)])).astype(BF)
            unit = s * pairs + p
            at = (unit // own) * 8 + unit % own
            tile = jnp.where(lane_at == at, top, tile)
            tile = jnp.where(lane_at == at + own, jnp.sum(expo, axis=1, keepdims=True), tile)
        return tile

    tile = lax.fori_loop(0, n_seq, over_tokens, jnp.zeros((PAIR, PAIR), F32))
    stat[...] = tile.T[: 8 * size].reshape(size, 8, PAIR)
    sums_in = group.push(
        2, lambda d: numer.at[owner_seq(d), :, owner_lanes(d)], nrecv.at[me]
    )
    stats_in = group.push(3, lambda d: stat.at[d], srecv.at[me])
    g_up.step_two()
    nrecv[me] = numer[owner_seq(me), :, owner_lanes(me)]
    srecv[me] = stat[me]

    block, unit_matrix = same_head(), eye()
    my_seq, my_pair = owner_seq(me), (me * own) % pairs
    for i in range(own):
        at = lanes(my_pair + i)
        score = nt(apart(landq[my_seq, :, at]), apart(landk[my_seq, :, at])) * scale
        score = jnp.where(block, score, -1e30)
        expo = jnp.exp(score - jnp.max(score, axis=1, keepdims=True))
        prob = expo / jnp.sum(expo, axis=1, keepdims=True)
        p2o[i] = prob
        zo[0, i] = pinv_start(prob)

    halo_in()
    per_step = n_seq * pairs // PINV_ITERS

    def over_landmarks(unit):
        s, p = unit // pairs, unit % pairs
        score = nt(apart(landk[s, :, lanes(p)]), q[s, :, lanes(p)]) * scale
        expo = jnp.exp(score - by_head(score, jnp.max))
        p1[unit] = expo / by_head(expo, jnp.sum)
        conv[s, :, lanes(p)] = conv_pair(table[p], vpad[s, :, lanes(p)])

    def pinv_step(step, carry):
        for i in range(own):
            z = split(zo[step, i])
            _, _, _, inner = pinv_terms(split(p2o[i]), z, unit_matrix)
            zo[step + 1, i] = 0.25 * three(nn, z, split(inner))
        for j in range(per_step):
            over_landmarks(step * per_step + j)
        return carry

    lax.fori_loop(0, PINV_ITERS // 2, pinv_step, 0)
    g_out.step_three()
    g_down.step_two()
    lax.fori_loop(PINV_ITERS // 2, PINV_ITERS, pinv_step, 0)

    for copy in sums_in + stats_in:
        copy.wait_recv()
    got = srecv[...]
    tops = got[:, :own]
    top = jnp.max(tops, axis=0, keepdims=True)
    factor = jnp.exp(tops - top)
    total = jnp.sum(factor * got[:, own : 2 * own], axis=0, keepdims=True)
    factor = factor / total
    spare = jnp.zeros((1, 8 - 2 * own, PAIR), F32)
    mstat[me] = jnp.concatenate([top, total, spare], axis=1)[0]
    spread = jnp.concatenate([factor, jnp.zeros((size, 8 - own, PAIR), F32)], axis=1)
    spread = spread.reshape(8 * size, PAIR)
    fcol[...] = jnp.concatenate([spread, jnp.zeros((PAIR - 8 * size, PAIR), F32)], axis=0).T
    half = PAIR // 2
    narrow = lax.broadcasted_iota(jnp.int32, (half, PAIR), 1) < half
    for i in range(own):
        at = pl.ds(i * PAIR, PAIR)
        mean = jnp.zeros((half, PAIR), F32)
        for src in range(size):
            column = fcol[:, src * 8 + i : src * 8 + i + 1]
            weight = jnp.where(narrow, column[:half], column[half:])
            mean = mean + weight * nrecv[src, :, at].astype(F32)
        lvo[:, at] = mean
        mixed = together(three(nn, split(zo[PINV_ITERS, i]), split(apart(mean))))
        mix[my_seq, :, lanes(my_pair + i)] = mixed.astype(BF)
    mixed_in = group.share(
        [
            (4, lambda d: mix.at[owner_seq(d), :, owner_lanes(d)]),
            (5, lambda d: mstat.at[d]),
        ]
    )
    g_up.step_three()
    mixed_in()

    rows = jnp.concatenate(
        [mstat[...].reshape(8 * size, PAIR), jnp.zeros((PAIR - 8 * size, PAIR), F32)], axis=0
    )
    rows = rows.T
    valid = (lane_at % 8 < own) & (lane_at < 8 * size)
    shift = jnp.where(valid, tile - rows, 0.0)
    den = jnp.where(valid, pltpu.roll(rows, PAIR - own, 1), 1.0)
    wt[...] = jnp.exp(shift) / den

    def result(s, carry):
        for p in range(pairs):
            low = p1[s * pairs + p].astype(BF)
            out = tn(low, apart(mix[s, :, lanes(p)])) + conv[s, :, lanes(p)]
            attn[s, :, lanes(p)] = out.astype(BF)
        return carry

    lax.fori_loop(0, n_seq, result, 0)
    g_down.step_three()
    for piece in (g_out, g_up, g_down):
        piece.close()
    halo_sent()
    group.finish()
    net.finish()


def front(tokens, matrices, table, lines, seq_size, reach):
    n_seq, length, width = tokens.shape
    pairs = width // PAIR
    units = n_seq * pairs
    own = units // seq_size
    n_dev = 4 * seq_size
    line_size = seq_size // 2
    vmem, hbm = pl.BlockSpec(memory_space=pltpu.VMEM), pl.BlockSpec(memory_space=pltpu.HBM)
    shape = jax.ShapeDtypeStruct
    land = shape((n_seq, LAND, width), BF)
    qkv_w, out_w, up_w, down_w = matrices
    whole = [shape((n_dev * x.shape[0], x.shape[1]), BF) for x in matrices]
    asm = [(table.shape[0], table.shape[1] // 2)] + [(qkv_w.shape[0], width // 2)] * 3
    asm += [(x.shape[0], x.shape[1] // 2) for x in (out_w, up_w, down_w)]
    n_sem = line_size + GATHER_SEMS
    return pl.pallas_call(
        functools.partial(front_kernel, reach),
        out_shape=whole
        + [
            shape((16, width), F32),
            shape(tokens.shape, BF), shape(tokens.shape, BF), shape(tokens.shape, BF),
            shape((n_seq, length + 2 * reach, width), BF), land, land, land,
            shape((units, PAIR, length), F32), shape((units, PAIR, length), BF),
            shape((PAIR, PAIR), F32), shape((own, PAIR, PAIR), F32),
            shape((PINV_ITERS + 1, own, PAIR, PAIR), F32), shape((LAND, own * PAIR), F32),
        ],
        in_specs=[vmem] * 7,
        out_specs=[vmem, hbm, hbm, hbm] + [vmem] * 14,
        scratch_shapes=[
            pltpu.VMEM(tokens.shape, BF),
            pltpu.VMEM((pairs, 4 * length, length + 2 * reach), BF),
            pltpu.VMEM((n_dev * table.shape[0], table.shape[1]), BF),
            pltpu.VMEM((seq_size, n_seq, 2 * LAND // seq_size, width), BF),
            pltpu.VMEM((n_seq, LAND, width), BF),
            pltpu.VMEM((seq_size, LAND, own * PAIR), BF),
            pltpu.VMEM((seq_size, 8, PAIR), F32),
            pltpu.VMEM((seq_size, 8, PAIR), F32),
            pltpu.VMEM((seq_size, 8, PAIR), F32),
            pltpu.VMEM((n_seq, length, width), F32),
            pltpu.VMEM((PAIR, PAIR), F32),
        ]
        + [pltpu.VMEM((2 * r, h), F32) for r, h in asm]
        + [pltpu.VMEM((2 * r, h), BF) for r, h in asm]
        + [
            pltpu.SemaphoreType.DMA((7, n_sem)),
            pltpu.SemaphoreType.DMA((7, n_sem)),
            pltpu.SemaphoreType.DMA((7,)),
            pltpu.SemaphoreType.DMA((6, seq_size)),
            pltpu.SemaphoreType.DMA((6, seq_size)),
        ],
        compiler_params=pltpu.CompilerParams(
            collective_id=0, has_side_effects=True, vmem_limit_bytes=56 * 1024 * 1024
        ),
        name="front",
    )(tokens.reshape(n_seq * length, width), *matrices, table, lines)


def gelu_parts(x):
    expo = jnp.exp(-0.5 * x * x)
    t = 1.0 / (1.0 + (0.3275911 * 0.7071067811865476) * jnp.abs(x))
    tail = -0.284496736 + t * (1.421413741 + t * (-1.453152027 + t * 1.061405429))
    tail = 0.5 * expo * t * (0.254829592 + t * tail)
    below = jnp.where(x >= 0.0, 1.0 - tail, tail)
    return x * below, below + x * expo * 0.3989422804014327


def norm_parts(resid):
    center = resid - jnp.mean(resid, axis=-1, keepdims=True)
    scale = lax.rsqrt(jnp.mean(center * center, axis=-1, keepdims=True) + norm_eps)
    return center * scale, scale


def norm_back(grad, gain, unit, scale):
    inner = grad * gain
    mean = jnp.mean(inner, axis=-1, keepdims=True)
    along = jnp.mean(inner * unit, axis=-1, keepdims=True)
    return scale * (inner - mean - unit * along)


def row_sum(x):
    return jnp.sum(x, axis=0, keepdims=True)


def feed_kernel(
    attn, tokens, cot, rows, h_out, h_up, h_down,
    layer_out, grad_one, ga, sums, d_down, d_up, d_out,
    w_out, w_up, w_down, g_down, g_up, g_out, active, slope, unit_one, scale_one, normed, low, low_t,
    total, grad_two, ff, attn_t, w_sem, o_sem,
):
    count, width = attn.shape
    hidden = w_up.shape[1]
    loads = [
        pltpu.make_async_copy(src, dst, w_sem.at[i])
        for i, (src, dst) in enumerate(((h_out, w_out), (h_up, w_up), (h_down, w_down)))
    ]
    for load in loads:
        load.start()
    block = 2 * PAIR
    n_rows, n_wide = count // block, width // block
    row_groups = hidden // width
    sums[...] = jnp.zeros(sums.shape, F32)

    def row(i):
        return rows[i : i + 1, :]

    def at_rows(i):
        return pl.ds(pl.multiple_of(i * block, block), block)

    loads[0].wait()

    def first(i, carry):
        at = at_rows(i)
        resid = tokens[at, :].astype(F32) + (nn(attn[at, :], w_out[...]) + row(2))
        unit, scale = norm_parts(resid)
        out = unit * row(6) + row(3)
        unit_one[at, :] = unit
        scale_one[at, :] = jnp.broadcast_to(scale, (block, PAIR))
        normed[at, :] = out
        low[at, :] = out.astype(BF)
        total[at, :] = jnp.broadcast_to(row(4), (block, width))
        return carry

    lax.fori_loop(0, n_rows, first, 0)
    low_t[...] = low[...].T
    attn_t[...] = attn[...].T
    loads[1].wait()
    loads[2].wait()

    def forward(r, carry):
        for j in range(n_wide):
            f = pl.ds(pl.multiple_of(r * width + j * block, block), block)
            bias = rows[pl.ds(8 + r, 1), j * block : (j + 1) * block]
            value, rate = gelu_parts(nn(low[...], w_up[:, f]) + bias)
            value = value.astype(BF)
            active[:, f] = value
            slope[:, f] = rate.astype(BF)
            total[...] += nn(value, w_down[f, :])
        return carry

    lax.fori_loop(0, row_groups, forward, 0)

    def second(i, carry):
        at = at_rows(i)
        unit, scale = norm_parts(normed[at, :] + total[at, :])
        layer_out[at, :] = (unit * row(7) + row(5)).astype(BF)
        up = cot[at, :].astype(F32)
        grad = norm_back(up, row(7), unit, scale)
        grad_two[at, :] = grad
        total[at, :] = grad
        grad = grad.astype(BF)
        ff[at, :] = grad
        sums[4:5, :] += row_sum(grad.astype(F32))
        sums[5:6, :] += row_sum(up)
        sums[7:8, :] += row_sum(up * unit)
        return carry

    lax.fori_loop(0, n_rows, second, 0)

    def backward(r, carry):
        for j in range(n_wide):
            f = pl.ds(pl.multiple_of(r * width + j * block, block), block)
            lane = slice(j * block, (j + 1) * block)
            grad = nt(ff[...], w_down[f, :]) * slope[:, f].astype(F32)
            grad = grad.astype(BF)
            sums[pl.ds(8 + r, 1), lane] = row_sum(grad.astype(F32))
            g_up[:, f] = nn(low_t[...], grad).astype(BF)
            g_down[f, :] = tn(active[:, f], ff[...]).astype(BF)
            total[...] += nt(grad, w_up[:, f])
        f = pl.ds(pl.multiple_of(r * width, width), width)
        pltpu.make_async_copy(g_down.at[f, :], d_down.at[f, :], o_sem.at[0, r]).start()
        pltpu.make_async_copy(g_up.at[:, f], d_up.at[:, f], o_sem.at[1, r]).start()
        return carry

    lax.fori_loop(0, row_groups, backward, 0)

    def third(i, carry):
        at = at_rows(i)
        unit = unit_one[at, :]
        up = total[at, :]
        grad = norm_back(up, row(6), unit, scale_one[at, :1])
        grad_one[at, :] = grad
        grad = grad.astype(BF)
        low[at, :] = grad
        ga[at, :] = nt(grad, w_out[...]).astype(BF)
        sums[2:3, :] += row_sum(grad.astype(F32))
        sums[3:4, :] += row_sum(up)
        sums[6:7, :] += row_sum(up * unit)
        return carry

    lax.fori_loop(0, n_rows, third, 0)
    g_out[...] = nn(attn_t[...], low[...]).astype(BF)
    last = pltpu.make_async_copy(g_out, d_out, o_sem.at[2, 0])
    last.start()
    for r in range(row_groups):
        f = pl.ds(r * width, width)
        pltpu.make_async_copy(g_down.at[f, :], d_down.at[f, :], o_sem.at[0, r]).wait()
        pltpu.make_async_copy(g_up.at[:, f], d_up.at[:, f], o_sem.at[1, r]).wait()
    last.wait()


def feed(attn, tokens, cot, rows, weights):
    count, width = attn.shape
    hidden = weights[1].shape[1]
    vmem, hbm = pl.BlockSpec(memory_space=pltpu.VMEM), pl.BlockSpec(memory_space=pltpu.HBM)
    shape = jax.ShapeDtypeStruct
    wide = [x.shape for x in weights]
    return pl.pallas_call(
        feed_kernel,
        out_shape=[
            shape(attn.shape, BF), shape(attn.shape, F32), shape(attn.shape, BF),
            shape(rows.shape, F32),
        ]
        + [shape(wide[i], BF) for i in (2, 1, 0)],
        in_specs=[vmem] * 4 + [hbm] * 3,
        out_specs=[vmem] * 4 + [hbm] * 3,
        scratch_shapes=[pltpu.VMEM(x, BF) for x in wide]
        + [pltpu.VMEM(wide[i], BF) for i in (2, 1, 0)]
        + [
            pltpu.VMEM((count, hidden), BF),
            pltpu.VMEM((count, hidden), BF),
            pltpu.VMEM((count, width), F32),
            pltpu.VMEM((count, PAIR), F32),
            pltpu.VMEM((count, width), F32),
            pltpu.VMEM((count, width), BF),
            pltpu.VMEM((width, count), BF),
            pltpu.VMEM((count, width), F32),
            pltpu.VMEM((count, width), F32),
            pltpu.VMEM((count, width), BF),
            pltpu.VMEM((width, count), BF),
            pltpu.SemaphoreType.DMA((3,)),
            pltpu.SemaphoreType.DMA((3, hidden // width)),
        ],
        compiler_params=pltpu.CompilerParams(vmem_limit_bytes=56 * 1024 * 1024),
        name="feed",
    )(attn, tokens, cot, rows, *weights)


def back_kernel(
    reach, n_taps,
    ga, tokens, resid, f_qkv, vec_rows, lines, d_down, d_up, d_out,
    q, k, vpad, landq, landk, mix, p1, e, wt, p2o, zo, lvo,
    input_grad, s_qkv, s_out, s_up, s_down, s_small,
    grad, tapg, table, tok_t, outbox, small_box,
    gpad, gmix, gmr, low, gfull, mstat, gcol, gq, gv, lkp, lpart, lpr, lsum, gsum, gpart, dz, dp,
    skew, own_g, *rest,
):
    bufs, (g_send, g_recv, g_local, send, recv) = rest[:-5], rest[-5:]
    net, group = Net(g_send, g_recv), Group(send, recv)
    me, size = group.me, group.size
    n_seq, length, width = q.shape
    pairs = width // PAIR
    own = n_seq * pairs // size
    each = own * PAIR
    land_local = LAND // size
    seg = length // land_local
    half = PAIR // 2
    scale = half**-0.5
    greet(group.peers() + [net.to_first, net.to_second])

    def owner_seq(d):
        return d * own // pairs

    def owner_lanes(d):
        return pl.ds(pl.multiple_of((d * own % pairs) * PAIR, PAIR), each)

    plan = [(s_down, 0), (s_up, 0), (s_out, 0)]
    plan += [(s_qkv, 2 * width), (s_qkv, 0), (s_qkv, width), (s_small, 0)]
    pieces = []
    for w, (out, base) in enumerate(plan):
        own_bufs = bufs[6 * w : 6 * w + 6]
        pieces.append(Scatter(net, w, out, base, own_bufs[0].shape[1], own_bufs))
    r_down, r_up, r_out, r_v, r_q, r_k, r_small = pieces

    def open_whole(w, src):
        piece = pieces[w]
        other, here = [columns(0, c, piece.half) for c in (1 - net.core, net.core)]
        own_part = pltpu.make_async_copy(src.at[:, here], piece.acc, g_local.at[w])
        piece.open(src.at[:, other], own_part)

    def open_weight(piece, box):
        step = 2 * PAIR
        rows = tok_t.shape[0]

        def one(i, carry):
            at = pl.ds(pl.multiple_of(i * step, step), step)
            x = tok_t[at, :]
            other, here = [columns(piece.base, c, piece.half) for c in (1 - net.core, net.core)]
            outbox[box, at, :] = nn(x, grad[:, other]).astype(BF)
            piece.acc[at, :] = nn(x, grad[:, here]).astype(BF)
            return carry

        lax.fori_loop(0, rows // step, one, 0)
        piece.open(outbox.at[box])

    open_whole(0, d_down)
    open_whole(1, d_up)
    open_whole(2, d_out)
    halo_in, halo_sent = group.halo(0, ga, gpad, reach)

    def first(s, carry):
        for p in range(pairs):
            unit, at = s * pairs + p, lanes(p)
            own_ga = ga[s, :, at]
            gpad[s, pl.ds(reach, length), at] = own_ga
            prob = p1[unit]
            gmix[s, :, at] = together(nn(prob.astype(BF), own_ga)).astype(BF)
            back = nt(apart(mix[s, :, at]), own_ga)
            low[unit] = (prob * (back - by_head(prob * back, jnp.sum))).astype(BF)
        return carry

    lax.fori_loop(0, n_seq, first, 0)
    chips, my_line, my_core = size // 2, me // 2, me % 2
    core_lanes = [pl.ds(pl.multiple_of(c * each, PAIR), each) for c in (my_core, 1 - my_core)]
    sibling = (group.row, 2 * my_line + 1 - my_core)
    gmix_sib = group.go(1, chips, gmix.at[:, :, core_lanes[1]], gsum, sibling)
    r_down.step_one()
    gmix_sib.wait_recv()
    gpart[...] = gmix[:, :, core_lanes[0]] + gsum[...]
    gmix_in = []
    for kk, device in enumerate(group.line_peers()):
        other = device[1] // 2
        gmix_in.append(group.go(1, kk, gpart.at[other], gmr.at[my_line], device))
    gmr[my_line] = gpart[my_line]
    r_up.step_one()
    fill_bands(lines, table, reach)
    halo_in()
    skew[...] = jnp.zeros(skew.shape, F32)

    def beside(s, carry):
        one, two_mask = lane_masks(BF)
        for p in range(pairs):
            unit, at = s * pairs + p, lanes(p)
            own_ga, padded = ga[s, :, at], vpad[s, :, at]
            gs = low[unit]
            gq[s, :, at] = tn(gs, apart(landk[s, :, at])) * scale
            lkp[s, :, at] = together(nn(gs, q[s, :, at])) * scale
            gv[s, :, at] = conv_pair(table[p], gpad[s, :, at])
            both = jnp.concatenate([own_ga * one, own_ga * two_mask], axis=0)
            skew[2 * p : 2 * p + 2, :, : length + 2 * reach] += nt(both, padded).reshape(
                2, length, length + 2 * reach
            )
        return carry

    lax.fori_loop(0, n_seq, beside, 0)
    lane_at = lax.broadcasted_iota(jnp.int32, (PAIR, PAIR), 1)
    wide = skew.shape[2]
    for h in range(2 * pairs):
        total = skew[h, :8, :]
        for row in range(8, length, 8):
            total = total + pltpu.roll(skew[h, row : row + 8, :], wide - row, 1)
        tapg[h] = total[:, :PAIR]
    r_down.step_two()
    r_out.step_one()
    tok_t[...] = tokens[...].T

    for copy in gmix_in:
        copy.wait_recv()
    my_seq, my_pair = owner_seq(me), (me * own) % pairs
    tile = jnp.zeros((PAIR, PAIR), F32)
    for i in range(own):
        at = pl.ds(i * PAIR, PAIR)
        total = gmr[0, :, at].astype(F32)
        for src in range(1, chips):
            total = total + gmr[src, :, at].astype(F32)
        total = split(apart(total))
        means = apart(lvo[:, at])
        back = together(three(tn, split(zo[PINV_ITERS, i]), total)).astype(BF)
        own_g[:, at] = back
        column = jnp.sum(apart(back.astype(F32)) * means, axis=1, keepdims=True)
        tile = jnp.where(lane_at == i, column, tile)
        dz[i] = three(nt, total, split(means))
        dp[i] = jnp.zeros((PAIR, PAIR), F32)
    mstat[me] = tile.T[:8]
    gfull[my_seq, :, owner_lanes(me)] = own_g[...]
    g_in = group.share(
        [
            (2, lambda d: gfull.at[owner_seq(d), :, owner_lanes(d)]),
            (3, lambda d: mstat.at[d]),
        ]
    )
    r_up.step_two()
    g_in()
    rows = jnp.concatenate(
        [mstat[...].reshape(8 * size, PAIR), jnp.zeros((PAIR - 8 * size, PAIR), F32)], axis=0
    )
    gcol[...] = rows.T
    unit_matrix = eye()

    def third(unit):
        s, p = unit // pairs, unit % pairs
        at = lanes(p)
        here = (unit // own) * 8 + unit % own
        picked = lane_at == here
        weight = jnp.sum(jnp.where(picked, wt[...], 0.0), axis=1, keepdims=True)
        offset = jnp.sum(jnp.where(picked, gcol[...], 0.0), axis=1, keepdims=True)
        g = apart(gfull[s, :, at])
        prob = e[unit].astype(F32) * weight
        back = nt(g, vpad[s, pl.ds(reach, length), at]) - offset
        gs = (prob * back).astype(BF)
        values = gv[s, :, at] + tn(prob.astype(BF), g)
        v_at = pl.ds(pl.multiple_of(2 * width + p * PAIR, PAIR), PAIR)
        rows = pl.ds(pl.multiple_of(s * length, length), length)
        grad[rows, v_at] = values.astype(BF)
        rows = pl.ds(pl.multiple_of(s * length, length), length)
        grad[rows, pl.ds(pl.multiple_of(width + p * PAIR, PAIR), PAIR)] = (
            tn(gs, apart(landq[s, :, at])) * scale
        ).astype(BF)
        lq = (together(nn(gs, k[s, :, at])) * scale).reshape(size, land_local, PAIR)
        lk = lkp[s, :, at].reshape(size, land_local, PAIR)
        both = jnp.concatenate([lq, lk], axis=1).astype(BF)
        lpart[:, :, s, :, at] = both.reshape(chips, 2, 2 * land_local, PAIR)

    per_step = n_seq * pairs // PINV_ITERS

    def pinv_back(step, carry):
        at_step = PINV_ITERS - 1 - step
        for i in range(own):
            p, z = split(p2o[i]), split(zo[at_step, i])
            prod, one, two_term, three_term = pinv_terms(p, z, unit_matrix)
            d_out = dz[i] * 0.25
            d_out_s = split(d_out)
            d_three = split(three(tn, z, d_out_s))
            d_two = split(-three(tn, prod, d_three))
            d_one = -three(tn, prod, d_two)
            d_prod = -three(nt, d_three, split(two_term)) - three(nt, d_two, split(one)) - d_one
            d_prod = split(d_prod)
            dp[i] += three(nt, d_prod, z)
            dz[i] = three(nt, d_out_s, split(three_term)) + three(tn, p, d_prod)
        for j in range(per_step):
            third(step * per_step + j)
        return carry

    lax.fori_loop(0, PINV_ITERS // 2, pinv_back, 0)
    r_down.step_three()
    r_out.step_two()
    lax.fori_loop(PINV_ITERS // 2, PINV_ITERS, pinv_back, 0)
    r_up.step_three()

    for i in range(own):
        at = pl.ds(i * PAIR, PAIR)
        prob = p2o[i]
        squares = by_head(jnp.sum(prob * prob, axis=1, keepdims=True), jnp.sum)
        d_start = dz[i].T
        inner = by_head(jnp.sum(d_start * prob, axis=1, keepdims=True), jnp.sum)
        d_prob = dp[i] + d_start / squares - 2.0 * prob * inner / (squares * squares)
        gs = prob * (d_prob - jnp.sum(prob * d_prob, axis=1, keepdims=True))
        gs = split(gs)
        here = lanes(my_pair + i)
        lq, lk = apart(landq[my_seq, :, here]), apart(landk[my_seq, :, here])
        query = together(nn(gs[0], lk) + nn(gs[1], lk)) * scale
        key = together(tn(gs[0], lq) + tn(gs[1], lq)) * scale
        both = [x.reshape(size, land_local, PAIR) for x in (query, key)]
        both = jnp.concatenate(both, axis=1).reshape(chips, 2, 2 * land_local, PAIR)
        lpart[:, :, my_seq, :, here] = (lpart[:, :, my_seq, :, here].astype(F32) + both).astype(BF)
    land_sib = group.go(4, chips, lpart.at[:, 1 - my_core], lsum, sibling)
    land_sib.wait_recv()

    def add_lands(i, carry):
        lsum[i] = lsum[i] + lpart[i, my_core]
        return carry

    lax.fori_loop(0, chips, add_lands, 0)
    lpr[my_line] = lsum[my_line]
    land_in = []
    for kk, device in enumerate(group.line_peers()):
        land_in.append(group.go(4, kk, lsum.at[device[1] // 2], lpr.at[my_line], device))
    open_weight(r_v, 0)
    r_down.step_four()
    for copy in land_in:
        copy.wait_recv()

    def close(s, carry):
        for p in range(pairs):
            at = lanes(p)
            total = lpr[0, s, :, at].astype(F32)
            for src in range(1, chips):
                total = total + lpr[src, s, :, at].astype(F32)
            total = total * (1.0 / seg)
            spread = [
                jnp.concatenate(
                    [jnp.broadcast_to(x[i : i + 1], (seg, PAIR)) for i in range(land_local)], axis=0
                )
                for x in (total[:land_local], total[land_local:])
            ]
            rows = pl.ds(pl.multiple_of(s * length, length), length)
            grad[rows, at] = (gq[s, :, at] + spread[0]).astype(BF)
            key_at = pl.ds(width + p * PAIR, PAIR)
            grad[rows, key_at] = (grad[rows, key_at].astype(F32) + spread[1]).astype(BF)
        return carry

    lax.fori_loop(0, n_seq, close, 0)
    open_weight(r_q, 1)
    r_v.step_one()
    open_weight(r_k, 2)
    r_q.step_one()
    r_out.step_three()

    def column_sums(base):
        total = jnp.zeros((1, width), F32)
        for s in range(n_seq):
            x = grad[s * length : (s + 1) * length, base : base + width].astype(F32)
            total = total + jnp.sum(x, axis=0, keepdims=True)
        return total

    count = vec_rows.shape[0]
    which = lax.broadcasted_iota(jnp.int32, (count, width), 0)
    table_rows = vec_rows[...]
    table_rows = jnp.where(which == 0, column_sums(0), table_rows)
    table_rows = jnp.where(which == 1, column_sums(2 * width), table_rows)
    table_rows = jnp.concatenate([table_rows, jnp.zeros((PAIR - count, width), F32)], axis=0)
    left = table_rows.T
    sums = tapg[:, 0, :]
    for b in range(1, 8):
        sums = sums + pltpu.roll(tapg[:, b, :], PAIR - b, 1)
    shard = r_small.rows
    sums = jnp.concatenate([sums, jnp.zeros((shard - sums.shape[0], PAIR), F32)], axis=0)
    right = jnp.broadcast_to(sums[None], (width // shard, shard, PAIR)).reshape(width, PAIR)
    zero = net.core == 0
    r_small.acc[...] = jnp.where(zero, left, right)
    small_box[...] = jnp.where(zero, right, left)
    r_small.open(small_box)
    r_v.step_two()
    r_k.step_one()

    def inputs(i, carry):
        step = 2 * PAIR
        rows = pl.ds(pl.multiple_of(i * step, step), step)
        for at in range(0, width, step):
            x = nt(grad[rows, :], f_qkv[at : at + step, :])
            out = x + resid[rows, at : at + step]
            input_grad[rows, at : at + step] = out.astype(BF)
        return carry

    lax.fori_loop(0, tokens.shape[0] // (2 * PAIR), inputs, 0)
    r_small.step_one()
    r_q.step_two()
    r_up.step_four()
    r_out.step_four()
    r_k.step_two()
    r_v.step_three()
    r_small.step_two()
    r_q.step_three()
    r_k.step_three()
    r_v.step_four()
    r_small.step_three()
    r_q.step_four()
    r_k.step_four()
    r_small.step_four()
    for piece in pieces:
        piece.close()
    halo_sent()
    group.finish()
    net.finish()


def back(
    ga, tokens, resid, f_qkv, vec_rows, lines, d_down, d_up, d_out, kept, shards, seq_size, reach
):
    q = kept[0]
    n_seq, length, width = q.shape
    pairs = width // PAIR
    units = n_seq * pairs
    own = units // seq_size
    line_size = seq_size // 2
    vmem, hbm = pl.BlockSpec(memory_space=pltpu.VMEM), pl.BlockSpec(memory_space=pltpu.HBM)
    shape = jax.ShapeDtypeStruct
    part = 2 * LAND // seq_size
    s_qkv, s_out, s_up, s_down = [shape(x.shape, F32) for x in shards]
    s_small = shape((s_qkv.shape[0], 2 * PAIR), F32)
    bufs = []
    for x in (s_down, s_up, s_out):
        bufs += scatter_scratch(x.shape[0], x.shape[1] // 2, BF, line_size)
    for _ in range(3):
        bufs += scatter_scratch(s_qkv.shape[0], width // 2, BF, line_size)
    bufs += scatter_scratch(s_qkv.shape[0], PAIR, F32, line_size)
    return pl.pallas_call(
        functools.partial(back_kernel, reach, 2 * reach + 1),
        out_shape=[shape(tokens.shape, BF), s_qkv, s_out, s_up, s_down, s_small],
        in_specs=[vmem] * 6 + [hbm] * 3 + [vmem] * 12,
        out_specs=[vmem] * 6,
        scratch_shapes=[
            pltpu.VMEM((n_seq * length, 3 * width), BF),
            pltpu.VMEM((2 * pairs, 8, PAIR), F32),
            pltpu.VMEM((pairs, 4 * length, length + 2 * reach), BF),
            pltpu.VMEM((width, n_seq * length), BF),
            pltpu.VMEM((3, width, width // 2), BF),
            pltpu.VMEM((width, PAIR), F32),
            pltpu.VMEM((n_seq, length + 2 * reach, width), BF),
            pltpu.VMEM((n_seq, LAND, width), BF),
            pltpu.VMEM((seq_size // 2, LAND, own * PAIR), BF),
            pltpu.VMEM((units, PAIR, length), BF),
            pltpu.VMEM((n_seq, LAND, width), BF),
            pltpu.VMEM((seq_size, 8, PAIR), F32),
            pltpu.VMEM((PAIR, PAIR), F32),
            pltpu.VMEM((n_seq, length, width), F32),
            pltpu.VMEM((n_seq, length, width), F32),
            pltpu.VMEM((n_seq, LAND, width), F32),
            pltpu.VMEM((seq_size // 2, 2, n_seq, part, width), BF),
            pltpu.VMEM((seq_size // 2, n_seq, part, width), BF),
            pltpu.VMEM((seq_size // 2, n_seq, part, width), BF),
            pltpu.VMEM((n_seq, LAND, own * PAIR), BF),
            pltpu.VMEM((n_seq, LAND, own * PAIR), BF),
            pltpu.VMEM((own, PAIR, PAIR), F32),
            pltpu.VMEM((own, PAIR, PAIR), F32),
            pltpu.VMEM((2 * pairs, length, 2 * PAIR), F32),
            pltpu.VMEM((LAND, own * PAIR), BF),
        ]
        + bufs
        + [
            pltpu.SemaphoreType.DMA((7, line_size + SCATTER_SEMS)),
            pltpu.SemaphoreType.DMA((7, line_size + SCATTER_SEMS)),
            pltpu.SemaphoreType.DMA((7,)),
            pltpu.SemaphoreType.DMA((6, seq_size)),
            pltpu.SemaphoreType.DMA((6, seq_size)),
        ],
        compiler_params=pltpu.CompilerParams(
            collective_id=1, has_side_effects=True, vmem_limit_bytes=60 * 1024 * 1024
        ),
        name="back",
    )(ga, tokens, resid, f_qkv, vec_rows, lines, d_down, d_up, d_out, *kept)


def kernels_fit(args):
    tokens, _, *matrices = args[:6]
    taps = args[7]
    seq_size = lax.axis_size("seq")
    n_seq, length, width = tokens.shape
    units = n_seq * width // PAIR
    own = units // seq_size
    return (
        lax.axis_size("rows") == 4
        and seq_size == 8
        and all(x.shape[0] % 24 == 0 and x.shape[1] % 256 == 0 for x in matrices)
        and width // taps.shape[0] == PAIR // 2
        and length == PAIR
        and taps.shape[1] == 33
        and taps.shape[0] <= matrices[0].shape[0]
        and units == own * seq_size
        and seq_size == 2 * n_seq
        and width == 2 * own * PAIR
        and 2 * own <= 8
        and (width // PAIR) % own == 0
        and units % PINV_ITERS == 0
        and LAND == 8 * seq_size
        and matrices[2].shape[1] == 4 * width
        and args[6].shape[0] == 12
    )


def with_kernels(
    tokens, cotangent, qkv_weight, out_weight, up_weight, down_weight, vectors, taps,
    qkv_first, qkv_second, out_first, out_second, up_first, up_second, down_first, down_second,
    vec_first, vec_second, tap_first, tap_second,
):
    seq_count, local_len, model_width = tokens.shape
    head_count, tap_count = taps.shape
    seq_size = lax.axis_size("seq")
    reach = tap_count // 2
    row_count = seq_count * local_len
    count = vectors.shape[0]
    matrices = (qkv_weight, out_weight, up_weight, down_weight)
    table = jnp.pad(vectors.T, ((0, 0), (0, 2 * PAIR - count)))
    lines = jnp.pad(taps, ((0, 0), (0, 2 * PAIR - tap_count)))
    flat_in = tokens.reshape(row_count, model_width)
    full_qkv, full_out, full_up, full_down, vec_float, *kept = front(
        tokens, matrices, table, lines, seq_size, reach
    )
    attn_low = kept.pop(2).reshape(row_count, model_width)
    queries, key_rows = kept[:2]
    layer_out, grad_resid_one, grad_attn, vec_rows, grad_down, grad_up, grad_out = feed(
        attn_low, flat_in, cotangent.reshape(row_count, model_width), vec_float,
        (full_out, full_up, full_down),
    )
    flipped = jnp.pad(taps[:, ::-1], ((0, 0), (0, 2 * PAIR - tap_count)))
    input_grad, summed_qkv, summed_out, summed_up, summed_down, small = back(
        grad_attn.reshape(tokens.shape), flat_in, grad_resid_one, full_qkv, vec_rows, flipped,
        grad_down, grad_up, grad_out,
        kept, matrices, seq_size, reach,
    )
    input_grad = input_grad.reshape(tokens.shape)
    summed_vec = small[:, :count].T
    summed_taps = small[:head_count, PAIR : PAIR + tap_count]
    new_qkv = adam_step(qkv_weight, qkv_first, qkv_second, summed_qkv, rate_matrix, decay_rate)
    new_out = adam_step(out_weight, out_first, out_second, summed_out, rate_output, decay_rate)
    new_up = adam_step(up_weight, up_first, up_second, summed_up, rate_matrix, decay_rate)
    new_down = adam_step(down_weight, down_first, down_second, summed_down, rate_matrix, decay_rate)
    new_vec = adam_step(vectors, vec_first, vec_second, summed_vec, rate_vector, 0.0)
    new_taps = adam_step(taps, tap_first, tap_second, summed_taps, rate_taps, 0.0)
    out_tokens = layer_out.reshape(tokens.shape)
    return (out_tokens, input_grad) + new_qkv + new_out + new_up + new_down + new_vec + new_taps


def on_device(*args):
    return with_kernels(*args) if kernels_fit(args) else with_collectives(*args)


def solution(mesh):
    return jax.shard_map(
        on_device,
        mesh=mesh,
        in_specs=(
            P("rows", "seq", None),
            P("rows", "seq", None),
            P(("rows", "seq"), None),
            P(("rows", "seq"), None),
            P(("rows", "seq"), None),
            P(("rows", "seq"), None),
            P(None, ("rows", "seq")),
            P(),
            P(("rows", "seq"), None),
            P(("rows", "seq"), None),
            P(("rows", "seq"), None),
            P(("rows", "seq"), None),
            P(("rows", "seq"), None),
            P(("rows", "seq"), None),
            P(("rows", "seq"), None),
            P(("rows", "seq"), None),
            P(None, ("rows", "seq")),
            P(None, ("rows", "seq")),
            P(),
            P(),
        ),
        out_specs=(
            P("rows", "seq", None),
            P("rows", "seq", None),
            P(("rows", "seq"), None),
            P(("rows", "seq"), None),
            P(("rows", "seq"), None),
            P(("rows", "seq"), None),
            P(("rows", "seq"), None),
            P(("rows", "seq"), None),
            P(("rows", "seq"), None),
            P(("rows", "seq"), None),
            P(("rows", "seq"), None),
            P(("rows", "seq"), None),
            P(("rows", "seq"), None),
            P(("rows", "seq"), None),
            P(None, ("rows", "seq")),
            P(None, ("rows", "seq")),
            P(None, ("rows", "seq")),
            P(),
            P(),
            P(),
        ),
        check_vma=False,
    )
```

```python
import functools

import jax
import jax.numpy as jnp
from jax import lax
from jax.experimental import pallas as pl
from jax.experimental.pallas import tpu as pltpu
from jax.sharding import PartitionSpec as P

LAND = 64
PINV_ITERS = 6


top_precision = lax.Precision.HIGHEST
norm_eps = 1e-05
beta_one = 0.9
beta_two = 0.999
corr_one = 1.0 - 0.9**10
corr_two = 1.0 - 0.999**10
adam_eps = 1e-08
decay_rate = 0.01
rate_matrix = 0.03
rate_output = 0.12
rate_vector = 0.3
rate_taps = 0.08


def with_halo(x, sides, width):
    for axis, dim in sides:
        size, length = (lax.axis_size(axis), x.shape[dim])
        up = [(i, (i + 1) % size) for i in range(size - 1)]
        down = [(j, i) for i, j in up]
        last = lax.slice_in_dim(x, length - width, length, axis=dim)
        initial = lax.slice_in_dim(x, 0, width, axis=dim)
        before = lax.ppermute(last, axis, up)
        after = lax.ppermute(initial, axis, down)
        x = jnp.concatenate([before, x, after], axis=dim)
    return x


def layer_norm(residual, gain_row, shift_row):
    center = residual - jnp.mean(residual, axis=-1, keepdims=True)
    spread = jnp.mean(center * center, axis=-1, keepdims=True)
    return center * lax.rsqrt(spread + norm_eps) * gain_row + shift_row


def normalized_rows(scores):
    expo = jnp.exp(scores - jnp.max(scores, axis=-1, keepdims=True))
    return expo / jnp.sum(expo, axis=-1, keepdims=True)


def softmax_back(probability, grad_in):
    return probability * (grad_in - jnp.sum(probability * grad_in, axis=-1, keepdims=True))


def gelu_exact(inputs):
    return jax.nn.gelu(inputs, approximate=False)


def pseudo_inverse(matrix):
    identity = jnp.eye(matrix.shape[-1], dtype=jnp.float32)
    approx = jnp.swapaxes(matrix, -1, -2) / jnp.sum(matrix * matrix, axis=(-2, -1), keepdims=True)
    for sweep_index in range(PINV_ITERS):
        product = jnp.matmul(matrix, approx, precision=top_precision)
        inner_term = 7.0 * identity - product
        inner_term = 15.0 * identity - jnp.matmul(product, inner_term, precision=top_precision)
        inner_term = 13.0 * identity - jnp.matmul(product, inner_term, precision=top_precision)
        approx = 0.25 * jnp.matmul(approx, inner_term, precision=top_precision)
    return approx


def adam_step(weight, first_moment, second, gradient, step_rate, decay_coef):
    new_first = beta_one * first_moment + (1.0 - beta_one) * gradient
    new_second = beta_two * second + (1.0 - beta_two) * gradient * gradient
    update = new_first / corr_one / (jnp.sqrt(new_second / corr_two) + adam_eps)
    return (new_first, new_second, weight - step_rate * (update + decay_coef * weight))


def with_collectives(
    tokens,
    cotangent,
    qkv_weight,
    out_weight,
    up_weight,
    down_weight,
    vectors,
    taps,
    qkv_first,
    qkv_second,
    out_first,
    out_second,
    up_first,
    up_second,
    down_first,
    down_second,
    vec_first,
    vec_second,
    tap_first,
    tap_second,
):
    seq_count, local_len, model_width = tokens.shape
    head_count, tap_count = taps.shape
    head_size = model_width // head_count
    hidden_width = up_weight.shape[1]
    land_local = LAND // lax.axis_size("seq")
    seg_len = local_len // land_local
    reach_width = tap_count // 2
    logit_scale_factor = head_size ** (-0.5)
    row_count = seq_count * local_len
    head_shape = (seq_count, local_len, head_count, head_size)
    land_shape = (seq_count, LAND, head_count, head_size)
    full_qkv, full_out, full_up, full_down, full_vec = (
        lax.all_gather(qkv_weight.astype(jnp.bfloat16), ("rows", "seq"), axis=0, tiled=True),
        lax.all_gather(out_weight.astype(jnp.bfloat16), ("rows", "seq"), axis=0, tiled=True),
        lax.all_gather(up_weight.astype(jnp.bfloat16), ("rows", "seq"), axis=0, tiled=True),
        lax.all_gather(down_weight.astype(jnp.bfloat16), ("rows", "seq"), axis=0, tiled=True),
        lax.all_gather(vectors.astype(jnp.bfloat16), ("rows", "seq"), axis=1, tiled=True),
    )
    vec_float = full_vec.astype(jnp.float32)
    flat_in = tokens.reshape(row_count, model_width)
    project = jnp.dot(flat_in, full_qkv, preferred_element_type=jnp.float32)
    queries = (project[:, :model_width] + vec_float[0]).astype(jnp.bfloat16)
    key_rows = project[:, model_width : 2 * model_width].astype(jnp.bfloat16)
    values = (project[:, 2 * model_width :] + vec_float[1]).astype(jnp.bfloat16)
    seg_shape = (seq_count, land_local, seg_len, model_width)
    own_q = jnp.mean(queries.reshape(seg_shape), axis=2, dtype=jnp.float32).astype(jnp.bfloat16)
    own_k = jnp.mean(key_rows.reshape(seg_shape), axis=2, dtype=jnp.float32).astype(jnp.bfloat16)
    land_q, land_k = (
        lax.all_gather(own_q, "seq", axis=1, tiled=True),
        lax.all_gather(own_k, "seq", axis=1, tiled=True),
    )
    query_heads = queries.reshape(head_shape)
    key_heads = key_rows.reshape(head_shape)
    value_heads = values.reshape(head_shape)
    landmark_query_heads = land_q.reshape(land_shape)
    landmark_key_heads = land_k.reshape(land_shape)
    lq_float = landmark_query_heads.astype(jnp.float32)
    lk_float = landmark_key_heads.astype(jnp.float32)
    score_one = (
        jnp.einsum(
            "sthd,slhd->shtl", query_heads, landmark_key_heads, preferred_element_type=jnp.float32
        )
        * logit_scale_factor
    )
    prob_one = normalized_rows(score_one)
    second_probability = normalized_rows(
        jnp.einsum("slhd,smhd->shlm", lq_float, lk_float, precision=top_precision)
        * logit_scale_factor
    )
    inverse_matrix, inverse_pull = jax.vjp(pseudo_inverse, second_probability)
    score_three = (
        jnp.einsum(
            "slhd,sthd->shlt", landmark_query_heads, key_heads, preferred_element_type=jnp.float32
        )
        * logit_scale_factor
    )
    row_max = lax.pmax(jnp.max(score_three, axis=-1), "seq")
    expo_three = jnp.exp(score_three - row_max[..., None])
    numer_local = jnp.einsum(
        "shlt,sthd->slhd",
        expo_three.astype(jnp.bfloat16),
        value_heads,
        preferred_element_type=jnp.float32,
    )
    numer, denom = (
        lax.psum(numer_local.astype(jnp.bfloat16), "seq").astype(jnp.float32),
        lax.psum(jnp.sum(expo_three, axis=-1).astype(jnp.bfloat16), "seq").astype(jnp.float32),
    )
    denom_swap = jnp.swapaxes(denom, 1, 2)[..., None]
    landmark_value_rows = numer / denom_swap
    mixing_kernel = jnp.einsum(
        "shlm,smhd->slhd", inverse_matrix, landmark_value_rows, precision=top_precision
    )
    mix_low = mixing_kernel.astype(jnp.bfloat16)
    prob_low = prob_one.astype(jnp.bfloat16)
    attend = jnp.einsum("shtl,slhd->sthd", prob_low, mix_low, preferred_element_type=jnp.float32)
    attend = attend.reshape(seq_count, local_len, model_width)
    tap_chan = jnp.repeat(taps, head_size, axis=0)
    padded_values = with_halo(
        values.reshape(seq_count, local_len, model_width), (("seq", 1),), reach_width
    )
    conv_out = jnp.zeros((seq_count, local_len, model_width), jnp.float32)
    for offset in range(tap_count):
        conv_out = conv_out + tap_chan[:, offset] * padded_values[
            :, offset : offset + local_len
        ].astype(jnp.float32)
    attn_low = (attend + conv_out).reshape(row_count, model_width).astype(jnp.bfloat16)
    branch = jnp.dot(attn_low, full_out, preferred_element_type=jnp.float32) + vec_float[2]
    resid_one = flat_in.astype(jnp.float32) + branch
    normed, norm_pull_one = jax.vjp(layer_norm, resid_one, vec_float[6], vec_float[3])
    normed_low = normed.astype(jnp.bfloat16)
    hidden_pre = jnp.dot(normed_low, full_up, preferred_element_type=jnp.float32) + vec_float[
        8:
    ].reshape(hidden_width)
    active, gelu_pull = jax.vjp(gelu_exact, hidden_pre)
    active_low = active.astype(jnp.bfloat16)
    ff_out = jnp.dot(active_low, full_down, preferred_element_type=jnp.float32) + vec_float[4]
    layer_out, norm_pull_two = jax.vjp(layer_norm, normed + ff_out, vec_float[7], vec_float[5])
    grad_resid_two, grad_gain_two, grad_shift_two = norm_pull_two(
        cotangent.reshape(row_count, model_width).astype(jnp.float32)
    )
    grad_ff = grad_resid_two.astype(jnp.bfloat16)
    grad_down = jnp.einsum("nf,nd->fd", active_low, grad_ff, preferred_element_type=jnp.float32)
    grad_active = jnp.einsum("nd,fd->nf", grad_ff, full_down, preferred_element_type=jnp.float32)
    grad_hidden = gelu_pull(grad_active)[0].astype(jnp.bfloat16)
    grad_up = jnp.einsum("nd,nf->df", normed_low, grad_hidden, preferred_element_type=jnp.float32)
    grad_normed = (
        jnp.einsum("nf,df->nd", grad_hidden, full_up, preferred_element_type=jnp.float32)
        + grad_resid_two
    )
    grad_resid_one, grad_gain_one, grad_shift_one = norm_pull_one(grad_normed)
    grad_branch = grad_resid_one.astype(jnp.bfloat16)
    grad_out = jnp.einsum("nd,ne->de", attn_low, grad_branch, preferred_element_type=jnp.float32)
    grad_attn = jnp.einsum(
        "ne,de->nd", grad_branch, full_out, preferred_element_type=jnp.float32
    ).astype(jnp.bfloat16)
    grad_attn_heads = grad_attn.reshape(head_shape)
    grad_prob_one = jnp.einsum(
        "sthd,slhd->shtl", grad_attn_heads, mix_low, preferred_element_type=jnp.float32
    )
    mixing_part = jnp.einsum(
        "shtl,sthd->slhd", prob_low, grad_attn_heads, preferred_element_type=jnp.float32
    )
    grad_mixing = lax.psum(mixing_part.astype(jnp.bfloat16), "seq").astype(jnp.float32)
    grad_score_one = softmax_back(prob_one, grad_prob_one).astype(jnp.bfloat16)
    query_local = (
        jnp.einsum(
            "shtl,slhd->sthd",
            grad_score_one,
            landmark_key_heads,
            preferred_element_type=jnp.float32,
        )
        * logit_scale_factor
    )
    land_k_part = (
        jnp.einsum(
            "shtl,sthd->slhd", grad_score_one, query_heads, preferred_element_type=jnp.float32
        )
        * logit_scale_factor
    )
    grad_pad = with_halo(
        grad_attn.reshape(seq_count, local_len, model_width), (("seq", 1),), reach_width
    )
    attn_float = grad_attn.reshape(seq_count, local_len, model_width).astype(jnp.float32)
    conv_back = jnp.zeros((seq_count, local_len, model_width), jnp.float32)
    tap_terms = []
    for offset in range(tap_count):
        start_row = 2 * reach_width - offset
        conv_back = conv_back + tap_chan[:, offset] * grad_pad[
            :, start_row : start_row + local_len
        ].astype(jnp.float32)
        tap_terms.append(
            jnp.sum(
                attn_float * padded_values[:, offset : offset + local_len].astype(jnp.float32),
                axis=(0, 1),
            )
        )
    grad_taps = jnp.sum(
        jnp.stack(tap_terms, axis=1).reshape(head_count, head_size, tap_count), axis=1
    )
    grad_inverse = jnp.einsum(
        "slhd,smhd->shlm", grad_mixing, landmark_value_rows, precision=top_precision
    )
    grad_land_values = jnp.einsum(
        "shlm,slhd->smhd", inverse_matrix, grad_mixing, precision=top_precision
    )
    land_grad_low = grad_land_values.astype(jnp.bfloat16).astype(jnp.float32)
    grad_prob_two = inverse_pull(grad_inverse)[0]
    grad_score_two = softmax_back(second_probability, grad_prob_two)
    query_two = (
        jnp.einsum("shlm,smhd->slhd", grad_score_two, lk_float, precision=top_precision)
        * logit_scale_factor
    )
    key_two = (
        jnp.einsum("shlm,slhd->smhd", grad_score_two, lq_float, precision=top_precision)
        * logit_scale_factor
    )
    grad_numer = land_grad_low / denom_swap
    expo_low = expo_three.astype(jnp.bfloat16).astype(jnp.float32)
    value_three = jnp.einsum("shlt,slhd->sthd", expo_low, grad_numer, precision=top_precision)
    grad_expo = jnp.einsum(
        "slhd,sthd->shlt", grad_numer, value_heads.astype(jnp.float32), precision=top_precision
    )
    grad_denom = jnp.swapaxes(jnp.sum(land_grad_low * landmark_value_rows, axis=-1), 1, 2) / denom
    grad_score_three = (expo_three * (grad_expo - grad_denom[..., None])).astype(jnp.bfloat16)
    land_q_part = (
        jnp.einsum(
            "shlt,sthd->slhd", grad_score_three, key_heads, preferred_element_type=jnp.float32
        )
        * logit_scale_factor
    )
    key_local = (
        jnp.einsum(
            "shlt,slhd->sthd",
            grad_score_three,
            landmark_query_heads,
            preferred_element_type=jnp.float32,
        )
        * logit_scale_factor
    )
    land_q_own, land_k_own = (
        lax.psum_scatter(
            land_q_part.astype(jnp.bfloat16), "seq", scatter_dimension=1, tiled=True
        ).astype(jnp.float32),
        lax.psum_scatter(
            land_k_part.astype(jnp.bfloat16), "seq", scatter_dimension=1, tiled=True
        ).astype(jnp.float32),
    )
    first_land = lax.axis_index("seq") * land_local
    land_q_own = land_q_own + lax.dynamic_slice_in_dim(query_two, first_land, land_local, 1)
    land_k_own = land_k_own + lax.dynamic_slice_in_dim(key_two, first_land, land_local, 1)
    spread_shape = (seq_count, land_local, seg_len, head_count, head_size)
    spread_q = jnp.broadcast_to((land_q_own / seg_len)[:, :, None], spread_shape).reshape(
        head_shape
    )
    spread_k = jnp.broadcast_to((land_k_own / seg_len)[:, :, None], spread_shape).reshape(
        head_shape
    )
    grad_query = (query_local + spread_q).reshape(row_count, model_width)
    grad_key = (key_local + spread_k).reshape(row_count, model_width)
    grad_value = value_three.reshape(row_count, model_width) + conv_back.reshape(
        row_count, model_width
    )
    grad_proj = jnp.concatenate([grad_query, grad_key, grad_value], axis=1).astype(jnp.bfloat16)
    grad_qkv = jnp.einsum("nd,ne->de", flat_in, grad_proj, preferred_element_type=jnp.float32)
    input_grad = (
        jnp.einsum("ne,de->nd", grad_proj, full_qkv, preferred_element_type=jnp.float32)
        + grad_resid_one
    )
    input_grad = input_grad.astype(jnp.bfloat16).reshape(tokens.shape)
    bias_sums = jnp.sum(grad_proj.astype(jnp.float32), axis=0)
    grad_vec = jnp.concatenate(
        [
            bias_sums[None, :model_width],
            bias_sums[None, 2 * model_width :],
            jnp.sum(grad_branch.astype(jnp.float32), axis=0)[None],
            grad_shift_one[None],
            jnp.sum(grad_ff.astype(jnp.float32), axis=0)[None],
            grad_shift_two[None],
            grad_gain_one[None],
            grad_gain_two[None],
            jnp.sum(grad_hidden.astype(jnp.float32), axis=0).reshape(-1, model_width),
        ],
        axis=0,
    )
    summed_qkv, summed_out, summed_up, summed_down, summed_vec = (
        lax.psum_scatter(grad_qkv, ("rows", "seq"), scatter_dimension=0, tiled=True),
        lax.psum_scatter(grad_out, ("rows", "seq"), scatter_dimension=0, tiled=True),
        lax.psum_scatter(grad_up, ("rows", "seq"), scatter_dimension=0, tiled=True),
        lax.psum_scatter(grad_down, ("rows", "seq"), scatter_dimension=0, tiled=True),
        lax.psum_scatter(grad_vec, ("rows", "seq"), scatter_dimension=1, tiled=True),
    )
    summed_taps = lax.psum(grad_taps, ("rows", "seq"))
    new_qkv = adam_step(qkv_weight, qkv_first, qkv_second, summed_qkv, rate_matrix, decay_rate)
    new_out = adam_step(out_weight, out_first, out_second, summed_out, rate_output, decay_rate)
    new_up = adam_step(up_weight, up_first, up_second, summed_up, rate_matrix, decay_rate)
    new_down = adam_step(down_weight, down_first, down_second, summed_down, rate_matrix, decay_rate)
    new_vec = adam_step(vectors, vec_first, vec_second, summed_vec, rate_vector, 0.0)
    new_taps = adam_step(taps, tap_first, tap_second, summed_taps, rate_taps, 0.0)
    out_tokens = layer_out.astype(jnp.bfloat16).reshape(tokens.shape)
    return (out_tokens, input_grad) + new_qkv + new_out + new_up + new_down + new_vec + new_taps


BF = jnp.bfloat16
F32 = jnp.float32
MESH = pl.DeviceIdType.MESH


def remote(src, dst, send_sem, recv_sem, device):
    return pltpu.make_async_remote_copy(
        src_ref=src, dst_ref=dst, send_sem=send_sem, recv_sem=recv_sem,
        device_id=device, device_id_type=MESH,
    )


def place():
    row, spot = lax.axis_index("rows"), lax.axis_index("seq")
    line, core = spot // 2, spot % 2
    flip_one = row + 1 - 2 * (row % 2)
    flip_two = row + 2 - 4 * (row // 2)
    first = (1 - core) * flip_one + core * flip_two
    second = (1 - core) * flip_two + core * flip_one
    return row, line, core, first, second, 3 - row


def greet(devices):
    barrier = pltpu.get_barrier_semaphore()
    for device in devices:
        pl.semaphore_signal(barrier, inc=1, device_id=device, device_id_type=MESH)
    pl.semaphore_wait(barrier, len(devices))


class Net:
    def __init__(self, send, recv):
        self.send, self.recv, self.started = send, recv, []
        self.row, self.line, self.core, self.first, self.second, self.across = place()
        self.line_size = lax.axis_size("seq") // 2
        own_spot = 2 * self.line + self.core
        self.sibling = (self.row, 2 * self.line + 1 - self.core)
        self.peers = [
            (self.row, 2 * ((self.line + k) % self.line_size) + self.core)
            for k in range(1, self.line_size)
        ]
        self.to_first, self.to_second = (self.first, own_spot), (self.second, own_spot)

    def go(self, w, k, src, dst, device):
        copy = remote(src, dst, self.send.at[w, k], self.recv.at[w, k], device)
        copy.start()
        self.started.append(copy)
        return copy

    def finish(self):
        for copy in self.started:
            copy.wait_send()


def columns(base, which, half):
    return pl.ds(pl.multiple_of(base + which * half, 128), half)


class Gather:
    def __init__(self, net, w, src, dst, base, half, asm, stage, local):
        self.net, self.w, self.dst, self.stage, self.asm = net, w, dst, stage, asm
        self.rows, self.base, self.half, self.local = src.shape[0], base, half, local
        part = pl.ds(pl.multiple_of(net.core * self.rows, 8), self.rows)
        there = columns(base, 1 - net.core, half)
        self.asm_copy = net.go(w, 0, src.at[:, there], asm.at[part, :], net.sibling)
        asm[part, :] = src[:, columns(base, net.core, half)]

    def block(self, start, size):
        at = pl.ds(pl.multiple_of(start, 16), size)
        return self.dst.at[at, columns(self.base, self.net.core, self.half)]

    def slab(self, index):
        size = 2 * self.rows * self.net.line_size
        return self.block(index * size, size)

    def spread(self):
        net = self.net
        self.asm_copy.wait_recv()
        self.stage[...] = self.asm[...].astype(BF)
        size = 2 * self.rows
        block = self.block((net.row * net.line_size + net.line) * size, size)
        self.z = [net.go(self.w, 1 + k, self.stage, block, d) for k, d in enumerate(net.peers)]
        self.own = pltpu.make_async_copy(self.stage, block, self.local)
        self.own.start()

    def step_one(self):
        net, w, z0 = self.net, self.w, self.net.line_size
        self.own.wait()
        for copy in self.z:
            copy.wait_recv()
        mine = self.slab(net.row)
        self.hop = [net.go(w, z0, mine, mine, net.to_first)]
        self.hop.append(net.go(w, z0 + 1, mine, mine, net.to_second))
        self.sib = [net.go(w, z0 + 3, mine, mine, net.sibling)]

    def step_two(self):
        net, w, z0 = self.net, self.w, self.net.line_size
        self.hop[0].wait_recv()
        got = self.slab(net.first)
        self.hop.append(net.go(w, z0 + 2, got, got, net.to_second))
        self.sib.append(net.go(w, z0 + 4, got, got, net.sibling))

    def step_three(self):
        net, w, z0 = self.net, self.w, self.net.line_size
        self.hop[1].wait_recv()
        got = self.slab(net.second)
        self.sib.append(net.go(w, z0 + 5, got, got, net.sibling))
        self.hop[2].wait_recv()
        got = self.slab(net.across)
        self.sib.append(net.go(w, z0 + 6, got, got, net.sibling))

    def close(self):
        for copy in self.sib:
            copy.wait_recv()


GATHER_SEMS = 7


class Scatter:
    def __init__(self, net, w, out, base, half, bufs):
        self.net, self.w, self.out, self.base, self.half = net, w, out, base, half
        self.acc, self.buf0, self.buf1, self.buf2, self.buf3, self.fin = bufs
        self.rows = out.shape[0]
        self.size = 2 * self.rows * net.line_size

    def open(self, outbox, own=None):
        self.sib = self.net.go(self.w, 0, outbox, self.buf0, self.net.sibling)
        self.own = own
        if own is not None:
            own.start()

    def slab(self, index):
        return pl.ds(pl.multiple_of(index * self.size, self.size), self.size)

    def add(self, index, other, start):
        step = 48
        acc = self.acc

        def one(i, carry):
            at = pl.ds(pl.multiple_of(index * self.size + i * step, 16), step)
            there = pl.ds(pl.multiple_of(start + i * step, 16), step)
            acc[at, :] = acc[at, :] + other[there, :]
            return carry

        lax.fori_loop(0, self.size // step, one, 0)

    def step_one(self):
        net, w = self.net, self.w
        if self.own is not None:
            self.own.wait()
        self.sib.wait_recv()
        self.add(net.across, self.buf0, net.across * self.size)
        acc = self.acc
        self.one = net.go(w, 1, acc.at[self.slab(net.across), :], self.buf1.at[0], net.to_second)
        self.add(net.second, self.buf0, net.second * self.size)
        self.two = net.go(w, 2, acc.at[self.slab(net.second), :], self.buf1.at[1], net.to_second)
        self.add(net.first, self.buf0, net.first * self.size)
        self.add(net.row, self.buf0, net.row * self.size)

    def step_two(self):
        net = self.net
        self.one.wait_recv()
        self.add(net.first, self.buf1.at[0], 0)
        src = self.acc.at[self.slab(net.first), :]
        self.three = net.go(self.w, 3, src, self.buf2, net.to_first)
        self.two.wait_recv()
        self.add(net.row, self.buf1.at[1], 0)

    def step_three(self):
        net = self.net
        self.three.wait_recv()
        self.add(net.row, self.buf2, 0)
        block, n = 2 * self.rows, net.line_size
        self.z = []

        def at(line):
            return pl.ds(pl.multiple_of((net.row * n + line) * block, block), block)

        for k, device in enumerate(net.peers):
            src = self.acc.at[at((net.line + 1 + k) % n), :]
            self.z.append(net.go(self.w, 4 + k, src, self.buf3.at[net.line], device))
        self.buf3[net.line] = self.acc[at(net.line), :]

    def step_four(self):
        net = self.net
        for copy in self.z:
            copy.wait_recv()
        total = self.buf3[0].astype(F32)
        for k in range(1, net.line_size):
            total = total + self.buf3[k].astype(F32)
        self.fin[...] = total
        part = pl.ds(pl.multiple_of((1 - net.core) * self.rows, 8), self.rows)
        here = columns(self.base, net.core, self.half)
        self.last = net.go(
            self.w, 3 + net.line_size, self.fin.at[part, :], self.out.at[:, here], net.sibling
        )
        part = pl.ds(pl.multiple_of(net.core * self.rows, 8), self.rows)
        self.out[:, here] = self.fin[part, :]

    def close(self):
        self.last.wait_recv()


SCATTER_SEMS = 4


def scatter_scratch(rows, half, dtype, line_size):
    quarter = 2 * rows * line_size
    return [
        pltpu.VMEM((4 * quarter, half), dtype),
        pltpu.VMEM((4 * quarter, half), dtype),
        pltpu.VMEM((2, quarter, half), dtype),
        pltpu.VMEM((quarter, half), dtype),
        pltpu.VMEM((line_size, 2 * rows, half), dtype),
        pltpu.VMEM((2 * rows, half), F32),
    ]


PAIR = 128


def nn(a, b):
    return jnp.dot(a, b, preferred_element_type=F32)


def nt(a, b):
    return lax.dot_general(a, b, (((1,), (1,)), ((), ())), preferred_element_type=F32)


def tn(a, b):
    return lax.dot_general(a, b, (((0,), (0,)), ((), ())), preferred_element_type=F32)


def split(x):
    high = x.astype(BF)
    return high, (x - high.astype(F32)).astype(BF)


def three(dot, a, b):
    return dot(a[0], b[0]) + (dot(a[0], b[1]) + dot(a[1], b[0]))


def lane_masks(dtype):
    lane = lax.broadcasted_iota(jnp.int32, (1, PAIR), 1)
    one = (lane < PAIR // 2).astype(F32)
    return one.astype(dtype), (1.0 - one).astype(dtype)


def apart(x):
    one, two = lane_masks(x.dtype)
    return jnp.concatenate([x * one, x * two], axis=0)


def together(x):
    half = PAIR // 2
    lane = lax.broadcasted_iota(jnp.int32, (half, PAIR), 1)
    return jnp.where(lane < half, x[:half], x[half:])


def same_head():
    half = PAIR // 2
    a = lax.broadcasted_iota(jnp.int32, (PAIR, PAIR), 0) // half
    b = lax.broadcasted_iota(jnp.int32, (PAIR, PAIR), 1) // half
    return a == b


def eye():
    a = lax.broadcasted_iota(jnp.int32, (PAIR, PAIR), 0)
    b = lax.broadcasted_iota(jnp.int32, (PAIR, PAIR), 1)
    return (a == b).astype(F32)


def by_head(x, reduce):
    half, width = PAIR // 2, x.shape[1]
    parts = [reduce(x[h * half : (h + 1) * half], axis=0, keepdims=True) for h in (0, 1)]
    return jnp.concatenate([jnp.broadcast_to(y, (half, width)) for y in parts], axis=0)


def lanes(p):
    if isinstance(p, int):
        return pl.ds(p * PAIR, PAIR)
    return pl.ds(pl.multiple_of(p * PAIR, PAIR), PAIR)


def conv_pair(table, padded):
    size = table.shape[0] // 4
    out = nn(table, padded)
    lane = lax.broadcasted_iota(jnp.int32, (size, PAIR), 1)
    return jnp.where(
        lane < PAIR // 2,
        out[:size] + out[2 * size : 3 * size],
        out[size : 2 * size] + out[3 * size :],
    )


class Group:
    def __init__(self, send, recv):
        self.row, self.me = lax.axis_index("rows"), lax.axis_index("seq")
        self.size = lax.axis_size("seq")
        self.send, self.recv, self.started = send, recv, []

    def peers(self):
        return [(self.row, (self.me + k) % self.size) for k in range(1, self.size)]

    def push(self, channel, pick_src, dst):
        copies = []
        for k, device in enumerate(self.peers()):
            copy = remote(
                pick_src(device[1]), dst, self.send.at[channel, k], self.recv.at[channel, k], device
            )
            copy.start()
            copies.append(copy)
        self.started += copies
        return copies

    def line_peers(self):
        n, line, core = self.size // 2, self.me // 2, self.me % 2
        return [(self.row, 2 * ((line + k) % n) + core) for k in range(1, n)]

    def go(self, channel, k, src, dst, device):
        copy = remote(src, dst, self.send.at[channel, k], self.recv.at[channel, k], device)
        copy.start()
        self.started.append(copy)
        return copy

    def share(self, parts):
        n, line, core = self.size // 2, self.me // 2, self.me % 2
        sibling = (self.row, 2 * line + 1 - core)
        there, here = [], []
        for channel, block in parts:
            mine = block(self.me)
            there.append(
                [self.go(channel, k, mine, mine, d) for k, d in enumerate(self.line_peers())]
            )
        for channel, block in parts:
            here.append(self.go(channel, n - 1, block(self.me), block(self.me), sibling))

        def arrive():
            for k in range(1, n):
                source = 2 * ((line - k + n) % n) + core
                for (channel, block), copies in zip(parts, there):
                    copies[k - 1].wait_recv()
                    got = block(source)
                    here.append(self.go(channel, n - 1 + k, got, got, sibling))
            for copy in here:
                copy.wait_recv()

        return arrive

    def halo(self, channel, source, padded, reach):
        length = source.shape[1]
        copies = []
        for which, (src_at, dst_at, step) in enumerate(
            ((length - reach, 0, 1), (0, length + reach, -1))
        ):
            there = (self.me + step + self.size) % self.size
            copy = remote(
                source.at[:, pl.ds(src_at, reach), :],
                padded.at[:, pl.ds(dst_at, reach), :],
                self.send.at[channel, which],
                self.recv.at[channel, which],
                (self.row, there),
            )
            goes = self.me < self.size - 1 if step == 1 else self.me > 0
            comes = self.me > 0 if step == 1 else self.me < self.size - 1
            pl.when(goes)(copy.start)
            copies.append((copy, goes, comes, dst_at))

        def arrive():
            for copy, goes, comes, dst_at in copies:
                pl.when(comes)(copy.wait_recv)

                @pl.when(jnp.logical_not(comes))
                def _():
                    shape = (padded.shape[0], reach, padded.shape[2])
                    padded[:, pl.ds(dst_at, reach), :] = jnp.zeros(shape, padded.dtype)

        def sent():
            for copy, goes, _, _ in copies:
                pl.when(goes)(copy.wait_send)

        return arrive, sent

    def finish(self):
        for copy in self.started:
            copy.wait_send()


def pinv_start(prob):
    total = by_head(jnp.sum(prob * prob, axis=1, keepdims=True), jnp.sum)
    return prob.T / total


def pinv_terms(p, z, unit):
    product = three(nn, p, z)
    prod = split(product)
    term_one = 7.0 * unit - product
    term_two = 15.0 * unit - three(nn, prod, split(term_one))
    term_three = 13.0 * unit - three(nn, prod, split(term_two))
    return prod, term_one, term_two, term_three


def band(line, length, reach):
    wide = jnp.broadcast_to(line, (length, line.shape[1]))
    return pltpu.roll(wide, 0, 1, stride=1, stride_axis=0)[:, : length + 2 * reach]


def fill_bands(lines, table, reach):
    pairs, rows = table.shape[0], table.shape[1] // 4
    for p in range(pairs):
        for h in (0, 1):
            high, low = split(band(lines[2 * p + h : 2 * p + h + 1, :], rows, reach))
            table[p, h * rows : (h + 1) * rows, :] = high
            table[p, (2 + h) * rows : (3 + h) * rows, :] = low


def front_kernel(
    reach,
    tokens, qkv_w, out_w, up_w, down_w, vec_w, lines,
    f_qkv, f_out, f_up, f_down, f_rows,
    q, k, attn, vpad, landq, landk, mix, p1, e, wt, p2o, zo, lvo,
    v, table, f_vec, lb, numer, nrecv, stat, srecv, mstat, conv, fcol, *rest,
):
    asm, stage = rest[:7], rest[7:14]
    g_send, g_recv, g_local, send, recv = rest[14:]
    net, group = Net(g_send, g_recv), Group(send, recv)
    me, size = group.me, group.size
    n_seq, length, width = q.shape
    pairs = width // PAIR
    own = n_seq * pairs // size
    each = own * PAIR
    land_local = LAND // size
    seg = length // land_local
    scale = (PAIR // 2) ** -0.5
    greet(group.peers() + [net.to_first, net.to_second])

    def owner_seq(d):
        return d * own // pairs

    def owner_lanes(d):
        return pl.ds(pl.multiple_of((d * own % pairs) * PAIR, PAIR), each)

    plan = [(vec_w, f_vec, 0), (qkv_w, f_qkv, width), (qkv_w, f_qkv, 0), (qkv_w, f_qkv, 2 * width)]
    plan += [(out_w, f_out, 0), (up_w, f_up, 0), (down_w, f_down, 0)]
    pieces = []
    for w, (src, dst, base) in enumerate(plan):
        half = asm[w].shape[1]
        pieces.append(Gather(net, w, src, dst, base, half, asm[w], stage[w], g_local.at[w]))
    g_vec, g_k, g_q, g_v, g_out, g_up, g_down = pieces
    for piece in pieces[:4]:
        piece.spread()
    g_out.spread()
    g_up.spread()
    fill_bands(lines, table, reach)

    def project(dst, base, bias):
        step = 2 * PAIR
        for at in range(0, width, step):
            x = nn(tokens[...], f_qkv[:, base + at : base + at + step])
            if bias is not None:
                x = x + f_rows[bias : bias + 1, at : at + step]
            dst[:, :, at : at + step] = x.astype(BF).reshape(n_seq, length, step)

    g_vec.step_one()
    g_k.step_one()
    g_q.step_one()
    g_vec.step_two()
    g_k.step_two()
    g_v.step_one()
    g_down.spread()
    g_vec.step_three()
    g_q.step_two()
    g_k.step_three()
    g_vec.close()
    f_rows[...] = f_vec[:, :PAIR].astype(F32).T[: f_rows.shape[0]]
    g_v.step_two()
    g_k.close()
    project(k, width, None)
    g_q.step_three()
    g_q.close()
    project(q, 0, 0)
    g_v.step_three()
    g_out.step_one()
    g_up.step_one()
    g_v.close()
    project(v, 2 * width, 1)

    def own_landmarks(s, carry):
        both = [
            jnp.mean(x[s].astype(F32).reshape(land_local, seg, width), axis=1) for x in (q, k)
        ]
        lb[me, s] = jnp.concatenate(both, axis=0).astype(BF)
        vpad[s, pl.ds(reach, length), :] = v[s]
        return carry

    lax.fori_loop(0, n_seq, own_landmarks, 0)
    landed = group.share([(1, lambda d: lb.at[d])])
    halo_in, halo_sent = group.halo(0, v, vpad, reach)
    g_out.step_two()
    g_down.step_one()
    landed()

    def whole_landmarks(s, carry):
        x = lb[:, s].astype(F32)
        landq[s] = x[:, :land_local].reshape(LAND, width).astype(BF)
        landk[s] = x[:, land_local:].reshape(LAND, width).astype(BF)
        return carry

    lax.fori_loop(0, n_seq, whole_landmarks, 0)
    lane_at = lax.broadcasted_iota(jnp.int32, (PAIR, PAIR), 1)

    def over_tokens(s, tile):
        for p in range(pairs):
            score = nt(apart(landq[s, :, lanes(p)]), k[s, :, lanes(p)]) * scale
            top = jnp.max(score, axis=1, keepdims=True)
            expo = jnp.exp(score - top)
            low = expo.astype(BF)
            e[s * pairs + p] = low
            numer[s, :, lanes(p)] = together(nn(low, v[s, :, lanes(p)])).astype(BF)
            unit = s * pairs + p
            at = (unit // own) * 8 + unit % own
            tile = jnp.where(lane_at == at, top, tile)
            tile = jnp.where(lane_at == at + own, jnp.sum(expo, axis=1, keepdims=True), tile)
        return tile

    tile = lax.fori_loop(0, n_seq, over_tokens, jnp.zeros((PAIR, PAIR), F32))
    stat[...] = tile.T[: 8 * size].reshape(size, 8, PAIR)
    sums_in = group.push(
        2, lambda d: numer.at[owner_seq(d), :, owner_lanes(d)], nrecv.at[me]
    )
    stats_in = group.push(3, lambda d: stat.at[d], srecv.at[me])
    g_up.step_two()
    nrecv[me] = numer[owner_seq(me), :, owner_lanes(me)]
    srecv[me] = stat[me]

    block, unit_matrix = same_head(), eye()
    my_seq, my_pair = owner_seq(me), (me * own) % pairs
    for i in range(own):
        at = lanes(my_pair + i)
        score = nt(apart(landq[my_seq, :, at]), apart(landk[my_seq, :, at])) * scale
        score = jnp.where(block, score, -1e30)
        expo = jnp.exp(score - jnp.max(score, axis=1, keepdims=True))
        prob = expo / jnp.sum(expo, axis=1, keepdims=True)
        p2o[i] = prob
        zo[0, i] = pinv_start(prob)

    halo_in()
    per_step = n_seq * pairs // PINV_ITERS

    def over_landmarks(unit):
        s, p = unit // pairs, unit % pairs
        score = nt(apart(landk[s, :, lanes(p)]), q[s, :, lanes(p)]) * scale
        expo = jnp.exp(score - by_head(score, jnp.max))
        p1[unit] = expo / by_head(expo, jnp.sum)
        conv[s, :, lanes(p)] = conv_pair(table[p], vpad[s, :, lanes(p)])

    def pinv_step(step, carry):
        for i in range(own):
            z = split(zo[step, i])
            _, _, _, inner = pinv_terms(split(p2o[i]), z, unit_matrix)
            zo[step + 1, i] = 0.25 * three(nn, z, split(inner))
        for j in range(per_step):
            over_landmarks(step * per_step + j)
        return carry

    lax.fori_loop(0, PINV_ITERS // 2, pinv_step, 0)
    g_out.step_three()
    g_down.step_two()
    lax.fori_loop(PINV_ITERS // 2, PINV_ITERS, pinv_step, 0)

    for copy in sums_in + stats_in:
        copy.wait_recv()
    got = srecv[...]
    tops = got[:, :own]
    top = jnp.max(tops, axis=0, keepdims=True)
    factor = jnp.exp(tops - top)
    total = jnp.sum(factor * got[:, own : 2 * own], axis=0, keepdims=True)
    factor = factor / total
    spare = jnp.zeros((1, 8 - 2 * own, PAIR), F32)
    mstat[me] = jnp.concatenate([top, total, spare], axis=1)[0]
    spread = jnp.concatenate([factor, jnp.zeros((size, 8 - own, PAIR), F32)], axis=1)
    spread = spread.reshape(8 * size, PAIR)
    fcol[...] = jnp.concatenate([spread, jnp.zeros((PAIR - 8 * size, PAIR), F32)], axis=0).T
    half = PAIR // 2
    narrow = lax.broadcasted_iota(jnp.int32, (half, PAIR), 1) < half
    for i in range(own):
        at = pl.ds(i * PAIR, PAIR)
        mean = jnp.zeros((half, PAIR), F32)
        for src in range(size):
            column = fcol[:, src * 8 + i : src * 8 + i + 1]
            weight = jnp.where(narrow, column[:half], column[half:])
            mean = mean + weight * nrecv[src, :, at].astype(F32)
        lvo[:, at] = mean
        mixed = together(three(nn, split(zo[PINV_ITERS, i]), split(apart(mean))))
        mix[my_seq, :, lanes(my_pair + i)] = mixed.astype(BF)
    mixed_in = group.share(
        [
            (4, lambda d: mix.at[owner_seq(d), :, owner_lanes(d)]),
            (5, lambda d: mstat.at[d]),
        ]
    )
    g_up.step_three()
    mixed_in()

    rows = jnp.concatenate(
        [mstat[...].reshape(8 * size, PAIR), jnp.zeros((PAIR - 8 * size, PAIR), F32)], axis=0
    )
    rows = rows.T
    valid = (lane_at % 8 < own) & (lane_at < 8 * size)
    shift = jnp.where(valid, tile - rows, 0.0)
    den = jnp.where(valid, pltpu.roll(rows, PAIR - own, 1), 1.0)
    wt[...] = jnp.exp(shift) / den

    def result(s, carry):
        for p in range(pairs):
            low = p1[s * pairs + p].astype(BF)
            out = tn(low, apart(mix[s, :, lanes(p)])) + conv[s, :, lanes(p)]
            attn[s, :, lanes(p)] = out.astype(BF)
        return carry

    lax.fori_loop(0, n_seq, result, 0)
    g_down.step_three()
    for piece in (g_out, g_up, g_down):
        piece.close()
    halo_sent()
    group.finish()
    net.finish()


def front(tokens, matrices, table, lines, seq_size, reach):
    n_seq, length, width = tokens.shape
    pairs = width // PAIR
    units = n_seq * pairs
    own = units // seq_size
    n_dev = 4 * seq_size
    line_size = seq_size // 2
    vmem, hbm = pl.BlockSpec(memory_space=pltpu.VMEM), pl.BlockSpec(memory_space=pltpu.HBM)
    shape = jax.ShapeDtypeStruct
    land = shape((n_seq, LAND, width), BF)
    qkv_w, out_w, up_w, down_w = matrices
    whole = [shape((n_dev * x.shape[0], x.shape[1]), BF) for x in matrices]
    asm = [(table.shape[0], table.shape[1] // 2)] + [(qkv_w.shape[0], width // 2)] * 3
    asm += [(x.shape[0], x.shape[1] // 2) for x in (out_w, up_w, down_w)]
    n_sem = line_size + GATHER_SEMS
    return pl.pallas_call(
        functools.partial(front_kernel, reach),
        out_shape=whole
        + [
            shape((16, width), F32),
            shape(tokens.shape, BF), shape(tokens.shape, BF), shape(tokens.shape, BF),
            shape((n_seq, length + 2 * reach, width), BF), land, land, land,
            shape((units, PAIR, length), F32), shape((units, PAIR, length), BF),
            shape((PAIR, PAIR), F32), shape((own, PAIR, PAIR), F32),
            shape((PINV_ITERS + 1, own, PAIR, PAIR), F32), shape((LAND, own * PAIR), F32),
        ],
        in_specs=[vmem] * 7,
        out_specs=[vmem, hbm, hbm, hbm] + [vmem] * 14,
        scratch_shapes=[
            pltpu.VMEM(tokens.shape, BF),
            pltpu.VMEM((pairs, 4 * length, length + 2 * reach), BF),
            pltpu.VMEM((n_dev * table.shape[0], table.shape[1]), BF),
            pltpu.VMEM((seq_size, n_seq, 2 * LAND // seq_size, width), BF),
            pltpu.VMEM((n_seq, LAND, width), BF),
            pltpu.VMEM((seq_size, LAND, own * PAIR), BF),
            pltpu.VMEM((seq_size, 8, PAIR), F32),
            pltpu.VMEM((seq_size, 8, PAIR), F32),
            pltpu.VMEM((seq_size, 8, PAIR), F32),
            pltpu.VMEM((n_seq, length, width), F32),
            pltpu.VMEM((PAIR, PAIR), F32),
        ]
        + [pltpu.VMEM((2 * r, h), F32) for r, h in asm]
        + [pltpu.VMEM((2 * r, h), BF) for r, h in asm]
        + [
            pltpu.SemaphoreType.DMA((7, n_sem)),
            pltpu.SemaphoreType.DMA((7, n_sem)),
            pltpu.SemaphoreType.DMA((7,)),
            pltpu.SemaphoreType.DMA((6, seq_size)),
            pltpu.SemaphoreType.DMA((6, seq_size)),
        ],
        compiler_params=pltpu.CompilerParams(
            collective_id=0, has_side_effects=True, vmem_limit_bytes=56 * 1024 * 1024
        ),
        name="front",
    )(tokens.reshape(n_seq * length, width), *matrices, table, lines)


def gelu_parts(x):
    expo = jnp.exp(-0.5 * x * x)
    t = 1.0 / (1.0 + (0.3275911 * 0.7071067811865476) * jnp.abs(x))
    tail = -0.284496736 + t * (1.421413741 + t * (-1.453152027 + t * 1.061405429))
    tail = 0.5 * expo * t * (0.254829592 + t * tail)
    below = jnp.where(x >= 0.0, 1.0 - tail, tail)
    return x * below, below + x * expo * 0.3989422804014327


def norm_parts(resid):
    center = resid - jnp.mean(resid, axis=-1, keepdims=True)
    scale = lax.rsqrt(jnp.mean(center * center, axis=-1, keepdims=True) + norm_eps)
    return center * scale, scale


def norm_back(grad, gain, unit, scale):
    inner = grad * gain
    mean = jnp.mean(inner, axis=-1, keepdims=True)
    along = jnp.mean(inner * unit, axis=-1, keepdims=True)
    return scale * (inner - mean - unit * along)


def row_sum(x):
    return jnp.sum(x, axis=0, keepdims=True)


def feed_kernel(
    attn, tokens, cot, rows, h_out, h_up, h_down,
    layer_out, grad_one, ga, sums, d_down, d_up, d_out,
    w_out, w_up, w_down, g_down, g_up, g_out, active, slope, unit_one, scale_one, normed, low, low_t,
    total, grad_two, ff, attn_t, w_sem, o_sem,
):
    count, width = attn.shape
    hidden = w_up.shape[1]
    loads = [
        pltpu.make_async_copy(src, dst, w_sem.at[i])
        for i, (src, dst) in enumerate(((h_out, w_out), (h_up, w_up), (h_down, w_down)))
    ]
    for load in loads:
        load.start()
    block = 2 * PAIR
    n_rows, n_wide = count // block, width // block
    row_groups = hidden // width
    sums[...] = jnp.zeros(sums.shape, F32)

    def row(i):
        return rows[i : i + 1, :]

    def at_rows(i):
        return pl.ds(pl.multiple_of(i * block, block), block)

    loads[0].wait()

    def first(i, carry):
        at = at_rows(i)
        resid = tokens[at, :].astype(F32) + (nn(attn[at, :], w_out[...]) + row(2))
        unit, scale = norm_parts(resid)
        out = unit * row(6) + row(3)
        unit_one[at, :] = unit
        scale_one[at, :] = jnp.broadcast_to(scale, (block, PAIR))
        normed[at, :] = out
        low[at, :] = out.astype(BF)
        total[at, :] = jnp.broadcast_to(row(4), (block, width))
        return carry

    lax.fori_loop(0, n_rows, first, 0)
    low_t[...] = low[...].T
    attn_t[...] = attn[...].T
    loads[1].wait()
    loads[2].wait()

    def forward(r, carry):
        for j in range(n_wide):
            f = pl.ds(pl.multiple_of(r * width + j * block, block), block)
            bias = rows[pl.ds(8 + r, 1), j * block : (j + 1) * block]
            value, rate = gelu_parts(nn(low[...], w_up[:, f]) + bias)
            value = value.astype(BF)
            active[:, f] = value
            slope[:, f] = rate.astype(BF)
            total[...] += nn(value, w_down[f, :])
        return carry

    lax.fori_loop(0, row_groups, forward, 0)

    def second(i, carry):
        at = at_rows(i)
        unit, scale = norm_parts(normed[at, :] + total[at, :])
        layer_out[at, :] = (unit * row(7) + row(5)).astype(BF)
        up = cot[at, :].astype(F32)
        grad = norm_back(up, row(7), unit, scale)
        grad_two[at, :] = grad
        total[at, :] = grad
        grad = grad.astype(BF)
        ff[at, :] = grad
        sums[4:5, :] += row_sum(grad.astype(F32))
        sums[5:6, :] += row_sum(up)
        sums[7:8, :] += row_sum(up * unit)
        return carry

    lax.fori_loop(0, n_rows, second, 0)

    def backward(r, carry):
        for j in range(n_wide):
            f = pl.ds(pl.multiple_of(r * width + j * block, block), block)
            lane = slice(j * block, (j + 1) * block)
            grad = nt(ff[...], w_down[f, :]) * slope[:, f].astype(F32)
            grad = grad.astype(BF)
            sums[pl.ds(8 + r, 1), lane] = row_sum(grad.astype(F32))
            g_up[:, f] = nn(low_t[...], grad).astype(BF)
            g_down[f, :] = tn(active[:, f], ff[...]).astype(BF)
            total[...] += nt(grad, w_up[:, f])
        f = pl.ds(pl.multiple_of(r * width, width), width)
        pltpu.make_async_copy(g_down.at[f, :], d_down.at[f, :], o_sem.at[0, r]).start()
        pltpu.make_async_copy(g_up.at[:, f], d_up.at[:, f], o_sem.at[1, r]).start()
        return carry

    lax.fori_loop(0, row_groups, backward, 0)

    def third(i, carry):
        at = at_rows(i)
        unit = unit_one[at, :]
        up = total[at, :]
        grad = norm_back(up, row(6), unit, scale_one[at, :1])
        grad_one[at, :] = grad
        grad = grad.astype(BF)
        low[at, :] = grad
        ga[at, :] = nt(grad, w_out[...]).astype(BF)
        sums[2:3, :] += row_sum(grad.astype(F32))
        sums[3:4, :] += row_sum(up)
        sums[6:7, :] += row_sum(up * unit)
        return carry

    lax.fori_loop(0, n_rows, third, 0)
    g_out[...] = nn(attn_t[...], low[...]).astype(BF)
    last = pltpu.make_async_copy(g_out, d_out, o_sem.at[2, 0])
    last.start()
    for r in range(row_groups):
        f = pl.ds(r * width, width)
        pltpu.make_async_copy(g_down.at[f, :], d_down.at[f, :], o_sem.at[0, r]).wait()
        pltpu.make_async_copy(g_up.at[:, f], d_up.at[:, f], o_sem.at[1, r]).wait()
    last.wait()


def feed(attn, tokens, cot, rows, weights):
    count, width = attn.shape
    hidden = weights[1].shape[1]
    vmem, hbm = pl.BlockSpec(memory_space=pltpu.VMEM), pl.BlockSpec(memory_space=pltpu.HBM)
    shape = jax.ShapeDtypeStruct
    wide = [x.shape for x in weights]
    return pl.pallas_call(
        feed_kernel,
        out_shape=[
            shape(attn.shape, BF), shape(attn.shape, F32), shape(attn.shape, BF),
            shape(rows.shape, F32),
        ]
        + [shape(wide[i], BF) for i in (2, 1, 0)],
        in_specs=[vmem] * 4 + [hbm] * 3,
        out_specs=[vmem] * 4 + [hbm] * 3,
        scratch_shapes=[pltpu.VMEM(x, BF) for x in wide]
        + [pltpu.VMEM(wide[i], BF) for i in (2, 1, 0)]
        + [
            pltpu.VMEM((count, hidden), BF),
            pltpu.VMEM((count, hidden), BF),
            pltpu.VMEM((count, width), F32),
            pltpu.VMEM((count, PAIR), F32),
            pltpu.VMEM((count, width), F32),
            pltpu.VMEM((count, width), BF),
            pltpu.VMEM((width, count), BF),
            pltpu.VMEM((count, width), F32),
            pltpu.VMEM((count, width), F32),
            pltpu.VMEM((count, width), BF),
            pltpu.VMEM((width, count), BF),
            pltpu.SemaphoreType.DMA((3,)),
            pltpu.SemaphoreType.DMA((3, hidden // width)),
        ],
        compiler_params=pltpu.CompilerParams(vmem_limit_bytes=56 * 1024 * 1024),
        name="feed",
    )(attn, tokens, cot, rows, *weights)


def back_kernel(
    reach, n_taps,
    ga, tokens, resid, f_qkv, vec_rows, lines, d_down, d_up, d_out,
    q, k, vpad, landq, landk, mix, p1, e, wt, p2o, zo, lvo,
    input_grad, s_qkv, s_out, s_up, s_down, s_small,
    grad, tapg, table, tok_t, outbox, small_box,
    gpad, gmix, gmr, low, gfull, mstat, gcol, gq, gv, lkp, lpart, lpr, lsum, gsum, gpart, dz, dp,
    skew, own_g, *rest,
):
    bufs, (g_send, g_recv, g_local, send, recv) = rest[:-5], rest[-5:]
    net, group = Net(g_send, g_recv), Group(send, recv)
    me, size = group.me, group.size
    n_seq, length, width = q.shape
    pairs = width // PAIR
    own = n_seq * pairs // size
    each = own * PAIR
    land_local = LAND // size
    seg = length // land_local
    half = PAIR // 2
    scale = half**-0.5
    greet(group.peers() + [net.to_first, net.to_second])

    def owner_seq(d):
        return d * own // pairs

    def owner_lanes(d):
        return pl.ds(pl.multiple_of((d * own % pairs) * PAIR, PAIR), each)

    plan = [(s_down, 0), (s_up, 0), (s_out, 0)]
    plan += [(s_qkv, 2 * width), (s_qkv, 0), (s_qkv, width), (s_small, 0)]
    pieces = []
    for w, (out, base) in enumerate(plan):
        own_bufs = bufs[6 * w : 6 * w + 6]
        pieces.append(Scatter(net, w, out, base, own_bufs[0].shape[1], own_bufs))
    r_down, r_up, r_out, r_v, r_q, r_k, r_small = pieces

    def open_whole(w, src):
        piece = pieces[w]
        other, here = [columns(0, c, piece.half) for c in (1 - net.core, net.core)]
        own_part = pltpu.make_async_copy(src.at[:, here], piece.acc, g_local.at[w])
        piece.open(src.at[:, other], own_part)

    def open_weight(piece, box):
        step = 2 * PAIR
        rows = tok_t.shape[0]

        def one(i, carry):
            at = pl.ds(pl.multiple_of(i * step, step), step)
            x = tok_t[at, :]
            other, here = [columns(piece.base, c, piece.half) for c in (1 - net.core, net.core)]
            outbox[box, at, :] = nn(x, grad[:, other]).astype(BF)
            piece.acc[at, :] = nn(x, grad[:, here]).astype(BF)
            return carry

        lax.fori_loop(0, rows // step, one, 0)
        piece.open(outbox.at[box])

    open_whole(0, d_down)
    halo_in, halo_sent = group.halo(0, ga, gpad, reach)

    def first(s, carry):
        for p in range(pairs):
            unit, at = s * pairs + p, lanes(p)
            own_ga = ga[s, :, at]
            gpad[s, pl.ds(reach, length), at] = own_ga
            prob = p1[unit]
            gmix[s, :, at] = together(nn(prob.astype(BF), own_ga)).astype(BF)
            back = nt(apart(mix[s, :, at]), own_ga)
            low[unit] = (prob * (back - by_head(prob * back, jnp.sum))).astype(BF)
        return carry

    lax.fori_loop(0, n_seq, first, 0)
    chips, my_line, my_core = size // 2, me // 2, me % 2
    core_lanes = [pl.ds(pl.multiple_of(c * each, PAIR), each) for c in (my_core, 1 - my_core)]
    sibling = (group.row, 2 * my_line + 1 - my_core)
    gmix_sib = group.go(1, chips, gmix.at[:, :, core_lanes[1]], gsum, sibling)
    r_down.step_one()
    gmix_sib.wait_recv()
    gpart[...] = gmix[:, :, core_lanes[0]] + gsum[...]
    gmix_in = []
    for kk, device in enumerate(group.line_peers()):
        other = device[1] // 2
        gmix_in.append(group.go(1, kk, gpart.at[other], gmr.at[my_line], device))
    gmr[my_line] = gpart[my_line]
    open_whole(1, d_up)
    open_whole(2, d_out)
    fill_bands(lines, table, reach)
    halo_in()
    skew[...] = jnp.zeros(skew.shape, F32)

    def beside(s, carry):
        one, two_mask = lane_masks(BF)
        for p in range(pairs):
            unit, at = s * pairs + p, lanes(p)
            own_ga, padded = ga[s, :, at], vpad[s, :, at]
            gs = low[unit]
            gq[s, :, at] = tn(gs, apart(landk[s, :, at])) * scale
            lkp[s, :, at] = together(nn(gs, q[s, :, at])) * scale
            gv[s, :, at] = conv_pair(table[p], gpad[s, :, at])
            both = jnp.concatenate([own_ga * one, own_ga * two_mask], axis=0)
            skew[2 * p : 2 * p + 2, :, : length + 2 * reach] += nt(both, padded).reshape(
                2, length, length + 2 * reach
            )
        return carry

    lax.fori_loop(0, n_seq, beside, 0)
    lane_at = lax.broadcasted_iota(jnp.int32, (PAIR, PAIR), 1)
    wide = skew.shape[2]
    for h in range(2 * pairs):
        total = skew[h, :8, :]
        for row in range(8, length, 8):
            total = total + pltpu.roll(skew[h, row : row + 8, :], wide - row, 1)
        tapg[h] = total[:, :PAIR]
    r_up.step_one()
    tok_t[...] = tokens[...].T

    for copy in gmix_in:
        copy.wait_recv()
    my_seq, my_pair = owner_seq(me), (me * own) % pairs
    tile = jnp.zeros((PAIR, PAIR), F32)
    for i in range(own):
        at = pl.ds(i * PAIR, PAIR)
        total = gmr[0, :, at].astype(F32)
        for src in range(1, chips):
            total = total + gmr[src, :, at].astype(F32)
        total = split(apart(total))
        means = apart(lvo[:, at])
        back = together(three(tn, split(zo[PINV_ITERS, i]), total)).astype(BF)
        own_g[:, at] = back
        column = jnp.sum(apart(back.astype(F32)) * means, axis=1, keepdims=True)
        tile = jnp.where(lane_at == i, column, tile)
        dz[i] = three(nt, total, split(means))
        dp[i] = jnp.zeros((PAIR, PAIR), F32)
    mstat[me] = tile.T[:8]
    gfull[my_seq, :, owner_lanes(me)] = own_g[...]
    g_in = group.share(
        [
            (2, lambda d: gfull.at[owner_seq(d), :, owner_lanes(d)]),
            (3, lambda d: mstat.at[d]),
        ]
    )
    g_in()
    rows = jnp.concatenate(
        [mstat[...].reshape(8 * size, PAIR), jnp.zeros((PAIR - 8 * size, PAIR), F32)], axis=0
    )
    gcol[...] = rows.T
    unit_matrix = eye()

    def third(unit):
        s, p = unit // pairs, unit % pairs
        at = lanes(p)
        here = (unit // own) * 8 + unit % own
        picked = lane_at == here
        weight = jnp.sum(jnp.where(picked, wt[...], 0.0), axis=1, keepdims=True)
        offset = jnp.sum(jnp.where(picked, gcol[...], 0.0), axis=1, keepdims=True)
        g = apart(gfull[s, :, at])
        prob = e[unit].astype(F32) * weight
        back = nt(g, vpad[s, pl.ds(reach, length), at]) - offset
        gs = (prob * back).astype(BF)
        values = gv[s, :, at] + tn(prob.astype(BF), g)
        v_at = pl.ds(pl.multiple_of(2 * width + p * PAIR, PAIR), PAIR)
        rows = pl.ds(pl.multiple_of(s * length, length), length)
        grad[rows, v_at] = values.astype(BF)
        rows = pl.ds(pl.multiple_of(s * length, length), length)
        grad[rows, pl.ds(pl.multiple_of(width + p * PAIR, PAIR), PAIR)] = (
            tn(gs, apart(landq[s, :, at])) * scale
        ).astype(BF)
        lq = (together(nn(gs, k[s, :, at])) * scale).reshape(size, land_local, PAIR)
        lk = lkp[s, :, at].reshape(size, land_local, PAIR)
        both = jnp.concatenate([lq, lk], axis=1).astype(BF)
        lpart[:, :, s, :, at] = both.reshape(chips, 2, 2 * land_local, PAIR)

    per_step = n_seq * pairs // PINV_ITERS

    def pinv_back(step, carry):
        at_step = PINV_ITERS - 1 - step
        for i in range(own):
            p, z = split(p2o[i]), split(zo[at_step, i])
            prod, one, two_term, three_term = pinv_terms(p, z, unit_matrix)
            d_out = dz[i] * 0.25
            d_out_s = split(d_out)
            d_three = split(three(tn, z, d_out_s))
            d_two = split(-three(tn, prod, d_three))
            d_one = -three(tn, prod, d_two)
            d_prod = -three(nt, d_three, split(two_term)) - three(nt, d_two, split(one)) - d_one
            d_prod = split(d_prod)
            dp[i] += three(nt, d_prod, z)
            dz[i] = three(nt, d_out_s, split(three_term)) + three(tn, p, d_prod)
        for j in range(per_step):
            third(step * per_step + j)
        return carry

    third_of = PINV_ITERS // 3
    lax.fori_loop(0, third_of, pinv_back, 0)
    r_down.step_two()
    r_out.step_one()
    lax.fori_loop(third_of, 2 * third_of, pinv_back, 0)
    lax.fori_loop(2 * third_of, PINV_ITERS, pinv_back, 0)
    r_up.step_two()
    r_out.step_two()

    for i in range(own):
        at = pl.ds(i * PAIR, PAIR)
        prob = p2o[i]
        squares = by_head(jnp.sum(prob * prob, axis=1, keepdims=True), jnp.sum)
        d_start = dz[i].T
        inner = by_head(jnp.sum(d_start * prob, axis=1, keepdims=True), jnp.sum)
        d_prob = dp[i] + d_start / squares - 2.0 * prob * inner / (squares * squares)
        gs = prob * (d_prob - jnp.sum(prob * d_prob, axis=1, keepdims=True))
        gs = split(gs)
        here = lanes(my_pair + i)
        lq, lk = apart(landq[my_seq, :, here]), apart(landk[my_seq, :, here])
        query = together(nn(gs[0], lk) + nn(gs[1], lk)) * scale
        key = together(tn(gs[0], lq) + tn(gs[1], lq)) * scale
        both = [x.reshape(size, land_local, PAIR) for x in (query, key)]
        both = jnp.concatenate(both, axis=1).reshape(chips, 2, 2 * land_local, PAIR)
        lpart[:, :, my_seq, :, here] = (lpart[:, :, my_seq, :, here].astype(F32) + both).astype(BF)
    land_sib = group.go(4, chips, lpart.at[:, 1 - my_core], lsum, sibling)
    land_sib.wait_recv()

    def add_lands(i, carry):
        lsum[i] = lsum[i] + lpart[i, my_core]
        return carry

    lax.fori_loop(0, chips, add_lands, 0)
    lpr[my_line] = lsum[my_line]
    land_in = []
    for kk, device in enumerate(group.line_peers()):
        land_in.append(group.go(4, kk, lsum.at[device[1] // 2], lpr.at[my_line], device))
    open_weight(r_v, 0)
    for copy in land_in:
        copy.wait_recv()

    def close(s, carry):
        for p in range(pairs):
            at = lanes(p)
            total = lpr[0, s, :, at].astype(F32)
            for src in range(1, chips):
                total = total + lpr[src, s, :, at].astype(F32)
            total = total * (1.0 / seg)
            spread = [
                jnp.concatenate(
                    [jnp.broadcast_to(x[i : i + 1], (seg, PAIR)) for i in range(land_local)], axis=0
                )
                for x in (total[:land_local], total[land_local:])
            ]
            rows = pl.ds(pl.multiple_of(s * length, length), length)
            grad[rows, at] = (gq[s, :, at] + spread[0]).astype(BF)
            key_at = pl.ds(width + p * PAIR, PAIR)
            grad[rows, key_at] = (grad[rows, key_at].astype(F32) + spread[1]).astype(BF)
        return carry

    lax.fori_loop(0, n_seq, close, 0)
    r_down.step_three()
    open_weight(r_q, 1)
    r_v.step_one()
    open_weight(r_k, 2)
    r_q.step_one()
    r_up.step_three()

    def column_sums(base):
        total = jnp.zeros((1, width), F32)
        for s in range(n_seq):
            x = grad[s * length : (s + 1) * length, base : base + width].astype(F32)
            total = total + jnp.sum(x, axis=0, keepdims=True)
        return total

    count = vec_rows.shape[0]
    which = lax.broadcasted_iota(jnp.int32, (count, width), 0)
    table_rows = vec_rows[...]
    table_rows = jnp.where(which == 0, column_sums(0), table_rows)
    table_rows = jnp.where(which == 1, column_sums(2 * width), table_rows)
    table_rows = jnp.concatenate([table_rows, jnp.zeros((PAIR - count, width), F32)], axis=0)
    left = table_rows.T
    sums = tapg[:, 0, :]
    for b in range(1, 8):
        sums = sums + pltpu.roll(tapg[:, b, :], PAIR - b, 1)
    shard = r_small.rows
    sums = jnp.concatenate([sums, jnp.zeros((shard - sums.shape[0], PAIR), F32)], axis=0)
    right = jnp.broadcast_to(sums[None], (width // shard, shard, PAIR)).reshape(width, PAIR)
    zero = net.core == 0
    r_small.acc[...] = jnp.where(zero, left, right)
    small_box[...] = jnp.where(zero, right, left)
    r_small.open(small_box)
    r_v.step_two()
    r_k.step_one()
    r_out.step_three()
    r_down.step_four()

    def inputs(i, carry):
        step = 2 * PAIR
        rows = pl.ds(pl.multiple_of(i * step, step), step)
        for at in range(0, width, step):
            x = nt(grad[rows, :], f_qkv[at : at + step, :])
            out = x + resid[rows, at : at + step]
            input_grad[rows, at : at + step] = out.astype(BF)
        return carry

    lax.fori_loop(0, tokens.shape[0] // (2 * PAIR), inputs, 0)
    r_small.step_one()
    r_q.step_two()
    r_k.step_two()
    r_v.step_three()
    r_small.step_two()
    r_up.step_four()
    r_q.step_three()
    r_k.step_three()
    r_out.step_four()
    r_v.step_four()
    r_small.step_three()
    r_q.step_four()
    r_k.step_four()
    r_small.step_four()
    for piece in pieces:
        piece.close()
    halo_sent()
    group.finish()
    net.finish()


def back(
    ga, tokens, resid, f_qkv, vec_rows, lines, d_down, d_up, d_out, kept, shards, seq_size, reach
):
    q = kept[0]
    n_seq, length, width = q.shape
    pairs = width // PAIR
    units = n_seq * pairs
    own = units // seq_size
    line_size = seq_size // 2
    vmem, hbm = pl.BlockSpec(memory_space=pltpu.VMEM), pl.BlockSpec(memory_space=pltpu.HBM)
    shape = jax.ShapeDtypeStruct
    part = 2 * LAND // seq_size
    s_qkv, s_out, s_up, s_down = [shape(x.shape, F32) for x in shards]
    s_small = shape((s_qkv.shape[0], 2 * PAIR), F32)
    bufs = []
    for x in (s_down, s_up, s_out):
        bufs += scatter_scratch(x.shape[0], x.shape[1] // 2, BF, line_size)
    for _ in range(3):
        bufs += scatter_scratch(s_qkv.shape[0], width // 2, BF, line_size)
    bufs += scatter_scratch(s_qkv.shape[0], PAIR, F32, line_size)
    return pl.pallas_call(
        functools.partial(back_kernel, reach, 2 * reach + 1),
        out_shape=[shape(tokens.shape, BF), s_qkv, s_out, s_up, s_down, s_small],
        in_specs=[vmem] * 6 + [hbm] * 3 + [vmem] * 12,
        out_specs=[vmem] * 6,
        scratch_shapes=[
            pltpu.VMEM((n_seq * length, 3 * width), BF),
            pltpu.VMEM((2 * pairs, 8, PAIR), F32),
            pltpu.VMEM((pairs, 4 * length, length + 2 * reach), BF),
            pltpu.VMEM((width, n_seq * length), BF),
            pltpu.VMEM((3, width, width // 2), BF),
            pltpu.VMEM((width, PAIR), F32),
            pltpu.VMEM((n_seq, length + 2 * reach, width), BF),
            pltpu.VMEM((n_seq, LAND, width), BF),
            pltpu.VMEM((seq_size // 2, LAND, own * PAIR), BF),
            pltpu.VMEM((units, PAIR, length), BF),
            pltpu.VMEM((n_seq, LAND, width), BF),
            pltpu.VMEM((seq_size, 8, PAIR), F32),
            pltpu.VMEM((PAIR, PAIR), F32),
            pltpu.VMEM((n_seq, length, width), F32),
            pltpu.VMEM((n_seq, length, width), F32),
            pltpu.VMEM((n_seq, LAND, width), F32),
            pltpu.VMEM((seq_size // 2, 2, n_seq, part, width), BF),
            pltpu.VMEM((seq_size // 2, n_seq, part, width), BF),
            pltpu.VMEM((seq_size // 2, n_seq, part, width), BF),
            pltpu.VMEM((n_seq, LAND, own * PAIR), BF),
            pltpu.VMEM((n_seq, LAND, own * PAIR), BF),
            pltpu.VMEM((own, PAIR, PAIR), F32),
            pltpu.VMEM((own, PAIR, PAIR), F32),
            pltpu.VMEM((2 * pairs, length, 2 * PAIR), F32),
            pltpu.VMEM((LAND, own * PAIR), BF),
        ]
        + bufs
        + [
            pltpu.SemaphoreType.DMA((7, line_size + SCATTER_SEMS)),
            pltpu.SemaphoreType.DMA((7, line_size + SCATTER_SEMS)),
            pltpu.SemaphoreType.DMA((7,)),
            pltpu.SemaphoreType.DMA((6, seq_size)),
            pltpu.SemaphoreType.DMA((6, seq_size)),
        ],
        compiler_params=pltpu.CompilerParams(
            collective_id=1, has_side_effects=True, vmem_limit_bytes=60 * 1024 * 1024
        ),
        name="back",
    )(ga, tokens, resid, f_qkv, vec_rows, lines, d_down, d_up, d_out, *kept)


def kernels_fit(args):
    tokens, _, *matrices = args[:6]
    taps = args[7]
    seq_size = lax.axis_size("seq")
    n_seq, length, width = tokens.shape
    units = n_seq * width // PAIR
    own = units // seq_size
    return (
        lax.axis_size("rows") == 4
        and seq_size == 8
        and all(x.shape[0] % 24 == 0 and x.shape[1] % 256 == 0 for x in matrices)
        and width // taps.shape[0] == PAIR // 2
        and length == PAIR
        and taps.shape[1] == 33
        and taps.shape[0] <= matrices[0].shape[0]
        and units == own * seq_size
        and seq_size == 2 * n_seq
        and width == 2 * own * PAIR
        and 2 * own <= 8
        and (width // PAIR) % own == 0
        and units % PINV_ITERS == 0
        and LAND == 8 * seq_size
        and matrices[2].shape[1] == 4 * width
        and args[6].shape[0] == 12
    )


def with_kernels(
    tokens, cotangent, qkv_weight, out_weight, up_weight, down_weight, vectors, taps,
    qkv_first, qkv_second, out_first, out_second, up_first, up_second, down_first, down_second,
    vec_first, vec_second, tap_first, tap_second,
):
    seq_count, local_len, model_width = tokens.shape
    head_count, tap_count = taps.shape
    seq_size = lax.axis_size("seq")
    reach = tap_count // 2
    row_count = seq_count * local_len
    count = vectors.shape[0]
    matrices = (qkv_weight, out_weight, up_weight, down_weight)
    table = jnp.pad(vectors.T, ((0, 0), (0, 2 * PAIR - count)))
    lines = jnp.pad(taps, ((0, 0), (0, 2 * PAIR - tap_count)))
    flat_in = tokens.reshape(row_count, model_width)
    full_qkv, full_out, full_up, full_down, vec_float, *kept = front(
        tokens, matrices, table, lines, seq_size, reach
    )
    attn_low = kept.pop(2).reshape(row_count, model_width)
    queries, key_rows = kept[:2]
    layer_out, grad_resid_one, grad_attn, vec_rows, grad_down, grad_up, grad_out = feed(
        attn_low, flat_in, cotangent.reshape(row_count, model_width), vec_float,
        (full_out, full_up, full_down),
    )
    flipped = jnp.pad(taps[:, ::-1], ((0, 0), (0, 2 * PAIR - tap_count)))
    input_grad, summed_qkv, summed_out, summed_up, summed_down, small = back(
        grad_attn.reshape(tokens.shape), flat_in, grad_resid_one, full_qkv, vec_rows, flipped,
        grad_down, grad_up, grad_out,
        kept, matrices, seq_size, reach,
    )
    input_grad = input_grad.reshape(tokens.shape)
    summed_vec = small[:, :count].T
    summed_taps = small[:head_count, PAIR : PAIR + tap_count]
    new_qkv = adam_step(qkv_weight, qkv_first, qkv_second, summed_qkv, rate_matrix, decay_rate)
    new_out = adam_step(out_weight, out_first, out_second, summed_out, rate_output, decay_rate)
    new_up = adam_step(up_weight, up_first, up_second, summed_up, rate_matrix, decay_rate)
    new_down = adam_step(down_weight, down_first, down_second, summed_down, rate_matrix, decay_rate)
    new_vec = adam_step(vectors, vec_first, vec_second, summed_vec, rate_vector, 0.0)
    new_taps = adam_step(taps, tap_first, tap_second, summed_taps, rate_taps, 0.0)
    out_tokens = layer_out.reshape(tokens.shape)
    return (out_tokens, input_grad) + new_qkv + new_out + new_up + new_down + new_vec + new_taps


def on_device(*args):
    return with_kernels(*args) if kernels_fit(args) else with_collectives(*args)


def solution(mesh):
    return jax.shard_map(
        on_device,
        mesh=mesh,
        in_specs=(
            P("rows", "seq", None),
            P("rows", "seq", None),
            P(("rows", "seq"), None),
            P(("rows", "seq"), None),
            P(("rows", "seq"), None),
            P(("rows", "seq"), None),
            P(None, ("rows", "seq")),
            P(),
            P(("rows", "seq"), None),
            P(("rows", "seq"), None),
            P(("rows", "seq"), None),
            P(("rows", "seq"), None),
            P(("rows", "seq"), None),
            P(("rows", "seq"), None),
            P(("rows", "seq"), None),
            P(("rows", "seq"), None),
            P(None, ("rows", "seq")),
            P(None, ("rows", "seq")),
            P(),
            P(),
        ),
        out_specs=(
            P("rows", "seq", None),
            P("rows", "seq", None),
            P(("rows", "seq"), None),
            P(("rows", "seq"), None),
            P(("rows", "seq"), None),
            P(("rows", "seq"), None),
            P(("rows", "seq"), None),
            P(("rows", "seq"), None),
            P(("rows", "seq"), None),
            P(("rows", "seq"), None),
            P(("rows", "seq"), None),
            P(("rows", "seq"), None),
            P(("rows", "seq"), None),
            P(("rows", "seq"), None),
            P(None, ("rows", "seq")),
            P(None, ("rows", "seq")),
            P(None, ("rows", "seq")),
            P(),
            P(),
            P(),
        ),
        check_vma=False,
    )
```

```python
import functools

import jax
import jax.numpy as jnp
from jax import lax
from jax.experimental import pallas as pl
from jax.experimental.pallas import tpu as pltpu
from jax.sharding import PartitionSpec as P

LAND = 64
PINV_ITERS = 6


top_precision = lax.Precision.HIGHEST
norm_eps = 1e-05
beta_one = 0.9
beta_two = 0.999
corr_one = 1.0 - 0.9**10
corr_two = 1.0 - 0.999**10
adam_eps = 1e-08
decay_rate = 0.01
rate_matrix = 0.03
rate_output = 0.12
rate_vector = 0.3
rate_taps = 0.08


def with_halo(x, sides, width):
    for axis, dim in sides:
        size, length = (lax.axis_size(axis), x.shape[dim])
        up = [(i, (i + 1) % size) for i in range(size - 1)]
        down = [(j, i) for i, j in up]
        last = lax.slice_in_dim(x, length - width, length, axis=dim)
        initial = lax.slice_in_dim(x, 0, width, axis=dim)
        before = lax.ppermute(last, axis, up)
        after = lax.ppermute(initial, axis, down)
        x = jnp.concatenate([before, x, after], axis=dim)
    return x


def layer_norm(residual, gain_row, shift_row):
    center = residual - jnp.mean(residual, axis=-1, keepdims=True)
    spread = jnp.mean(center * center, axis=-1, keepdims=True)
    return center * lax.rsqrt(spread + norm_eps) * gain_row + shift_row


def normalized_rows(scores):
    expo = jnp.exp(scores - jnp.max(scores, axis=-1, keepdims=True))
    return expo / jnp.sum(expo, axis=-1, keepdims=True)


def softmax_back(probability, grad_in):
    return probability * (grad_in - jnp.sum(probability * grad_in, axis=-1, keepdims=True))


def gelu_exact(inputs):
    return jax.nn.gelu(inputs, approximate=False)


def pseudo_inverse(matrix):
    identity = jnp.eye(matrix.shape[-1], dtype=jnp.float32)
    approx = jnp.swapaxes(matrix, -1, -2) / jnp.sum(matrix * matrix, axis=(-2, -1), keepdims=True)
    for sweep_index in range(PINV_ITERS):
        product = jnp.matmul(matrix, approx, precision=top_precision)
        inner_term = 7.0 * identity - product
        inner_term = 15.0 * identity - jnp.matmul(product, inner_term, precision=top_precision)
        inner_term = 13.0 * identity - jnp.matmul(product, inner_term, precision=top_precision)
        approx = 0.25 * jnp.matmul(approx, inner_term, precision=top_precision)
    return approx


def adam_step(weight, first_moment, second, gradient, step_rate, decay_coef):
    new_first = beta_one * first_moment + (1.0 - beta_one) * gradient
    new_second = beta_two * second + (1.0 - beta_two) * gradient * gradient
    update = new_first / corr_one / (jnp.sqrt(new_second / corr_two) + adam_eps)
    return (new_first, new_second, weight - step_rate * (update + decay_coef * weight))


def with_collectives(
    tokens,
    cotangent,
    qkv_weight,
    out_weight,
    up_weight,
    down_weight,
    vectors,
    taps,
    qkv_first,
    qkv_second,
    out_first,
    out_second,
    up_first,
    up_second,
    down_first,
    down_second,
    vec_first,
    vec_second,
    tap_first,
    tap_second,
):
    seq_count, local_len, model_width = tokens.shape
    head_count, tap_count = taps.shape
    head_size = model_width // head_count
    hidden_width = up_weight.shape[1]
    land_local = LAND // lax.axis_size("seq")
    seg_len = local_len // land_local
    reach_width = tap_count // 2
    logit_scale_factor = head_size ** (-0.5)
    row_count = seq_count * local_len
    head_shape = (seq_count, local_len, head_count, head_size)
    land_shape = (seq_count, LAND, head_count, head_size)
    full_qkv, full_out, full_up, full_down, full_vec = (
        lax.all_gather(qkv_weight.astype(jnp.bfloat16), ("rows", "seq"), axis=0, tiled=True),
        lax.all_gather(out_weight.astype(jnp.bfloat16), ("rows", "seq"), axis=0, tiled=True),
        lax.all_gather(up_weight.astype(jnp.bfloat16), ("rows", "seq"), axis=0, tiled=True),
        lax.all_gather(down_weight.astype(jnp.bfloat16), ("rows", "seq"), axis=0, tiled=True),
        lax.all_gather(vectors.astype(jnp.bfloat16), ("rows", "seq"), axis=1, tiled=True),
    )
    vec_float = full_vec.astype(jnp.float32)
    flat_in = tokens.reshape(row_count, model_width)
    project = jnp.dot(flat_in, full_qkv, preferred_element_type=jnp.float32)
    queries = (project[:, :model_width] + vec_float[0]).astype(jnp.bfloat16)
    key_rows = project[:, model_width : 2 * model_width].astype(jnp.bfloat16)
    values = (project[:, 2 * model_width :] + vec_float[1]).astype(jnp.bfloat16)
    seg_shape = (seq_count, land_local, seg_len, model_width)
    own_q = jnp.mean(queries.reshape(seg_shape), axis=2, dtype=jnp.float32).astype(jnp.bfloat16)
    own_k = jnp.mean(key_rows.reshape(seg_shape), axis=2, dtype=jnp.float32).astype(jnp.bfloat16)
    land_q, land_k = (
        lax.all_gather(own_q, "seq", axis=1, tiled=True),
        lax.all_gather(own_k, "seq", axis=1, tiled=True),
    )
    query_heads = queries.reshape(head_shape)
    key_heads = key_rows.reshape(head_shape)
    value_heads = values.reshape(head_shape)
    landmark_query_heads = land_q.reshape(land_shape)
    landmark_key_heads = land_k.reshape(land_shape)
    lq_float = landmark_query_heads.astype(jnp.float32)
    lk_float = landmark_key_heads.astype(jnp.float32)
    score_one = (
        jnp.einsum(
            "sthd,slhd->shtl", query_heads, landmark_key_heads, preferred_element_type=jnp.float32
        )
        * logit_scale_factor
    )
    prob_one = normalized_rows(score_one)
    second_probability = normalized_rows(
        jnp.einsum("slhd,smhd->shlm", lq_float, lk_float, precision=top_precision)
        * logit_scale_factor
    )
    inverse_matrix, inverse_pull = jax.vjp(pseudo_inverse, second_probability)
    score_three = (
        jnp.einsum(
            "slhd,sthd->shlt", landmark_query_heads, key_heads, preferred_element_type=jnp.float32
        )
        * logit_scale_factor
    )
    row_max = lax.pmax(jnp.max(score_three, axis=-1), "seq")
    expo_three = jnp.exp(score_three - row_max[..., None])
    numer_local = jnp.einsum(
        "shlt,sthd->slhd",
        expo_three.astype(jnp.bfloat16),
        value_heads,
        preferred_element_type=jnp.float32,
    )
    numer, denom = (
        lax.psum(numer_local.astype(jnp.bfloat16), "seq").astype(jnp.float32),
        lax.psum(jnp.sum(expo_three, axis=-1).astype(jnp.bfloat16), "seq").astype(jnp.float32),
    )
    denom_swap = jnp.swapaxes(denom, 1, 2)[..., None]
    landmark_value_rows = numer / denom_swap
    mixing_kernel = jnp.einsum(
        "shlm,smhd->slhd", inverse_matrix, landmark_value_rows, precision=top_precision
    )
    mix_low = mixing_kernel.astype(jnp.bfloat16)
    prob_low = prob_one.astype(jnp.bfloat16)
    attend = jnp.einsum("shtl,slhd->sthd", prob_low, mix_low, preferred_element_type=jnp.float32)
    attend = attend.reshape(seq_count, local_len, model_width)
    tap_chan = jnp.repeat(taps, head_size, axis=0)
    padded_values = with_halo(
        values.reshape(seq_count, local_len, model_width), (("seq", 1),), reach_width
    )
    conv_out = jnp.zeros((seq_count, local_len, model_width), jnp.float32)
    for offset in range(tap_count):
        conv_out = conv_out + tap_chan[:, offset] * padded_values[
            :, offset : offset + local_len
        ].astype(jnp.float32)
    attn_low = (attend + conv_out).reshape(row_count, model_width).astype(jnp.bfloat16)
    branch = jnp.dot(attn_low, full_out, preferred_element_type=jnp.float32) + vec_float[2]
    resid_one = flat_in.astype(jnp.float32) + branch
    normed, norm_pull_one = jax.vjp(layer_norm, resid_one, vec_float[6], vec_float[3])
    normed_low = normed.astype(jnp.bfloat16)
    hidden_pre = jnp.dot(normed_low, full_up, preferred_element_type=jnp.float32) + vec_float[
        8:
    ].reshape(hidden_width)
    active, gelu_pull = jax.vjp(gelu_exact, hidden_pre)
    active_low = active.astype(jnp.bfloat16)
    ff_out = jnp.dot(active_low, full_down, preferred_element_type=jnp.float32) + vec_float[4]
    layer_out, norm_pull_two = jax.vjp(layer_norm, normed + ff_out, vec_float[7], vec_float[5])
    grad_resid_two, grad_gain_two, grad_shift_two = norm_pull_two(
        cotangent.reshape(row_count, model_width).astype(jnp.float32)
    )
    grad_ff = grad_resid_two.astype(jnp.bfloat16)
    grad_down = jnp.einsum("nf,nd->fd", active_low, grad_ff, preferred_element_type=jnp.float32)
    grad_active = jnp.einsum("nd,fd->nf", grad_ff, full_down, preferred_element_type=jnp.float32)
    grad_hidden = gelu_pull(grad_active)[0].astype(jnp.bfloat16)
    grad_up = jnp.einsum("nd,nf->df", normed_low, grad_hidden, preferred_element_type=jnp.float32)
    grad_normed = (
        jnp.einsum("nf,df->nd", grad_hidden, full_up, preferred_element_type=jnp.float32)
        + grad_resid_two
    )
    grad_resid_one, grad_gain_one, grad_shift_one = norm_pull_one(grad_normed)
    grad_branch = grad_resid_one.astype(jnp.bfloat16)
    grad_out = jnp.einsum("nd,ne->de", attn_low, grad_branch, preferred_element_type=jnp.float32)
    grad_attn = jnp.einsum(
        "ne,de->nd", grad_branch, full_out, preferred_element_type=jnp.float32
    ).astype(jnp.bfloat16)
    grad_attn_heads = grad_attn.reshape(head_shape)
    grad_prob_one = jnp.einsum(
        "sthd,slhd->shtl", grad_attn_heads, mix_low, preferred_element_type=jnp.float32
    )
    mixing_part = jnp.einsum(
        "shtl,sthd->slhd", prob_low, grad_attn_heads, preferred_element_type=jnp.float32
    )
    grad_mixing = lax.psum(mixing_part.astype(jnp.bfloat16), "seq").astype(jnp.float32)
    grad_score_one = softmax_back(prob_one, grad_prob_one).astype(jnp.bfloat16)
    query_local = (
        jnp.einsum(
            "shtl,slhd->sthd",
            grad_score_one,
            landmark_key_heads,
            preferred_element_type=jnp.float32,
        )
        * logit_scale_factor
    )
    land_k_part = (
        jnp.einsum(
            "shtl,sthd->slhd", grad_score_one, query_heads, preferred_element_type=jnp.float32
        )
        * logit_scale_factor
    )
    grad_pad = with_halo(
        grad_attn.reshape(seq_count, local_len, model_width), (("seq", 1),), reach_width
    )
    attn_float = grad_attn.reshape(seq_count, local_len, model_width).astype(jnp.float32)
    conv_back = jnp.zeros((seq_count, local_len, model_width), jnp.float32)
    tap_terms = []
    for offset in range(tap_count):
        start_row = 2 * reach_width - offset
        conv_back = conv_back + tap_chan[:, offset] * grad_pad[
            :, start_row : start_row + local_len
        ].astype(jnp.float32)
        tap_terms.append(
            jnp.sum(
                attn_float * padded_values[:, offset : offset + local_len].astype(jnp.float32),
                axis=(0, 1),
            )
        )
    grad_taps = jnp.sum(
        jnp.stack(tap_terms, axis=1).reshape(head_count, head_size, tap_count), axis=1
    )
    grad_inverse = jnp.einsum(
        "slhd,smhd->shlm", grad_mixing, landmark_value_rows, precision=top_precision
    )
    grad_land_values = jnp.einsum(
        "shlm,slhd->smhd", inverse_matrix, grad_mixing, precision=top_precision
    )
    land_grad_low = grad_land_values.astype(jnp.bfloat16).astype(jnp.float32)
    grad_prob_two = inverse_pull(grad_inverse)[0]
    grad_score_two = softmax_back(second_probability, grad_prob_two)
    query_two = (
        jnp.einsum("shlm,smhd->slhd", grad_score_two, lk_float, precision=top_precision)
        * logit_scale_factor
    )
    key_two = (
        jnp.einsum("shlm,slhd->smhd", grad_score_two, lq_float, precision=top_precision)
        * logit_scale_factor
    )
    grad_numer = land_grad_low / denom_swap
    expo_low = expo_three.astype(jnp.bfloat16).astype(jnp.float32)
    value_three = jnp.einsum("shlt,slhd->sthd", expo_low, grad_numer, precision=top_precision)
    grad_expo = jnp.einsum(
        "slhd,sthd->shlt", grad_numer, value_heads.astype(jnp.float32), precision=top_precision
    )
    grad_denom = jnp.swapaxes(jnp.sum(land_grad_low * landmark_value_rows, axis=-1), 1, 2) / denom
    grad_score_three = (expo_three * (grad_expo - grad_denom[..., None])).astype(jnp.bfloat16)
    land_q_part = (
        jnp.einsum(
            "shlt,sthd->slhd", grad_score_three, key_heads, preferred_element_type=jnp.float32
        )
        * logit_scale_factor
    )
    key_local = (
        jnp.einsum(
            "shlt,slhd->sthd",
            grad_score_three,
            landmark_query_heads,
            preferred_element_type=jnp.float32,
        )
        * logit_scale_factor
    )
    land_q_own, land_k_own = (
        lax.psum_scatter(
            land_q_part.astype(jnp.bfloat16), "seq", scatter_dimension=1, tiled=True
        ).astype(jnp.float32),
        lax.psum_scatter(
            land_k_part.astype(jnp.bfloat16), "seq", scatter_dimension=1, tiled=True
        ).astype(jnp.float32),
    )
    first_land = lax.axis_index("seq") * land_local
    land_q_own = land_q_own + lax.dynamic_slice_in_dim(query_two, first_land, land_local, 1)
    land_k_own = land_k_own + lax.dynamic_slice_in_dim(key_two, first_land, land_local, 1)
    spread_shape = (seq_count, land_local, seg_len, head_count, head_size)
    spread_q = jnp.broadcast_to((land_q_own / seg_len)[:, :, None], spread_shape).reshape(
        head_shape
    )
    spread_k = jnp.broadcast_to((land_k_own / seg_len)[:, :, None], spread_shape).reshape(
        head_shape
    )
    grad_query = (query_local + spread_q).reshape(row_count, model_width)
    grad_key = (key_local + spread_k).reshape(row_count, model_width)
    grad_value = value_three.reshape(row_count, model_width) + conv_back.reshape(
        row_count, model_width
    )
    grad_proj = jnp.concatenate([grad_query, grad_key, grad_value], axis=1).astype(jnp.bfloat16)
    grad_qkv = jnp.einsum("nd,ne->de", flat_in, grad_proj, preferred_element_type=jnp.float32)
    input_grad = (
        jnp.einsum("ne,de->nd", grad_proj, full_qkv, preferred_element_type=jnp.float32)
        + grad_resid_one
    )
    input_grad = input_grad.astype(jnp.bfloat16).reshape(tokens.shape)
    bias_sums = jnp.sum(grad_proj.astype(jnp.float32), axis=0)
    grad_vec = jnp.concatenate(
        [
            bias_sums[None, :model_width],
            bias_sums[None, 2 * model_width :],
            jnp.sum(grad_branch.astype(jnp.float32), axis=0)[None],
            grad_shift_one[None],
            jnp.sum(grad_ff.astype(jnp.float32), axis=0)[None],
            grad_shift_two[None],
            grad_gain_one[None],
            grad_gain_two[None],
            jnp.sum(grad_hidden.astype(jnp.float32), axis=0).reshape(-1, model_width),
        ],
        axis=0,
    )
    summed_qkv, summed_out, summed_up, summed_down, summed_vec = (
        lax.psum_scatter(grad_qkv, ("rows", "seq"), scatter_dimension=0, tiled=True),
        lax.psum_scatter(grad_out, ("rows", "seq"), scatter_dimension=0, tiled=True),
        lax.psum_scatter(grad_up, ("rows", "seq"), scatter_dimension=0, tiled=True),
        lax.psum_scatter(grad_down, ("rows", "seq"), scatter_dimension=0, tiled=True),
        lax.psum_scatter(grad_vec, ("rows", "seq"), scatter_dimension=1, tiled=True),
    )
    summed_taps = lax.psum(grad_taps, ("rows", "seq"))
    new_qkv = adam_step(qkv_weight, qkv_first, qkv_second, summed_qkv, rate_matrix, decay_rate)
    new_out = adam_step(out_weight, out_first, out_second, summed_out, rate_output, decay_rate)
    new_up = adam_step(up_weight, up_first, up_second, summed_up, rate_matrix, decay_rate)
    new_down = adam_step(down_weight, down_first, down_second, summed_down, rate_matrix, decay_rate)
    new_vec = adam_step(vectors, vec_first, vec_second, summed_vec, rate_vector, 0.0)
    new_taps = adam_step(taps, tap_first, tap_second, summed_taps, rate_taps, 0.0)
    out_tokens = layer_out.astype(jnp.bfloat16).reshape(tokens.shape)
    return (out_tokens, input_grad) + new_qkv + new_out + new_up + new_down + new_vec + new_taps


BF = jnp.bfloat16
F32 = jnp.float32
MESH = pl.DeviceIdType.MESH


def remote(src, dst, send_sem, recv_sem, device):
    return pltpu.make_async_remote_copy(
        src_ref=src, dst_ref=dst, send_sem=send_sem, recv_sem=recv_sem,
        device_id=device, device_id_type=MESH,
    )


def place():
    row, spot = lax.axis_index("rows"), lax.axis_index("seq")
    line, core = spot // 2, spot % 2
    flip_one = row + 1 - 2 * (row % 2)
    flip_two = row + 2 - 4 * (row // 2)
    first = (1 - core) * flip_one + core * flip_two
    second = (1 - core) * flip_two + core * flip_one
    return row, line, core, first, second, 3 - row


def greet(devices):
    barrier = pltpu.get_barrier_semaphore()
    for device in devices:
        pl.semaphore_signal(barrier, inc=1, device_id=device, device_id_type=MESH)
    pl.semaphore_wait(barrier, len(devices))


class Net:
    def __init__(self, send, recv):
        self.send, self.recv, self.started = send, recv, []
        self.row, self.line, self.core, self.first, self.second, self.across = place()
        self.line_size = lax.axis_size("seq") // 2
        own_spot = 2 * self.line + self.core
        self.sibling = (self.row, 2 * self.line + 1 - self.core)
        self.peers = [
            (self.row, 2 * ((self.line + k) % self.line_size) + self.core)
            for k in range(1, self.line_size)
        ]
        self.to_first, self.to_second = (self.first, own_spot), (self.second, own_spot)

    def go(self, w, k, src, dst, device):
        copy = remote(src, dst, self.send.at[w, k], self.recv.at[w, k], device)
        copy.start()
        self.started.append(copy)
        return copy

    def finish(self):
        for copy in self.started:
            copy.wait_send()


def columns(base, which, half):
    return pl.ds(pl.multiple_of(base + which * half, 128), half)


class Gather:
    def __init__(self, net, w, src, dst, base, half, asm, stage, local):
        self.net, self.w, self.dst, self.stage, self.asm = net, w, dst, stage, asm
        self.rows, self.base, self.half, self.local = src.shape[0], base, half, local
        part = pl.ds(pl.multiple_of(net.core * self.rows, 8), self.rows)
        there = columns(base, 1 - net.core, half)
        self.asm_copy = net.go(w, 0, src.at[:, there], asm.at[part, :], net.sibling)
        asm[part, :] = src[:, columns(base, net.core, half)]

    def block(self, start, size):
        at = pl.ds(pl.multiple_of(start, 16), size)
        return self.dst.at[at, columns(self.base, self.net.core, self.half)]

    def slab(self, index):
        size = 2 * self.rows * self.net.line_size
        return self.block(index * size, size)

    def spread(self):
        net = self.net
        self.asm_copy.wait_recv()
        self.stage[...] = self.asm[...].astype(BF)
        size = 2 * self.rows
        block = self.block((net.row * net.line_size + net.line) * size, size)
        self.z = [net.go(self.w, 1 + k, self.stage, block, d) for k, d in enumerate(net.peers)]
        self.own = pltpu.make_async_copy(self.stage, block, self.local)
        self.own.start()

    def step_one(self):
        net, w, z0 = self.net, self.w, self.net.line_size
        self.own.wait()
        for copy in self.z:
            copy.wait_recv()
        mine = self.slab(net.row)
        self.hop = [net.go(w, z0, mine, mine, net.to_first)]
        self.hop.append(net.go(w, z0 + 1, mine, mine, net.to_second))
        self.sib = [net.go(w, z0 + 3, mine, mine, net.sibling)]

    def step_two(self):
        net, w, z0 = self.net, self.w, self.net.line_size
        self.hop[0].wait_recv()
        got = self.slab(net.first)
        self.hop.append(net.go(w, z0 + 2, got, got, net.to_second))
        self.sib.append(net.go(w, z0 + 4, got, got, net.sibling))

    def step_three(self):
        net, w, z0 = self.net, self.w, self.net.line_size
        self.hop[1].wait_recv()
        got = self.slab(net.second)
        self.sib.append(net.go(w, z0 + 5, got, got, net.sibling))
        self.hop[2].wait_recv()
        got = self.slab(net.across)
        self.sib.append(net.go(w, z0 + 6, got, got, net.sibling))

    def close(self):
        for copy in self.sib:
            copy.wait_recv()


GATHER_SEMS = 7


class Scatter:
    def __init__(self, net, w, out, base, half, bufs):
        self.net, self.w, self.out, self.base, self.half = net, w, out, base, half
        self.acc, self.buf0, self.buf1, self.buf2, self.buf3, self.fin = bufs
        self.rows = out.shape[0]
        self.size = 2 * self.rows * net.line_size

    def open(self, outbox, own=None):
        self.sib = self.net.go(self.w, 0, outbox, self.buf0, self.net.sibling)
        self.own = own
        if own is not None:
            own.start()

    def slab(self, index):
        return pl.ds(pl.multiple_of(index * self.size, self.size), self.size)

    def add(self, index, other, start):
        step = 48
        acc = self.acc

        def one(i, carry):
            at = pl.ds(pl.multiple_of(index * self.size + i * step, 16), step)
            there = pl.ds(pl.multiple_of(start + i * step, 16), step)
            acc[at, :] = acc[at, :] + other[there, :]
            return carry

        lax.fori_loop(0, self.size // step, one, 0)

    def step_one(self):
        net, w = self.net, self.w
        if self.own is not None:
            self.own.wait()
        self.sib.wait_recv()
        self.add(net.across, self.buf0, net.across * self.size)
        acc = self.acc
        self.one = net.go(w, 1, acc.at[self.slab(net.across), :], self.buf1.at[0], net.to_second)
        self.add(net.second, self.buf0, net.second * self.size)
        self.two = net.go(w, 2, acc.at[self.slab(net.second), :], self.buf1.at[1], net.to_second)
        self.add(net.first, self.buf0, net.first * self.size)
        self.add(net.row, self.buf0, net.row * self.size)

    def step_two(self):
        net = self.net
        self.one.wait_recv()
        self.add(net.first, self.buf1.at[0], 0)
        src = self.acc.at[self.slab(net.first), :]
        self.three = net.go(self.w, 3, src, self.buf2, net.to_first)
        self.two.wait_recv()
        self.add(net.row, self.buf1.at[1], 0)

    def step_three(self):
        net = self.net
        self.three.wait_recv()
        self.add(net.row, self.buf2, 0)
        block, n = 2 * self.rows, net.line_size
        self.z = []

        def at(line):
            return pl.ds(pl.multiple_of((net.row * n + line) * block, block), block)

        for k, device in enumerate(net.peers):
            src = self.acc.at[at((net.line + 1 + k) % n), :]
            self.z.append(net.go(self.w, 4 + k, src, self.buf3.at[net.line], device))
        self.buf3[net.line] = self.acc[at(net.line), :]

    def step_four(self):
        net = self.net
        for copy in self.z:
            copy.wait_recv()
        total = self.buf3[0].astype(F32)
        for k in range(1, net.line_size):
            total = total + self.buf3[k].astype(F32)
        self.fin[...] = total
        part = pl.ds(pl.multiple_of((1 - net.core) * self.rows, 8), self.rows)
        here = columns(self.base, net.core, self.half)
        self.last = net.go(
            self.w, 3 + net.line_size, self.fin.at[part, :], self.out.at[:, here], net.sibling
        )
        part = pl.ds(pl.multiple_of(net.core * self.rows, 8), self.rows)
        self.out[:, here] = self.fin[part, :]

    def close(self):
        self.last.wait_recv()


SCATTER_SEMS = 4


def scatter_scratch(rows, half, dtype, line_size):
    quarter = 2 * rows * line_size
    return [
        pltpu.VMEM((4 * quarter, half), dtype),
        pltpu.VMEM((4 * quarter, half), dtype),
        pltpu.VMEM((2, quarter, half), dtype),
        pltpu.VMEM((quarter, half), dtype),
        pltpu.VMEM((line_size, 2 * rows, half), dtype),
        pltpu.VMEM((2 * rows, half), F32),
    ]


PAIR = 128


def nn(a, b):
    return jnp.dot(a, b, preferred_element_type=F32)


def nt(a, b):
    return lax.dot_general(a, b, (((1,), (1,)), ((), ())), preferred_element_type=F32)


def tn(a, b):
    return lax.dot_general(a, b, (((0,), (0,)), ((), ())), preferred_element_type=F32)


def split(x):
    high = x.astype(BF)
    return high, (x - high.astype(F32)).astype(BF)


def three(dot, a, b):
    return dot(a[0], b[0]) + (dot(a[0], b[1]) + dot(a[1], b[0]))


def lane_masks(dtype):
    lane = lax.broadcasted_iota(jnp.int32, (1, PAIR), 1)
    one = (lane < PAIR // 2).astype(F32)
    return one.astype(dtype), (1.0 - one).astype(dtype)


def apart(x):
    one, two = lane_masks(x.dtype)
    return jnp.concatenate([x * one, x * two], axis=0)


def together(x):
    half = PAIR // 2
    lane = lax.broadcasted_iota(jnp.int32, (half, PAIR), 1)
    return jnp.where(lane < half, x[:half], x[half:])


def same_head():
    half = PAIR // 2
    a = lax.broadcasted_iota(jnp.int32, (PAIR, PAIR), 0) // half
    b = lax.broadcasted_iota(jnp.int32, (PAIR, PAIR), 1) // half
    return a == b


def eye():
    a = lax.broadcasted_iota(jnp.int32, (PAIR, PAIR), 0)
    b = lax.broadcasted_iota(jnp.int32, (PAIR, PAIR), 1)
    return (a == b).astype(F32)


def by_head(x, reduce):
    half, width = PAIR // 2, x.shape[1]
    parts = [reduce(x[h * half : (h + 1) * half], axis=0, keepdims=True) for h in (0, 1)]
    return jnp.concatenate([jnp.broadcast_to(y, (half, width)) for y in parts], axis=0)


def lanes(p):
    if isinstance(p, int):
        return pl.ds(p * PAIR, PAIR)
    return pl.ds(pl.multiple_of(p * PAIR, PAIR), PAIR)


def conv_pair(table, padded):
    size = table.shape[0] // 4
    out = nn(table, padded)
    lane = lax.broadcasted_iota(jnp.int32, (size, PAIR), 1)
    return jnp.where(
        lane < PAIR // 2,
        out[:size] + out[2 * size : 3 * size],
        out[size : 2 * size] + out[3 * size :],
    )


class Group:
    def __init__(self, send, recv):
        self.row, self.me = lax.axis_index("rows"), lax.axis_index("seq")
        self.size = lax.axis_size("seq")
        self.send, self.recv, self.started = send, recv, []

    def peers(self):
        return [(self.row, (self.me + k) % self.size) for k in range(1, self.size)]

    def push(self, channel, pick_src, dst):
        copies = []
        for k, device in enumerate(self.peers()):
            copy = remote(
                pick_src(device[1]), dst, self.send.at[channel, k], self.recv.at[channel, k], device
            )
            copy.start()
            copies.append(copy)
        self.started += copies
        return copies

    def line_peers(self):
        n, line, core = self.size // 2, self.me // 2, self.me % 2
        return [(self.row, 2 * ((line + k) % n) + core) for k in range(1, n)]

    def go(self, channel, k, src, dst, device):
        copy = remote(src, dst, self.send.at[channel, k], self.recv.at[channel, k], device)
        copy.start()
        self.started.append(copy)
        return copy

    def share(self, parts):
        n, line, core = self.size // 2, self.me // 2, self.me % 2
        sibling = (self.row, 2 * line + 1 - core)
        there, here = [], []
        for channel, block in parts:
            mine = block(self.me)
            there.append(
                [self.go(channel, k, mine, mine, d) for k, d in enumerate(self.line_peers())]
            )
        for channel, block in parts:
            here.append(self.go(channel, n - 1, block(self.me), block(self.me), sibling))

        def arrive():
            for k in range(1, n):
                source = 2 * ((line - k + n) % n) + core
                for (channel, block), copies in zip(parts, there):
                    copies[k - 1].wait_recv()
                    got = block(source)
                    here.append(self.go(channel, n - 1 + k, got, got, sibling))
            for copy in here:
                copy.wait_recv()

        return arrive

    def halo(self, channel, source, padded, reach):
        length = source.shape[1]
        copies = []
        for which, (src_at, dst_at, step) in enumerate(
            ((length - reach, 0, 1), (0, length + reach, -1))
        ):
            there = (self.me + step + self.size) % self.size
            copy = remote(
                source.at[:, pl.ds(src_at, reach), :],
                padded.at[:, pl.ds(dst_at, reach), :],
                self.send.at[channel, which],
                self.recv.at[channel, which],
                (self.row, there),
            )
            goes = self.me < self.size - 1 if step == 1 else self.me > 0
            comes = self.me > 0 if step == 1 else self.me < self.size - 1
            pl.when(goes)(copy.start)
            copies.append((copy, goes, comes, dst_at))

        def arrive():
            for copy, goes, comes, dst_at in copies:
                pl.when(comes)(copy.wait_recv)

                @pl.when(jnp.logical_not(comes))
                def _():
                    shape = (padded.shape[0], reach, padded.shape[2])
                    padded[:, pl.ds(dst_at, reach), :] = jnp.zeros(shape, padded.dtype)

        def sent():
            for copy, goes, _, _ in copies:
                pl.when(goes)(copy.wait_send)

        return arrive, sent

    def finish(self):
        for copy in self.started:
            copy.wait_send()


def pinv_start(prob):
    total = by_head(jnp.sum(prob * prob, axis=1, keepdims=True), jnp.sum)
    return prob.T / total


def pinv_terms(p, z, unit):
    product = three(nn, p, z)
    prod = split(product)
    term_one = 7.0 * unit - product
    term_two = 15.0 * unit - three(nn, prod, split(term_one))
    term_three = 13.0 * unit - three(nn, prod, split(term_two))
    return prod, term_one, term_two, term_three


def band(line, length, reach):
    wide = jnp.broadcast_to(line, (length, line.shape[1]))
    return pltpu.roll(wide, 0, 1, stride=1, stride_axis=0)[:, : length + 2 * reach]


def set_lines(taps, lines, flip):
    count = taps.shape[1]
    lines[...] = jnp.zeros(lines.shape, F32)
    lines[:, :count] = taps[...]
    if flip:
        a = lax.broadcasted_iota(jnp.int32, (PAIR, PAIR), 0)
        b = lax.broadcasted_iota(jnp.int32, (PAIR, PAIR), 1)
        turn = (a + b == count - 1).astype(F32).astype(BF)
        high, low = split(lines[:, :PAIR])
        lines[:, :PAIR] = nn(high, turn) + nn(low, turn)


def fill_bands(lines, table, reach):
    pairs, rows = table.shape[0], table.shape[1] // 4
    for p in range(pairs):
        for h in (0, 1):
            high, low = split(band(lines[2 * p + h : 2 * p + h + 1, :], rows, reach))
            table[p, h * rows : (h + 1) * rows, :] = high
            table[p, (2 + h) * rows : (3 + h) * rows, :] = low


def gelu_parts(x):
    expo = jnp.exp(-0.5 * x * x)
    t = 1.0 / (1.0 + (0.3275911 * 0.7071067811865476) * jnp.abs(x))
    tail = -0.284496736 + t * (1.421413741 + t * (-1.453152027 + t * 1.061405429))
    tail = 0.5 * expo * t * (0.254829592 + t * tail)
    below = jnp.where(x >= 0.0, 1.0 - tail, tail)
    return x * below, below + x * expo * 0.3989422804014327


def norm_parts(resid):
    center = resid - jnp.mean(resid, axis=-1, keepdims=True)
    scale = lax.rsqrt(jnp.mean(center * center, axis=-1, keepdims=True) + norm_eps)
    return center * scale, scale


def norm_back(grad, gain, unit, scale):
    inner = grad * gain
    mean = jnp.mean(inner, axis=-1, keepdims=True)
    along = jnp.mean(inner * unit, axis=-1, keepdims=True)
    return scale * (inner - mean - unit * along)


def row_sum(x):
    return jnp.sum(x, axis=0, keepdims=True)


def front_kernel(
    reach,
    tokens, cot, qkv_w, out_w, up_w, down_w, vectors, taps,
    layer_out, grad_one, ga, sums, d_down, d_up, d_out,
    h_qkv, h_q, h_k, h_vpad, h_landq, h_landk, h_mix, h_p1, h_e, h_wt, h_p2o, h_zo, h_lvo,
    f_qkv, q, k, vpad, landq, landk, mix, p1, e, wt, p2o, zo, lvo,
    w_out, w_up, w_down, vecs, attn, v, table, f_vec, lb, numer, nrecv, stat, srecv, mstat, conv, fcol,
    g_down, g_up, active, slope, unit_one, scale_one, normed, low, low_t, total, ff, attn_t, *rest,
):
    keep_sem, o_sem, lines, vec_w, square = rest[-5:]
    rest = rest[:-5]
    set_lines(taps, lines, False)
    square[...] = jnp.zeros(square.shape, F32)
    square[: vectors.shape[0], : vectors.shape[1]] = vectors[...]
    vec_w[...] = jnp.zeros(vec_w.shape, F32)
    vec_w[:, :PAIR] = square[...].T[: vec_w.shape[0]]
    asm, stage = rest[:7], rest[7:14]
    g_send, g_recv, g_local, send, recv = rest[14:19]
    net, group = Net(g_send, g_recv), Group(send, recv)
    me, size = group.me, group.size
    n_seq, length, width = q.shape
    pairs = width // PAIR
    own = n_seq * pairs // size
    each = own * PAIR
    land_local = LAND // size
    seg = length // land_local
    scale = (PAIR // 2) ** -0.5
    greet(group.peers() + [net.to_first, net.to_second])

    def owner_seq(d):
        return d * own // pairs

    def owner_lanes(d):
        return pl.ds(pl.multiple_of((d * own % pairs) * PAIR, PAIR), each)

    plan = [(vec_w, f_vec, 0), (qkv_w, f_qkv, width), (qkv_w, f_qkv, 0), (qkv_w, f_qkv, 2 * width)]
    plan += [(out_w, w_out, 0), (up_w, w_up, 0), (down_w, w_down, 0)]
    pieces = []
    for w, (src, dst, base) in enumerate(plan):
        half = asm[w].shape[1]
        pieces.append(Gather(net, w, src, dst, base, half, asm[w], stage[w], g_local.at[w]))
    t_vec, t_k, t_q, t_v, t_out, t_up, t_down = pieces
    for piece in pieces[:4]:
        piece.spread()
    t_out.spread()
    t_up.spread()
    fill_bands(lines, table, reach)

    def project(dst, base, bias):
        step = 2 * PAIR
        for at in range(0, width, step):
            x = nn(tokens[...], f_qkv[:, base + at : base + at + step])
            if bias is not None:
                x = x + vecs[bias : bias + 1, at : at + step]
            dst[:, :, at : at + step] = x.astype(BF).reshape(n_seq, length, step)

    t_vec.step_one()
    t_k.step_one()
    t_q.step_one()
    t_vec.step_two()
    t_k.step_two()
    t_v.step_one()
    t_down.spread()
    t_vec.step_three()
    t_q.step_two()
    t_k.step_three()
    t_vec.close()
    vecs[...] = f_vec[:, :PAIR].astype(F32).T[: vecs.shape[0]]
    t_v.step_two()
    t_k.close()
    project(k, width, None)
    t_q.step_three()
    t_q.close()
    project(q, 0, 0)
    t_v.step_three()
    t_out.step_one()
    t_up.step_one()
    t_v.close()
    project(v, 2 * width, 1)

    def own_landmarks(s, carry):
        both = [
            jnp.mean(x[s].astype(F32).reshape(land_local, seg, width), axis=1) for x in (q, k)
        ]
        lb[me, s] = jnp.concatenate(both, axis=0).astype(BF)
        vpad[s, pl.ds(reach, length), :] = v[s]
        return carry

    lax.fori_loop(0, n_seq, own_landmarks, 0)
    landed = group.share([(1, lambda d: lb.at[d])])
    halo_in, halo_sent = group.halo(0, v, vpad, reach)
    t_out.step_two()
    t_down.step_one()
    landed()

    def whole_landmarks(s, carry):
        x = lb[:, s].astype(F32)
        landq[s] = x[:, :land_local].reshape(LAND, width).astype(BF)
        landk[s] = x[:, land_local:].reshape(LAND, width).astype(BF)
        return carry

    lax.fori_loop(0, n_seq, whole_landmarks, 0)
    lane_at = lax.broadcasted_iota(jnp.int32, (PAIR, PAIR), 1)

    def over_tokens(s, tile):
        for p in range(pairs):
            score = nt(apart(landq[s, :, lanes(p)]), k[s, :, lanes(p)]) * scale
            top = jnp.max(score, axis=1, keepdims=True)
            expo = jnp.exp(score - top)
            expo_low = expo.astype(BF)
            e[s * pairs + p] = expo_low
            numer[s, :, lanes(p)] = together(nn(expo_low, v[s, :, lanes(p)])).astype(BF)
            unit = s * pairs + p
            at = (unit // own) * 8 + unit % own
            tile = jnp.where(lane_at == at, top, tile)
            tile = jnp.where(lane_at == at + own, jnp.sum(expo, axis=1, keepdims=True), tile)
        return tile

    tile = lax.fori_loop(0, n_seq, over_tokens, jnp.zeros((PAIR, PAIR), F32))
    stat[...] = tile.T[: 8 * size].reshape(size, 8, PAIR)
    sums_in = group.push(
        2, lambda d: numer.at[owner_seq(d), :, owner_lanes(d)], nrecv.at[me]
    )
    stats_in = group.push(3, lambda d: stat.at[d], srecv.at[me])
    t_up.step_two()
    nrecv[me] = numer[owner_seq(me), :, owner_lanes(me)]
    srecv[me] = stat[me]

    block, unit_matrix = same_head(), eye()
    my_seq, my_pair = owner_seq(me), (me * own) % pairs
    for i in range(own):
        at = lanes(my_pair + i)
        score = nt(apart(landq[my_seq, :, at]), apart(landk[my_seq, :, at])) * scale
        score = jnp.where(block, score, -1e30)
        expo = jnp.exp(score - jnp.max(score, axis=1, keepdims=True))
        prob = expo / jnp.sum(expo, axis=1, keepdims=True)
        p2o[i] = prob
        zo[0, i] = pinv_start(prob)

    halo_in()
    per_step = n_seq * pairs // PINV_ITERS

    def over_landmarks(unit):
        s, p = unit // pairs, unit % pairs
        score = nt(apart(landk[s, :, lanes(p)]), q[s, :, lanes(p)]) * scale
        expo = jnp.exp(score - by_head(score, jnp.max))
        p1[unit] = expo / by_head(expo, jnp.sum)
        conv[s, :, lanes(p)] = conv_pair(table[p], vpad[s, :, lanes(p)])

    def pinv_step(step, carry):
        for i in range(own):
            z = split(zo[step, i])
            _, _, _, inner = pinv_terms(split(p2o[i]), z, unit_matrix)
            zo[step + 1, i] = 0.25 * three(nn, z, split(inner))
        for j in range(per_step):
            over_landmarks(step * per_step + j)
        return carry

    lax.fori_loop(0, PINV_ITERS // 2, pinv_step, 0)
    t_out.step_three()
    t_down.step_two()
    lax.fori_loop(PINV_ITERS // 2, PINV_ITERS, pinv_step, 0)

    for copy in sums_in + stats_in:
        copy.wait_recv()
    got = srecv[...]
    tops = got[:, :own]
    top = jnp.max(tops, axis=0, keepdims=True)
    factor = jnp.exp(tops - top)
    weight_sum = jnp.sum(factor * got[:, own : 2 * own], axis=0, keepdims=True)
    factor = factor / weight_sum
    spare = jnp.zeros((1, 8 - 2 * own, PAIR), F32)
    mstat[me] = jnp.concatenate([top, weight_sum, spare], axis=1)[0]
    spread = jnp.concatenate([factor, jnp.zeros((size, 8 - own, PAIR), F32)], axis=1)
    spread = spread.reshape(8 * size, PAIR)
    fcol[...] = jnp.concatenate([spread, jnp.zeros((PAIR - 8 * size, PAIR), F32)], axis=0).T
    half = PAIR // 2
    narrow = lax.broadcasted_iota(jnp.int32, (half, PAIR), 1) < half
    for i in range(own):
        at = pl.ds(i * PAIR, PAIR)
        mean = jnp.zeros((half, PAIR), F32)
        for src in range(size):
            column = fcol[:, src * 8 + i : src * 8 + i + 1]
            weight = jnp.where(narrow, column[:half], column[half:])
            mean = mean + weight * nrecv[src, :, at].astype(F32)
        lvo[:, at] = mean
        mixed = together(three(nn, split(zo[PINV_ITERS, i]), split(apart(mean))))
        mix[my_seq, :, lanes(my_pair + i)] = mixed.astype(BF)
    mixed_in = group.share(
        [
            (4, lambda d: mix.at[owner_seq(d), :, owner_lanes(d)]),
            (5, lambda d: mstat.at[d]),
        ]
    )
    t_up.step_three()
    mixed_in()

    rows = jnp.concatenate(
        [mstat[...].reshape(8 * size, PAIR), jnp.zeros((PAIR - 8 * size, PAIR), F32)], axis=0
    )
    rows = rows.T
    valid = (lane_at % 8 < own) & (lane_at < 8 * size)
    shift = jnp.where(valid, tile - rows, 0.0)
    den = jnp.where(valid, pltpu.roll(rows, PAIR - own, 1), 1.0)
    wt[...] = jnp.exp(shift) / den

    def result(s, carry):
        for p in range(pairs):
            prob = p1[s * pairs + p].astype(BF)
            out = tn(prob, apart(mix[s, :, lanes(p)])) + conv[s, :, lanes(p)]
            at = pl.ds(pl.multiple_of(s * length, length), length)
            attn[at, lanes(p)] = out.astype(BF)
        return carry

    lax.fori_loop(0, n_seq, result, 0)
    held = [f_qkv, q, k, vpad, landq, landk, mix, p1, e, wt, p2o, zo, lvo]
    homes = [h_qkv, h_q, h_k, h_vpad, h_landq, h_landk, h_mix, h_p1, h_e, h_wt, h_p2o, h_zo, h_lvo]
    keeps = [
        pltpu.make_async_copy(a, b, keep_sem.at[i]) for i, (a, b) in enumerate(zip(held, homes))
    ]
    for keep in keeps:
        keep.start()
    count = tokens.shape[0]
    hidden = w_up.shape[1]
    chunk_size = 2 * PAIR
    n_rows, n_wide = count // chunk_size, width // chunk_size
    row_groups = hidden // width
    sums[...] = jnp.zeros(sums.shape, F32)

    def row(i):
        return vecs[i : i + 1, :]

    def row_block(i):
        return pl.ds(pl.multiple_of(i * chunk_size, chunk_size), chunk_size)

    t_out.close()

    def first(i, carry):
        at = row_block(i)
        resid = tokens[at, :].astype(F32) + (nn(attn[at, :], w_out[...]) + row(2))
        unit, scale = norm_parts(resid)
        out = unit * row(6) + row(3)
        unit_one[at, :] = unit
        scale_one[at, :] = jnp.broadcast_to(scale, (chunk_size, PAIR))
        normed[at, :] = out
        low[at, :] = out.astype(BF)
        total[at, :] = jnp.broadcast_to(row(4), (chunk_size, width))
        return carry

    lax.fori_loop(0, n_rows, first, 0)
    t_down.step_three()
    t_up.close()
    low_t[...] = low[...].T
    attn_t[...] = attn[...].T

    def chunk(r, j):
        start = r * width + j * chunk_size
        return slice(start, start + chunk_size)

    def whole(r):
        return slice(r * width, (r + 1) * width)

    def gather_down(r):
        for n in range(n_wide):
            at = slice(n * chunk_size, (n + 1) * chunk_size)
            total[:, at] += nn(active[:, whole(r)], w_down[whole(r), at])

    for r in range(row_groups):
        for j in range(n_wide):
            f = chunk(r, j)
            bias = vecs[8 + r : 9 + r, j * chunk_size : (j + 1) * chunk_size]
            value, rate = gelu_parts(nn(low[...], w_up[:, f]) + bias)
            active[:, f] = value.astype(BF)
            slope[:, f] = rate.astype(BF)
        if r == 1:
            t_down.close()
        if r > 0:
            gather_down(r - 1)
    gather_down(row_groups - 1)

    def second(i, carry):
        at = row_block(i)
        unit, scale = norm_parts(normed[at, :] + total[at, :])
        layer_out[at, :] = (unit * row(7) + row(5)).astype(BF)
        up = cot[at, :].astype(F32)
        grad = norm_back(up, row(7), unit, scale)
        total[at, :] = grad
        grad = grad.astype(BF)
        ff[at, :] = grad
        sums[4:5, :] += row_sum(grad.astype(F32))
        sums[5:6, :] += row_sum(up)
        sums[7:8, :] += row_sum(up * unit)
        return carry

    lax.fori_loop(0, n_rows, second, 0)

    def leave(r):
        f = whole(r)
        return [
            pltpu.make_async_copy(g_down.at[r % 2], d_down.at[f, :], o_sem.at[0, r]),
            pltpu.make_async_copy(g_up.at[r % 2], d_up.at[:, f], o_sem.at[1, r]),
        ]

    def weight_grads(r):
        if r > 1:
            for copy in leave(r - 2):
                copy.wait()
        for j in range(n_wide):
            f = chunk(r, j)
            at = slice(j * chunk_size, (j + 1) * chunk_size)
            g_up[r % 2, :, at] = nn(low_t[...], slope[:, f]).astype(BF)
            g_down[r % 2, at, :] = tn(active[:, f], ff[...]).astype(BF)
        for n in range(n_wide):
            at = slice(n * chunk_size, (n + 1) * chunk_size)
            total[:, at] += nt(slope[:, whole(r)], w_up[at, whole(r)])
        for copy in leave(r):
            copy.start()

    for r in range(row_groups):
        for j in range(n_wide):
            f = chunk(r, j)
            grad = (nt(ff[...], w_down[f, :]) * slope[:, f].astype(F32)).astype(BF)
            sums[8 + r : 9 + r, j * chunk_size : (j + 1) * chunk_size] = row_sum(grad.astype(F32))
            slope[:, f] = grad
        if r > 0:
            weight_grads(r - 1)
    weight_grads(row_groups - 1)

    def third(i, carry):
        at = row_block(i)
        unit = unit_one[at, :]
        up = total[at, :]
        grad = norm_back(up, row(6), unit, scale_one[at, :1])
        grad_one[at, :] = grad
        grad = grad.astype(BF)
        low[at, :] = grad
        ga[at, :] = nt(grad, w_out[...]).astype(BF)
        sums[2:3, :] += row_sum(grad.astype(F32))
        sums[3:4, :] += row_sum(up)
        sums[6:7, :] += row_sum(up * unit)
        return carry

    lax.fori_loop(0, n_rows, third, 0)
    for r in (row_groups - 2, row_groups - 1):
        for copy in leave(r):
            copy.wait()
    g_up[0] = nn(attn_t[...], low[...]).astype(BF)
    last = pltpu.make_async_copy(g_up.at[0], d_out, o_sem.at[2, 0])
    last.start()
    for keep in keeps:
        keep.wait()
    last.wait()
    halo_sent()
    group.finish()
    net.finish()


def front(tokens, cot, matrices, vectors, taps, seq_size, reach):
    n_seq, length, width = tokens.shape
    pairs = width // PAIR
    units = n_seq * pairs
    own = units // seq_size
    n_dev = 4 * seq_size
    table = jax.ShapeDtypeStruct((vectors.shape[1], 2 * PAIR), F32)
    line_size = seq_size // 2
    vmem, hbm = pl.BlockSpec(memory_space=pltpu.VMEM), pl.BlockSpec(memory_space=pltpu.HBM)
    shape = jax.ShapeDtypeStruct
    land = shape((n_seq, LAND, width), BF)
    qkv_w, out_w, up_w, down_w = matrices
    count, hidden = n_seq * length, up_w.shape[1]
    flat = (count, width)
    whole = [shape((n_dev * x.shape[0], x.shape[1]), BF) for x in matrices]
    asm = [(table.shape[0], table.shape[1] // 2)] + [(qkv_w.shape[0], width // 2)] * 3
    asm += [(x.shape[0], x.shape[1] // 2) for x in (out_w, up_w, down_w)]
    n_sem = line_size + GATHER_SEMS
    kept = [
        whole[0],
        shape(tokens.shape, BF), shape(tokens.shape, BF),
        shape((n_seq, length + 2 * reach, width), BF), land, land, land,
        shape((units, PAIR, length), F32), shape((units, PAIR, length), BF),
        shape((PAIR, PAIR), F32), shape((own, PAIR, PAIR), F32),
        shape((PINV_ITERS + 1, own, PAIR, PAIR), F32), shape((LAND, own * PAIR), F32),
    ]
    return pl.pallas_call(
        functools.partial(front_kernel, reach),
        out_shape=[shape(flat, BF), shape(flat, F32), shape(flat, BF), shape((16, width), F32)]
        + [whole[3], whole[2], whole[1]]
        + kept,
        in_specs=[vmem] * 8,
        out_specs=[vmem] * 4 + [hbm] * (3 + len(kept)),
        scratch_shapes=[pltpu.VMEM(x.shape, x.dtype) for x in kept]
        + [pltpu.VMEM(x.shape, BF) for x in whole[1:]]
        + [
            pltpu.VMEM((16, width), F32),
            pltpu.VMEM(flat, BF),
            pltpu.VMEM(tokens.shape, BF),
            pltpu.VMEM((pairs, 4 * length, length + 2 * reach), BF),
            pltpu.VMEM((n_dev * table.shape[0], table.shape[1]), BF),
            pltpu.VMEM((seq_size, n_seq, 2 * LAND // seq_size, width), BF),
            pltpu.VMEM((n_seq, LAND, width), BF),
            pltpu.VMEM((seq_size, LAND, own * PAIR), BF),
            pltpu.VMEM((seq_size, 8, PAIR), F32),
            pltpu.VMEM((seq_size, 8, PAIR), F32),
            pltpu.VMEM((seq_size, 8, PAIR), F32),
            pltpu.VMEM((n_seq, length, width), F32),
            pltpu.VMEM((PAIR, PAIR), F32),
            pltpu.VMEM((2, width, width), BF),
            pltpu.VMEM((2, width, width), BF),
            pltpu.VMEM((count, hidden), BF),
            pltpu.VMEM((count, hidden), BF),
            pltpu.VMEM(flat, F32),
            pltpu.VMEM((count, PAIR), F32),
            pltpu.VMEM(flat, F32),
            pltpu.VMEM(flat, BF),
            pltpu.VMEM((width, count), BF),
            pltpu.VMEM(flat, F32),
            pltpu.VMEM(flat, BF),
            pltpu.VMEM((width, count), BF),
        ]
        + [pltpu.VMEM((2 * r, h), F32) for r, h in asm]
        + [pltpu.VMEM((2 * r, h), BF) for r, h in asm]
        + [
            pltpu.SemaphoreType.DMA((7, n_sem)),
            pltpu.SemaphoreType.DMA((7, n_sem)),
            pltpu.SemaphoreType.DMA((7,)),
            pltpu.SemaphoreType.DMA((6, seq_size)),
            pltpu.SemaphoreType.DMA((6, seq_size)),
            pltpu.SemaphoreType.DMA((len(kept),)),
            pltpu.SemaphoreType.DMA((3, hidden // width)),
            pltpu.VMEM((2 * pairs, 2 * PAIR), F32),
            pltpu.VMEM(table.shape, F32),
            pltpu.VMEM((PAIR, PAIR), F32),
        ],
        compiler_params=pltpu.CompilerParams(
            collective_id=0, has_side_effects=True, vmem_limit_bytes=61 * 1024 * 1024
        ),
        name="front",
    )(tokens.reshape(flat), cot.reshape(flat), *matrices, vectors, taps)


def back_kernel(
    reach, n_taps,
    ga, tokens, resid, f_qkv, vec_rows, taps, d_down, d_up, d_out,
    q, k, vpad, landq, landk, mix, p1, e, wt, p2o, zo, lvo,
    input_grad, s_qkv, s_out, s_up, s_down, s_small,
    grad, tapg, table, tok_t, outbox, small_box,
    gpad, gmix, gmr, low, gfull, mstat, gcol, gq, gv, lkp, lpart, lpr, lsum, gsum, gpart, dz, dp,
    skew, own_g, *rest,
):
    bufs, (g_send, g_recv, g_local, send, recv, lines) = rest[:-6], rest[-6:]
    net, group = Net(g_send, g_recv), Group(send, recv)
    me, size = group.me, group.size
    n_seq, length, width = q.shape
    pairs = width // PAIR
    own = n_seq * pairs // size
    each = own * PAIR
    land_local = LAND // size
    seg = length // land_local
    half = PAIR // 2
    scale = half**-0.5
    greet(group.peers() + [net.to_first, net.to_second])

    def owner_seq(d):
        return d * own // pairs

    def owner_lanes(d):
        return pl.ds(pl.multiple_of((d * own % pairs) * PAIR, PAIR), each)

    plan = [(s_down, 0), (s_up, 0), (s_out, 0)]
    plan += [(s_qkv, 2 * width), (s_qkv, 0), (s_qkv, width), (s_small, 0)]
    pieces = []
    for w, (out, base) in enumerate(plan):
        own_bufs = bufs[6 * w : 6 * w + 6]
        pieces.append(Scatter(net, w, out, base, own_bufs[0].shape[1], own_bufs))
    r_down, r_up, r_out, r_v, r_q, r_k, r_small = pieces

    def open_whole(w, src):
        piece = pieces[w]
        other, here = [columns(0, c, piece.half) for c in (1 - net.core, net.core)]
        own_part = pltpu.make_async_copy(src.at[:, here], piece.acc, g_local.at[w])
        piece.open(src.at[:, other], own_part)

    def open_weight(piece, box):
        step = 2 * PAIR
        rows = tok_t.shape[0]

        def one(i, carry):
            at = pl.ds(pl.multiple_of(i * step, step), step)
            x = tok_t[at, :]
            other, here = [columns(piece.base, c, piece.half) for c in (1 - net.core, net.core)]
            outbox[box, at, :] = nn(x, grad[:, other]).astype(BF)
            piece.acc[at, :] = nn(x, grad[:, here]).astype(BF)
            return carry

        lax.fori_loop(0, rows // step, one, 0)
        piece.open(outbox.at[box])

    open_whole(0, d_down)
    halo_in, halo_sent = group.halo(0, ga, gpad, reach)

    def first(s, carry):
        for p in range(pairs):
            unit, at = s * pairs + p, lanes(p)
            own_ga = ga[s, :, at]
            gpad[s, pl.ds(reach, length), at] = own_ga
            prob = p1[unit]
            gmix[s, :, at] = together(nn(prob.astype(BF), own_ga)).astype(BF)
            back = nt(apart(mix[s, :, at]), own_ga)
            low[unit] = (prob * (back - by_head(prob * back, jnp.sum))).astype(BF)
        return carry

    lax.fori_loop(0, n_seq, first, 0)
    chips, my_line, my_core = size // 2, me // 2, me % 2
    core_lanes = [pl.ds(pl.multiple_of(c * each, PAIR), each) for c in (my_core, 1 - my_core)]
    sibling = (group.row, 2 * my_line + 1 - my_core)
    gmix_sib = group.go(1, chips, gmix.at[:, :, core_lanes[1]], gsum, sibling)
    r_down.step_one()
    gmix_sib.wait_recv()
    gpart[...] = gmix[:, :, core_lanes[0]] + gsum[...]
    gmix_in = []
    for kk, device in enumerate(group.line_peers()):
        other = device[1] // 2
        gmix_in.append(group.go(1, kk, gpart.at[other], gmr.at[my_line], device))
    gmr[my_line] = gpart[my_line]
    open_whole(1, d_up)
    open_whole(2, d_out)
    set_lines(taps, lines, True)
    fill_bands(lines, table, reach)
    halo_in()
    skew[...] = jnp.zeros(skew.shape, F32)

    def beside(s, carry):
        one, two_mask = lane_masks(BF)
        for p in range(pairs):
            unit, at = s * pairs + p, lanes(p)
            own_ga, padded = ga[s, :, at], vpad[s, :, at]
            gs = low[unit]
            gq[s, :, at] = tn(gs, apart(landk[s, :, at])) * scale
            lkp[s, :, at] = together(nn(gs, q[s, :, at])) * scale
            gv[s, :, at] = conv_pair(table[p], gpad[s, :, at])
            both = jnp.concatenate([own_ga * one, own_ga * two_mask], axis=0)
            skew[2 * p : 2 * p + 2, :, : length + 2 * reach] += nt(both, padded).reshape(
                2, length, length + 2 * reach
            )
        return carry

    lax.fori_loop(0, n_seq, beside, 0)
    lane_at = lax.broadcasted_iota(jnp.int32, (PAIR, PAIR), 1)
    wide = skew.shape[2]
    for h in range(2 * pairs):
        total = skew[h, :8, :]
        for row in range(8, length, 8):
            total = total + pltpu.roll(skew[h, row : row + 8, :], wide - row, 1)
        tapg[h] = total[:, :PAIR]
    r_up.step_one()
    tok_t[...] = tokens[...].T

    for copy in gmix_in:
        copy.wait_recv()
    my_seq, my_pair = owner_seq(me), (me * own) % pairs
    tile = jnp.zeros((PAIR, PAIR), F32)
    for i in range(own):
        at = pl.ds(i * PAIR, PAIR)
        total = gmr[0, :, at].astype(F32)
        for src in range(1, chips):
            total = total + gmr[src, :, at].astype(F32)
        total = split(apart(total))
        means = apart(lvo[:, at])
        back = together(three(tn, split(zo[PINV_ITERS, i]), total)).astype(BF)
        own_g[:, at] = back
        column = jnp.sum(apart(back.astype(F32)) * means, axis=1, keepdims=True)
        tile = jnp.where(lane_at == i, column, tile)
        dz[i] = three(nt, total, split(means))
        dp[i] = jnp.zeros((PAIR, PAIR), F32)
    mstat[me] = tile.T[:8]
    gfull[my_seq, :, owner_lanes(me)] = own_g[...]
    g_in = group.share(
        [
            (2, lambda d: gfull.at[owner_seq(d), :, owner_lanes(d)]),
            (3, lambda d: mstat.at[d]),
        ]
    )
    g_in()
    rows = jnp.concatenate(
        [mstat[...].reshape(8 * size, PAIR), jnp.zeros((PAIR - 8 * size, PAIR), F32)], axis=0
    )
    gcol[...] = rows.T
    unit_matrix = eye()

    def third(unit):
        s, p = unit // pairs, unit % pairs
        at = lanes(p)
        here = (unit // own) * 8 + unit % own
        picked = lane_at == here
        weight = jnp.sum(jnp.where(picked, wt[...], 0.0), axis=1, keepdims=True)
        offset = jnp.sum(jnp.where(picked, gcol[...], 0.0), axis=1, keepdims=True)
        g = apart(gfull[s, :, at])
        prob = e[unit].astype(F32) * weight
        back = nt(g, vpad[s, pl.ds(reach, length), at]) - offset
        gs = (prob * back).astype(BF)
        values = gv[s, :, at] + tn(prob.astype(BF), g)
        v_at = pl.ds(pl.multiple_of(2 * width + p * PAIR, PAIR), PAIR)
        rows = pl.ds(pl.multiple_of(s * length, length), length)
        grad[rows, v_at] = values.astype(BF)
        rows = pl.ds(pl.multiple_of(s * length, length), length)
        grad[rows, pl.ds(pl.multiple_of(width + p * PAIR, PAIR), PAIR)] = (
            tn(gs, apart(landq[s, :, at])) * scale
        ).astype(BF)
        lq = (together(nn(gs, k[s, :, at])) * scale).reshape(size, land_local, PAIR)
        lk = lkp[s, :, at].reshape(size, land_local, PAIR)
        both = jnp.concatenate([lq, lk], axis=1).astype(BF)
        lpart[:, :, s, :, at] = both.reshape(chips, 2, 2 * land_local, PAIR)

    per_step = n_seq * pairs // PINV_ITERS

    def pinv_back(step, carry):
        at_step = PINV_ITERS - 1 - step
        for i in range(own):
            p, z = split(p2o[i]), split(zo[at_step, i])
            prod, one, two_term, three_term = pinv_terms(p, z, unit_matrix)
            d_out = dz[i] * 0.25
            d_out_s = split(d_out)
            d_three = split(three(tn, z, d_out_s))
            d_two = split(-three(tn, prod, d_three))
            d_one = -three(tn, prod, d_two)
            d_prod = -three(nt, d_three, split(two_term)) - three(nt, d_two, split(one)) - d_one
            d_prod = split(d_prod)
            dp[i] += three(nt, d_prod, z)
            dz[i] = three(nt, d_out_s, split(three_term)) + three(tn, p, d_prod)
        for j in range(per_step):
            third(step * per_step + j)
        return carry

    third_of = PINV_ITERS // 3
    lax.fori_loop(0, third_of, pinv_back, 0)
    r_down.step_two()
    r_out.step_one()
    lax.fori_loop(third_of, 2 * third_of, pinv_back, 0)
    lax.fori_loop(2 * third_of, PINV_ITERS, pinv_back, 0)
    r_up.step_two()
    r_out.step_two()

    for i in range(own):
        at = pl.ds(i * PAIR, PAIR)
        prob = p2o[i]
        squares = by_head(jnp.sum(prob * prob, axis=1, keepdims=True), jnp.sum)
        d_start = dz[i].T
        inner = by_head(jnp.sum(d_start * prob, axis=1, keepdims=True), jnp.sum)
        d_prob = dp[i] + d_start / squares - 2.0 * prob * inner / (squares * squares)
        gs = prob * (d_prob - jnp.sum(prob * d_prob, axis=1, keepdims=True))
        gs = split(gs)
        here = lanes(my_pair + i)
        lq, lk = apart(landq[my_seq, :, here]), apart(landk[my_seq, :, here])
        query = together(nn(gs[0], lk) + nn(gs[1], lk)) * scale
        key = together(tn(gs[0], lq) + tn(gs[1], lq)) * scale
        both = [x.reshape(size, land_local, PAIR) for x in (query, key)]
        both = jnp.concatenate(both, axis=1).reshape(chips, 2, 2 * land_local, PAIR)
        lpart[:, :, my_seq, :, here] = (lpart[:, :, my_seq, :, here].astype(F32) + both).astype(BF)
    land_sib = group.go(4, chips, lpart.at[:, 1 - my_core], lsum, sibling)
    land_sib.wait_recv()

    def add_lands(i, carry):
        lsum[i] = lsum[i] + lpart[i, my_core]
        return carry

    lax.fori_loop(0, chips, add_lands, 0)
    lpr[my_line] = lsum[my_line]
    land_in = []
    for kk, device in enumerate(group.line_peers()):
        land_in.append(group.go(4, kk, lsum.at[device[1] // 2], lpr.at[my_line], device))
    open_weight(r_v, 0)
    for copy in land_in:
        copy.wait_recv()

    def close(s, carry):
        for p in range(pairs):
            at = lanes(p)
            total = lpr[0, s, :, at].astype(F32)
            for src in range(1, chips):
                total = total + lpr[src, s, :, at].astype(F32)
            total = total * (1.0 / seg)
            spread = [
                jnp.concatenate(
                    [jnp.broadcast_to(x[i : i + 1], (seg, PAIR)) for i in range(land_local)], axis=0
                )
                for x in (total[:land_local], total[land_local:])
            ]
            rows = pl.ds(pl.multiple_of(s * length, length), length)
            grad[rows, at] = (gq[s, :, at] + spread[0]).astype(BF)
            key_at = pl.ds(width + p * PAIR, PAIR)
            grad[rows, key_at] = (grad[rows, key_at].astype(F32) + spread[1]).astype(BF)
        return carry

    lax.fori_loop(0, n_seq, close, 0)
    r_down.step_three()
    open_weight(r_q, 1)
    r_v.step_one()
    open_weight(r_k, 2)
    r_q.step_one()
    r_up.step_three()

    def column_sums(base):
        total = jnp.zeros((1, width), F32)
        for s in range(n_seq):
            x = grad[s * length : (s + 1) * length, base : base + width].astype(F32)
            total = total + jnp.sum(x, axis=0, keepdims=True)
        return total

    count = vec_rows.shape[0]
    which = lax.broadcasted_iota(jnp.int32, (count, width), 0)
    table_rows = vec_rows[...]
    table_rows = jnp.where(which == 0, column_sums(0), table_rows)
    table_rows = jnp.where(which == 1, column_sums(2 * width), table_rows)
    table_rows = jnp.concatenate([table_rows, jnp.zeros((PAIR - count, width), F32)], axis=0)
    left = table_rows.T
    sums = tapg[:, 0, :]
    for b in range(1, 8):
        sums = sums + pltpu.roll(tapg[:, b, :], PAIR - b, 1)
    shard = r_small.rows
    sums = jnp.concatenate([sums, jnp.zeros((shard - sums.shape[0], PAIR), F32)], axis=0)
    right = jnp.broadcast_to(sums[None], (width // shard, shard, PAIR)).reshape(width, PAIR)
    zero = net.core == 0
    r_small.acc[...] = jnp.where(zero, left, right)
    small_box[...] = jnp.where(zero, right, left)
    r_small.open(small_box)
    r_v.step_two()
    r_k.step_one()
    r_out.step_three()
    r_down.step_four()

    def inputs(i, carry):
        step = 2 * PAIR
        rows = pl.ds(pl.multiple_of(i * step, step), step)
        for at in range(0, width, step):
            x = nt(grad[rows, :], f_qkv[at : at + step, :])
            out = x + resid[rows, at : at + step]
            input_grad[rows, at : at + step] = out.astype(BF)
        return carry

    lax.fori_loop(0, tokens.shape[0] // (2 * PAIR), inputs, 0)
    r_small.step_one()
    r_q.step_two()
    r_k.step_two()
    r_v.step_three()
    r_small.step_two()
    r_up.step_four()
    r_q.step_three()
    r_k.step_three()
    r_out.step_four()
    r_v.step_four()
    r_small.step_three()
    r_q.step_four()
    r_k.step_four()
    r_small.step_four()
    for piece in pieces:
        piece.close()
    halo_sent()
    group.finish()
    net.finish()


def back(
    ga, tokens, resid, f_qkv, vec_rows, taps, d_down, d_up, d_out, kept, shards, seq_size, reach
):
    q = kept[0]
    n_seq, length, width = q.shape
    pairs = width // PAIR
    units = n_seq * pairs
    own = units // seq_size
    line_size = seq_size // 2
    vmem, hbm = pl.BlockSpec(memory_space=pltpu.VMEM), pl.BlockSpec(memory_space=pltpu.HBM)
    shape = jax.ShapeDtypeStruct
    part = 2 * LAND // seq_size
    s_qkv, s_out, s_up, s_down = [shape(x.shape, F32) for x in shards]
    s_small = shape((s_qkv.shape[0], 2 * PAIR), F32)
    bufs = []
    for x in (s_down, s_up, s_out):
        bufs += scatter_scratch(x.shape[0], x.shape[1] // 2, BF, line_size)
    for _ in range(3):
        bufs += scatter_scratch(s_qkv.shape[0], width // 2, BF, line_size)
    bufs += scatter_scratch(s_qkv.shape[0], PAIR, F32, line_size)
    return pl.pallas_call(
        functools.partial(back_kernel, reach, 2 * reach + 1),
        out_shape=[shape(tokens.shape, BF), s_qkv, s_out, s_up, s_down, s_small],
        in_specs=[vmem] * 6 + [hbm] * 3 + [vmem] * 12,
        out_specs=[vmem] * 6,
        scratch_shapes=[
            pltpu.VMEM((n_seq * length, 3 * width), BF),
            pltpu.VMEM((2 * pairs, 8, PAIR), F32),
            pltpu.VMEM((pairs, 4 * length, length + 2 * reach), BF),
            pltpu.VMEM((width, n_seq * length), BF),
            pltpu.VMEM((3, width, width // 2), BF),
            pltpu.VMEM((width, PAIR), F32),
            pltpu.VMEM((n_seq, length + 2 * reach, width), BF),
            pltpu.VMEM((n_seq, LAND, width), BF),
            pltpu.VMEM((seq_size // 2, LAND, own * PAIR), BF),
            pltpu.VMEM((units, PAIR, length), BF),
            pltpu.VMEM((n_seq, LAND, width), BF),
            pltpu.VMEM((seq_size, 8, PAIR), F32),
            pltpu.VMEM((PAIR, PAIR), F32),
            pltpu.VMEM((n_seq, length, width), F32),
            pltpu.VMEM((n_seq, length, width), F32),
            pltpu.VMEM((n_seq, LAND, width), F32),
            pltpu.VMEM((seq_size // 2, 2, n_seq, part, width), BF),
            pltpu.VMEM((seq_size // 2, n_seq, part, width), BF),
            pltpu.VMEM((seq_size // 2, n_seq, part, width), BF),
            pltpu.VMEM((n_seq, LAND, own * PAIR), BF),
            pltpu.VMEM((n_seq, LAND, own * PAIR), BF),
            pltpu.VMEM((own, PAIR, PAIR), F32),
            pltpu.VMEM((own, PAIR, PAIR), F32),
            pltpu.VMEM((2 * pairs, length, 2 * PAIR), F32),
            pltpu.VMEM((LAND, own * PAIR), BF),
        ]
        + bufs
        + [
            pltpu.SemaphoreType.DMA((7, line_size + SCATTER_SEMS)),
            pltpu.SemaphoreType.DMA((7, line_size + SCATTER_SEMS)),
            pltpu.SemaphoreType.DMA((7,)),
            pltpu.SemaphoreType.DMA((6, seq_size)),
            pltpu.SemaphoreType.DMA((6, seq_size)),
            pltpu.VMEM((2 * pairs, 2 * PAIR), F32),
        ],
        compiler_params=pltpu.CompilerParams(
            collective_id=1, has_side_effects=True, vmem_limit_bytes=60 * 1024 * 1024
        ),
        name="back",
    )(ga, tokens, resid, f_qkv, vec_rows, taps, d_down, d_up, d_out, *kept)


def update_kernel(rates, n_in, *refs):
    n_mat = len(rates) - 2
    homes, outs = refs[:n_in], refs[n_in : n_in + 3 * n_mat + 8]
    ins, sem = refs[n_in + 3 * n_mat + 8 : -1], refs[-1]
    own = 4 * n_mat + 7
    moves = []
    for i, (src, dst) in enumerate(zip(homes, ins)):
        moves.append(pltpu.make_async_copy(src, dst, sem.at[i]))
        moves[-1].start()
    for i in range(n_mat):
        for move in moves[4 * i : 4 * i + 4]:
            move.wait()
        weight, first, second, grad = ins[4 * i : 4 * i + 4]
        new = adam_step(weight[...], first[...], second[...], grad[...], *rates[i])
        for out, value in zip(outs[3 * i : 3 * i + 3], new):
            out[...] = value
    passed = []
    for i in range(n_in - own):
        moves[own + i].wait()
        out = outs[3 * n_mat + 6 + i]
        passed.append(pltpu.make_async_copy(ins[own + i], out, sem.at[n_in + i]))
        passed[-1].start()
    for move in moves[4 * n_mat : own]:
        move.wait()
    small = ins[4 * n_mat]
    vec, tap = ins[own - 6 : own - 3], ins[own - 3 : own]
    rows, count = vec[0].shape
    grad = small[:, :PAIR].T[:rows, :count]
    new = adam_step(*[x[...] for x in vec], grad, *rates[n_mat])
    for out, value in zip(outs[3 * n_mat : 3 * n_mat + 3], new):
        out[...] = value
    heads, taps = tap[0].shape
    grad = small[:, PAIR:][:heads, :taps]
    new = adam_step(*[x[...] for x in tap], grad, *rates[n_mat + 1])
    for out, value in zip(outs[3 * n_mat + 3 : 3 * n_mat + 6], new):
        out[...] = value
    for move in passed:
        move.wait()


def update(matrices, small, vec, tap, others):
    decay = ((rate_matrix, decay_rate), (rate_output, decay_rate))
    rates = [decay[0], decay[1], decay[0], decay[0], (rate_vector, 0.0), (rate_taps, 0.0)]
    vmem = pl.BlockSpec(memory_space=pltpu.VMEM)
    shape = [jax.ShapeDtypeStruct(x[0].shape, F32) for x in (*matrices, vec, tap) for _ in range(3)]
    shape += [jax.ShapeDtypeStruct(x.shape, x.dtype) for x in others]
    args = [x for group in matrices for x in group] + [small, *vec, *tap]
    hbm = pl.BlockSpec(memory_space=pltpu.HBM)
    n_in = len(args) + len(others)
    return pl.pallas_call(
        functools.partial(update_kernel, rates, n_in),
        out_shape=shape,
        in_specs=[hbm] * n_in,
        out_specs=[vmem] * (len(shape) - len(others)) + [hbm] * len(others),
        scratch_shapes=[pltpu.VMEM(x.shape, x.dtype) for x in (*args, *others)]
        + [pltpu.SemaphoreType.DMA((n_in + len(others),))],
        compiler_params=pltpu.CompilerParams(vmem_limit_bytes=60 * 1024 * 1024),
        name="update",
    )(*args, *others)


def kernels_fit(args):
    tokens, _, *matrices = args[:6]
    taps = args[7]
    seq_size = lax.axis_size("seq")
    n_seq, length, width = tokens.shape
    units = n_seq * width // PAIR
    own = units // seq_size
    return (
        lax.axis_size("rows") == 4
        and seq_size == 8
        and all(x.shape[0] % 24 == 0 and x.shape[1] % 256 == 0 for x in matrices)
        and width // taps.shape[0] == PAIR // 2
        and length == PAIR
        and taps.shape[1] == 33
        and taps.shape[0] <= matrices[0].shape[0]
        and units == own * seq_size
        and seq_size == 2 * n_seq
        and width == 2 * own * PAIR
        and 2 * own <= 8
        and (width // PAIR) % own == 0
        and units % PINV_ITERS == 0
        and LAND == 8 * seq_size
        and matrices[2].shape[1] == 4 * width
        and args[6].shape[0] == 12
    )


def with_kernels(
    tokens, cotangent, qkv_weight, out_weight, up_weight, down_weight, vectors, taps,
    qkv_first, qkv_second, out_first, out_second, up_first, up_second, down_first, down_second,
    vec_first, vec_second, tap_first, tap_second,
):
    seq_count, local_len, model_width = tokens.shape
    head_count, tap_count = taps.shape
    seq_size = lax.axis_size("seq")
    reach = tap_count // 2
    row_count = seq_count * local_len
    matrices = (qkv_weight, out_weight, up_weight, down_weight)
    flat_in = tokens.reshape(row_count, model_width)
    layer_out, grad_resid_one, grad_attn, vec_rows, grad_down, grad_up, grad_out, full_qkv, *kept = (
        front(tokens, cotangent, matrices, vectors, taps, seq_size, reach)
    )
    input_grad, summed_qkv, summed_out, summed_up, summed_down, small = back(
        grad_attn.reshape(tokens.shape), flat_in, grad_resid_one, full_qkv, vec_rows, taps,
        grad_down, grad_up, grad_out,
        kept, matrices, seq_size, reach,
    )
    *new, out_tokens, input_grad = update(
        [
            (qkv_weight, qkv_first, qkv_second, summed_qkv),
            (out_weight, out_first, out_second, summed_out),
            (up_weight, up_first, up_second, summed_up),
            (down_weight, down_first, down_second, summed_down),
        ],
        small,
        (vectors, vec_first, vec_second),
        (taps, tap_first, tap_second),
        (layer_out, input_grad),
    )
    return (out_tokens.reshape(tokens.shape), input_grad.reshape(tokens.shape), *new)


def on_device(*args):
    return with_kernels(*args) if kernels_fit(args) else with_collectives(*args)


def solution(mesh):
    return jax.shard_map(
        on_device,
        mesh=mesh,
        in_specs=(
            P("rows", "seq", None),
            P("rows", "seq", None),
            P(("rows", "seq"), None),
            P(("rows", "seq"), None),
            P(("rows", "seq"), None),
            P(("rows", "seq"), None),
            P(None, ("rows", "seq")),
            P(),
            P(("rows", "seq"), None),
            P(("rows", "seq"), None),
            P(("rows", "seq"), None),
            P(("rows", "seq"), None),
            P(("rows", "seq"), None),
            P(("rows", "seq"), None),
            P(("rows", "seq"), None),
            P(("rows", "seq"), None),
            P(None, ("rows", "seq")),
            P(None, ("rows", "seq")),
            P(),
            P(),
        ),
        out_specs=(
            P("rows", "seq", None),
            P("rows", "seq", None),
            P(("rows", "seq"), None),
            P(("rows", "seq"), None),
            P(("rows", "seq"), None),
            P(("rows", "seq"), None),
            P(("rows", "seq"), None),
            P(("rows", "seq"), None),
            P(("rows", "seq"), None),
            P(("rows", "seq"), None),
            P(("rows", "seq"), None),
            P(("rows", "seq"), None),
            P(("rows", "seq"), None),
            P(("rows", "seq"), None),
            P(None, ("rows", "seq")),
            P(None, ("rows", "seq")),
            P(None, ("rows", "seq")),
            P(),
            P(),
            P(),
        ),
        check_vma=False,
    )
```

```python
import functools

import jax
import jax.numpy as jnp
from jax import lax
from jax.experimental import pallas as pl
from jax.experimental.pallas import tpu as pltpu
from jax.sharding import PartitionSpec as P

LAND = 64
PINV_ITERS = 6


top_precision = lax.Precision.HIGHEST
norm_eps = 1e-05
beta_one = 0.9
beta_two = 0.999
corr_one = 1.0 - 0.9**10
corr_two = 1.0 - 0.999**10
adam_eps = 1e-08
decay_rate = 0.01
rate_matrix = 0.03
rate_output = 0.12
rate_vector = 0.3
rate_taps = 0.08


def with_halo(x, sides, width):
    for axis, dim in sides:
        size, length = (lax.axis_size(axis), x.shape[dim])
        up = [(i, (i + 1) % size) for i in range(size - 1)]
        down = [(j, i) for i, j in up]
        last = lax.slice_in_dim(x, length - width, length, axis=dim)
        initial = lax.slice_in_dim(x, 0, width, axis=dim)
        before = lax.ppermute(last, axis, up)
        after = lax.ppermute(initial, axis, down)
        x = jnp.concatenate([before, x, after], axis=dim)
    return x


def layer_norm(residual, gain_row, shift_row):
    center = residual - jnp.mean(residual, axis=-1, keepdims=True)
    spread = jnp.mean(center * center, axis=-1, keepdims=True)
    return center * lax.rsqrt(spread + norm_eps) * gain_row + shift_row


def normalized_rows(scores):
    expo = jnp.exp(scores - jnp.max(scores, axis=-1, keepdims=True))
    return expo / jnp.sum(expo, axis=-1, keepdims=True)


def softmax_back(probability, grad_in):
    return probability * (grad_in - jnp.sum(probability * grad_in, axis=-1, keepdims=True))


def gelu_exact(inputs):
    return jax.nn.gelu(inputs, approximate=False)


def pseudo_inverse(matrix):
    identity = jnp.eye(matrix.shape[-1], dtype=jnp.float32)
    approx = jnp.swapaxes(matrix, -1, -2) / jnp.sum(matrix * matrix, axis=(-2, -1), keepdims=True)
    for sweep_index in range(PINV_ITERS):
        product = jnp.matmul(matrix, approx, precision=top_precision)
        inner_term = 7.0 * identity - product
        inner_term = 15.0 * identity - jnp.matmul(product, inner_term, precision=top_precision)
        inner_term = 13.0 * identity - jnp.matmul(product, inner_term, precision=top_precision)
        approx = 0.25 * jnp.matmul(approx, inner_term, precision=top_precision)
    return approx


def adam_step(weight, first_moment, second, gradient, step_rate, decay_coef):
    new_first = beta_one * first_moment + (1.0 - beta_one) * gradient
    new_second = beta_two * second + (1.0 - beta_two) * gradient * gradient
    update = new_first / corr_one / (jnp.sqrt(new_second / corr_two) + adam_eps)
    return (new_first, new_second, weight - step_rate * (update + decay_coef * weight))


def with_collectives(
    tokens,
    cotangent,
    qkv_weight,
    out_weight,
    up_weight,
    down_weight,
    vectors,
    taps,
    qkv_first,
    qkv_second,
    out_first,
    out_second,
    up_first,
    up_second,
    down_first,
    down_second,
    vec_first,
    vec_second,
    tap_first,
    tap_second,
):
    seq_count, local_len, model_width = tokens.shape
    head_count, tap_count = taps.shape
    head_size = model_width // head_count
    hidden_width = up_weight.shape[1]
    land_local = LAND // lax.axis_size("seq")
    seg_len = local_len // land_local
    reach_width = tap_count // 2
    logit_scale_factor = head_size ** (-0.5)
    row_count = seq_count * local_len
    head_shape = (seq_count, local_len, head_count, head_size)
    land_shape = (seq_count, LAND, head_count, head_size)
    full_qkv, full_out, full_up, full_down, full_vec = (
        lax.all_gather(qkv_weight.astype(jnp.bfloat16), ("rows", "seq"), axis=0, tiled=True),
        lax.all_gather(out_weight.astype(jnp.bfloat16), ("rows", "seq"), axis=0, tiled=True),
        lax.all_gather(up_weight.astype(jnp.bfloat16), ("rows", "seq"), axis=0, tiled=True),
        lax.all_gather(down_weight.astype(jnp.bfloat16), ("rows", "seq"), axis=0, tiled=True),
        lax.all_gather(vectors.astype(jnp.bfloat16), ("rows", "seq"), axis=1, tiled=True),
    )
    vec_float = full_vec.astype(jnp.float32)
    flat_in = tokens.reshape(row_count, model_width)
    project = jnp.dot(flat_in, full_qkv, preferred_element_type=jnp.float32)
    queries = (project[:, :model_width] + vec_float[0]).astype(jnp.bfloat16)
    key_rows = project[:, model_width : 2 * model_width].astype(jnp.bfloat16)
    values = (project[:, 2 * model_width :] + vec_float[1]).astype(jnp.bfloat16)
    seg_shape = (seq_count, land_local, seg_len, model_width)
    own_q = jnp.mean(queries.reshape(seg_shape), axis=2, dtype=jnp.float32).astype(jnp.bfloat16)
    own_k = jnp.mean(key_rows.reshape(seg_shape), axis=2, dtype=jnp.float32).astype(jnp.bfloat16)
    land_q, land_k = (
        lax.all_gather(own_q, "seq", axis=1, tiled=True),
        lax.all_gather(own_k, "seq", axis=1, tiled=True),
    )
    query_heads = queries.reshape(head_shape)
    key_heads = key_rows.reshape(head_shape)
    value_heads = values.reshape(head_shape)
    landmark_query_heads = land_q.reshape(land_shape)
    landmark_key_heads = land_k.reshape(land_shape)
    lq_float = landmark_query_heads.astype(jnp.float32)
    lk_float = landmark_key_heads.astype(jnp.float32)
    score_one = (
        jnp.einsum(
            "sthd,slhd->shtl", query_heads, landmark_key_heads, preferred_element_type=jnp.float32
        )
        * logit_scale_factor
    )
    prob_one = normalized_rows(score_one)
    second_probability = normalized_rows(
        jnp.einsum("slhd,smhd->shlm", lq_float, lk_float, precision=top_precision)
        * logit_scale_factor
    )
    inverse_matrix, inverse_pull = jax.vjp(pseudo_inverse, second_probability)
    score_three = (
        jnp.einsum(
            "slhd,sthd->shlt", landmark_query_heads, key_heads, preferred_element_type=jnp.float32
        )
        * logit_scale_factor
    )
    row_max = lax.pmax(jnp.max(score_three, axis=-1), "seq")
    expo_three = jnp.exp(score_three - row_max[..., None])
    numer_local = jnp.einsum(
        "shlt,sthd->slhd",
        expo_three.astype(jnp.bfloat16),
        value_heads,
        preferred_element_type=jnp.float32,
    )
    numer, denom = (
        lax.psum(numer_local.astype(jnp.bfloat16), "seq").astype(jnp.float32),
        lax.psum(jnp.sum(expo_three, axis=-1).astype(jnp.bfloat16), "seq").astype(jnp.float32),
    )
    denom_swap = jnp.swapaxes(denom, 1, 2)[..., None]
    landmark_value_rows = numer / denom_swap
    mixing_kernel = jnp.einsum(
        "shlm,smhd->slhd", inverse_matrix, landmark_value_rows, precision=top_precision
    )
    mix_low = mixing_kernel.astype(jnp.bfloat16)
    prob_low = prob_one.astype(jnp.bfloat16)
    attend = jnp.einsum("shtl,slhd->sthd", prob_low, mix_low, preferred_element_type=jnp.float32)
    attend = attend.reshape(seq_count, local_len, model_width)
    tap_chan = jnp.repeat(taps, head_size, axis=0)
    padded_values = with_halo(
        values.reshape(seq_count, local_len, model_width), (("seq", 1),), reach_width
    )
    conv_out = jnp.zeros((seq_count, local_len, model_width), jnp.float32)
    for offset in range(tap_count):
        conv_out = conv_out + tap_chan[:, offset] * padded_values[
            :, offset : offset + local_len
        ].astype(jnp.float32)
    attn_low = (attend + conv_out).reshape(row_count, model_width).astype(jnp.bfloat16)
    branch = jnp.dot(attn_low, full_out, preferred_element_type=jnp.float32) + vec_float[2]
    resid_one = flat_in.astype(jnp.float32) + branch
    normed, norm_pull_one = jax.vjp(layer_norm, resid_one, vec_float[6], vec_float[3])
    normed_low = normed.astype(jnp.bfloat16)
    hidden_pre = jnp.dot(normed_low, full_up, preferred_element_type=jnp.float32) + vec_float[
        8:
    ].reshape(hidden_width)
    active, gelu_pull = jax.vjp(gelu_exact, hidden_pre)
    active_low = active.astype(jnp.bfloat16)
    ff_out = jnp.dot(active_low, full_down, preferred_element_type=jnp.float32) + vec_float[4]
    layer_out, norm_pull_two = jax.vjp(layer_norm, normed + ff_out, vec_float[7], vec_float[5])
    grad_resid_two, grad_gain_two, grad_shift_two = norm_pull_two(
        cotangent.reshape(row_count, model_width).astype(jnp.float32)
    )
    grad_ff = grad_resid_two.astype(jnp.bfloat16)
    grad_down = jnp.einsum("nf,nd->fd", active_low, grad_ff, preferred_element_type=jnp.float32)
    grad_active = jnp.einsum("nd,fd->nf", grad_ff, full_down, preferred_element_type=jnp.float32)
    grad_hidden = gelu_pull(grad_active)[0].astype(jnp.bfloat16)
    grad_up = jnp.einsum("nd,nf->df", normed_low, grad_hidden, preferred_element_type=jnp.float32)
    grad_normed = (
        jnp.einsum("nf,df->nd", grad_hidden, full_up, preferred_element_type=jnp.float32)
        + grad_resid_two
    )
    grad_resid_one, grad_gain_one, grad_shift_one = norm_pull_one(grad_normed)
    grad_branch = grad_resid_one.astype(jnp.bfloat16)
    grad_out = jnp.einsum("nd,ne->de", attn_low, grad_branch, preferred_element_type=jnp.float32)
    grad_attn = jnp.einsum(
        "ne,de->nd", grad_branch, full_out, preferred_element_type=jnp.float32
    ).astype(jnp.bfloat16)
    grad_attn_heads = grad_attn.reshape(head_shape)
    grad_prob_one = jnp.einsum(
        "sthd,slhd->shtl", grad_attn_heads, mix_low, preferred_element_type=jnp.float32
    )
    mixing_part = jnp.einsum(
        "shtl,sthd->slhd", prob_low, grad_attn_heads, preferred_element_type=jnp.float32
    )
    grad_mixing = lax.psum(mixing_part.astype(jnp.bfloat16), "seq").astype(jnp.float32)
    grad_score_one = softmax_back(prob_one, grad_prob_one).astype(jnp.bfloat16)
    query_local = (
        jnp.einsum(
            "shtl,slhd->sthd",
            grad_score_one,
            landmark_key_heads,
            preferred_element_type=jnp.float32,
        )
        * logit_scale_factor
    )
    land_k_part = (
        jnp.einsum(
            "shtl,sthd->slhd", grad_score_one, query_heads, preferred_element_type=jnp.float32
        )
        * logit_scale_factor
    )
    grad_pad = with_halo(
        grad_attn.reshape(seq_count, local_len, model_width), (("seq", 1),), reach_width
    )
    attn_float = grad_attn.reshape(seq_count, local_len, model_width).astype(jnp.float32)
    conv_back = jnp.zeros((seq_count, local_len, model_width), jnp.float32)
    tap_terms = []
    for offset in range(tap_count):
        start_row = 2 * reach_width - offset
        conv_back = conv_back + tap_chan[:, offset] * grad_pad[
            :, start_row : start_row + local_len
        ].astype(jnp.float32)
        tap_terms.append(
            jnp.sum(
                attn_float * padded_values[:, offset : offset + local_len].astype(jnp.float32),
                axis=(0, 1),
            )
        )
    grad_taps = jnp.sum(
        jnp.stack(tap_terms, axis=1).reshape(head_count, head_size, tap_count), axis=1
    )
    grad_inverse = jnp.einsum(
        "slhd,smhd->shlm", grad_mixing, landmark_value_rows, precision=top_precision
    )
    grad_land_values = jnp.einsum(
        "shlm,slhd->smhd", inverse_matrix, grad_mixing, precision=top_precision
    )
    land_grad_low = grad_land_values.astype(jnp.bfloat16).astype(jnp.float32)
    grad_prob_two = inverse_pull(grad_inverse)[0]
    grad_score_two = softmax_back(second_probability, grad_prob_two)
    query_two = (
        jnp.einsum("shlm,smhd->slhd", grad_score_two, lk_float, precision=top_precision)
        * logit_scale_factor
    )
    key_two = (
        jnp.einsum("shlm,slhd->smhd", grad_score_two, lq_float, precision=top_precision)
        * logit_scale_factor
    )
    grad_numer = land_grad_low / denom_swap
    expo_low = expo_three.astype(jnp.bfloat16).astype(jnp.float32)
    value_three = jnp.einsum("shlt,slhd->sthd", expo_low, grad_numer, precision=top_precision)
    grad_expo = jnp.einsum(
        "slhd,sthd->shlt", grad_numer, value_heads.astype(jnp.float32), precision=top_precision
    )
    grad_denom = jnp.swapaxes(jnp.sum(land_grad_low * landmark_value_rows, axis=-1), 1, 2) / denom
    grad_score_three = (expo_three * (grad_expo - grad_denom[..., None])).astype(jnp.bfloat16)
    land_q_part = (
        jnp.einsum(
            "shlt,sthd->slhd", grad_score_three, key_heads, preferred_element_type=jnp.float32
        )
        * logit_scale_factor
    )
    key_local = (
        jnp.einsum(
            "shlt,slhd->sthd",
            grad_score_three,
            landmark_query_heads,
            preferred_element_type=jnp.float32,
        )
        * logit_scale_factor
    )
    land_q_own, land_k_own = (
        lax.psum_scatter(
            land_q_part.astype(jnp.bfloat16), "seq", scatter_dimension=1, tiled=True
        ).astype(jnp.float32),
        lax.psum_scatter(
            land_k_part.astype(jnp.bfloat16), "seq", scatter_dimension=1, tiled=True
        ).astype(jnp.float32),
    )
    first_land = lax.axis_index("seq") * land_local
    land_q_own = land_q_own + lax.dynamic_slice_in_dim(query_two, first_land, land_local, 1)
    land_k_own = land_k_own + lax.dynamic_slice_in_dim(key_two, first_land, land_local, 1)
    spread_shape = (seq_count, land_local, seg_len, head_count, head_size)
    spread_q = jnp.broadcast_to((land_q_own / seg_len)[:, :, None], spread_shape).reshape(
        head_shape
    )
    spread_k = jnp.broadcast_to((land_k_own / seg_len)[:, :, None], spread_shape).reshape(
        head_shape
    )
    grad_query = (query_local + spread_q).reshape(row_count, model_width)
    grad_key = (key_local + spread_k).reshape(row_count, model_width)
    grad_value = value_three.reshape(row_count, model_width) + conv_back.reshape(
        row_count, model_width
    )
    grad_proj = jnp.concatenate([grad_query, grad_key, grad_value], axis=1).astype(jnp.bfloat16)
    grad_qkv = jnp.einsum("nd,ne->de", flat_in, grad_proj, preferred_element_type=jnp.float32)
    input_grad = (
        jnp.einsum("ne,de->nd", grad_proj, full_qkv, preferred_element_type=jnp.float32)
        + grad_resid_one
    )
    input_grad = input_grad.astype(jnp.bfloat16).reshape(tokens.shape)
    bias_sums = jnp.sum(grad_proj.astype(jnp.float32), axis=0)
    grad_vec = jnp.concatenate(
        [
            bias_sums[None, :model_width],
            bias_sums[None, 2 * model_width :],
            jnp.sum(grad_branch.astype(jnp.float32), axis=0)[None],
            grad_shift_one[None],
            jnp.sum(grad_ff.astype(jnp.float32), axis=0)[None],
            grad_shift_two[None],
            grad_gain_one[None],
            grad_gain_two[None],
            jnp.sum(grad_hidden.astype(jnp.float32), axis=0).reshape(-1, model_width),
        ],
        axis=0,
    )
    summed_qkv, summed_out, summed_up, summed_down, summed_vec = (
        lax.psum_scatter(grad_qkv, ("rows", "seq"), scatter_dimension=0, tiled=True),
        lax.psum_scatter(grad_out, ("rows", "seq"), scatter_dimension=0, tiled=True),
        lax.psum_scatter(grad_up, ("rows", "seq"), scatter_dimension=0, tiled=True),
        lax.psum_scatter(grad_down, ("rows", "seq"), scatter_dimension=0, tiled=True),
        lax.psum_scatter(grad_vec, ("rows", "seq"), scatter_dimension=1, tiled=True),
    )
    summed_taps = lax.psum(grad_taps, ("rows", "seq"))
    new_qkv = adam_step(qkv_weight, qkv_first, qkv_second, summed_qkv, rate_matrix, decay_rate)
    new_out = adam_step(out_weight, out_first, out_second, summed_out, rate_output, decay_rate)
    new_up = adam_step(up_weight, up_first, up_second, summed_up, rate_matrix, decay_rate)
    new_down = adam_step(down_weight, down_first, down_second, summed_down, rate_matrix, decay_rate)
    new_vec = adam_step(vectors, vec_first, vec_second, summed_vec, rate_vector, 0.0)
    new_taps = adam_step(taps, tap_first, tap_second, summed_taps, rate_taps, 0.0)
    out_tokens = layer_out.astype(jnp.bfloat16).reshape(tokens.shape)
    return (out_tokens, input_grad) + new_qkv + new_out + new_up + new_down + new_vec + new_taps


BF = jnp.bfloat16
F32 = jnp.float32
MESH = pl.DeviceIdType.MESH


def remote(src, dst, send_sem, recv_sem, device):
    return pltpu.make_async_remote_copy(
        src_ref=src, dst_ref=dst, send_sem=send_sem, recv_sem=recv_sem,
        device_id=device, device_id_type=MESH,
    )


def place():
    row, spot = lax.axis_index("rows"), lax.axis_index("seq")
    line, core = spot // 2, spot % 2
    flip_one = row + 1 - 2 * (row % 2)
    flip_two = row + 2 - 4 * (row // 2)
    first = (1 - core) * flip_one + core * flip_two
    second = (1 - core) * flip_two + core * flip_one
    return row, line, core, first, second, 3 - row


def greet(devices):
    barrier = pltpu.get_barrier_semaphore()
    for device in devices:
        pl.semaphore_signal(barrier, inc=1, device_id=device, device_id_type=MESH)
    pl.semaphore_wait(barrier, len(devices))


class Net:
    def __init__(self, send, recv):
        self.send, self.recv, self.started = send, recv, []
        self.row, self.line, self.core, self.first, self.second, self.across = place()
        self.line_size = lax.axis_size("seq") // 2
        own_spot = 2 * self.line + self.core
        self.sibling = (self.row, 2 * self.line + 1 - self.core)
        self.peers = [
            (self.row, 2 * ((self.line + k) % self.line_size) + self.core)
            for k in range(1, self.line_size)
        ]
        self.to_first, self.to_second = (self.first, own_spot), (self.second, own_spot)

    def go(self, w, k, src, dst, device):
        copy = remote(src, dst, self.send.at[w, k], self.recv.at[w, k], device)
        copy.start()
        self.started.append(copy)
        return copy

    def finish(self):
        for copy in self.started:
            copy.wait_send()


def columns(base, which, half):
    return pl.ds(pl.multiple_of(base + which * half, 128), half)


class Gather:
    def __init__(self, net, w, src, dst, base, half, asm, stage, local):
        self.net, self.w, self.dst, self.stage, self.asm = net, w, dst, stage, asm
        self.rows, self.base, self.half, self.local = src.shape[0], base, half, local
        part = pl.ds(pl.multiple_of(net.core * self.rows, 8), self.rows)
        there = columns(base, 1 - net.core, half)
        self.asm_copy = net.go(w, 0, src.at[:, there], asm.at[part, :], net.sibling)
        asm[part, :] = src[:, columns(base, net.core, half)]

    def block(self, start, size):
        at = pl.ds(pl.multiple_of(start, 16), size)
        return self.dst.at[at, columns(self.base, self.net.core, self.half)]

    def slab(self, index):
        size = 2 * self.rows * self.net.line_size
        return self.block(index * size, size)

    def spread(self):
        net = self.net
        self.asm_copy.wait_recv()
        self.stage[...] = self.asm[...].astype(BF)
        size = 2 * self.rows
        block = self.block((net.row * net.line_size + net.line) * size, size)
        self.z = [net.go(self.w, 1 + k, self.stage, block, d) for k, d in enumerate(net.peers)]
        self.own = pltpu.make_async_copy(self.stage, block, self.local)
        self.own.start()

    def step_one(self):
        net, w, z0 = self.net, self.w, self.net.line_size
        self.own.wait()
        for copy in self.z:
            copy.wait_recv()
        mine = self.slab(net.row)
        self.hop = [net.go(w, z0, mine, mine, net.to_first)]
        self.hop.append(net.go(w, z0 + 1, mine, mine, net.to_second))
        self.sib = [net.go(w, z0 + 3, mine, mine, net.sibling)]

    def step_two(self):
        net, w, z0 = self.net, self.w, self.net.line_size
        self.hop[0].wait_recv()
        got = self.slab(net.first)
        self.hop.append(net.go(w, z0 + 2, got, got, net.to_second))
        self.sib.append(net.go(w, z0 + 4, got, got, net.sibling))

    def step_three(self):
        net, w, z0 = self.net, self.w, self.net.line_size
        self.hop[1].wait_recv()
        got = self.slab(net.second)
        self.sib.append(net.go(w, z0 + 5, got, got, net.sibling))
        self.hop[2].wait_recv()
        got = self.slab(net.across)
        self.sib.append(net.go(w, z0 + 6, got, got, net.sibling))

    def close(self):
        for copy in self.sib:
            copy.wait_recv()


GATHER_SEMS = 7


class Scatter:
    def __init__(self, net, w, out, base, half, bufs):
        self.net, self.w, self.out, self.base, self.half = net, w, out, base, half
        self.acc, self.buf0, self.buf1, self.buf2, self.buf3, self.fin = bufs
        self.rows = out.shape[0]
        self.size = 2 * self.rows * net.line_size

    def open(self, outbox, own=None):
        self.sib = self.net.go(self.w, 0, outbox, self.buf0, self.net.sibling)
        self.own = own
        if own is not None:
            own.start()

    def slab(self, index):
        return pl.ds(pl.multiple_of(index * self.size, self.size), self.size)

    def add(self, index, other, start):
        step = 48
        acc = self.acc

        def one(i, carry):
            at = pl.ds(pl.multiple_of(index * self.size + i * step, 16), step)
            there = pl.ds(pl.multiple_of(start + i * step, 16), step)
            acc[at, :] = acc[at, :] + other[there, :]
            return carry

        lax.fori_loop(0, self.size // step, one, 0)

    def step_one(self):
        net, w = self.net, self.w
        if self.own is not None:
            self.own.wait()
        self.sib.wait_recv()
        self.add(net.across, self.buf0, net.across * self.size)
        acc = self.acc
        self.one = net.go(w, 1, acc.at[self.slab(net.across), :], self.buf1.at[0], net.to_second)
        self.add(net.second, self.buf0, net.second * self.size)
        self.two = net.go(w, 2, acc.at[self.slab(net.second), :], self.buf1.at[1], net.to_second)
        self.add(net.first, self.buf0, net.first * self.size)
        self.add(net.row, self.buf0, net.row * self.size)

    def step_two(self):
        net = self.net
        self.one.wait_recv()
        self.add(net.first, self.buf1.at[0], 0)
        src = self.acc.at[self.slab(net.first), :]
        self.three = net.go(self.w, 3, src, self.buf2, net.to_first)
        self.two.wait_recv()
        self.add(net.row, self.buf1.at[1], 0)

    def step_three(self):
        net = self.net
        self.three.wait_recv()
        self.add(net.row, self.buf2, 0)
        block, n = 2 * self.rows, net.line_size
        self.z = []

        def at(line):
            return pl.ds(pl.multiple_of((net.row * n + line) * block, block), block)

        for k, device in enumerate(net.peers):
            src = self.acc.at[at((net.line + 1 + k) % n), :]
            self.z.append(net.go(self.w, 4 + k, src, self.buf3.at[net.line], device))
        self.buf3[net.line] = self.acc[at(net.line), :]

    def step_four(self):
        net = self.net
        for copy in self.z:
            copy.wait_recv()
        total = self.buf3[0].astype(F32)
        for k in range(1, net.line_size):
            total = total + self.buf3[k].astype(F32)
        self.fin[...] = total
        part = pl.ds(pl.multiple_of((1 - net.core) * self.rows, 8), self.rows)
        here = columns(self.base, net.core, self.half)
        self.last = net.go(
            self.w, 3 + net.line_size, self.fin.at[part, :], self.out.at[:, here], net.sibling
        )
        part = pl.ds(pl.multiple_of(net.core * self.rows, 8), self.rows)
        self.out[:, here] = self.fin[part, :]

    def close(self):
        self.last.wait_recv()


SCATTER_SEMS = 4


def scatter_scratch(rows, half, dtype, line_size):
    quarter = 2 * rows * line_size
    return [
        pltpu.VMEM((4 * quarter, half), dtype),
        pltpu.VMEM((4 * quarter, half), dtype),
        pltpu.VMEM((2, quarter, half), dtype),
        pltpu.VMEM((quarter, half), dtype),
        pltpu.VMEM((line_size, 2 * rows, half), dtype),
        pltpu.VMEM((2 * rows, half), F32),
    ]


class Many:
    def __init__(self, pieces):
        self.pieces = list(pieces)

    def each(self, step):
        for piece in self.pieces:
            getattr(piece, step)()

    def spread(self):
        self.each("spread")

    def step_one(self):
        self.each("step_one")

    def step_two(self):
        self.each("step_two")

    def step_three(self):
        self.each("step_three")

    def step_four(self):
        self.each("step_four")

    def close(self):
        self.each("close")


PAIR = 128


def nn(a, b):
    return jnp.dot(a, b, preferred_element_type=F32)


def nt(a, b):
    return lax.dot_general(a, b, (((1,), (1,)), ((), ())), preferred_element_type=F32)


def tn(a, b):
    return lax.dot_general(a, b, (((0,), (0,)), ((), ())), preferred_element_type=F32)


def split(x):
    high = x.astype(BF)
    return high, (x - high.astype(F32)).astype(BF)


def three(dot, a, b):
    return dot(a[0], b[0]) + (dot(a[0], b[1]) + dot(a[1], b[0]))


def lane_masks(dtype):
    lane = lax.broadcasted_iota(jnp.int32, (1, PAIR), 1)
    one = (lane < PAIR // 2).astype(F32)
    return one.astype(dtype), (1.0 - one).astype(dtype)


def apart(x):
    one, two = lane_masks(x.dtype)
    return jnp.concatenate([x * one, x * two], axis=0)


def together(x):
    half = PAIR // 2
    lane = lax.broadcasted_iota(jnp.int32, (half, PAIR), 1)
    return jnp.where(lane < half, x[:half], x[half:])


def same_head():
    half = PAIR // 2
    a = lax.broadcasted_iota(jnp.int32, (PAIR, PAIR), 0) // half
    b = lax.broadcasted_iota(jnp.int32, (PAIR, PAIR), 1) // half
    return a == b


def eye():
    a = lax.broadcasted_iota(jnp.int32, (PAIR, PAIR), 0)
    b = lax.broadcasted_iota(jnp.int32, (PAIR, PAIR), 1)
    return (a == b).astype(F32)


def by_head(x, reduce):
    half, width = PAIR // 2, x.shape[1]
    parts = [reduce(x[h * half : (h + 1) * half], axis=0, keepdims=True) for h in (0, 1)]
    return jnp.concatenate([jnp.broadcast_to(y, (half, width)) for y in parts], axis=0)


def lanes(p):
    if isinstance(p, int):
        return pl.ds(p * PAIR, PAIR)
    return pl.ds(pl.multiple_of(p * PAIR, PAIR), PAIR)


def conv_pair(table, padded):
    size = table.shape[0] // 4
    out = nn(table, padded)
    lane = lax.broadcasted_iota(jnp.int32, (size, PAIR), 1)
    return jnp.where(
        lane < PAIR // 2,
        out[:size] + out[2 * size : 3 * size],
        out[size : 2 * size] + out[3 * size :],
    )


class Group:
    def __init__(self, send, recv):
        self.row, self.me = lax.axis_index("rows"), lax.axis_index("seq")
        self.size = lax.axis_size("seq")
        self.send, self.recv, self.started = send, recv, []

    def peers(self):
        return [(self.row, (self.me + k) % self.size) for k in range(1, self.size)]

    def push(self, channel, pick_src, dst):
        copies = []
        for k, device in enumerate(self.peers()):
            copy = remote(
                pick_src(device[1]), dst, self.send.at[channel, k], self.recv.at[channel, k], device
            )
            copy.start()
            copies.append(copy)
        self.started += copies
        return copies

    def line_peers(self):
        n, line, core = self.size // 2, self.me // 2, self.me % 2
        return [(self.row, 2 * ((line + k) % n) + core) for k in range(1, n)]

    def go(self, channel, k, src, dst, device):
        copy = remote(src, dst, self.send.at[channel, k], self.recv.at[channel, k], device)
        copy.start()
        self.started.append(copy)
        return copy

    def share(self, parts):
        n, line, core = self.size // 2, self.me // 2, self.me % 2
        sibling = (self.row, 2 * line + 1 - core)
        there, here = [], []
        for channel, block in parts:
            mine = block(self.me)
            there.append(
                [self.go(channel, k, mine, mine, d) for k, d in enumerate(self.line_peers())]
            )
        for channel, block in parts:
            here.append(self.go(channel, n - 1, block(self.me), block(self.me), sibling))

        def arrive():
            for k in range(1, n):
                source = 2 * ((line - k + n) % n) + core
                for (channel, block), copies in zip(parts, there):
                    copies[k - 1].wait_recv()
                    got = block(source)
                    here.append(self.go(channel, n - 1 + k, got, got, sibling))
            for copy in here:
                copy.wait_recv()

        return arrive

    def halo(self, channel, source, padded, reach):
        length = source.shape[1]
        copies = []
        for which, (src_at, dst_at, step) in enumerate(
            ((length - reach, 0, 1), (0, length + reach, -1))
        ):
            there = (self.me + step + self.size) % self.size
            copy = remote(
                source.at[:, pl.ds(src_at, reach), :],
                padded.at[:, pl.ds(dst_at, reach), :],
                self.send.at[channel, which],
                self.recv.at[channel, which],
                (self.row, there),
            )
            goes = self.me < self.size - 1 if step == 1 else self.me > 0
            comes = self.me > 0 if step == 1 else self.me < self.size - 1
            pl.when(goes)(copy.start)
            copies.append((copy, goes, comes, dst_at))

        def arrive():
            for copy, goes, comes, dst_at in copies:
                pl.when(comes)(copy.wait_recv)

                @pl.when(jnp.logical_not(comes))
                def _():
                    shape = (padded.shape[0], reach, padded.shape[2])
                    padded[:, pl.ds(dst_at, reach), :] = jnp.zeros(shape, padded.dtype)

        def sent():
            for copy, goes, _, _ in copies:
                pl.when(goes)(copy.wait_send)

        return arrive, sent

    def finish(self):
        for copy in self.started:
            copy.wait_send()


def pinv_start(prob):
    total = by_head(jnp.sum(prob * prob, axis=1, keepdims=True), jnp.sum)
    return prob.T / total


def pinv_terms(p, z, unit):
    product = three(nn, p, z)
    prod = split(product)
    term_one = 7.0 * unit - product
    term_two = 15.0 * unit - three(nn, prod, split(term_one))
    term_three = 13.0 * unit - three(nn, prod, split(term_two))
    return prod, term_one, term_two, term_three


def band(line, length, reach):
    wide = jnp.broadcast_to(line, (length, line.shape[1]))
    return pltpu.roll(wide, 0, 1, stride=1, stride_axis=0)[:, : length + 2 * reach]


def set_lines(taps, lines, flip):
    count = taps.shape[1]
    lines[...] = jnp.zeros(lines.shape, F32)
    lines[:, :count] = taps[...]
    if flip:
        a = lax.broadcasted_iota(jnp.int32, (PAIR, PAIR), 0)
        b = lax.broadcasted_iota(jnp.int32, (PAIR, PAIR), 1)
        turn = (a + b == count - 1).astype(F32).astype(BF)
        high, low = split(lines[:, :PAIR])
        lines[:, :PAIR] = nn(high, turn) + nn(low, turn)


def fill_bands(lines, table, reach):
    pairs, rows = table.shape[0], table.shape[1] // 4
    for p in range(pairs):
        for h in (0, 1):
            high, low = split(band(lines[2 * p + h : 2 * p + h + 1, :], rows, reach))
            table[p, h * rows : (h + 1) * rows, :] = high
            table[p, (2 + h) * rows : (3 + h) * rows, :] = low


def gelu_parts(x):
    expo = jnp.exp(-0.5 * x * x)
    t = 1.0 / (1.0 + (0.3275911 * 0.7071067811865476) * jnp.abs(x))
    tail = -0.284496736 + t * (1.421413741 + t * (-1.453152027 + t * 1.061405429))
    tail = 0.5 * expo * t * (0.254829592 + t * tail)
    below = jnp.where(x >= 0.0, 1.0 - tail, tail)
    return x * below, below + x * expo * 0.3989422804014327


def norm_parts(resid):
    center = resid - jnp.mean(resid, axis=-1, keepdims=True)
    scale = lax.rsqrt(jnp.mean(center * center, axis=-1, keepdims=True) + norm_eps)
    return center * scale, scale


def norm_back(grad, gain, unit, scale):
    inner = grad * gain
    mean = jnp.mean(inner, axis=-1, keepdims=True)
    along = jnp.mean(inner * unit, axis=-1, keepdims=True)
    return scale * (inner - mean - unit * along)


def row_sum(x):
    return jnp.sum(x, axis=0, keepdims=True)


def front_kernel(
    reach,
    tokens, cot, qkv_w, out_w, up_w, down_w, vectors, taps,
    layer_out, grad_one, ga, sums, d_down, d_up, d_out,
    h_qkv, h_q, h_k, h_vpad, h_landq, h_landk, h_mix, h_p1, h_e, h_wt, h_p2o, h_zo, h_lvo,
    f_qkv, q, k, vpad, landq, landk, mix, p1, e, wt, p2o, zo, lvo,
    w_out, w_up, w_down, vecs, attn, v, table, f_vec, lb, numer, nrecv, stat, srecv, mstat, conv, fcol,
    g_down, g_up, active, slope, unit_one, scale_one, normed, low, low_t, total, ff, attn_t, *rest,
):
    keep_sem, o_sem, lines, vec_w, square = rest[-5:]
    rest = rest[:-5]
    set_lines(taps, lines, False)
    square[...] = jnp.zeros(square.shape, F32)
    square[: vectors.shape[0], : vectors.shape[1]] = vectors[...]
    vec_w[...] = jnp.zeros(vec_w.shape, F32)
    vec_w[:, :PAIR] = square[...].T[: vec_w.shape[0]]
    asm, stage = rest[:7], rest[7:14]
    g_send, g_recv, g_local, send, recv = rest[14:19]
    net, group = Net(g_send, g_recv), Group(send, recv)
    me, size = group.me, group.size
    n_seq, length, width = q.shape
    pairs = width // PAIR
    own = n_seq * pairs // size
    each = own * PAIR
    land_local = LAND // size
    seg = length // land_local
    scale = (PAIR // 2) ** -0.5
    greet(group.peers() + [net.to_first, net.to_second])

    def owner_seq(d):
        return d * own // pairs

    def owner_lanes(d):
        return pl.ds(pl.multiple_of((d * own % pairs) * PAIR, PAIR), each)

    plan = [(vec_w, f_vec, 0), (qkv_w, f_qkv, width), (qkv_w, f_qkv, 0), (qkv_w, f_qkv, 2 * width)]
    plan += [(out_w, w_out, 0), (up_w, w_up, 0), (down_w, w_down, 0)]
    pieces = []
    for w, (src, dst, base) in enumerate(plan):
        half = asm[w].shape[1]
        pieces.append(Gather(net, w, src, dst, base, half, asm[w], stage[w], g_local.at[w]))
    t_vec, t_k, t_q, t_v, t_out, t_up, t_down = pieces
    for piece in pieces[:4]:
        piece.spread()
    t_out.spread()
    t_up.spread()
    fill_bands(lines, table, reach)

    def project(dst, base, bias):
        step = 2 * PAIR
        for at in range(0, width, step):
            x = nn(tokens[...], f_qkv[:, base + at : base + at + step])
            if bias is not None:
                x = x + vecs[bias : bias + 1, at : at + step]
            dst[:, :, at : at + step] = x.astype(BF).reshape(n_seq, length, step)

    t_vec.step_one()
    t_k.step_one()
    t_q.step_one()
    t_vec.step_two()
    t_k.step_two()
    t_v.step_one()
    t_down.spread()
    t_vec.step_three()
    t_q.step_two()
    t_k.step_three()
    t_vec.close()
    vecs[...] = f_vec[:, :PAIR].astype(F32).T[: vecs.shape[0]]
    t_v.step_two()
    t_k.close()
    project(k, width, None)
    t_q.step_three()
    t_q.close()
    project(q, 0, 0)
    t_v.step_three()
    t_out.step_one()
    t_up.step_one()
    t_v.close()
    project(v, 2 * width, 1)

    def own_landmarks(s, carry):
        both = [
            jnp.mean(x[s].astype(F32).reshape(land_local, seg, width), axis=1) for x in (q, k)
        ]
        lb[me, s] = jnp.concatenate(both, axis=0).astype(BF)
        vpad[s, pl.ds(reach, length), :] = v[s]
        return carry

    lax.fori_loop(0, n_seq, own_landmarks, 0)
    landed = group.share([(1, lambda d: lb.at[d])])
    halo_in, halo_sent = group.halo(0, v, vpad, reach)
    t_out.step_two()
    t_down.step_one()
    landed()

    def whole_landmarks(s, carry):
        x = lb[:, s].astype(F32)
        landq[s] = x[:, :land_local].reshape(LAND, width).astype(BF)
        landk[s] = x[:, land_local:].reshape(LAND, width).astype(BF)
        return carry

    lax.fori_loop(0, n_seq, whole_landmarks, 0)
    lane_at = lax.broadcasted_iota(jnp.int32, (PAIR, PAIR), 1)

    def over_tokens(s, tile):
        for p in range(pairs):
            score = nt(apart(landq[s, :, lanes(p)]), k[s, :, lanes(p)]) * scale
            top = jnp.max(score, axis=1, keepdims=True)
            expo = jnp.exp(score - top)
            expo_low = expo.astype(BF)
            e[s * pairs + p] = expo_low
            numer[s, :, lanes(p)] = together(nn(expo_low, v[s, :, lanes(p)])).astype(BF)
            unit = s * pairs + p
            at = (unit // own) * 8 + unit % own
            tile = jnp.where(lane_at == at, top, tile)
            tile = jnp.where(lane_at == at + own, jnp.sum(expo, axis=1, keepdims=True), tile)
        return tile

    tile = lax.fori_loop(0, n_seq, over_tokens, jnp.zeros((PAIR, PAIR), F32))
    stat[...] = tile.T[: 8 * size].reshape(size, 8, PAIR)
    sums_in = group.push(
        2, lambda d: numer.at[owner_seq(d), :, owner_lanes(d)], nrecv.at[me]
    )
    stats_in = group.push(3, lambda d: stat.at[d], srecv.at[me])
    t_up.step_two()
    nrecv[me] = numer[owner_seq(me), :, owner_lanes(me)]
    srecv[me] = stat[me]

    block, unit_matrix = same_head(), eye()
    my_seq, my_pair = owner_seq(me), (me * own) % pairs
    for i in range(own):
        at = lanes(my_pair + i)
        score = nt(apart(landq[my_seq, :, at]), apart(landk[my_seq, :, at])) * scale
        score = jnp.where(block, score, -1e30)
        expo = jnp.exp(score - jnp.max(score, axis=1, keepdims=True))
        prob = expo / jnp.sum(expo, axis=1, keepdims=True)
        p2o[i] = prob
        zo[0, i] = pinv_start(prob)

    halo_in()
    per_step = n_seq * pairs // PINV_ITERS

    def over_landmarks(unit):
        s, p = unit // pairs, unit % pairs
        score = nt(apart(landk[s, :, lanes(p)]), q[s, :, lanes(p)]) * scale
        expo = jnp.exp(score - by_head(score, jnp.max))
        p1[unit] = expo / by_head(expo, jnp.sum)
        conv[s, :, lanes(p)] = conv_pair(table[p], vpad[s, :, lanes(p)])

    def pinv_step(step, carry):
        for i in range(own):
            z = split(zo[step, i])
            _, _, _, inner = pinv_terms(split(p2o[i]), z, unit_matrix)
            zo[step + 1, i] = 0.25 * three(nn, z, split(inner))
        for j in range(per_step):
            over_landmarks(step * per_step + j)
        return carry

    lax.fori_loop(0, PINV_ITERS // 2, pinv_step, 0)
    t_out.step_three()
    t_down.step_two()
    lax.fori_loop(PINV_ITERS // 2, PINV_ITERS, pinv_step, 0)

    for copy in sums_in + stats_in:
        copy.wait_recv()
    got = srecv[...]
    tops = got[:, :own]
    top = jnp.max(tops, axis=0, keepdims=True)
    factor = jnp.exp(tops - top)
    weight_sum = jnp.sum(factor * got[:, own : 2 * own], axis=0, keepdims=True)
    factor = factor / weight_sum
    spare = jnp.zeros((1, 8 - 2 * own, PAIR), F32)
    mstat[me] = jnp.concatenate([top, weight_sum, spare], axis=1)[0]
    spread = jnp.concatenate([factor, jnp.zeros((size, 8 - own, PAIR), F32)], axis=1)
    spread = spread.reshape(8 * size, PAIR)
    fcol[...] = jnp.concatenate([spread, jnp.zeros((PAIR - 8 * size, PAIR), F32)], axis=0).T
    half = PAIR // 2
    narrow = lax.broadcasted_iota(jnp.int32, (half, PAIR), 1) < half
    for i in range(own):
        at = pl.ds(i * PAIR, PAIR)
        mean = jnp.zeros((half, PAIR), F32)
        for src in range(size):
            column = fcol[:, src * 8 + i : src * 8 + i + 1]
            weight = jnp.where(narrow, column[:half], column[half:])
            mean = mean + weight * nrecv[src, :, at].astype(F32)
        lvo[:, at] = mean
        mixed = together(three(nn, split(zo[PINV_ITERS, i]), split(apart(mean))))
        mix[my_seq, :, lanes(my_pair + i)] = mixed.astype(BF)
    mixed_in = group.share(
        [
            (4, lambda d: mix.at[owner_seq(d), :, owner_lanes(d)]),
            (5, lambda d: mstat.at[d]),
        ]
    )
    t_up.step_three()
    mixed_in()

    rows = jnp.concatenate(
        [mstat[...].reshape(8 * size, PAIR), jnp.zeros((PAIR - 8 * size, PAIR), F32)], axis=0
    )
    rows = rows.T
    valid = (lane_at % 8 < own) & (lane_at < 8 * size)
    shift = jnp.where(valid, tile - rows, 0.0)
    den = jnp.where(valid, pltpu.roll(rows, PAIR - own, 1), 1.0)
    wt[...] = jnp.exp(shift) / den

    def result(s, carry):
        for p in range(pairs):
            prob = p1[s * pairs + p].astype(BF)
            out = tn(prob, apart(mix[s, :, lanes(p)])) + conv[s, :, lanes(p)]
            at = pl.ds(pl.multiple_of(s * length, length), length)
            attn[at, lanes(p)] = out.astype(BF)
        return carry

    lax.fori_loop(0, n_seq, result, 0)
    held = [f_qkv, q, k, vpad, landq, landk, mix, p1, e, wt, p2o, zo, lvo]
    homes = [h_qkv, h_q, h_k, h_vpad, h_landq, h_landk, h_mix, h_p1, h_e, h_wt, h_p2o, h_zo, h_lvo]
    keeps = [
        pltpu.make_async_copy(a, b, keep_sem.at[i]) for i, (a, b) in enumerate(zip(held, homes))
    ]
    for keep in keeps:
        keep.start()
    count = tokens.shape[0]
    hidden = w_up.shape[1]
    chunk_size = 2 * PAIR
    n_rows, n_wide = count // chunk_size, width // chunk_size
    row_groups = hidden // width
    sums[...] = jnp.zeros(sums.shape, F32)

    def row(i):
        return vecs[i : i + 1, :]

    def row_block(i):
        return pl.ds(pl.multiple_of(i * chunk_size, chunk_size), chunk_size)

    t_out.close()

    def first(i, carry):
        at = row_block(i)
        resid = tokens[at, :].astype(F32) + (nn(attn[at, :], w_out[...]) + row(2))
        unit, scale = norm_parts(resid)
        out = unit * row(6) + row(3)
        unit_one[at, :] = unit
        scale_one[at, :] = jnp.broadcast_to(scale, (chunk_size, PAIR))
        normed[at, :] = out
        low[at, :] = out.astype(BF)
        total[at, :] = jnp.broadcast_to(row(4), (chunk_size, width))
        return carry

    lax.fori_loop(0, n_rows, first, 0)
    t_down.step_three()
    t_up.close()
    low_t[...] = low[...].T
    attn_t[...] = attn[...].T

    def chunk(r, j):
        start = r * width + j * chunk_size
        return slice(start, start + chunk_size)

    def whole(r):
        return slice(r * width, (r + 1) * width)

    def gather_down(r):
        for n in range(n_wide):
            at = slice(n * chunk_size, (n + 1) * chunk_size)
            total[:, at] += nn(active[:, whole(r)], w_down[whole(r), at])

    for r in range(row_groups):
        for j in range(n_wide):
            f = chunk(r, j)
            bias = vecs[8 + r : 9 + r, j * chunk_size : (j + 1) * chunk_size]
            value, rate = gelu_parts(nn(low[...], w_up[:, f]) + bias)
            active[:, f] = value.astype(BF)
            slope[:, f] = rate.astype(BF)
        if r == 1:
            t_down.close()
        if r > 0:
            gather_down(r - 1)
    gather_down(row_groups - 1)

    def second(i, carry):
        at = row_block(i)
        unit, scale = norm_parts(normed[at, :] + total[at, :])
        layer_out[at, :] = (unit * row(7) + row(5)).astype(BF)
        up = cot[at, :].astype(F32)
        grad = norm_back(up, row(7), unit, scale)
        total[at, :] = grad
        grad = grad.astype(BF)
        ff[at, :] = grad
        sums[4:5, :] += row_sum(grad.astype(F32))
        sums[5:6, :] += row_sum(up)
        sums[7:8, :] += row_sum(up * unit)
        return carry

    lax.fori_loop(0, n_rows, second, 0)

    def leave(r):
        f = whole(r)
        return [
            pltpu.make_async_copy(g_down.at[r % 2], d_down.at[f, :], o_sem.at[0, r]),
            pltpu.make_async_copy(g_up.at[r % 2], d_up.at[:, f], o_sem.at[1, r]),
        ]

    def weight_grads(r):
        if r > 1:
            for copy in leave(r - 2):
                copy.wait()
        for j in range(n_wide):
            f = chunk(r, j)
            at = slice(j * chunk_size, (j + 1) * chunk_size)
            g_up[r % 2, :, at] = nn(low_t[...], slope[:, f]).astype(BF)
            g_down[r % 2, at, :] = tn(active[:, f], ff[...]).astype(BF)
        for n in range(n_wide):
            at = slice(n * chunk_size, (n + 1) * chunk_size)
            total[:, at] += nt(slope[:, whole(r)], w_up[at, whole(r)])
        for copy in leave(r):
            copy.start()

    for r in range(row_groups):
        for j in range(n_wide):
            f = chunk(r, j)
            grad = (nt(ff[...], w_down[f, :]) * slope[:, f].astype(F32)).astype(BF)
            sums[8 + r : 9 + r, j * chunk_size : (j + 1) * chunk_size] = row_sum(grad.astype(F32))
            slope[:, f] = grad
        if r > 0:
            weight_grads(r - 1)
    weight_grads(row_groups - 1)

    def third(i, carry):
        at = row_block(i)
        unit = unit_one[at, :]
        up = total[at, :]
        grad = norm_back(up, row(6), unit, scale_one[at, :1])
        grad_one[at, :] = grad
        grad = grad.astype(BF)
        low[at, :] = grad
        ga[at, :] = nt(grad, w_out[...]).astype(BF)
        sums[2:3, :] += row_sum(grad.astype(F32))
        sums[3:4, :] += row_sum(up)
        sums[6:7, :] += row_sum(up * unit)
        return carry

    lax.fori_loop(0, n_rows, third, 0)
    for r in (row_groups - 2, row_groups - 1):
        for copy in leave(r):
            copy.wait()
    g_up[0] = nn(attn_t[...], low[...]).astype(BF)
    last = pltpu.make_async_copy(g_up.at[0], d_out, o_sem.at[2, 0])
    last.start()
    for keep in keeps:
        keep.wait()
    last.wait()
    halo_sent()
    group.finish()
    net.finish()


def front(tokens, cot, matrices, vectors, taps, seq_size, reach):
    n_seq, length, width = tokens.shape
    pairs = width // PAIR
    units = n_seq * pairs
    own = units // seq_size
    n_dev = 4 * seq_size
    table = jax.ShapeDtypeStruct((vectors.shape[1], 2 * PAIR), F32)
    line_size = seq_size // 2
    vmem, hbm = pl.BlockSpec(memory_space=pltpu.VMEM), pl.BlockSpec(memory_space=pltpu.HBM)
    shape = jax.ShapeDtypeStruct
    land = shape((n_seq, LAND, width), BF)
    qkv_w, out_w, up_w, down_w = matrices
    count, hidden = n_seq * length, up_w.shape[1]
    flat = (count, width)
    whole = [shape((n_dev * x.shape[0], x.shape[1]), BF) for x in matrices]
    asm = [(table.shape[0], table.shape[1] // 2)] + [(qkv_w.shape[0], width // 2)] * 3
    asm += [(x.shape[0], x.shape[1] // 2) for x in (out_w, up_w, down_w)]
    n_sem = line_size + GATHER_SEMS
    kept = [
        whole[0],
        shape(tokens.shape, BF), shape(tokens.shape, BF),
        shape((n_seq, length + 2 * reach, width), BF), land, land, land,
        shape((units, PAIR, length), F32), shape((units, PAIR, length), BF),
        shape((PAIR, PAIR), F32), shape((own, PAIR, PAIR), F32),
        shape((PINV_ITERS + 1, own, PAIR, PAIR), F32), shape((LAND, own * PAIR), F32),
    ]
    return pl.pallas_call(
        functools.partial(front_kernel, reach),
        out_shape=[shape(flat, BF), shape(flat, F32), shape(flat, BF), shape((16, width), F32)]
        + [whole[3], whole[2], whole[1]]
        + kept,
        in_specs=[vmem] * 8,
        out_specs=[vmem] * 4 + [hbm] * (3 + len(kept)),
        scratch_shapes=[pltpu.VMEM(x.shape, x.dtype) for x in kept]
        + [pltpu.VMEM(x.shape, BF) for x in whole[1:]]
        + [
            pltpu.VMEM((16, width), F32),
            pltpu.VMEM(flat, BF),
            pltpu.VMEM(tokens.shape, BF),
            pltpu.VMEM((pairs, 4 * length, length + 2 * reach), BF),
            pltpu.VMEM((n_dev * table.shape[0], table.shape[1]), BF),
            pltpu.VMEM((seq_size, n_seq, 2 * LAND // seq_size, width), BF),
            pltpu.VMEM((n_seq, LAND, width), BF),
            pltpu.VMEM((seq_size, LAND, own * PAIR), BF),
            pltpu.VMEM((seq_size, 8, PAIR), F32),
            pltpu.VMEM((seq_size, 8, PAIR), F32),
            pltpu.VMEM((seq_size, 8, PAIR), F32),
            pltpu.VMEM((n_seq, length, width), F32),
            pltpu.VMEM((PAIR, PAIR), F32),
            pltpu.VMEM((2, width, width), BF),
            pltpu.VMEM((2, width, width), BF),
            pltpu.VMEM((count, hidden), BF),
            pltpu.VMEM((count, hidden), BF),
            pltpu.VMEM(flat, F32),
            pltpu.VMEM((count, PAIR), F32),
            pltpu.VMEM(flat, F32),
            pltpu.VMEM(flat, BF),
            pltpu.VMEM((width, count), BF),
            pltpu.VMEM(flat, F32),
            pltpu.VMEM(flat, BF),
            pltpu.VMEM((width, count), BF),
        ]
        + [pltpu.VMEM((2 * r, h), F32) for r, h in asm]
        + [pltpu.VMEM((2 * r, h), BF) for r, h in asm]
        + [
            pltpu.SemaphoreType.DMA((7, n_sem)),
            pltpu.SemaphoreType.DMA((7, n_sem)),
            pltpu.SemaphoreType.DMA((7,)),
            pltpu.SemaphoreType.DMA((6, seq_size)),
            pltpu.SemaphoreType.DMA((6, seq_size)),
            pltpu.SemaphoreType.DMA((len(kept),)),
            pltpu.SemaphoreType.DMA((3, hidden // width)),
            pltpu.VMEM((2 * pairs, 2 * PAIR), F32),
            pltpu.VMEM(table.shape, F32),
            pltpu.VMEM((PAIR, PAIR), F32),
        ],
        compiler_params=pltpu.CompilerParams(
            collective_id=0, has_side_effects=True, vmem_limit_bytes=61 * 1024 * 1024
        ),
        name="front",
    )(tokens.reshape(flat), cot.reshape(flat), *matrices, vectors, taps)


def back_kernel(
    reach, n_taps,
    h_ga, h_tokens, h_resid, h_qkv, h_rows, taps, d_down, d_up, d_out,
    h_q, h_k, h_vpad, h_landq, h_landk, h_mix, h_p1, h_e, h_wt, h_p2o, h_zo, h_lvo,
    input_grad, s_qkv, s_out, s_up, s_down, s_small,
    grad, tapg, table, tok_t, outbox, small_box,
    gpad, gmix, gmr, low, gfull, mstat, gcol, gq, gv, lkp, lpart, lpr, lsum, gsum, gpart, dz, dp,
    skew, own_g,
    ga, tokens, resid, f_qkv, vec_rows, q, k, vpad, landq, landk, mix, p1, e, wt, p2o, zo, lvo,
    load_sem, *rest,
):
    ways = [(h_ga, ga), (h_mix, mix), (h_p1, p1), (h_landk, landk), (h_q, q), (h_vpad, vpad)]
    ways += [(h_tokens, tokens), (h_lvo, lvo), (h_zo, zo), (h_p2o, p2o), (h_e, e), (h_wt, wt)]
    ways += [(h_landq, landq), (h_k, k), (h_rows, vec_rows), (h_qkv, f_qkv), (h_resid, resid)]
    loads = [pltpu.make_async_copy(a, c, load_sem.at[i]) for i, (a, c) in enumerate(ways)]
    for load in loads:
        load.start()

    def loaded(start, stop):
        for load in loads[start:stop]:
            load.wait()

    bufs, (g_send, g_recv, g_local, send, recv, lines) = rest[:-6], rest[-6:]
    net, group = Net(g_send, g_recv), Group(send, recv)
    me, size = group.me, group.size
    n_seq, length, width = q.shape
    pairs = width // PAIR
    own = n_seq * pairs // size
    each = own * PAIR
    land_local = LAND // size
    seg = length // land_local
    half = PAIR // 2
    scale = half**-0.5
    greet(group.peers() + [net.to_first, net.to_second])

    def owner_seq(d):
        return d * own // pairs

    def owner_lanes(d):
        return pl.ds(pl.multiple_of((d * own % pairs) * PAIR, PAIR), each)

    plan = [(s_down, 0), (s_up, 0), (s_out, 0)]
    plan += [(s_qkv, 2 * width), (s_qkv, 0), (s_qkv, width), (s_small, 0)]
    pieces = []
    for w, (out, base) in enumerate(plan):
        own_bufs = bufs[6 * w : 6 * w + 6]
        pieces.append(Scatter(net, w, out, base, own_bufs[0].shape[1], own_bufs))
    r_down, r_up, r_out, r_v, r_q, r_k, r_small = pieces

    def open_whole(w, src):
        piece = pieces[w]
        other, here = [columns(0, c, piece.half) for c in (1 - net.core, net.core)]
        own_part = pltpu.make_async_copy(src.at[:, here], piece.acc, g_local.at[w])
        piece.open(src.at[:, other], own_part)

    def open_weight(piece, box):
        step = 2 * PAIR
        rows = tok_t.shape[0]

        def one(i, carry):
            at = pl.ds(pl.multiple_of(i * step, step), step)
            x = tok_t[at, :]
            other, here = [columns(piece.base, c, piece.half) for c in (1 - net.core, net.core)]
            outbox[box, at, :] = nn(x, grad[:, other]).astype(BF)
            piece.acc[at, :] = nn(x, grad[:, here]).astype(BF)
            return carry

        lax.fori_loop(0, rows // step, one, 0)
        piece.open(outbox.at[box])

    open_whole(0, d_down)
    loaded(0, 3)
    halo_in, halo_sent = group.halo(0, ga, gpad, reach)

    def first(s, carry):
        for p in range(pairs):
            unit, at = s * pairs + p, lanes(p)
            own_ga = ga[s, :, at]
            gpad[s, pl.ds(reach, length), at] = own_ga
            prob = p1[unit]
            gmix[s, :, at] = together(nn(prob.astype(BF), own_ga)).astype(BF)
            back = nt(apart(mix[s, :, at]), own_ga)
            low[unit] = (prob * (back - by_head(prob * back, jnp.sum))).astype(BF)
        return carry

    lax.fori_loop(0, n_seq, first, 0)
    chips, my_line, my_core = size // 2, me // 2, me % 2
    core_lanes = [pl.ds(pl.multiple_of(c * each, PAIR), each) for c in (my_core, 1 - my_core)]
    sibling = (group.row, 2 * my_line + 1 - my_core)
    gmix_sib = group.go(1, chips, gmix.at[:, :, core_lanes[1]], gsum, sibling)
    r_down.step_one()
    gmix_sib.wait_recv()
    gpart[...] = gmix[:, :, core_lanes[0]] + gsum[...]
    gmix_in = []
    for kk, device in enumerate(group.line_peers()):
        other = device[1] // 2
        gmix_in.append(group.go(1, kk, gpart.at[other], gmr.at[my_line], device))
    gmr[my_line] = gpart[my_line]
    open_whole(1, d_up)
    open_whole(2, d_out)
    set_lines(taps, lines, True)
    fill_bands(lines, table, reach)
    halo_in()
    skew[...] = jnp.zeros(skew.shape, F32)

    def beside(s, carry):
        one, two_mask = lane_masks(BF)
        for p in range(pairs):
            unit, at = s * pairs + p, lanes(p)
            own_ga, padded = ga[s, :, at], vpad[s, :, at]
            gs = low[unit]
            gq[s, :, at] = tn(gs, apart(landk[s, :, at])) * scale
            lkp[s, :, at] = together(nn(gs, q[s, :, at])) * scale
            gv[s, :, at] = conv_pair(table[p], gpad[s, :, at])
            both = jnp.concatenate([own_ga * one, own_ga * two_mask], axis=0)
            skew[2 * p : 2 * p + 2, :, : length + 2 * reach] += nt(both, padded).reshape(
                2, length, length + 2 * reach
            )
        return carry

    loaded(3, 6)
    lax.fori_loop(0, n_seq, beside, 0)
    lane_at = lax.broadcasted_iota(jnp.int32, (PAIR, PAIR), 1)
    wide = skew.shape[2]
    for h in range(2 * pairs):
        total = skew[h, :8, :]
        for row in range(8, length, 8):
            total = total + pltpu.roll(skew[h, row : row + 8, :], wide - row, 1)
        tapg[h] = total[:, :PAIR]
    loaded(6, 7)
    r_up.step_one()
    tok_t[...] = tokens[...].T

    loaded(7, 10)
    for copy in gmix_in:
        copy.wait_recv()
    my_seq, my_pair = owner_seq(me), (me * own) % pairs
    tile = jnp.zeros((PAIR, PAIR), F32)
    for i in range(own):
        at = pl.ds(i * PAIR, PAIR)
        total = gmr[0, :, at].astype(F32)
        for src in range(1, chips):
            total = total + gmr[src, :, at].astype(F32)
        total = split(apart(total))
        means = apart(lvo[:, at])
        back = together(three(tn, split(zo[PINV_ITERS, i]), total)).astype(BF)
        own_g[:, at] = back
        column = jnp.sum(apart(back.astype(F32)) * means, axis=1, keepdims=True)
        tile = jnp.where(lane_at == i, column, tile)
        dz[i] = three(nt, total, split(means))
        dp[i] = jnp.zeros((PAIR, PAIR), F32)
    mstat[me] = tile.T[:8]
    gfull[my_seq, :, owner_lanes(me)] = own_g[...]
    g_in = group.share(
        [
            (2, lambda d: gfull.at[owner_seq(d), :, owner_lanes(d)]),
            (3, lambda d: mstat.at[d]),
        ]
    )
    loaded(10, 14)
    g_in()
    rows = jnp.concatenate(
        [mstat[...].reshape(8 * size, PAIR), jnp.zeros((PAIR - 8 * size, PAIR), F32)], axis=0
    )
    gcol[...] = rows.T
    unit_matrix = eye()

    def third(unit):
        s, p = unit // pairs, unit % pairs
        at = lanes(p)
        here = (unit // own) * 8 + unit % own
        picked = lane_at == here
        weight = jnp.sum(jnp.where(picked, wt[...], 0.0), axis=1, keepdims=True)
        offset = jnp.sum(jnp.where(picked, gcol[...], 0.0), axis=1, keepdims=True)
        g = apart(gfull[s, :, at])
        prob = e[unit].astype(F32) * weight
        back = nt(g, vpad[s, pl.ds(reach, length), at]) - offset
        gs = (prob * back).astype(BF)
        values = gv[s, :, at] + tn(prob.astype(BF), g)
        v_at = pl.ds(pl.multiple_of(2 * width + p * PAIR, PAIR), PAIR)
        rows = pl.ds(pl.multiple_of(s * length, length), length)
        grad[rows, v_at] = values.astype(BF)
        rows = pl.ds(pl.multiple_of(s * length, length), length)
        grad[rows, pl.ds(pl.multiple_of(width + p * PAIR, PAIR), PAIR)] = (
            tn(gs, apart(landq[s, :, at])) * scale
        ).astype(BF)
        lq = (together(nn(gs, k[s, :, at])) * scale).reshape(size, land_local, PAIR)
        lk = lkp[s, :, at].reshape(size, land_local, PAIR)
        both = jnp.concatenate([lq, lk], axis=1).astype(BF)
        lpart[:, :, s, :, at] = both.reshape(chips, 2, 2 * land_local, PAIR)

    per_step = n_seq * pairs // PINV_ITERS

    def pinv_back(step, carry):
        at_step = PINV_ITERS - 1 - step
        for i in range(own):
            p, z = split(p2o[i]), split(zo[at_step, i])
            prod, one, two_term, three_term = pinv_terms(p, z, unit_matrix)
            d_out = dz[i] * 0.25
            d_out_s = split(d_out)
            d_three = split(three(tn, z, d_out_s))
            d_two = split(-three(tn, prod, d_three))
            d_one = -three(tn, prod, d_two)
            d_prod = -three(nt, d_three, split(two_term)) - three(nt, d_two, split(one)) - d_one
            d_prod = split(d_prod)
            dp[i] += three(nt, d_prod, z)
            dz[i] = three(nt, d_out_s, split(three_term)) + three(tn, p, d_prod)
        for j in range(per_step):
            third(step * per_step + j)
        return carry

    third_of = PINV_ITERS // 3
    lax.fori_loop(0, third_of, pinv_back, 0)
    r_down.step_two()
    r_out.step_one()
    lax.fori_loop(third_of, 2 * third_of, pinv_back, 0)
    lax.fori_loop(2 * third_of, PINV_ITERS, pinv_back, 0)
    r_up.step_two()
    r_out.step_two()

    for i in range(own):
        at = pl.ds(i * PAIR, PAIR)
        prob = p2o[i]
        squares = by_head(jnp.sum(prob * prob, axis=1, keepdims=True), jnp.sum)
        d_start = dz[i].T
        inner = by_head(jnp.sum(d_start * prob, axis=1, keepdims=True), jnp.sum)
        d_prob = dp[i] + d_start / squares - 2.0 * prob * inner / (squares * squares)
        gs = prob * (d_prob - jnp.sum(prob * d_prob, axis=1, keepdims=True))
        gs = split(gs)
        here = lanes(my_pair + i)
        lq, lk = apart(landq[my_seq, :, here]), apart(landk[my_seq, :, here])
        query = together(nn(gs[0], lk) + nn(gs[1], lk)) * scale
        key = together(tn(gs[0], lq) + tn(gs[1], lq)) * scale
        both = [x.reshape(size, land_local, PAIR) for x in (query, key)]
        both = jnp.concatenate(both, axis=1).reshape(chips, 2, 2 * land_local, PAIR)
        lpart[:, :, my_seq, :, here] = (lpart[:, :, my_seq, :, here].astype(F32) + both).astype(BF)
    land_sib = group.go(4, chips, lpart.at[:, 1 - my_core], lsum, sibling)
    land_sib.wait_recv()

    def add_lands(i, carry):
        lsum[i] = lsum[i] + lpart[i, my_core]
        return carry

    lax.fori_loop(0, chips, add_lands, 0)
    lpr[my_line] = lsum[my_line]
    land_in = []
    for kk, device in enumerate(group.line_peers()):
        land_in.append(group.go(4, kk, lsum.at[device[1] // 2], lpr.at[my_line], device))
    open_weight(r_v, 0)
    for copy in land_in:
        copy.wait_recv()

    def close(s, carry):
        for p in range(pairs):
            at = lanes(p)
            total = lpr[0, s, :, at].astype(F32)
            for src in range(1, chips):
                total = total + lpr[src, s, :, at].astype(F32)
            total = total * (1.0 / seg)
            spread = [
                jnp.concatenate(
                    [jnp.broadcast_to(x[i : i + 1], (seg, PAIR)) for i in range(land_local)], axis=0
                )
                for x in (total[:land_local], total[land_local:])
            ]
            rows = pl.ds(pl.multiple_of(s * length, length), length)
            grad[rows, at] = (gq[s, :, at] + spread[0]).astype(BF)
            key_at = pl.ds(width + p * PAIR, PAIR)
            grad[rows, key_at] = (grad[rows, key_at].astype(F32) + spread[1]).astype(BF)
        return carry

    lax.fori_loop(0, n_seq, close, 0)
    r_down.step_three()
    open_weight(r_q, 1)
    r_v.step_one()
    open_weight(r_k, 2)
    r_q.step_one()
    r_up.step_three()

    loaded(14, 17)
    def column_sums(base):
        total = jnp.zeros((1, width), F32)
        for s in range(n_seq):
            x = grad[s * length : (s + 1) * length, base : base + width].astype(F32)
            total = total + jnp.sum(x, axis=0, keepdims=True)
        return total

    count = vec_rows.shape[0]
    which = lax.broadcasted_iota(jnp.int32, (count, width), 0)
    table_rows = vec_rows[...]
    table_rows = jnp.where(which == 0, column_sums(0), table_rows)
    table_rows = jnp.where(which == 1, column_sums(2 * width), table_rows)
    table_rows = jnp.concatenate([table_rows, jnp.zeros((PAIR - count, width), F32)], axis=0)
    left = table_rows.T
    sums = tapg[:, 0, :]
    for b in range(1, 8):
        sums = sums + pltpu.roll(tapg[:, b, :], PAIR - b, 1)
    shard = r_small.rows
    sums = jnp.concatenate([sums, jnp.zeros((shard - sums.shape[0], PAIR), F32)], axis=0)
    right = jnp.broadcast_to(sums[None], (width // shard, shard, PAIR)).reshape(width, PAIR)
    zero = net.core == 0
    r_small.acc[...] = jnp.where(zero, left, right)
    small_box[...] = jnp.where(zero, right, left)
    r_small.open(small_box)
    r_v.step_two()
    r_k.step_one()
    r_out.step_three()
    r_down.step_four()

    def inputs(i, carry):
        step = 2 * PAIR
        rows = pl.ds(pl.multiple_of(i * step, step), step)
        for at in range(0, width, step):
            x = nt(grad[rows, :], f_qkv[at : at + step, :])
            out = x + resid[rows, at : at + step]
            input_grad[rows, at : at + step] = out.astype(BF)
        return carry

    lax.fori_loop(0, tokens.shape[0] // (2 * PAIR), inputs, 0)
    r_small.step_one()
    r_q.step_two()
    r_k.step_two()
    r_v.step_three()
    r_small.step_two()
    r_up.step_four()
    r_q.step_three()
    r_k.step_three()
    r_out.step_four()
    r_v.step_four()
    r_small.step_three()
    r_q.step_four()
    r_k.step_four()
    r_small.step_four()
    for piece in pieces:
        piece.close()
    halo_sent()
    group.finish()
    net.finish()


def back(
    ga, tokens, resid, f_qkv, vec_rows, taps, d_down, d_up, d_out, kept, shards, seq_size, reach
):
    q = kept[0]
    n_seq, length, width = q.shape
    pairs = width // PAIR
    units = n_seq * pairs
    own = units // seq_size
    line_size = seq_size // 2
    vmem, hbm = pl.BlockSpec(memory_space=pltpu.VMEM), pl.BlockSpec(memory_space=pltpu.HBM)
    shape = jax.ShapeDtypeStruct
    part = 2 * LAND // seq_size
    s_qkv, s_out, s_up, s_down = [shape(x.shape, F32) for x in shards]
    s_small = shape((s_qkv.shape[0], 2 * PAIR), F32)
    bufs = []
    for x in (s_down, s_up, s_out):
        bufs += scatter_scratch(x.shape[0], x.shape[1] // 2, BF, line_size)
    for _ in range(3):
        bufs += scatter_scratch(s_qkv.shape[0], width // 2, BF, line_size)
    bufs += scatter_scratch(s_qkv.shape[0], PAIR, F32, line_size)
    return pl.pallas_call(
        functools.partial(back_kernel, reach, 2 * reach + 1),
        out_shape=[shape(tokens.shape, BF), s_qkv, s_out, s_up, s_down, s_small],
        in_specs=[hbm] * 5 + [vmem] + [hbm] * 15,
        out_specs=[vmem] * 6,
        scratch_shapes=[
            pltpu.VMEM((n_seq * length, 3 * width), BF),
            pltpu.VMEM((2 * pairs, 8, PAIR), F32),
            pltpu.VMEM((pairs, 4 * length, length + 2 * reach), BF),
            pltpu.VMEM((width, n_seq * length), BF),
            pltpu.VMEM((3, width, width // 2), BF),
            pltpu.VMEM((width, PAIR), F32),
            pltpu.VMEM((n_seq, length + 2 * reach, width), BF),
            pltpu.VMEM((n_seq, LAND, width), BF),
            pltpu.VMEM((seq_size // 2, LAND, own * PAIR), BF),
            pltpu.VMEM((units, PAIR, length), BF),
            pltpu.VMEM((n_seq, LAND, width), BF),
            pltpu.VMEM((seq_size, 8, PAIR), F32),
            pltpu.VMEM((PAIR, PAIR), F32),
            pltpu.VMEM((n_seq, length, width), F32),
            pltpu.VMEM((n_seq, length, width), F32),
            pltpu.VMEM((n_seq, LAND, width), F32),
            pltpu.VMEM((seq_size // 2, 2, n_seq, part, width), BF),
            pltpu.VMEM((seq_size // 2, n_seq, part, width), BF),
            pltpu.VMEM((seq_size // 2, n_seq, part, width), BF),
            pltpu.VMEM((n_seq, LAND, own * PAIR), BF),
            pltpu.VMEM((n_seq, LAND, own * PAIR), BF),
            pltpu.VMEM((own, PAIR, PAIR), F32),
            pltpu.VMEM((own, PAIR, PAIR), F32),
            pltpu.VMEM((2 * pairs, length, 2 * PAIR), F32),
            pltpu.VMEM((LAND, own * PAIR), BF),
        ]
        + [pltpu.VMEM(x.shape, x.dtype) for x in (ga, tokens, resid, f_qkv, vec_rows, *kept)]
        + [pltpu.SemaphoreType.DMA((5 + len(kept),))]
        + bufs
        + [
            pltpu.SemaphoreType.DMA((7, line_size + SCATTER_SEMS)),
            pltpu.SemaphoreType.DMA((7, line_size + SCATTER_SEMS)),
            pltpu.SemaphoreType.DMA((7,)),
            pltpu.SemaphoreType.DMA((6, seq_size)),
            pltpu.SemaphoreType.DMA((6, seq_size)),
            pltpu.VMEM((2 * pairs, 2 * PAIR), F32),
        ],
        compiler_params=pltpu.CompilerParams(
            collective_id=1, has_side_effects=True, vmem_limit_bytes=61 * 1024 * 1024
        ),
        name="back",
    )(ga, tokens, resid, f_qkv, vec_rows, taps, d_down, d_up, d_out, *kept)


def update_kernel(rates, n_in, *refs):
    n_mat = len(rates) - 2
    homes, outs = refs[:n_in], refs[n_in : n_in + 3 * n_mat + 8]
    ins, sem = refs[n_in + 3 * n_mat + 8 : -1], refs[-1]
    own = 4 * n_mat + 7
    moves = []
    for i, (src, dst) in enumerate(zip(homes, ins)):
        moves.append(pltpu.make_async_copy(src, dst, sem.at[i]))
        moves[-1].start()
    for i in range(n_mat):
        for move in moves[4 * i : 4 * i + 4]:
            move.wait()
        weight, first, second, grad = ins[4 * i : 4 * i + 4]
        new = adam_step(weight[...], first[...], second[...], grad[...], *rates[i])
        for out, value in zip(outs[3 * i : 3 * i + 3], new):
            out[...] = value
    passed = []
    for i in range(n_in - own):
        moves[own + i].wait()
        out = outs[3 * n_mat + 6 + i]
        passed.append(pltpu.make_async_copy(ins[own + i], out, sem.at[n_in + i]))
        passed[-1].start()
    for move in moves[4 * n_mat : own]:
        move.wait()
    small = ins[4 * n_mat]
    vec, tap = ins[own - 6 : own - 3], ins[own - 3 : own]
    rows, count = vec[0].shape
    grad = small[:, :PAIR].T[:rows, :count]
    new = adam_step(*[x[...] for x in vec], grad, *rates[n_mat])
    for out, value in zip(outs[3 * n_mat : 3 * n_mat + 3], new):
        out[...] = value
    heads, taps = tap[0].shape
    grad = small[:, PAIR:][:heads, :taps]
    new = adam_step(*[x[...] for x in tap], grad, *rates[n_mat + 1])
    for out, value in zip(outs[3 * n_mat + 3 : 3 * n_mat + 6], new):
        out[...] = value
    for move in passed:
        move.wait()


def update(matrices, small, vec, tap, others):
    decay = ((rate_matrix, decay_rate), (rate_output, decay_rate))
    rates = [decay[0], decay[1], decay[0], decay[0], (rate_vector, 0.0), (rate_taps, 0.0)]
    vmem = pl.BlockSpec(memory_space=pltpu.VMEM)
    shape = [jax.ShapeDtypeStruct(x[0].shape, F32) for x in (*matrices, vec, tap) for _ in range(3)]
    shape += [jax.ShapeDtypeStruct(x.shape, x.dtype) for x in others]
    args = [x for group in matrices for x in group] + [small, *vec, *tap]
    hbm = pl.BlockSpec(memory_space=pltpu.HBM)
    n_in = len(args) + len(others)
    return pl.pallas_call(
        functools.partial(update_kernel, rates, n_in),
        out_shape=shape,
        in_specs=[hbm] * n_in,
        out_specs=[vmem] * (len(shape) - len(others)) + [hbm] * len(others),
        scratch_shapes=[pltpu.VMEM(x.shape, x.dtype) for x in (*args, *others)]
        + [pltpu.SemaphoreType.DMA((n_in + len(others),))],
        compiler_params=pltpu.CompilerParams(vmem_limit_bytes=60 * 1024 * 1024),
        name="update",
    )(*args, *others)


def kernels_fit(args):
    tokens, _, *matrices = args[:6]
    taps = args[7]
    seq_size = lax.axis_size("seq")
    n_seq, length, width = tokens.shape
    units = n_seq * width // PAIR
    own = units // seq_size
    return (
        lax.axis_size("rows") == 4
        and seq_size == 8
        and all(x.shape[0] % 24 == 0 and x.shape[1] % 256 == 0 for x in matrices)
        and width // taps.shape[0] == PAIR // 2
        and length == PAIR
        and taps.shape[1] == 33
        and taps.shape[0] <= matrices[0].shape[0]
        and units == own * seq_size
        and seq_size == 2 * n_seq
        and width == 2 * own * PAIR
        and 2 * own <= 8
        and (width // PAIR) % own == 0
        and units % PINV_ITERS == 0
        and LAND == 8 * seq_size
        and matrices[2].shape[1] == 4 * width
        and args[6].shape[0] == 12
    )


def with_kernels(
    tokens, cotangent, qkv_weight, out_weight, up_weight, down_weight, vectors, taps,
    qkv_first, qkv_second, out_first, out_second, up_first, up_second, down_first, down_second,
    vec_first, vec_second, tap_first, tap_second,
):
    seq_count, local_len, model_width = tokens.shape
    head_count, tap_count = taps.shape
    seq_size = lax.axis_size("seq")
    reach = tap_count // 2
    row_count = seq_count * local_len
    matrices = (qkv_weight, out_weight, up_weight, down_weight)
    flat_in = tokens.reshape(row_count, model_width)
    layer_out, grad_resid_one, grad_attn, vec_rows, grad_down, grad_up, grad_out, full_qkv, *kept = (
        front(tokens, cotangent, matrices, vectors, taps, seq_size, reach)
    )
    input_grad, summed_qkv, summed_out, summed_up, summed_down, small = back(
        grad_attn.reshape(tokens.shape), flat_in, grad_resid_one, full_qkv, vec_rows, taps,
        grad_down, grad_up, grad_out,
        kept, matrices, seq_size, reach,
    )
    *new, out_tokens, input_grad = update(
        [
            (qkv_weight, qkv_first, qkv_second, summed_qkv),
            (out_weight, out_first, out_second, summed_out),
            (up_weight, up_first, up_second, summed_up),
            (down_weight, down_first, down_second, summed_down),
        ],
        small,
        (vectors, vec_first, vec_second),
        (taps, tap_first, tap_second),
        (layer_out, input_grad),
    )
    return (out_tokens.reshape(tokens.shape), input_grad.reshape(tokens.shape), *new)


def on_device(*args):
    return with_kernels(*args) if kernels_fit(args) else with_collectives(*args)


def solution(mesh):
    return jax.shard_map(
        on_device,
        mesh=mesh,
        in_specs=(
            P("rows", "seq", None),
            P("rows", "seq", None),
            P(("rows", "seq"), None),
            P(("rows", "seq"), None),
            P(("rows", "seq"), None),
            P(("rows", "seq"), None),
            P(None, ("rows", "seq")),
            P(),
            P(("rows", "seq"), None),
            P(("rows", "seq"), None),
            P(("rows", "seq"), None),
            P(("rows", "seq"), None),
            P(("rows", "seq"), None),
            P(("rows", "seq"), None),
            P(("rows", "seq"), None),
            P(("rows", "seq"), None),
            P(None, ("rows", "seq")),
            P(None, ("rows", "seq")),
            P(),
            P(),
        ),
        out_specs=(
            P("rows", "seq", None),
            P("rows", "seq", None),
            P(("rows", "seq"), None),
            P(("rows", "seq"), None),
            P(("rows", "seq"), None),
            P(("rows", "seq"), None),
            P(("rows", "seq"), None),
            P(("rows", "seq"), None),
            P(("rows", "seq"), None),
            P(("rows", "seq"), None),
            P(("rows", "seq"), None),
            P(("rows", "seq"), None),
            P(("rows", "seq"), None),
            P(("rows", "seq"), None),
            P(None, ("rows", "seq")),
            P(None, ("rows", "seq")),
            P(None, ("rows", "seq")),
            P(),
            P(),
            P(),
        ),
        check_vma=False,
    )
```

```python
import functools

import jax
import jax.numpy as jnp
from jax import lax
from jax.experimental import pallas as pl
from jax.experimental.pallas import tpu as pltpu
from jax.sharding import PartitionSpec as P

LAND = 64
PINV_ITERS = 6


top_precision = lax.Precision.HIGHEST
norm_eps = 1e-05
beta_one = 0.9
beta_two = 0.999
corr_one = 1.0 - 0.9**10
corr_two = 1.0 - 0.999**10
adam_eps = 1e-08
decay_rate = 0.01
rate_matrix = 0.03
rate_output = 0.12
rate_vector = 0.3
rate_taps = 0.08


def with_halo(x, sides, width):
    for axis, dim in sides:
        size, length = (lax.axis_size(axis), x.shape[dim])
        up = [(i, (i + 1) % size) for i in range(size - 1)]
        down = [(j, i) for i, j in up]
        last = lax.slice_in_dim(x, length - width, length, axis=dim)
        initial = lax.slice_in_dim(x, 0, width, axis=dim)
        before = lax.ppermute(last, axis, up)
        after = lax.ppermute(initial, axis, down)
        x = jnp.concatenate([before, x, after], axis=dim)
    return x


def layer_norm(residual, gain_row, shift_row):
    center = residual - jnp.mean(residual, axis=-1, keepdims=True)
    spread = jnp.mean(center * center, axis=-1, keepdims=True)
    return center * lax.rsqrt(spread + norm_eps) * gain_row + shift_row


def normalized_rows(scores):
    expo = jnp.exp(scores - jnp.max(scores, axis=-1, keepdims=True))
    return expo / jnp.sum(expo, axis=-1, keepdims=True)


def softmax_back(probability, grad_in):
    return probability * (grad_in - jnp.sum(probability * grad_in, axis=-1, keepdims=True))


def gelu_exact(inputs):
    return jax.nn.gelu(inputs, approximate=False)


def pseudo_inverse(matrix):
    identity = jnp.eye(matrix.shape[-1], dtype=jnp.float32)
    approx = jnp.swapaxes(matrix, -1, -2) / jnp.sum(matrix * matrix, axis=(-2, -1), keepdims=True)
    for sweep_index in range(PINV_ITERS):
        product = jnp.matmul(matrix, approx, precision=top_precision)
        inner_term = 7.0 * identity - product
        inner_term = 15.0 * identity - jnp.matmul(product, inner_term, precision=top_precision)
        inner_term = 13.0 * identity - jnp.matmul(product, inner_term, precision=top_precision)
        approx = 0.25 * jnp.matmul(approx, inner_term, precision=top_precision)
    return approx


def adam_step(weight, first_moment, second, gradient, step_rate, decay_coef):
    new_first = beta_one * first_moment + (1.0 - beta_one) * gradient
    new_second = beta_two * second + (1.0 - beta_two) * gradient * gradient
    update = new_first / corr_one / (jnp.sqrt(new_second / corr_two) + adam_eps)
    return (new_first, new_second, weight - step_rate * (update + decay_coef * weight))


def with_collectives(
    tokens,
    cotangent,
    qkv_weight,
    out_weight,
    up_weight,
    down_weight,
    vectors,
    taps,
    qkv_first,
    qkv_second,
    out_first,
    out_second,
    up_first,
    up_second,
    down_first,
    down_second,
    vec_first,
    vec_second,
    tap_first,
    tap_second,
):
    seq_count, local_len, model_width = tokens.shape
    head_count, tap_count = taps.shape
    head_size = model_width // head_count
    hidden_width = up_weight.shape[1]
    land_local = LAND // lax.axis_size("seq")
    seg_len = local_len // land_local
    reach_width = tap_count // 2
    logit_scale_factor = head_size ** (-0.5)
    row_count = seq_count * local_len
    head_shape = (seq_count, local_len, head_count, head_size)
    land_shape = (seq_count, LAND, head_count, head_size)
    full_qkv, full_out, full_up, full_down, full_vec = (
        lax.all_gather(qkv_weight.astype(jnp.bfloat16), ("rows", "seq"), axis=0, tiled=True),
        lax.all_gather(out_weight.astype(jnp.bfloat16), ("rows", "seq"), axis=0, tiled=True),
        lax.all_gather(up_weight.astype(jnp.bfloat16), ("rows", "seq"), axis=0, tiled=True),
        lax.all_gather(down_weight.astype(jnp.bfloat16), ("rows", "seq"), axis=0, tiled=True),
        lax.all_gather(vectors.astype(jnp.bfloat16), ("rows", "seq"), axis=1, tiled=True),
    )
    vec_float = full_vec.astype(jnp.float32)
    flat_in = tokens.reshape(row_count, model_width)
    project = jnp.dot(flat_in, full_qkv, preferred_element_type=jnp.float32)
    queries = (project[:, :model_width] + vec_float[0]).astype(jnp.bfloat16)
    key_rows = project[:, model_width : 2 * model_width].astype(jnp.bfloat16)
    values = (project[:, 2 * model_width :] + vec_float[1]).astype(jnp.bfloat16)
    seg_shape = (seq_count, land_local, seg_len, model_width)
    own_q = jnp.mean(queries.reshape(seg_shape), axis=2, dtype=jnp.float32).astype(jnp.bfloat16)
    own_k = jnp.mean(key_rows.reshape(seg_shape), axis=2, dtype=jnp.float32).astype(jnp.bfloat16)
    land_q, land_k = (
        lax.all_gather(own_q, "seq", axis=1, tiled=True),
        lax.all_gather(own_k, "seq", axis=1, tiled=True),
    )
    query_heads = queries.reshape(head_shape)
    key_heads = key_rows.reshape(head_shape)
    value_heads = values.reshape(head_shape)
    landmark_query_heads = land_q.reshape(land_shape)
    landmark_key_heads = land_k.reshape(land_shape)
    lq_float = landmark_query_heads.astype(jnp.float32)
    lk_float = landmark_key_heads.astype(jnp.float32)
    score_one = (
        jnp.einsum(
            "sthd,slhd->shtl", query_heads, landmark_key_heads, preferred_element_type=jnp.float32
        )
        * logit_scale_factor
    )
    prob_one = normalized_rows(score_one)
    second_probability = normalized_rows(
        jnp.einsum("slhd,smhd->shlm", lq_float, lk_float, precision=top_precision)
        * logit_scale_factor
    )
    inverse_matrix, inverse_pull = jax.vjp(pseudo_inverse, second_probability)
    score_three = (
        jnp.einsum(
            "slhd,sthd->shlt", landmark_query_heads, key_heads, preferred_element_type=jnp.float32
        )
        * logit_scale_factor
    )
    row_max = lax.pmax(jnp.max(score_three, axis=-1), "seq")
    expo_three = jnp.exp(score_three - row_max[..., None])
    numer_local = jnp.einsum(
        "shlt,sthd->slhd",
        expo_three.astype(jnp.bfloat16),
        value_heads,
        preferred_element_type=jnp.float32,
    )
    numer, denom = (
        lax.psum(numer_local.astype(jnp.bfloat16), "seq").astype(jnp.float32),
        lax.psum(jnp.sum(expo_three, axis=-1).astype(jnp.bfloat16), "seq").astype(jnp.float32),
    )
    denom_swap = jnp.swapaxes(denom, 1, 2)[..., None]
    landmark_value_rows = numer / denom_swap
    mixing_kernel = jnp.einsum(
        "shlm,smhd->slhd", inverse_matrix, landmark_value_rows, precision=top_precision
    )
    mix_low = mixing_kernel.astype(jnp.bfloat16)
    prob_low = prob_one.astype(jnp.bfloat16)
    attend = jnp.einsum("shtl,slhd->sthd", prob_low, mix_low, preferred_element_type=jnp.float32)
    attend = attend.reshape(seq_count, local_len, model_width)
    tap_chan = jnp.repeat(taps, head_size, axis=0)
    padded_values = with_halo(
        values.reshape(seq_count, local_len, model_width), (("seq", 1),), reach_width
    )
    conv_out = jnp.zeros((seq_count, local_len, model_width), jnp.float32)
    for offset in range(tap_count):
        conv_out = conv_out + tap_chan[:, offset] * padded_values[
            :, offset : offset + local_len
        ].astype(jnp.float32)
    attn_low = (attend + conv_out).reshape(row_count, model_width).astype(jnp.bfloat16)
    branch = jnp.dot(attn_low, full_out, preferred_element_type=jnp.float32) + vec_float[2]
    resid_one = flat_in.astype(jnp.float32) + branch
    normed, norm_pull_one = jax.vjp(layer_norm, resid_one, vec_float[6], vec_float[3])
    normed_low = normed.astype(jnp.bfloat16)
    hidden_pre = jnp.dot(normed_low, full_up, preferred_element_type=jnp.float32) + vec_float[
        8:
    ].reshape(hidden_width)
    active, gelu_pull = jax.vjp(gelu_exact, hidden_pre)
    active_low = active.astype(jnp.bfloat16)
    ff_out = jnp.dot(active_low, full_down, preferred_element_type=jnp.float32) + vec_float[4]
    layer_out, norm_pull_two = jax.vjp(layer_norm, normed + ff_out, vec_float[7], vec_float[5])
    grad_resid_two, grad_gain_two, grad_shift_two = norm_pull_two(
        cotangent.reshape(row_count, model_width).astype(jnp.float32)
    )
    grad_ff = grad_resid_two.astype(jnp.bfloat16)
    grad_down = jnp.einsum("nf,nd->fd", active_low, grad_ff, preferred_element_type=jnp.float32)
    grad_active = jnp.einsum("nd,fd->nf", grad_ff, full_down, preferred_element_type=jnp.float32)
    grad_hidden = gelu_pull(grad_active)[0].astype(jnp.bfloat16)
    grad_up = jnp.einsum("nd,nf->df", normed_low, grad_hidden, preferred_element_type=jnp.float32)
    grad_normed = (
        jnp.einsum("nf,df->nd", grad_hidden, full_up, preferred_element_type=jnp.float32)
        + grad_resid_two
    )
    grad_resid_one, grad_gain_one, grad_shift_one = norm_pull_one(grad_normed)
    grad_branch = grad_resid_one.astype(jnp.bfloat16)
    grad_out = jnp.einsum("nd,ne->de", attn_low, grad_branch, preferred_element_type=jnp.float32)
    grad_attn = jnp.einsum(
        "ne,de->nd", grad_branch, full_out, preferred_element_type=jnp.float32
    ).astype(jnp.bfloat16)
    grad_attn_heads = grad_attn.reshape(head_shape)
    grad_prob_one = jnp.einsum(
        "sthd,slhd->shtl", grad_attn_heads, mix_low, preferred_element_type=jnp.float32
    )
    mixing_part = jnp.einsum(
        "shtl,sthd->slhd", prob_low, grad_attn_heads, preferred_element_type=jnp.float32
    )
    grad_mixing = lax.psum(mixing_part.astype(jnp.bfloat16), "seq").astype(jnp.float32)
    grad_score_one = softmax_back(prob_one, grad_prob_one).astype(jnp.bfloat16)
    query_local = (
        jnp.einsum(
            "shtl,slhd->sthd",
            grad_score_one,
            landmark_key_heads,
            preferred_element_type=jnp.float32,
        )
        * logit_scale_factor
    )
    land_k_part = (
        jnp.einsum(
            "shtl,sthd->slhd", grad_score_one, query_heads, preferred_element_type=jnp.float32
        )
        * logit_scale_factor
    )
    grad_pad = with_halo(
        grad_attn.reshape(seq_count, local_len, model_width), (("seq", 1),), reach_width
    )
    attn_float = grad_attn.reshape(seq_count, local_len, model_width).astype(jnp.float32)
    conv_back = jnp.zeros((seq_count, local_len, model_width), jnp.float32)
    tap_terms = []
    for offset in range(tap_count):
        start_row = 2 * reach_width - offset
        conv_back = conv_back + tap_chan[:, offset] * grad_pad[
            :, start_row : start_row + local_len
        ].astype(jnp.float32)
        tap_terms.append(
            jnp.sum(
                attn_float * padded_values[:, offset : offset + local_len].astype(jnp.float32),
                axis=(0, 1),
            )
        )
    grad_taps = jnp.sum(
        jnp.stack(tap_terms, axis=1).reshape(head_count, head_size, tap_count), axis=1
    )
    grad_inverse = jnp.einsum(
        "slhd,smhd->shlm", grad_mixing, landmark_value_rows, precision=top_precision
    )
    grad_land_values = jnp.einsum(
        "shlm,slhd->smhd", inverse_matrix, grad_mixing, precision=top_precision
    )
    land_grad_low = grad_land_values.astype(jnp.bfloat16).astype(jnp.float32)
    grad_prob_two = inverse_pull(grad_inverse)[0]
    grad_score_two = softmax_back(second_probability, grad_prob_two)
    query_two = (
        jnp.einsum("shlm,smhd->slhd", grad_score_two, lk_float, precision=top_precision)
        * logit_scale_factor
    )
    key_two = (
        jnp.einsum("shlm,slhd->smhd", grad_score_two, lq_float, precision=top_precision)
        * logit_scale_factor
    )
    grad_numer = land_grad_low / denom_swap
    expo_low = expo_three.astype(jnp.bfloat16).astype(jnp.float32)
    value_three = jnp.einsum("shlt,slhd->sthd", expo_low, grad_numer, precision=top_precision)
    grad_expo = jnp.einsum(
        "slhd,sthd->shlt", grad_numer, value_heads.astype(jnp.float32), precision=top_precision
    )
    grad_denom = jnp.swapaxes(jnp.sum(land_grad_low * landmark_value_rows, axis=-1), 1, 2) / denom
    grad_score_three = (expo_three * (grad_expo - grad_denom[..., None])).astype(jnp.bfloat16)
    land_q_part = (
        jnp.einsum(
            "shlt,sthd->slhd", grad_score_three, key_heads, preferred_element_type=jnp.float32
        )
        * logit_scale_factor
    )
    key_local = (
        jnp.einsum(
            "shlt,slhd->sthd",
            grad_score_three,
            landmark_query_heads,
            preferred_element_type=jnp.float32,
        )
        * logit_scale_factor
    )
    land_q_own, land_k_own = (
        lax.psum_scatter(
            land_q_part.astype(jnp.bfloat16), "seq", scatter_dimension=1, tiled=True
        ).astype(jnp.float32),
        lax.psum_scatter(
            land_k_part.astype(jnp.bfloat16), "seq", scatter_dimension=1, tiled=True
        ).astype(jnp.float32),
    )
    first_land = lax.axis_index("seq") * land_local
    land_q_own = land_q_own + lax.dynamic_slice_in_dim(query_two, first_land, land_local, 1)
    land_k_own = land_k_own + lax.dynamic_slice_in_dim(key_two, first_land, land_local, 1)
    spread_shape = (seq_count, land_local, seg_len, head_count, head_size)
    spread_q = jnp.broadcast_to((land_q_own / seg_len)[:, :, None], spread_shape).reshape(
        head_shape
    )
    spread_k = jnp.broadcast_to((land_k_own / seg_len)[:, :, None], spread_shape).reshape(
        head_shape
    )
    grad_query = (query_local + spread_q).reshape(row_count, model_width)
    grad_key = (key_local + spread_k).reshape(row_count, model_width)
    grad_value = value_three.reshape(row_count, model_width) + conv_back.reshape(
        row_count, model_width
    )
    grad_proj = jnp.concatenate([grad_query, grad_key, grad_value], axis=1).astype(jnp.bfloat16)
    grad_qkv = jnp.einsum("nd,ne->de", flat_in, grad_proj, preferred_element_type=jnp.float32)
    input_grad = (
        jnp.einsum("ne,de->nd", grad_proj, full_qkv, preferred_element_type=jnp.float32)
        + grad_resid_one
    )
    input_grad = input_grad.astype(jnp.bfloat16).reshape(tokens.shape)
    bias_sums = jnp.sum(grad_proj.astype(jnp.float32), axis=0)
    grad_vec = jnp.concatenate(
        [
            bias_sums[None, :model_width],
            bias_sums[None, 2 * model_width :],
            jnp.sum(grad_branch.astype(jnp.float32), axis=0)[None],
            grad_shift_one[None],
            jnp.sum(grad_ff.astype(jnp.float32), axis=0)[None],
            grad_shift_two[None],
            grad_gain_one[None],
            grad_gain_two[None],
            jnp.sum(grad_hidden.astype(jnp.float32), axis=0).reshape(-1, model_width),
        ],
        axis=0,
    )
    summed_qkv, summed_out, summed_up, summed_down, summed_vec = (
        lax.psum_scatter(grad_qkv, ("rows", "seq"), scatter_dimension=0, tiled=True),
        lax.psum_scatter(grad_out, ("rows", "seq"), scatter_dimension=0, tiled=True),
        lax.psum_scatter(grad_up, ("rows", "seq"), scatter_dimension=0, tiled=True),
        lax.psum_scatter(grad_down, ("rows", "seq"), scatter_dimension=0, tiled=True),
        lax.psum_scatter(grad_vec, ("rows", "seq"), scatter_dimension=1, tiled=True),
    )
    summed_taps = lax.psum(grad_taps, ("rows", "seq"))
    new_qkv = adam_step(qkv_weight, qkv_first, qkv_second, summed_qkv, rate_matrix, decay_rate)
    new_out = adam_step(out_weight, out_first, out_second, summed_out, rate_output, decay_rate)
    new_up = adam_step(up_weight, up_first, up_second, summed_up, rate_matrix, decay_rate)
    new_down = adam_step(down_weight, down_first, down_second, summed_down, rate_matrix, decay_rate)
    new_vec = adam_step(vectors, vec_first, vec_second, summed_vec, rate_vector, 0.0)
    new_taps = adam_step(taps, tap_first, tap_second, summed_taps, rate_taps, 0.0)
    out_tokens = layer_out.astype(jnp.bfloat16).reshape(tokens.shape)
    return (out_tokens, input_grad) + new_qkv + new_out + new_up + new_down + new_vec + new_taps


BF = jnp.bfloat16
F32 = jnp.float32
MESH = pl.DeviceIdType.MESH


def remote(src, dst, send_sem, recv_sem, device):
    return pltpu.make_async_remote_copy(
        src_ref=src, dst_ref=dst, send_sem=send_sem, recv_sem=recv_sem,
        device_id=device, device_id_type=MESH,
    )


def place():
    row, spot = lax.axis_index("rows"), lax.axis_index("seq")
    line, core = spot // 2, spot % 2
    flip_one = row + 1 - 2 * (row % 2)
    flip_two = row + 2 - 4 * (row // 2)
    first = (1 - core) * flip_one + core * flip_two
    second = (1 - core) * flip_two + core * flip_one
    return row, line, core, first, second, 3 - row


def greet(devices):
    barrier = pltpu.get_barrier_semaphore()
    for device in devices:
        pl.semaphore_signal(barrier, inc=1, device_id=device, device_id_type=MESH)
    pl.semaphore_wait(barrier, len(devices))


class Net:
    def __init__(self, send, recv):
        self.send, self.recv, self.started = send, recv, []
        self.row, self.line, self.core, self.first, self.second, self.across = place()
        self.line_size = lax.axis_size("seq") // 2
        own_spot = 2 * self.line + self.core
        self.sibling = (self.row, 2 * self.line + 1 - self.core)
        self.peers = [
            (self.row, 2 * ((self.line + k) % self.line_size) + self.core)
            for k in range(1, self.line_size)
        ]
        self.to_first, self.to_second = (self.first, own_spot), (self.second, own_spot)

    def go(self, w, k, src, dst, device):
        copy = remote(src, dst, self.send.at[w, k], self.recv.at[w, k], device)
        copy.start()
        self.started.append(copy)
        return copy

    def finish(self):
        for copy in self.started:
            copy.wait_send()


def columns(base, which, half):
    return pl.ds(pl.multiple_of(base + which * half, 128), half)


class Gather:
    def __init__(self, net, w, src, dst, base, half, asm, stage, local):
        self.net, self.w, self.dst, self.stage, self.asm = net, w, dst, stage, asm
        self.rows, self.base, self.half, self.local = src.shape[0], base, half, local
        part = pl.ds(pl.multiple_of(net.core * self.rows, 8), self.rows)
        there = columns(base, 1 - net.core, half)
        self.asm_copy = net.go(w, 0, src.at[:, there], asm.at[part, :], net.sibling)
        asm[part, :] = src[:, columns(base, net.core, half)]

    def block(self, start, size):
        at = pl.ds(pl.multiple_of(start, 16), size)
        return self.dst.at[at, columns(self.base, self.net.core, self.half)]

    def slab(self, index):
        size = 2 * self.rows * self.net.line_size
        return self.block(index * size, size)

    def spread(self):
        net = self.net
        self.asm_copy.wait_recv()
        self.stage[...] = self.asm[...].astype(BF)
        size = 2 * self.rows
        block = self.block((net.row * net.line_size + net.line) * size, size)
        self.z = [net.go(self.w, 1 + k, self.stage, block, d) for k, d in enumerate(net.peers)]
        self.own = pltpu.make_async_copy(self.stage, block, self.local)
        self.own.start()

    def step_one(self):
        net, w, z0 = self.net, self.w, self.net.line_size
        self.own.wait()
        for copy in self.z:
            copy.wait_recv()
        mine = self.slab(net.row)
        self.hop = [net.go(w, z0, mine, mine, net.to_first)]
        self.hop.append(net.go(w, z0 + 1, mine, mine, net.to_second))
        self.sib = [net.go(w, z0 + 3, mine, mine, net.sibling)]

    def step_two(self):
        net, w, z0 = self.net, self.w, self.net.line_size
        self.hop[0].wait_recv()
        got = self.slab(net.first)
        self.hop.append(net.go(w, z0 + 2, got, got, net.to_second))
        self.sib.append(net.go(w, z0 + 4, got, got, net.sibling))

    def step_three(self):
        net, w, z0 = self.net, self.w, self.net.line_size
        self.hop[1].wait_recv()
        got = self.slab(net.second)
        self.sib.append(net.go(w, z0 + 5, got, got, net.sibling))
        self.hop[2].wait_recv()
        got = self.slab(net.across)
        self.sib.append(net.go(w, z0 + 6, got, got, net.sibling))

    def close(self):
        for copy in self.sib:
            copy.wait_recv()


GATHER_SEMS = 7


class Scatter:
    def __init__(self, net, w, out, base, half, bufs):
        self.net, self.w, self.out, self.base, self.half = net, w, out, base, half
        self.acc, self.buf0, self.buf1, self.buf2, self.buf3, self.fin = bufs
        self.rows = out.shape[0]
        self.size = 2 * self.rows * net.line_size

    def open(self, outbox, own=None):
        self.sib = self.net.go(self.w, 0, outbox, self.buf0, self.net.sibling)
        self.own = own
        if own is not None:
            own.start()

    def slab(self, index):
        return pl.ds(pl.multiple_of(index * self.size, self.size), self.size)

    def add(self, index, other, start):
        step = 48
        acc = self.acc

        def one(i, carry):
            at = pl.ds(pl.multiple_of(index * self.size + i * step, 16), step)
            there = pl.ds(pl.multiple_of(start + i * step, 16), step)
            acc[at, :] = acc[at, :] + other[there, :]
            return carry

        lax.fori_loop(0, self.size // step, one, 0)

    def step_one(self):
        net, w = self.net, self.w
        if self.own is not None:
            self.own.wait()
        self.sib.wait_recv()
        self.add(net.across, self.buf0, net.across * self.size)
        acc = self.acc
        self.one = net.go(w, 1, acc.at[self.slab(net.across), :], self.buf1.at[0], net.to_second)
        self.add(net.second, self.buf0, net.second * self.size)
        self.two = net.go(w, 2, acc.at[self.slab(net.second), :], self.buf1.at[1], net.to_second)
        self.add(net.first, self.buf0, net.first * self.size)
        self.add(net.row, self.buf0, net.row * self.size)

    def step_two(self):
        net = self.net
        self.one.wait_recv()
        self.add(net.first, self.buf1.at[0], 0)
        src = self.acc.at[self.slab(net.first), :]
        self.three = net.go(self.w, 3, src, self.buf2, net.to_first)
        self.two.wait_recv()
        self.add(net.row, self.buf1.at[1], 0)

    def step_three(self):
        net = self.net
        self.three.wait_recv()
        self.add(net.row, self.buf2, 0)
        block, n = 2 * self.rows, net.line_size
        self.z = []

        def at(line):
            return pl.ds(pl.multiple_of((net.row * n + line) * block, block), block)

        for k, device in enumerate(net.peers):
            src = self.acc.at[at((net.line + 1 + k) % n), :]
            self.z.append(net.go(self.w, 4 + k, src, self.buf3.at[net.line], device))
        self.buf3[net.line] = self.acc[at(net.line), :]

    def step_four(self):
        net = self.net
        for copy in self.z:
            copy.wait_recv()
        total = self.buf3[0].astype(F32)
        for k in range(1, net.line_size):
            total = total + self.buf3[k].astype(F32)
        self.fin[...] = total
        part = pl.ds(pl.multiple_of((1 - net.core) * self.rows, 8), self.rows)
        here = columns(self.base, net.core, self.half)
        self.last = net.go(
            self.w, 3 + net.line_size, self.fin.at[part, :], self.out.at[:, here], net.sibling
        )
        part = pl.ds(pl.multiple_of(net.core * self.rows, 8), self.rows)
        self.out[:, here] = self.fin[part, :]

    def close(self):
        self.last.wait_recv()


SCATTER_SEMS = 4


def scatter_scratch(rows, half, dtype, line_size):
    quarter = 2 * rows * line_size
    return [
        pltpu.VMEM((4 * quarter, half), dtype),
        pltpu.VMEM((4 * quarter, half), dtype),
        pltpu.VMEM((2, quarter, half), dtype),
        pltpu.VMEM((quarter, half), dtype),
        pltpu.VMEM((line_size, 2 * rows, half), dtype),
        pltpu.VMEM((2 * rows, half), F32),
    ]


class Many:
    def __init__(self, pieces):
        self.pieces = list(pieces)

    def each(self, step):
        for piece in self.pieces:
            getattr(piece, step)()

    def spread(self):
        self.each("spread")

    def step_one(self):
        self.each("step_one")

    def step_two(self):
        self.each("step_two")

    def step_three(self):
        self.each("step_three")

    def step_four(self):
        self.each("step_four")

    def close(self):
        self.each("close")


PAIR = 128


def nn(a, b):
    return jnp.dot(a, b, preferred_element_type=F32)


def nt(a, b):
    return lax.dot_general(a, b, (((1,), (1,)), ((), ())), preferred_element_type=F32)


def tn(a, b):
    return lax.dot_general(a, b, (((0,), (0,)), ((), ())), preferred_element_type=F32)


def split(x):
    high = x.astype(BF)
    return high, (x - high.astype(F32)).astype(BF)


def three(dot, a, b):
    return dot(a[0], b[0]) + (dot(a[0], b[1]) + dot(a[1], b[0]))


def lane_masks(dtype):
    lane = lax.broadcasted_iota(jnp.int32, (1, PAIR), 1)
    one = (lane < PAIR // 2).astype(F32)
    return one.astype(dtype), (1.0 - one).astype(dtype)


def apart(x):
    one, two = lane_masks(x.dtype)
    return jnp.concatenate([x * one, x * two], axis=0)


def together(x):
    half = PAIR // 2
    lane = lax.broadcasted_iota(jnp.int32, (half, PAIR), 1)
    return jnp.where(lane < half, x[:half], x[half:])


def same_head():
    half = PAIR // 2
    a = lax.broadcasted_iota(jnp.int32, (PAIR, PAIR), 0) // half
    b = lax.broadcasted_iota(jnp.int32, (PAIR, PAIR), 1) // half
    return a == b


def eye():
    a = lax.broadcasted_iota(jnp.int32, (PAIR, PAIR), 0)
    b = lax.broadcasted_iota(jnp.int32, (PAIR, PAIR), 1)
    return (a == b).astype(F32)


def by_head(x, reduce):
    half, width = PAIR // 2, x.shape[1]
    parts = [reduce(x[h * half : (h + 1) * half], axis=0, keepdims=True) for h in (0, 1)]
    return jnp.concatenate([jnp.broadcast_to(y, (half, width)) for y in parts], axis=0)


def lanes(p):
    if isinstance(p, int):
        return pl.ds(p * PAIR, PAIR)
    return pl.ds(pl.multiple_of(p * PAIR, PAIR), PAIR)


def conv_pair(table, padded):
    size = table.shape[0] // 4
    out = nn(table, padded)
    lane = lax.broadcasted_iota(jnp.int32, (size, PAIR), 1)
    return jnp.where(
        lane < PAIR // 2,
        out[:size] + out[2 * size : 3 * size],
        out[size : 2 * size] + out[3 * size :],
    )


class Group:
    def __init__(self, send, recv):
        self.row, self.me = lax.axis_index("rows"), lax.axis_index("seq")
        self.size = lax.axis_size("seq")
        self.send, self.recv, self.started = send, recv, []

    def peers(self):
        return [(self.row, (self.me + k) % self.size) for k in range(1, self.size)]

    def push(self, channel, pick_src, dst):
        copies = []
        for k, device in enumerate(self.peers()):
            copy = remote(
                pick_src(device[1]), dst, self.send.at[channel, k], self.recv.at[channel, k], device
            )
            copy.start()
            copies.append(copy)
        self.started += copies
        return copies

    def line_peers(self):
        n, line, core = self.size // 2, self.me // 2, self.me % 2
        return [(self.row, 2 * ((line + k) % n) + core) for k in range(1, n)]

    def go(self, channel, k, src, dst, device):
        copy = remote(src, dst, self.send.at[channel, k], self.recv.at[channel, k], device)
        copy.start()
        self.started.append(copy)
        return copy

    def share(self, parts):
        n, line, core = self.size // 2, self.me // 2, self.me % 2
        sibling = (self.row, 2 * line + 1 - core)
        there, here = [], []
        for channel, block in parts:
            mine = block(self.me)
            there.append(
                [self.go(channel, k, mine, mine, d) for k, d in enumerate(self.line_peers())]
            )
        for channel, block in parts:
            here.append(self.go(channel, n - 1, block(self.me), block(self.me), sibling))

        def arrive():
            for k in range(1, n):
                source = 2 * ((line - k + n) % n) + core
                for (channel, block), copies in zip(parts, there):
                    copies[k - 1].wait_recv()
                    got = block(source)
                    here.append(self.go(channel, n - 1 + k, got, got, sibling))
            for copy in here:
                copy.wait_recv()

        return arrive

    def halo(self, channel, source, padded, reach):
        length = source.shape[1]
        copies = []
        for which, (src_at, dst_at, step) in enumerate(
            ((length - reach, 0, 1), (0, length + reach, -1))
        ):
            there = (self.me + step + self.size) % self.size
            copy = remote(
                source.at[:, pl.ds(src_at, reach), :],
                padded.at[:, pl.ds(dst_at, reach), :],
                self.send.at[channel, which],
                self.recv.at[channel, which],
                (self.row, there),
            )
            goes = self.me < self.size - 1 if step == 1 else self.me > 0
            comes = self.me > 0 if step == 1 else self.me < self.size - 1
            pl.when(goes)(copy.start)
            copies.append((copy, goes, comes, dst_at))

        def arrive():
            for copy, goes, comes, dst_at in copies:
                pl.when(comes)(copy.wait_recv)

                @pl.when(jnp.logical_not(comes))
                def _():
                    shape = (padded.shape[0], reach, padded.shape[2])
                    padded[:, pl.ds(dst_at, reach), :] = jnp.zeros(shape, padded.dtype)

        def sent():
            for copy, goes, _, _ in copies:
                pl.when(goes)(copy.wait_send)

        return arrive, sent

    def finish(self):
        for copy in self.started:
            copy.wait_send()


def pinv_start(prob):
    total = by_head(jnp.sum(prob * prob, axis=1, keepdims=True), jnp.sum)
    return prob.T / total


def pinv_terms(p, z, unit):
    product = three(nn, p, z)
    prod = split(product)
    term_one = 7.0 * unit - product
    term_two = 15.0 * unit - three(nn, prod, split(term_one))
    term_three = 13.0 * unit - three(nn, prod, split(term_two))
    return prod, term_one, term_two, term_three


def band(line, length, reach):
    wide = jnp.broadcast_to(line, (length, line.shape[1]))
    return pltpu.roll(wide, 0, 1, stride=1, stride_axis=0)[:, : length + 2 * reach]


def set_lines(taps, lines, flip):
    count = taps.shape[1]
    lines[...] = jnp.zeros(lines.shape, F32)
    lines[:, :count] = taps[...]
    if flip:
        a = lax.broadcasted_iota(jnp.int32, (PAIR, PAIR), 0)
        b = lax.broadcasted_iota(jnp.int32, (PAIR, PAIR), 1)
        turn = (a + b == count - 1).astype(F32).astype(BF)
        high, low = split(lines[:, :PAIR])
        lines[:, :PAIR] = nn(high, turn) + nn(low, turn)


def fill_bands(lines, table, reach):
    pairs, rows = table.shape[0], table.shape[1] // 4
    for p in range(pairs):
        for h in (0, 1):
            high, low = split(band(lines[2 * p + h : 2 * p + h + 1, :], rows, reach))
            table[p, h * rows : (h + 1) * rows, :] = high
            table[p, (2 + h) * rows : (3 + h) * rows, :] = low


def gelu_parts(x):
    expo = jnp.exp(-0.5 * x * x)
    t = 1.0 / (1.0 + (0.3275911 * 0.7071067811865476) * jnp.abs(x))
    tail = -0.284496736 + t * (1.421413741 + t * (-1.453152027 + t * 1.061405429))
    tail = 0.5 * expo * t * (0.254829592 + t * tail)
    below = jnp.where(x >= 0.0, 1.0 - tail, tail)
    return x * below, below + x * expo * 0.3989422804014327


def norm_parts(resid):
    center = resid - jnp.mean(resid, axis=-1, keepdims=True)
    scale = lax.rsqrt(jnp.mean(center * center, axis=-1, keepdims=True) + norm_eps)
    return center * scale, scale


def norm_back(grad, gain, unit, scale):
    inner = grad * gain
    mean = jnp.mean(inner, axis=-1, keepdims=True)
    along = jnp.mean(inner * unit, axis=-1, keepdims=True)
    return scale * (inner - mean - unit * along)


def row_sum(x):
    return jnp.sum(x, axis=0, keepdims=True)


def front_kernel(
    reach,
    tokens, h_cot, qkv_w, out_w, up_w, down_w, vectors, taps,
    h_layer, h_one, h_ga, sums, d_down, d_up, d_out,
    h_qkv, h_q, h_k, h_vpad, h_landq, h_landk, h_mix, h_p1, h_e, h_wt, h_p2o, h_zo, h_lvo,
    f_qkv, q, k, vpad, landq, landk, mix, p1, e, wt, p2o, zo, lvo,
    w_out, w_up, w_down, vecs, attn, v, table, f_vec, lb, numer, nrecv, stat, srecv, mstat, conv, fcol,
    g_down, g_up, active, slope, unit_one, scale_one, normed, low, low_t, total, ff, attn_t, *rest,
):
    keep_sem, o_sem, lines, vec_w, square, cot, layer_out, grad_one, ga, way_sem = rest[-10:]
    rest = rest[:-10]
    cot_in = pltpu.make_async_copy(h_cot, cot, way_sem.at[0])
    cot_in.start()
    results = [
        pltpu.make_async_copy(a, b, way_sem.at[1 + i])
        for i, (a, b) in enumerate(((layer_out, h_layer), (grad_one, h_one), (ga, h_ga)))
    ]
    set_lines(taps, lines, False)
    square[...] = jnp.zeros(square.shape, F32)
    square[: vectors.shape[0], : vectors.shape[1]] = vectors[...]
    vec_w[...] = jnp.zeros(vec_w.shape, F32)
    vec_w[:, :PAIR] = square[...].T[: vec_w.shape[0]]
    asm, stage = rest[:7], rest[7:14]
    g_send, g_recv, g_local, send, recv = rest[14:19]
    net, group = Net(g_send, g_recv), Group(send, recv)
    me, size = group.me, group.size
    n_seq, length, width = q.shape
    pairs = width // PAIR
    own = n_seq * pairs // size
    each = own * PAIR
    land_local = LAND // size
    seg = length // land_local
    scale = (PAIR // 2) ** -0.5
    greet(group.peers() + [net.to_first, net.to_second])

    def owner_seq(d):
        return d * own // pairs

    def owner_lanes(d):
        return pl.ds(pl.multiple_of((d * own % pairs) * PAIR, PAIR), each)

    plan = [(vec_w, f_vec, 0), (qkv_w, f_qkv, width), (qkv_w, f_qkv, 0), (qkv_w, f_qkv, 2 * width)]
    plan += [(out_w, w_out, 0), (up_w, w_up, 0), (down_w, w_down, 0)]
    pieces = []
    for w, (src, dst, base) in enumerate(plan):
        half = asm[w].shape[1]
        pieces.append(Gather(net, w, src, dst, base, half, asm[w], stage[w], g_local.at[w]))
    t_vec, t_k, t_q, t_v, t_out, t_up, t_down = pieces
    for piece in pieces[:4]:
        piece.spread()
    t_out.spread()
    t_up.spread()
    fill_bands(lines, table, reach)

    def project(dst, base, bias):
        step = 2 * PAIR
        for at in range(0, width, step):
            x = nn(tokens[...], f_qkv[:, base + at : base + at + step])
            if bias is not None:
                x = x + vecs[bias : bias + 1, at : at + step]
            dst[:, :, at : at + step] = x.astype(BF).reshape(n_seq, length, step)

    t_vec.step_one()
    t_k.step_one()
    t_q.step_one()
    t_vec.step_two()
    t_k.step_two()
    t_v.step_one()
    t_down.spread()
    t_vec.step_three()
    t_q.step_two()
    t_k.step_three()
    t_vec.close()
    vecs[...] = f_vec[:, :PAIR].astype(F32).T[: vecs.shape[0]]
    t_v.step_two()
    t_k.close()
    project(k, width, None)
    t_q.step_three()
    t_q.close()
    project(q, 0, 0)
    t_v.step_three()
    t_out.step_one()
    t_up.step_one()
    t_v.close()
    project(v, 2 * width, 1)

    def own_landmarks(s, carry):
        both = [
            jnp.mean(x[s].astype(F32).reshape(land_local, seg, width), axis=1) for x in (q, k)
        ]
        lb[me, s] = jnp.concatenate(both, axis=0).astype(BF)
        vpad[s, pl.ds(reach, length), :] = v[s]
        return carry

    lax.fori_loop(0, n_seq, own_landmarks, 0)
    landed = group.share([(1, lambda d: lb.at[d])])
    halo_in, halo_sent = group.halo(0, v, vpad, reach)
    t_out.step_two()
    t_down.step_one()
    landed()

    def whole_landmarks(s, carry):
        x = lb[:, s].astype(F32)
        landq[s] = x[:, :land_local].reshape(LAND, width).astype(BF)
        landk[s] = x[:, land_local:].reshape(LAND, width).astype(BF)
        return carry

    lax.fori_loop(0, n_seq, whole_landmarks, 0)
    lane_at = lax.broadcasted_iota(jnp.int32, (PAIR, PAIR), 1)

    def over_tokens(s, tile):
        for p in range(pairs):
            score = nt(apart(landq[s, :, lanes(p)]), k[s, :, lanes(p)]) * scale
            top = jnp.max(score, axis=1, keepdims=True)
            expo = jnp.exp(score - top)
            expo_low = expo.astype(BF)
            e[s * pairs + p] = expo_low
            numer[s, :, lanes(p)] = together(nn(expo_low, v[s, :, lanes(p)])).astype(BF)
            unit = s * pairs + p
            at = (unit // own) * 8 + unit % own
            tile = jnp.where(lane_at == at, top, tile)
            tile = jnp.where(lane_at == at + own, jnp.sum(expo, axis=1, keepdims=True), tile)
        return tile

    tile = lax.fori_loop(0, n_seq, over_tokens, jnp.zeros((PAIR, PAIR), F32))
    stat[...] = tile.T[: 8 * size].reshape(size, 8, PAIR)
    sums_in = group.push(
        2, lambda d: numer.at[owner_seq(d), :, owner_lanes(d)], nrecv.at[me]
    )
    stats_in = group.push(3, lambda d: stat.at[d], srecv.at[me])
    t_up.step_two()
    nrecv[me] = numer[owner_seq(me), :, owner_lanes(me)]
    srecv[me] = stat[me]

    block, unit_matrix = same_head(), eye()
    my_seq, my_pair = owner_seq(me), (me * own) % pairs
    for i in range(own):
        at = lanes(my_pair + i)
        score = nt(apart(landq[my_seq, :, at]), apart(landk[my_seq, :, at])) * scale
        score = jnp.where(block, score, -1e30)
        expo = jnp.exp(score - jnp.max(score, axis=1, keepdims=True))
        prob = expo / jnp.sum(expo, axis=1, keepdims=True)
        p2o[i] = prob
        zo[0, i] = pinv_start(prob)

    halo_in()
    per_step = n_seq * pairs // PINV_ITERS

    def over_landmarks(unit):
        s, p = unit // pairs, unit % pairs
        score = nt(apart(landk[s, :, lanes(p)]), q[s, :, lanes(p)]) * scale
        expo = jnp.exp(score - by_head(score, jnp.max))
        p1[unit] = expo / by_head(expo, jnp.sum)
        conv[s, :, lanes(p)] = conv_pair(table[p], vpad[s, :, lanes(p)])

    def pinv_step(step, carry):
        for i in range(own):
            z = split(zo[step, i])
            _, _, _, inner = pinv_terms(split(p2o[i]), z, unit_matrix)
            zo[step + 1, i] = 0.25 * three(nn, z, split(inner))
        for j in range(per_step):
            over_landmarks(step * per_step + j)
        return carry

    lax.fori_loop(0, PINV_ITERS // 2, pinv_step, 0)
    t_out.step_three()
    lax.fori_loop(PINV_ITERS // 2, PINV_ITERS, pinv_step, 0)
    t_down.step_two()

    for copy in sums_in + stats_in:
        copy.wait_recv()
    got = srecv[...]
    tops = got[:, :own]
    top = jnp.max(tops, axis=0, keepdims=True)
    factor = jnp.exp(tops - top)
    weight_sum = jnp.sum(factor * got[:, own : 2 * own], axis=0, keepdims=True)
    factor = factor / weight_sum
    spare = jnp.zeros((1, 8 - 2 * own, PAIR), F32)
    mstat[me] = jnp.concatenate([top, weight_sum, spare], axis=1)[0]
    spread = jnp.concatenate([factor, jnp.zeros((size, 8 - own, PAIR), F32)], axis=1)
    spread = spread.reshape(8 * size, PAIR)
    fcol[...] = jnp.concatenate([spread, jnp.zeros((PAIR - 8 * size, PAIR), F32)], axis=0).T
    half = PAIR // 2
    narrow = lax.broadcasted_iota(jnp.int32, (half, PAIR), 1) < half
    for i in range(own):
        at = pl.ds(i * PAIR, PAIR)
        mean = jnp.zeros((half, PAIR), F32)
        for src in range(size):
            column = fcol[:, src * 8 + i : src * 8 + i + 1]
            weight = jnp.where(narrow, column[:half], column[half:])
            mean = mean + weight * nrecv[src, :, at].astype(F32)
        lvo[:, at] = mean
        mixed = together(three(nn, split(zo[PINV_ITERS, i]), split(apart(mean))))
        mix[my_seq, :, lanes(my_pair + i)] = mixed.astype(BF)
    mixed_in = group.share(
        [
            (4, lambda d: mix.at[owner_seq(d), :, owner_lanes(d)]),
            (5, lambda d: mstat.at[d]),
        ]
    )
    t_up.step_three()
    mixed_in()

    rows = jnp.concatenate(
        [mstat[...].reshape(8 * size, PAIR), jnp.zeros((PAIR - 8 * size, PAIR), F32)], axis=0
    )
    rows = rows.T
    valid = (lane_at % 8 < own) & (lane_at < 8 * size)
    shift = jnp.where(valid, tile - rows, 0.0)
    den = jnp.where(valid, pltpu.roll(rows, PAIR - own, 1), 1.0)
    wt[...] = jnp.exp(shift) / den

    def result(s, carry):
        for p in range(pairs):
            prob = p1[s * pairs + p].astype(BF)
            out = tn(prob, apart(mix[s, :, lanes(p)])) + conv[s, :, lanes(p)]
            at = pl.ds(pl.multiple_of(s * length, length), length)
            attn[at, lanes(p)] = out.astype(BF)
        return carry

    lax.fori_loop(0, n_seq, result, 0)
    held = [f_qkv, q, k, vpad, landq, landk, mix, p1, e, wt, p2o, zo, lvo]
    homes = [h_qkv, h_q, h_k, h_vpad, h_landq, h_landk, h_mix, h_p1, h_e, h_wt, h_p2o, h_zo, h_lvo]
    keeps = [
        pltpu.make_async_copy(a, b, keep_sem.at[i]) for i, (a, b) in enumerate(zip(held, homes))
    ]
    for keep in keeps:
        keep.start()
    count = tokens.shape[0]
    hidden = w_up.shape[1]
    chunk_size = 2 * PAIR
    n_rows, n_wide = count // chunk_size, width // chunk_size
    row_groups = hidden // width
    sums[...] = jnp.zeros(sums.shape, F32)

    def row(i):
        return vecs[i : i + 1, :]

    def row_block(i):
        return pl.ds(pl.multiple_of(i * chunk_size, chunk_size), chunk_size)

    t_out.close()

    def first(i, carry):
        at = row_block(i)
        resid = tokens[at, :].astype(F32) + (nn(attn[at, :], w_out[...]) + row(2))
        unit, scale = norm_parts(resid)
        out = unit * row(6) + row(3)
        unit_one[at, :] = unit
        scale_one[at, :] = jnp.broadcast_to(scale, (chunk_size, PAIR))
        normed[at, :] = out
        low[at, :] = out.astype(BF)
        total[at, :] = jnp.broadcast_to(row(4), (chunk_size, width))
        return carry

    lax.fori_loop(0, n_rows, first, 0)
    t_down.step_three()
    t_up.close()
    low_t[...] = low[...].T
    attn_t[...] = attn[...].T

    def chunk(r, j):
        start = r * width + j * chunk_size
        return slice(start, start + chunk_size)

    def whole(r):
        return slice(r * width, (r + 1) * width)

    def gather_down(r):
        for n in range(n_wide):
            at = slice(n * chunk_size, (n + 1) * chunk_size)
            total[:, at] += nn(active[:, whole(r)], w_down[whole(r), at])

    for r in range(row_groups):
        for j in range(n_wide):
            f = chunk(r, j)
            bias = vecs[8 + r : 9 + r, j * chunk_size : (j + 1) * chunk_size]
            value, rate = gelu_parts(nn(low[...], w_up[:, f]) + bias)
            active[:, f] = value.astype(BF)
            slope[:, f] = rate.astype(BF)
        if r == 1:
            t_down.close()
        if r > 0:
            gather_down(r - 1)
    gather_down(row_groups - 1)

    def second(i, carry):
        at = row_block(i)
        unit, scale = norm_parts(normed[at, :] + total[at, :])
        layer_out[at, :] = (unit * row(7) + row(5)).astype(BF)
        up = cot[at, :].astype(F32)
        grad = norm_back(up, row(7), unit, scale)
        total[at, :] = grad
        grad = grad.astype(BF)
        ff[at, :] = grad
        sums[4:5, :] += row_sum(grad.astype(F32))
        sums[5:6, :] += row_sum(up)
        sums[7:8, :] += row_sum(up * unit)
        return carry

    cot_in.wait()
    lax.fori_loop(0, n_rows, second, 0)
    results[0].start()

    def leave(r):
        f = whole(r)
        return [
            pltpu.make_async_copy(g_down.at[r % 2], d_down.at[f, :], o_sem.at[0, r]),
            pltpu.make_async_copy(g_up.at[r % 2], d_up.at[:, f], o_sem.at[1, r]),
        ]

    def weight_grads(r):
        if r > 1:
            for copy in leave(r - 2):
                copy.wait()
        for j in range(n_wide):
            f = chunk(r, j)
            at = slice(j * chunk_size, (j + 1) * chunk_size)
            g_up[r % 2, :, at] = nn(low_t[...], slope[:, f]).astype(BF)
            g_down[r % 2, at, :] = tn(active[:, f], ff[...]).astype(BF)
        for n in range(n_wide):
            at = slice(n * chunk_size, (n + 1) * chunk_size)
            total[:, at] += nt(slope[:, whole(r)], w_up[at, whole(r)])
        for copy in leave(r):
            copy.start()

    for r in range(row_groups):
        for j in range(n_wide):
            f = chunk(r, j)
            grad = (nt(ff[...], w_down[f, :]) * slope[:, f].astype(F32)).astype(BF)
            sums[8 + r : 9 + r, j * chunk_size : (j + 1) * chunk_size] = row_sum(grad.astype(F32))
            slope[:, f] = grad
        if r > 0:
            weight_grads(r - 1)
    weight_grads(row_groups - 1)

    def third(i, carry):
        at = row_block(i)
        unit = unit_one[at, :]
        up = total[at, :]
        grad = norm_back(up, row(6), unit, scale_one[at, :1])
        grad_one[at, :] = grad
        grad = grad.astype(BF)
        low[at, :] = grad
        ga[at, :] = nt(grad, w_out[...]).astype(BF)
        sums[2:3, :] += row_sum(grad.astype(F32))
        sums[3:4, :] += row_sum(up)
        sums[6:7, :] += row_sum(up * unit)
        return carry

    lax.fori_loop(0, n_rows, third, 0)
    results[1].start()
    results[2].start()
    for r in (row_groups - 2, row_groups - 1):
        for copy in leave(r):
            copy.wait()
    g_up[0] = nn(attn_t[...], low[...]).astype(BF)
    last = pltpu.make_async_copy(g_up.at[0], d_out, o_sem.at[2, 0])
    last.start()
    for keep in keeps + results:
        keep.wait()
    last.wait()
    halo_sent()
    group.finish()
    net.finish()


def front(tokens, cot, matrices, vectors, taps, seq_size, reach):
    n_seq, length, width = tokens.shape
    pairs = width // PAIR
    units = n_seq * pairs
    own = units // seq_size
    n_dev = 4 * seq_size
    table = jax.ShapeDtypeStruct((vectors.shape[1], 2 * PAIR), F32)
    line_size = seq_size // 2
    vmem, hbm = pl.BlockSpec(memory_space=pltpu.VMEM), pl.BlockSpec(memory_space=pltpu.HBM)
    shape = jax.ShapeDtypeStruct
    land = shape((n_seq, LAND, width), BF)
    qkv_w, out_w, up_w, down_w = matrices
    count, hidden = n_seq * length, up_w.shape[1]
    flat = (count, width)
    whole = [shape((n_dev * x.shape[0], x.shape[1]), BF) for x in matrices]
    asm = [(table.shape[0], table.shape[1] // 2)] + [(qkv_w.shape[0], width // 2)] * 3
    asm += [(x.shape[0], x.shape[1] // 2) for x in (out_w, up_w, down_w)]
    n_sem = line_size + GATHER_SEMS
    kept = [
        whole[0],
        shape(tokens.shape, BF), shape(tokens.shape, BF),
        shape((n_seq, length + 2 * reach, width), BF), land, land, land,
        shape((units, PAIR, length), F32), shape((units, PAIR, length), BF),
        shape((PAIR, PAIR), F32), shape((own, PAIR, PAIR), F32),
        shape((PINV_ITERS + 1, own, PAIR, PAIR), F32), shape((LAND, own * PAIR), F32),
    ]
    return pl.pallas_call(
        functools.partial(front_kernel, reach),
        out_shape=[shape(flat, BF), shape(flat, F32), shape(flat, BF), shape((16, width), F32)]
        + [whole[3], whole[2], whole[1]]
        + kept,
        in_specs=[vmem, hbm] + [vmem] * 6,
        out_specs=[hbm] * 3 + [vmem] + [hbm] * (3 + len(kept)),
        scratch_shapes=[pltpu.VMEM(x.shape, x.dtype) for x in kept]
        + [pltpu.VMEM(x.shape, BF) for x in whole[1:]]
        + [
            pltpu.VMEM((16, width), F32),
            pltpu.VMEM(flat, BF),
            pltpu.VMEM(tokens.shape, BF),
            pltpu.VMEM((pairs, 4 * length, length + 2 * reach), BF),
            pltpu.VMEM((n_dev * table.shape[0], table.shape[1]), BF),
            pltpu.VMEM((seq_size, n_seq, 2 * LAND // seq_size, width), BF),
            pltpu.VMEM((n_seq, LAND, width), BF),
            pltpu.VMEM((seq_size, LAND, own * PAIR), BF),
            pltpu.VMEM((seq_size, 8, PAIR), F32),
            pltpu.VMEM((seq_size, 8, PAIR), F32),
            pltpu.VMEM((seq_size, 8, PAIR), F32),
            pltpu.VMEM((n_seq, length, width), F32),
            pltpu.VMEM((PAIR, PAIR), F32),
            pltpu.VMEM((2, width, width), BF),
            pltpu.VMEM((2, width, width), BF),
            pltpu.VMEM((count, hidden), BF),
            pltpu.VMEM((count, hidden), BF),
            pltpu.VMEM(flat, F32),
            pltpu.VMEM((count, PAIR), F32),
            pltpu.VMEM(flat, F32),
            pltpu.VMEM(flat, BF),
            pltpu.VMEM((width, count), BF),
            pltpu.VMEM(flat, F32),
            pltpu.VMEM(flat, BF),
            pltpu.VMEM((width, count), BF),
        ]
        + [pltpu.VMEM((2 * r, h), F32) for r, h in asm]
        + [pltpu.VMEM((2 * r, h), BF) for r, h in asm]
        + [
            pltpu.SemaphoreType.DMA((7, n_sem)),
            pltpu.SemaphoreType.DMA((7, n_sem)),
            pltpu.SemaphoreType.DMA((7,)),
            pltpu.SemaphoreType.DMA((6, seq_size)),
            pltpu.SemaphoreType.DMA((6, seq_size)),
            pltpu.SemaphoreType.DMA((len(kept),)),
            pltpu.SemaphoreType.DMA((3, hidden // width)),
            pltpu.VMEM((2 * pairs, 2 * PAIR), F32),
            pltpu.VMEM(table.shape, F32),
            pltpu.VMEM((PAIR, PAIR), F32),
            pltpu.VMEM(flat, BF),
            pltpu.VMEM(flat, BF),
            pltpu.VMEM(flat, F32),
            pltpu.VMEM(flat, BF),
            pltpu.SemaphoreType.DMA((4,)),
        ],
        compiler_params=pltpu.CompilerParams(
            collective_id=0, has_side_effects=True, vmem_limit_bytes=61 * 1024 * 1024
        ),
        name="front",
    )(tokens.reshape(flat), cot.reshape(flat), *matrices, vectors, taps)


def back_kernel(
    reach, n_taps,
    h_ga, h_tokens, h_resid, h_qkv, h_rows, taps, d_down, d_up, d_out,
    h_q, h_k, h_vpad, h_landq, h_landk, h_mix, h_p1, h_e, h_wt, h_p2o, h_zo, h_lvo,
    input_grad, s_qkv, s_out, s_up, s_down, s_small,
    grad, tapg, table, tok_t, outbox, small_box,
    gpad, gmix, gmr, low, gfull, mstat, gcol, gq, gv, lkp, lpart, lpr, lsum, gsum, gpart, dz, dp,
    skew, own_g,
    ga, tokens, resid, f_qkv, vec_rows, q, k, vpad, landq, landk, mix, p1, e, wt, p2o, zo, lvo,
    load_sem, *rest,
):
    ways = [(h_ga, ga), (h_mix, mix), (h_p1, p1), (h_landk, landk), (h_q, q), (h_vpad, vpad)]
    ways += [(h_tokens, tokens), (h_lvo, lvo), (h_zo, zo), (h_p2o, p2o), (h_e, e), (h_wt, wt)]
    ways += [(h_landq, landq), (h_k, k), (h_rows, vec_rows), (h_qkv, f_qkv), (h_resid, resid)]
    loads = [pltpu.make_async_copy(a, c, load_sem.at[i]) for i, (a, c) in enumerate(ways)]
    for load in loads:
        load.start()

    def loaded(start, stop):
        for load in loads[start:stop]:
            load.wait()

    bufs, (g_send, g_recv, g_local, send, recv, lines) = rest[:-6], rest[-6:]
    net, group = Net(g_send, g_recv), Group(send, recv)
    me, size = group.me, group.size
    n_seq, length, width = q.shape
    pairs = width // PAIR
    own = n_seq * pairs // size
    each = own * PAIR
    land_local = LAND // size
    seg = length // land_local
    half = PAIR // 2
    scale = half**-0.5
    greet(group.peers() + [net.to_first, net.to_second])

    def owner_seq(d):
        return d * own // pairs

    def owner_lanes(d):
        return pl.ds(pl.multiple_of((d * own % pairs) * PAIR, PAIR), each)

    plan = [(s_down, 0), (s_up, 0), (s_out, 0)]
    plan += [(s_qkv, 2 * width), (s_qkv, 0), (s_qkv, width), (s_small, 0)]
    pieces = []
    for w, (out, base) in enumerate(plan):
        own_bufs = bufs[6 * w : 6 * w + 6]
        pieces.append(Scatter(net, w, out, base, own_bufs[0].shape[1], own_bufs))
    r_down, r_up, r_out, r_v, r_q, r_k, r_small = pieces

    def open_whole(w, src):
        piece = pieces[w]
        other, here = [columns(0, c, piece.half) for c in (1 - net.core, net.core)]
        own_part = pltpu.make_async_copy(src.at[:, here], piece.acc, g_local.at[w])
        piece.open(src.at[:, other], own_part)

    def open_weight(piece, box):
        step = 2 * PAIR
        rows = tok_t.shape[0]

        def one(i, carry):
            at = pl.ds(pl.multiple_of(i * step, step), step)
            x = tok_t[at, :]
            other, here = [columns(piece.base, c, piece.half) for c in (1 - net.core, net.core)]
            outbox[box, at, :] = nn(x, grad[:, other]).astype(BF)
            piece.acc[at, :] = nn(x, grad[:, here]).astype(BF)
            return carry

        lax.fori_loop(0, rows // step, one, 0)
        piece.open(outbox.at[box])

    open_whole(0, d_down)
    loaded(0, 3)
    halo_in, halo_sent = group.halo(0, ga, gpad, reach)

    def first(s, carry):
        for p in range(pairs):
            unit, at = s * pairs + p, lanes(p)
            own_ga = ga[s, :, at]
            gpad[s, pl.ds(reach, length), at] = own_ga
            prob = p1[unit]
            gmix[s, :, at] = together(nn(prob.astype(BF), own_ga)).astype(BF)
            back = nt(apart(mix[s, :, at]), own_ga)
            low[unit] = (prob * (back - by_head(prob * back, jnp.sum))).astype(BF)
        return carry

    lax.fori_loop(0, n_seq, first, 0)
    chips, my_line, my_core = size // 2, me // 2, me % 2
    core_lanes = [pl.ds(pl.multiple_of(c * each, PAIR), each) for c in (my_core, 1 - my_core)]
    sibling = (group.row, 2 * my_line + 1 - my_core)
    gmix_sib = group.go(1, chips, gmix.at[:, :, core_lanes[1]], gsum, sibling)
    r_down.step_one()
    gmix_sib.wait_recv()
    gpart[...] = gmix[:, :, core_lanes[0]] + gsum[...]
    gmix_in = []
    for kk, device in enumerate(group.line_peers()):
        other = device[1] // 2
        gmix_in.append(group.go(1, kk, gpart.at[other], gmr.at[my_line], device))
    gmr[my_line] = gpart[my_line]
    open_whole(1, d_up)
    open_whole(2, d_out)
    set_lines(taps, lines, True)
    fill_bands(lines, table, reach)
    halo_in()
    skew[...] = jnp.zeros(skew.shape, F32)

    def beside(s, carry):
        one, two_mask = lane_masks(BF)
        for p in range(pairs):
            unit, at = s * pairs + p, lanes(p)
            own_ga, padded = ga[s, :, at], vpad[s, :, at]
            gs = low[unit]
            gq[s, :, at] = tn(gs, apart(landk[s, :, at])) * scale
            lkp[s, :, at] = together(nn(gs, q[s, :, at])) * scale
            gv[s, :, at] = conv_pair(table[p], gpad[s, :, at])
            both = jnp.concatenate([own_ga * one, own_ga * two_mask], axis=0)
            skew[2 * p : 2 * p + 2, :, : length + 2 * reach] += nt(both, padded).reshape(
                2, length, length + 2 * reach
            )
        return carry

    loaded(3, 6)
    lax.fori_loop(0, n_seq, beside, 0)
    lane_at = lax.broadcasted_iota(jnp.int32, (PAIR, PAIR), 1)
    wide = skew.shape[2]
    for h in range(2 * pairs):
        total = skew[h, :8, :]
        for row in range(8, length, 8):
            total = total + pltpu.roll(skew[h, row : row + 8, :], wide - row, 1)
        tapg[h] = total[:, :PAIR]
    loaded(6, 7)
    r_up.step_one()
    tok_t[...] = tokens[...].T

    loaded(7, 10)
    for copy in gmix_in:
        copy.wait_recv()
    my_seq, my_pair = owner_seq(me), (me * own) % pairs
    tile = jnp.zeros((PAIR, PAIR), F32)
    for i in range(own):
        at = pl.ds(i * PAIR, PAIR)
        total = gmr[0, :, at].astype(F32)
        for src in range(1, chips):
            total = total + gmr[src, :, at].astype(F32)
        total = split(apart(total))
        means = apart(lvo[:, at])
        back = together(three(tn, split(zo[PINV_ITERS, i]), total)).astype(BF)
        own_g[:, at] = back
        column = jnp.sum(apart(back.astype(F32)) * means, axis=1, keepdims=True)
        tile = jnp.where(lane_at == i, column, tile)
        dz[i] = three(nt, total, split(means))
        dp[i] = jnp.zeros((PAIR, PAIR), F32)
    mstat[me] = tile.T[:8]
    gfull[my_seq, :, owner_lanes(me)] = own_g[...]
    g_in = group.share(
        [
            (2, lambda d: gfull.at[owner_seq(d), :, owner_lanes(d)]),
            (3, lambda d: mstat.at[d]),
        ]
    )
    loaded(10, 14)
    g_in()
    rows = jnp.concatenate(
        [mstat[...].reshape(8 * size, PAIR), jnp.zeros((PAIR - 8 * size, PAIR), F32)], axis=0
    )
    gcol[...] = rows.T
    unit_matrix = eye()

    def third(unit):
        s, p = unit // pairs, unit % pairs
        at = lanes(p)
        here = (unit // own) * 8 + unit % own
        picked = lane_at == here
        weight = jnp.sum(jnp.where(picked, wt[...], 0.0), axis=1, keepdims=True)
        offset = jnp.sum(jnp.where(picked, gcol[...], 0.0), axis=1, keepdims=True)
        g = apart(gfull[s, :, at])
        prob = e[unit].astype(F32) * weight
        back = nt(g, vpad[s, pl.ds(reach, length), at]) - offset
        gs = (prob * back).astype(BF)
        values = gv[s, :, at] + tn(prob.astype(BF), g)
        v_at = pl.ds(pl.multiple_of(2 * width + p * PAIR, PAIR), PAIR)
        rows = pl.ds(pl.multiple_of(s * length, length), length)
        grad[rows, v_at] = values.astype(BF)
        rows = pl.ds(pl.multiple_of(s * length, length), length)
        grad[rows, pl.ds(pl.multiple_of(width + p * PAIR, PAIR), PAIR)] = (
            tn(gs, apart(landq[s, :, at])) * scale
        ).astype(BF)
        lq = (together(nn(gs, k[s, :, at])) * scale).reshape(size, land_local, PAIR)
        lk = lkp[s, :, at].reshape(size, land_local, PAIR)
        both = jnp.concatenate([lq, lk], axis=1).astype(BF)
        lpart[:, :, s, :, at] = both.reshape(chips, 2, 2 * land_local, PAIR)

    per_step = n_seq * pairs // PINV_ITERS

    def pinv_back(step, carry):
        at_step = PINV_ITERS - 1 - step
        for i in range(own):
            p, z = split(p2o[i]), split(zo[at_step, i])
            prod, one, two_term, three_term = pinv_terms(p, z, unit_matrix)
            d_out = dz[i] * 0.25
            d_out_s = split(d_out)
            d_three = split(three(tn, z, d_out_s))
            d_two = split(-three(tn, prod, d_three))
            d_one = -three(tn, prod, d_two)
            d_prod = -three(nt, d_three, split(two_term)) - three(nt, d_two, split(one)) - d_one
            d_prod = split(d_prod)
            dp[i] += three(nt, d_prod, z)
            dz[i] = three(nt, d_out_s, split(three_term)) + three(tn, p, d_prod)
        for j in range(per_step):
            third(step * per_step + j)
        return carry

    third_of = PINV_ITERS // 3
    lax.fori_loop(0, third_of, pinv_back, 0)
    r_down.step_two()
    r_out.step_one()
    lax.fori_loop(third_of, 2 * third_of, pinv_back, 0)
    lax.fori_loop(2 * third_of, PINV_ITERS, pinv_back, 0)
    r_up.step_two()
    r_out.step_two()

    for i in range(own):
        at = pl.ds(i * PAIR, PAIR)
        prob = p2o[i]
        squares = by_head(jnp.sum(prob * prob, axis=1, keepdims=True), jnp.sum)
        d_start = dz[i].T
        inner = by_head(jnp.sum(d_start * prob, axis=1, keepdims=True), jnp.sum)
        d_prob = dp[i] + d_start / squares - 2.0 * prob * inner / (squares * squares)
        gs = prob * (d_prob - jnp.sum(prob * d_prob, axis=1, keepdims=True))
        gs = split(gs)
        here = lanes(my_pair + i)
        lq, lk = apart(landq[my_seq, :, here]), apart(landk[my_seq, :, here])
        query = together(nn(gs[0], lk) + nn(gs[1], lk)) * scale
        key = together(tn(gs[0], lq) + tn(gs[1], lq)) * scale
        both = [x.reshape(size, land_local, PAIR) for x in (query, key)]
        both = jnp.concatenate(both, axis=1).reshape(chips, 2, 2 * land_local, PAIR)
        lpart[:, :, my_seq, :, here] = (lpart[:, :, my_seq, :, here].astype(F32) + both).astype(BF)
    land_sib = group.go(4, chips, lpart.at[:, 1 - my_core], lsum, sibling)
    land_sib.wait_recv()

    def add_lands(i, carry):
        lsum[i] = lsum[i] + lpart[i, my_core]
        return carry

    lax.fori_loop(0, chips, add_lands, 0)
    lpr[my_line] = lsum[my_line]
    land_in = []
    for kk, device in enumerate(group.line_peers()):
        land_in.append(group.go(4, kk, lsum.at[device[1] // 2], lpr.at[my_line], device))
    open_weight(r_v, 0)
    for copy in land_in:
        copy.wait_recv()

    r_down.step_three()
    def close(s, carry):
        for p in range(pairs):
            at = lanes(p)
            total = lpr[0, s, :, at].astype(F32)
            for src in range(1, chips):
                total = total + lpr[src, s, :, at].astype(F32)
            total = total * (1.0 / seg)
            spread = [
                jnp.concatenate(
                    [jnp.broadcast_to(x[i : i + 1], (seg, PAIR)) for i in range(land_local)], axis=0
                )
                for x in (total[:land_local], total[land_local:])
            ]
            rows = pl.ds(pl.multiple_of(s * length, length), length)
            grad[rows, at] = (gq[s, :, at] + spread[0]).astype(BF)
            key_at = pl.ds(width + p * PAIR, PAIR)
            grad[rows, key_at] = (grad[rows, key_at].astype(F32) + spread[1]).astype(BF)
        return carry

    lax.fori_loop(0, n_seq, close, 0)
    open_weight(r_q, 1)
    r_v.step_one()
    open_weight(r_k, 2)
    r_q.step_one()
    r_up.step_three()

    loaded(14, 17)
    def column_sums(base):
        total = jnp.zeros((1, width), F32)
        for s in range(n_seq):
            x = grad[s * length : (s + 1) * length, base : base + width].astype(F32)
            total = total + jnp.sum(x, axis=0, keepdims=True)
        return total

    count = vec_rows.shape[0]
    which = lax.broadcasted_iota(jnp.int32, (count, width), 0)
    table_rows = vec_rows[...]
    table_rows = jnp.where(which == 0, column_sums(0), table_rows)
    table_rows = jnp.where(which == 1, column_sums(2 * width), table_rows)
    table_rows = jnp.concatenate([table_rows, jnp.zeros((PAIR - count, width), F32)], axis=0)
    left = table_rows.T
    sums = tapg[:, 0, :]
    for b in range(1, 8):
        sums = sums + pltpu.roll(tapg[:, b, :], PAIR - b, 1)
    shard = r_small.rows
    sums = jnp.concatenate([sums, jnp.zeros((shard - sums.shape[0], PAIR), F32)], axis=0)
    right = jnp.broadcast_to(sums[None], (width // shard, shard, PAIR)).reshape(width, PAIR)
    zero = net.core == 0
    r_small.acc[...] = jnp.where(zero, left, right)
    small_box[...] = jnp.where(zero, right, left)
    r_small.open(small_box)
    r_v.step_two()
    r_k.step_one()
    r_out.step_three()
    r_down.step_four()

    def inputs(i, carry):
        step = 2 * PAIR
        rows = pl.ds(pl.multiple_of(i * step, step), step)
        for at in range(0, width, step):
            x = nt(grad[rows, :], f_qkv[at : at + step, :])
            out = x + resid[rows, at : at + step]
            input_grad[rows, at : at + step] = out.astype(BF)
        return carry

    lax.fori_loop(0, tokens.shape[0] // (2 * PAIR), inputs, 0)
    r_small.step_one()
    r_q.step_two()
    r_k.step_two()
    r_v.step_three()
    r_small.step_two()
    r_up.step_four()
    r_q.step_three()
    r_k.step_three()
    r_out.step_four()
    r_v.step_four()
    r_small.step_three()
    r_q.step_four()
    r_k.step_four()
    r_small.step_four()
    for piece in pieces:
        piece.close()
    halo_sent()
    group.finish()
    net.finish()


def back(
    ga, tokens, resid, f_qkv, vec_rows, taps, d_down, d_up, d_out, kept, shards, seq_size, reach
):
    q = kept[0]
    n_seq, length, width = q.shape
    pairs = width // PAIR
    units = n_seq * pairs
    own = units // seq_size
    line_size = seq_size // 2
    vmem, hbm = pl.BlockSpec(memory_space=pltpu.VMEM), pl.BlockSpec(memory_space=pltpu.HBM)
    shape = jax.ShapeDtypeStruct
    part = 2 * LAND // seq_size
    s_qkv, s_out, s_up, s_down = [shape(x.shape, F32) for x in shards]
    s_small = shape((s_qkv.shape[0], 2 * PAIR), F32)
    bufs = []
    for x in (s_down, s_up, s_out):
        bufs += scatter_scratch(x.shape[0], x.shape[1] // 2, BF, line_size)
    for _ in range(3):
        bufs += scatter_scratch(s_qkv.shape[0], width // 2, BF, line_size)
    bufs += scatter_scratch(s_qkv.shape[0], PAIR, F32, line_size)
    return pl.pallas_call(
        functools.partial(back_kernel, reach, 2 * reach + 1),
        out_shape=[shape(tokens.shape, BF), s_qkv, s_out, s_up, s_down, s_small],
        in_specs=[hbm] * 5 + [vmem] + [hbm] * 15,
        out_specs=[vmem] * 6,
        scratch_shapes=[
            pltpu.VMEM((n_seq * length, 3 * width), BF),
            pltpu.VMEM((2 * pairs, 8, PAIR), F32),
            pltpu.VMEM((pairs, 4 * length, length + 2 * reach), BF),
            pltpu.VMEM((width, n_seq * length), BF),
            pltpu.VMEM((3, width, width // 2), BF),
            pltpu.VMEM((width, PAIR), F32),
            pltpu.VMEM((n_seq, length + 2 * reach, width), BF),
            pltpu.VMEM((n_seq, LAND, width), BF),
            pltpu.VMEM((seq_size // 2, LAND, own * PAIR), BF),
            pltpu.VMEM((units, PAIR, length), BF),
            pltpu.VMEM((n_seq, LAND, width), BF),
            pltpu.VMEM((seq_size, 8, PAIR), F32),
            pltpu.VMEM((PAIR, PAIR), F32),
            pltpu.VMEM((n_seq, length, width), F32),
            pltpu.VMEM((n_seq, length, width), F32),
            pltpu.VMEM((n_seq, LAND, width), F32),
            pltpu.VMEM((seq_size // 2, 2, n_seq, part, width), BF),
            pltpu.VMEM((seq_size // 2, n_seq, part, width), BF),
            pltpu.VMEM((seq_size // 2, n_seq, part, width), BF),
            pltpu.VMEM((n_seq, LAND, own * PAIR), BF),
            pltpu.VMEM((n_seq, LAND, own * PAIR), BF),
            pltpu.VMEM((own, PAIR, PAIR), F32),
            pltpu.VMEM((own, PAIR, PAIR), F32),
            pltpu.VMEM((2 * pairs, length, 2 * PAIR), F32),
            pltpu.VMEM((LAND, own * PAIR), BF),
        ]
        + [pltpu.VMEM(x.shape, x.dtype) for x in (ga, tokens, resid, f_qkv, vec_rows, *kept)]
        + [pltpu.SemaphoreType.DMA((5 + len(kept),))]
        + bufs
        + [
            pltpu.SemaphoreType.DMA((7, line_size + SCATTER_SEMS)),
            pltpu.SemaphoreType.DMA((7, line_size + SCATTER_SEMS)),
            pltpu.SemaphoreType.DMA((7,)),
            pltpu.SemaphoreType.DMA((6, seq_size)),
            pltpu.SemaphoreType.DMA((6, seq_size)),
            pltpu.VMEM((2 * pairs, 2 * PAIR), F32),
        ],
        compiler_params=pltpu.CompilerParams(
            collective_id=1, has_side_effects=True, vmem_limit_bytes=61 * 1024 * 1024
        ),
        name="back",
    )(ga, tokens, resid, f_qkv, vec_rows, taps, d_down, d_up, d_out, *kept)


def update_kernel(rates, n_in, *refs):
    n_mat = len(rates) - 2
    homes, outs = refs[:n_in], refs[n_in : n_in + 3 * n_mat + 8]
    ins, sem = refs[n_in + 3 * n_mat + 8 : -1], refs[-1]
    own = 4 * n_mat + 7
    moves = []
    for i, (src, dst) in enumerate(zip(homes, ins)):
        moves.append(pltpu.make_async_copy(src, dst, sem.at[i]))
        moves[-1].start()
    passed = []

    def leave(src, out):
        passed.append(pltpu.make_async_copy(src, out, sem.at[n_in + len(passed)]))
        passed[-1].start()

    for i in range(n_mat):
        for move in moves[4 * i : 4 * i + 4]:
            move.wait()
        weight, first, second, grad = ins[4 * i : 4 * i + 4]
        new = adam_step(weight[...], first[...], second[...], grad[...], *rates[i])
        for place, value, out in zip((first, second, weight), new, outs[3 * i : 3 * i + 3]):
            place[...] = value
            leave(place, out)
    for i in range(n_in - own):
        moves[own + i].wait()
        leave(ins[own + i], outs[3 * n_mat + 6 + i])
    for move in moves[4 * n_mat : own]:
        move.wait()
    small = ins[4 * n_mat]
    vec, tap = ins[own - 6 : own - 3], ins[own - 3 : own]
    rows, count = vec[0].shape
    grad = small[:, :PAIR].T[:rows, :count]
    new = adam_step(*[x[...] for x in vec], grad, *rates[n_mat])
    for out, value in zip(outs[3 * n_mat : 3 * n_mat + 3], new):
        out[...] = value
    heads, taps = tap[0].shape
    grad = small[:, PAIR:][:heads, :taps]
    new = adam_step(*[x[...] for x in tap], grad, *rates[n_mat + 1])
    for out, value in zip(outs[3 * n_mat + 3 : 3 * n_mat + 6], new):
        out[...] = value
    for move in passed:
        move.wait()


def update(matrices, small, vec, tap, others):
    decay = ((rate_matrix, decay_rate), (rate_output, decay_rate))
    rates = [decay[0], decay[1], decay[0], decay[0], (rate_vector, 0.0), (rate_taps, 0.0)]
    vmem = pl.BlockSpec(memory_space=pltpu.VMEM)
    shape = [jax.ShapeDtypeStruct(x[0].shape, F32) for x in (*matrices, vec, tap) for _ in range(3)]
    shape += [jax.ShapeDtypeStruct(x.shape, x.dtype) for x in others]
    args = [x for group in matrices for x in group] + [small, *vec, *tap]
    hbm = pl.BlockSpec(memory_space=pltpu.HBM)
    n_in = len(args) + len(others)
    return pl.pallas_call(
        functools.partial(update_kernel, rates, n_in),
        out_shape=shape,
        in_specs=[hbm] * n_in,
        out_specs=[hbm] * (3 * len(matrices)) + [vmem] * 6 + [hbm] * len(others),
        scratch_shapes=[pltpu.VMEM(x.shape, x.dtype) for x in (*args, *others)]
        + [pltpu.SemaphoreType.DMA((n_in + 3 * len(matrices) + len(others),))],
        compiler_params=pltpu.CompilerParams(vmem_limit_bytes=60 * 1024 * 1024),
        name="update",
    )(*args, *others)


def kernels_fit(args):
    tokens, _, *matrices = args[:6]
    taps = args[7]
    seq_size = lax.axis_size("seq")
    n_seq, length, width = tokens.shape
    units = n_seq * width // PAIR
    own = units // seq_size
    return (
        lax.axis_size("rows") == 4
        and seq_size == 8
        and all(x.shape[0] % 24 == 0 and x.shape[1] % 256 == 0 for x in matrices)
        and width // taps.shape[0] == PAIR // 2
        and length == PAIR
        and taps.shape[1] == 33
        and taps.shape[0] <= matrices[0].shape[0]
        and units == own * seq_size
        and seq_size == 2 * n_seq
        and width == 2 * own * PAIR
        and 2 * own <= 8
        and (width // PAIR) % own == 0
        and units % PINV_ITERS == 0
        and LAND == 8 * seq_size
        and matrices[2].shape[1] == 4 * width
        and args[6].shape[0] == 12
    )


def with_kernels(
    tokens, cotangent, qkv_weight, out_weight, up_weight, down_weight, vectors, taps,
    qkv_first, qkv_second, out_first, out_second, up_first, up_second, down_first, down_second,
    vec_first, vec_second, tap_first, tap_second,
):
    seq_count, local_len, model_width = tokens.shape
    head_count, tap_count = taps.shape
    seq_size = lax.axis_size("seq")
    reach = tap_count // 2
    row_count = seq_count * local_len
    matrices = (qkv_weight, out_weight, up_weight, down_weight)
    flat_in = tokens.reshape(row_count, model_width)
    layer_out, grad_resid_one, grad_attn, vec_rows, grad_down, grad_up, grad_out, full_qkv, *kept = (
        front(tokens, cotangent, matrices, vectors, taps, seq_size, reach)
    )
    input_grad, summed_qkv, summed_out, summed_up, summed_down, small = back(
        grad_attn.reshape(tokens.shape), flat_in, grad_resid_one, full_qkv, vec_rows, taps,
        grad_down, grad_up, grad_out,
        kept, matrices, seq_size, reach,
    )
    *new, out_tokens, input_grad = update(
        [
            (qkv_weight, qkv_first, qkv_second, summed_qkv),
            (out_weight, out_first, out_second, summed_out),
            (up_weight, up_first, up_second, summed_up),
            (down_weight, down_first, down_second, summed_down),
        ],
        small,
        (vectors, vec_first, vec_second),
        (taps, tap_first, tap_second),
        (layer_out, input_grad),
    )
    return (out_tokens.reshape(tokens.shape), input_grad.reshape(tokens.shape), *new)


def on_device(*args):
    return with_kernels(*args) if kernels_fit(args) else with_collectives(*args)


def solution(mesh):
    return jax.shard_map(
        on_device,
        mesh=mesh,
        in_specs=(
            P("rows", "seq", None),
            P("rows", "seq", None),
            P(("rows", "seq"), None),
            P(("rows", "seq"), None),
            P(("rows", "seq"), None),
            P(("rows", "seq"), None),
            P(None, ("rows", "seq")),
            P(),
            P(("rows", "seq"), None),
            P(("rows", "seq"), None),
            P(("rows", "seq"), None),
            P(("rows", "seq"), None),
            P(("rows", "seq"), None),
            P(("rows", "seq"), None),
            P(("rows", "seq"), None),
            P(("rows", "seq"), None),
            P(None, ("rows", "seq")),
            P(None, ("rows", "seq")),
            P(),
            P(),
        ),
        out_specs=(
            P("rows", "seq", None),
            P("rows", "seq", None),
            P(("rows", "seq"), None),
            P(("rows", "seq"), None),
            P(("rows", "seq"), None),
            P(("rows", "seq"), None),
            P(("rows", "seq"), None),
            P(("rows", "seq"), None),
            P(("rows", "seq"), None),
            P(("rows", "seq"), None),
            P(("rows", "seq"), None),
            P(("rows", "seq"), None),
            P(("rows", "seq"), None),
            P(("rows", "seq"), None),
            P(None, ("rows", "seq")),
            P(None, ("rows", "seq")),
            P(None, ("rows", "seq")),
            P(),
            P(),
            P(),
        ),
        check_vma=False,
    )
```
